128 devices in a mesh: dp: 32 (over x, z, core), head: 4 (over y).
Axes of the slice: x: 4, y: 4, z: 4, core: 2. Of those that a mesh axis runs over, the one named last changes fastest.
Arguments:
- layer_input: bfloat16 [96, 1024, 768], P('dp', 'head'), may hold values from -6 to 6
- lengths: int32 [96], P('dp'), may hold values from 64 to 1024, as said below
- cotangent: bfloat16 [96, 1024, 768], P('dp', 'head'), may hold values from -6 to 6
- w_query: bfloat16 [768, 768], replicated, may hold values from -0.21875 to 0.21875
- w_key: bfloat16 [768, 768], replicated, may hold values from -0.21875 to 0.21875
- w_value: bfloat16 [768, 768], replicated, may hold values from -0.21875 to 0.21875
- conv_query: float32 [3, 768], replicated, may hold values from -3 to 3
- conv_key: float32 [3, 768], replicated, may hold values from -3 to 3
- conv_value: float32 [3, 768], replicated, may hold values from -3 to 3
- w_out: bfloat16 [768, 768], replicated, may hold values from -1.75 to 1.75
- w_up: bfloat16 [768, 3072], replicated, may hold values from -0.21875 to 0.21875
- w_down: bfloat16 [3072, 768], replicated, may hold values from -0.109375 to 0.109375
- gain_attn: float32 [768], replicated, may hold values from 0.25 to 1.75
- bias_attn: float32 [768], replicated, may hold values from -1.5 to 1.5
- gain_ffn: float32 [768], replicated, may hold values from 0.25 to 1.75
- bias_ffn: float32 [768], replicated, may hold values from -1.5 to 1.5
Outputs:
- layer_output: bfloat16 [96, 1024, 768], P('dp', 'head')
- input_grad: float32 [96, 1024, 768], P('dp', 'head')
- grad_w_query: float32 [768, 768], replicated
- grad_w_key: float32 [768, 768], replicated
- grad_w_value: float32 [768, 768], replicated
- grad_conv_query: float32 [3, 768], replicated
- grad_conv_key: float32 [3, 768], replicated
- grad_conv_value: float32 [3, 768], replicated
- grad_w_out: float32 [768, 768], replicated
- grad_w_up: float32 [768, 3072], replicated
- grad_w_down: float32 [3072, 768], replicated
- grad_gain_attn: float32 [768], replicated
- grad_bias_attn: float32 [768], replicated
- grad_gain_ffn: float32 [768], replicated
- grad_bias_ffn: float32 [768], replicated
The draws below stay inside these ranges and needn't reach their ends.
Inputs may be any that keep to these rules, and one draw needn't show every extreme that they name: Of each 3 consecutive sequences (those of one index of dp) one, drawn from the seed, has length exactly 1024; the others follow a law heavily skewed toward short lengths.
All inputs are finite; a program needn't handle non-finite values.
Results may differ from the reference program's by a relative error of at most 0.013.
Values may be sent and summed in bfloat16 or wider, within the bound.
No kernel may reach another device: no remote copies, remote signals or barrier semaphores. Data moves between devices by JAX's collectives and lax.ppermute only.
A program may use at most 256 MiB of HBM per device.

```python
import jax
import jax.numpy as jnp
from jax import lax

D = 768
HEADS = 12
HDIM = 64
FF = 3072
LEN = 1024
SEQS = 3
SEQUENCES = 96


def draw_lengths(key, part):
    key = jax.random.fold_in(key, 7)
    lowest = max(LEN // 16, 1)
    length_span = LEN - lowest
    key_one, key_two, key_three, key_four = jax.random.split(key, 4)
    factor_one = jax.random.randint(key_one, (SEQUENCES,), 0, length_span + 1)
    factor_two = jax.random.randint(key_two, (SEQUENCES,), 0, length_span + 1)
    factor_three = jax.random.randint(key_three, (SEQUENCES,), 0, length_span + 1)
    tailed = lowest + factor_one * factor_two // max(length_span, 1) * factor_three // max(length_span, 1)
    longest = jax.random.randint(key_four, (SEQUENCES // SEQS,), 0, SEQS)
    slot_index = jnp.arange(SEQUENCES, dtype=jnp.int32) % SEQS
    chosen = slot_index == jnp.repeat(longest, SEQS)
    return jnp.where(chosen, LEN, tailed).astype(jnp.int32)


def shard_levels(key, dims, shards, low, largest):
    factor_of = 1.0
    for axis_at, parts in shards:
        draws = jax.random.uniform(jax.random.fold_in(jax.random.fold_in(key, 6), axis_at), (parts,), jnp.float32, low / len(shards), largest / len(shards))
        factor_of = factor_of * jnp.repeat(jnp.exp(draws), dims[axis_at] // parts).reshape((-1,) + (1,) * (len(dims) - 1 - axis_at))
    return factor_of


def noise(stream_key, extent, scale, limit, cuts=(), held_as=jnp.bfloat16):
    values = scale * jax.random.normal(stream_key, extent, jnp.float32)
    if cuts:
        values = values * shard_levels(stream_key, extent, cuts, -0.22, 0.18)
    return jnp.clip(values, -limit, limit).astype(held_as)


def setup_inputs(seed: int = 0) -> dict:
    key_of = jax.random.split(jax.random.key(seed), 17)
    return {
        "layer_input": noise(key_of[0], (SEQUENCES, LEN, D), 1.0, 6.0, ((0, 32), (1, 4))),
        "lengths": draw_lengths(jax.random.fold_in(key_of[16], 71), 0),
        "cotangent": noise(key_of[2], (SEQUENCES, LEN, D), 1.0, 6.0, ((0, 32), (1, 4))),
        "w_query": noise(key_of[3], (D, D), D ** -0.5, 0.21875),
        "w_key": noise(key_of[4], (D, D), D ** -0.5, 0.21875),
        "w_value": noise(key_of[5], (D, D), D ** -0.5, 0.21875),
        "conv_query": noise(key_of[6], (3, D), 0.6, 3.0, (), jnp.float32),
        "conv_key": noise(key_of[7], (3, D), 0.6, 3.0, (), jnp.float32),
        "conv_value": noise(key_of[8], (3, D), 0.6, 3.0, (), jnp.float32),
        "w_out": noise(key_of[9], (D, D), (D // 64) ** -0.5, 1.75),
        "w_up": noise(key_of[10], (D, FF), D ** -0.5, 0.21875),
        "w_down": noise(key_of[11], (FF, D), FF ** -0.5, 0.109375),
        "gain_attn": jnp.clip(1.0 + 0.15 * jax.random.normal(key_of[12], (D,), jnp.float32), 0.25, 1.75),
        "bias_attn": noise(key_of[13], (D,), 0.3, 1.5, (), jnp.float32),
        "gain_ffn": jnp.clip(1.0 + 0.15 * jax.random.normal(key_of[14], (D,), jnp.float32), 0.25, 1.75),
        "bias_ffn": noise(key_of[15], (D,), 0.3, 1.5, (), jnp.float32),
    }


@jax.custom_vjp
def low(v):
    return lax.optimization_barrier(v.astype(jnp.bfloat16)).astype(jnp.float32)

@jax.custom_vjp
def low_back(v):
    return v

def low_keep(v):
    return (low(v), None)

def low_pass(kept, grad):
    return (grad,)

def back_keep(v):
    return (v, None)

def back_low(kept, grad):
    return (low(grad),)
low.defvjp(low_keep, low_pass)
low_back.defvjp(back_keep, back_low)

def highest(left, right):
    return jnp.dot(left, right, precision=lax.Precision.HIGHEST)

def layer_norm(rows, gain, bias):
    average = lax.optimization_barrier(jnp.mean(rows, axis=-1, keepdims=True))
    centred = rows - average
    variance = lax.optimization_barrier(jnp.mean(centred * centred, axis=-1, keepdims=True))
    return centred * lax.rsqrt(variance + 1e-05) * gain + bias

def causal_conv(raw, kernel):
    shift_one = jnp.pad(raw, ((1, 0), (0, 0)))[:-1]
    shift_two = jnp.pad(raw, ((2, 0), (0, 0)))[:-2]
    return kernel[0] * raw + kernel[1] * shift_one + kernel[2] * shift_two

def forward(inputs, weights_in, row_mask):
    w_query, w_key, w_value, conv_query, conv_key, conv_value, w_out, w_up, w_down, gain_attn, bias_attn, gain_ffn, bias_ffn = weights_in
    normed = low(layer_norm(inputs, gain_attn, bias_attn))
    query_raw = low_back(low(highest(normed, w_query)))
    key_raw = low_back(low(highest(normed, w_key)))
    value_raw = low_back(low(highest(normed, w_value)))
    queries = low(causal_conv(query_raw, conv_query)).reshape(LEN, HEADS, HDIM)
    keys_all = low(causal_conv(key_raw, conv_key)).reshape(LEN, HEADS, HDIM)
    values_all = low(causal_conv(value_raw, conv_value)).reshape(LEN, HEADS, HDIM)
    scores = jnp.einsum('ihd,jhd->hij', queries, keys_all, precision=lax.Precision.HIGHEST)
    scores = low_back(scores * HDIM ** (-0.5))
    row_ids = lax.broadcasted_iota(jnp.int32, (LEN, LEN), 0)
    col_ids = lax.broadcasted_iota(jnp.int32, (LEN, LEN), 1)
    scores = jnp.where((col_ids <= row_ids)[None], scores, -1e+30)
    top = lax.optimization_barrier(jnp.max(scores, axis=-1, keepdims=True))
    expo = jnp.exp(scores - top)
    probs = low(expo / lax.optimization_barrier(jnp.sum(expo, axis=-1, keepdims=True)))
    mixed = jnp.einsum('hij,jhd->ihd', probs, values_all, precision=lax.Precision.HIGHEST).reshape(LEN, D)
    mixed = low_back(low(mixed))
    middle = inputs + low_back(highest(mixed, w_out))
    normed_ffn = low(layer_norm(middle, gain_ffn, bias_ffn))
    hidden = low_back(highest(normed_ffn, w_up))
    squared = low(jnp.square(jnp.maximum(hidden, 0.0)))
    ffn_out = low_back(highest(squared, w_down))
    return (middle + ffn_out) * row_mask

def reference(layer_input, lengths, cotangent, w_query, w_key, w_value, conv_query, conv_key, conv_value, w_out, w_up, w_down, gain_attn, bias_attn, gain_ffn, bias_ffn):
    weights = tuple((member.astype(jnp.float32) for member in (w_query, w_key, w_value, conv_query, conv_key, conv_value, w_out, w_up, w_down, gain_attn, bias_attn, gain_ffn, bias_ffn)))
    positions = jnp.arange(LEN, dtype=jnp.int32)

    def one_sequence(totals, element):
        seq_input, seq_cotangent, length = element
        row_mask = (positions < length).astype(jnp.float32)[:, None]

        def apply_layer(inputs, weights_in):
            return forward(inputs, weights_in, row_mask)
        result, pullback = jax.vjp(apply_layer, seq_input.astype(jnp.float32), weights)
        grad_input, grad_weights = pullback(seq_cotangent.astype(jnp.float32))
        totals = jax.tree.map(jnp.add, totals, grad_weights)
        return (totals, (result.astype(jnp.bfloat16), grad_input))
    initial = jax.tree.map(jnp.zeros_like, weights)
    totals, (layer_output, input_grad) = lax.scan(one_sequence, initial, (layer_input, cotangent, lengths))
    return (layer_output, input_grad, totals[0], totals[1], totals[2], totals[3], totals[4], totals[5], totals[6], totals[7], totals[8], totals[9], totals[10], totals[11], totals[12])
```

```python
import functools

import jax
import jax.numpy as jnp
from jax import lax
from jax.experimental import pallas as pl
from jax.experimental.pallas import tpu as pltpu
from jax.sharding import Mesh
from jax.sharding import PartitionSpec as P

HDIM = 64
GROUPS = 4
BLOCK = 256
FULL = 1024
WIDTH = 768
COLS = 192
FF = 3072
SEQS = 3
CHUNK = 512
HEADS_HERE = 3
PACK_ROWS = 640
F32 = jnp.float32
BF16 = jnp.bfloat16
NN = (((1,), (0,)), ((), ()))
NT = (((1,), (1,)), ((), ()))
TN = (((0,), (0,)), ((), ()))


def dot(left, right, dims):
    return lax.dot_general(left, right, dims, preferred_element_type=F32)


def cost(flops, nbytes, transcendentals=0):
    return pl.CostEstimate(
        flops=int(flops), bytes_accessed=int(nbytes), transcendentals=int(transcendentals)
    )


def vmem():
    return pl.BlockSpec(memory_space=pltpu.VMEM)


def params(mib):
    return pltpu.CompilerParams(vmem_limit_bytes=mib << 20)


def unit_rows(rows):
    average = jnp.mean(rows, axis=-1, keepdims=True)
    centred = rows - average
    variance = jnp.mean(centred * centred, axis=-1, keepdims=True)
    inverse = lax.rsqrt(variance + 1e-05)
    return centred * inverse, inverse


def head_masks():
    lane = lax.broadcasted_iota(jnp.int32, (1, COLS), 1)
    return [
        jnp.where((lane >= h * HDIM) & (lane < (h + 1) * HDIM), 1.0, 0.0).astype(F32)
        for h in range(HEADS_HERE)
    ]


def conv_rows(raw_f, taps, tap_row, start):
    total = taps[tap_row : tap_row + 1, :] * raw_f[8 + start : 8 + start + BLOCK, :]
    for m in (1, 2):
        total += (
            taps[tap_row + m : tap_row + m + 1, :]
            * raw_f[8 + start - m : 8 + start - m + BLOCK, :]
        )
    return total


def attend_kernel(
    info, x0, x1, x2_lo, x2_hi, x3, w_mine, taps, gain, bias,
    normed, raw_q, raw_k, raw_v, mixed, m0, m_next, m_prev, lse_t,
    pad_q, pad_k, pad_v, q_s, k_s, v_s, below,
):
    here, length = info[0], info[1]
    blocks = (length + BLOCK - 1) // BLOCK
    masks = head_masks()

    for piece, ahead, shift in ((x0, 0, 0), (x1, 1, 0), (x2_lo, 2, 0), (x2_hi, 2, 128), (x3, 3, 0)):
        home = lax.rem(here + ahead, GROUPS)
        size = piece.shape[-2]

        @pl.when(home < blocks)
        def _(piece=piece, home=home, shift=shift, size=size):
            rows = piece[...].reshape(size, WIDTH).astype(F32)
            unit, _ = unit_rows(rows)
            low = (unit * gain[...] + bias[...]).astype(BF16)
            at = pl.multiple_of(home * BLOCK + shift, 128)
            normed[pl.ds(at, size), :] = low
            for n, (raw, pad) in enumerate(((raw_q, pad_q), (raw_k, pad_k), (raw_v, pad_v))):
                value = dot(low, w_mine[n * COLS : (n + 1) * COLS, :], NT).astype(BF16)
                raw[pl.ds(at, size), :] = value
                pad[pl.ds(at + 8, size), :] = value.astype(F32)

    for pad in (pad_q, pad_k, pad_v):
        pad[0:8, :] = jnp.zeros((8, COLS), F32)
    row = lax.broadcasted_iota(jnp.int32, (BLOCK, BLOCK), 0)
    col = lax.broadcasted_iota(jnp.int32, (BLOCK, BLOCK), 1)
    below[...] = jnp.where(col <= row, 0.0, -1e30).astype(F32)

    for b in range(GROUPS):

        @pl.when(b < blocks)
        def _(b=b):
            at = slice(b * BLOCK, (b + 1) * BLOCK)
            q_s[at, :] = (conv_rows(pad_q, taps, 0, b * BLOCK).astype(BF16).astype(F32) * 0.125).astype(BF16)
            k_s[at, :] = conv_rows(pad_k, taps, 3, b * BLOCK).astype(BF16)
            v_s[at, :] = conv_rows(pad_v, taps, 6, b * BLOCK).astype(BF16)
            reach = (b + 1) * BLOCK
            lane = lax.broadcasted_iota(jnp.int32, (BLOCK, 128), 1)
            total_out = jnp.zeros((BLOCK, COLS), F32)
            logs = jnp.zeros((BLOCK, 128), F32)
            for h in range(HEADS_HERE):
                q_h = q_s[at, :] * masks[h].astype(BF16)
                diag = dot(q_h, k_s[at, :], NT) + below[...]
                top = jnp.max(diag, axis=-1, keepdims=True)
                if b:
                    left = dot(q_h, k_s[0 : b * BLOCK, :], NT)
                    top = jnp.maximum(top, jnp.max(left, axis=-1, keepdims=True))
                    expo_left = jnp.exp(left - top)
                expo = jnp.exp(diag - top)
                total = jnp.sum(expo, axis=-1, keepdims=True)
                out = dot(expo.astype(BF16), v_s[at, :], NN)
                if b:
                    total += jnp.sum(expo_left, axis=-1, keepdims=True)
                    out += dot(expo_left.astype(BF16), v_s[0 : b * BLOCK, :], NN)
                total_out = total_out + (out * masks[h]) * (1.0 / total)
                logs = jnp.where(lane == h, top + jnp.log(total), logs)
            mixed[at, :] = total_out.astype(BF16)
            lse_t[:, at] = jnp.transpose(logs)[0:8, :]

        @pl.when(b >= blocks)
        def _(b=b):
            mixed[b * BLOCK : (b + 1) * BLOCK, :] = jnp.zeros((BLOCK, COLS), BF16)

    def rows_of(ahead, shift, size):
        at = pl.multiple_of(lax.rem(here + ahead, GROUPS) * BLOCK + shift, 128)
        return mixed[pl.ds(at, size), :]

    m0[...] = rows_of(0, 0, BLOCK)
    m_next[0:BLOCK, :] = rows_of(1, 0, BLOCK)
    m_next[BLOCK:, :] = rows_of(2, 0, 128)
    m_prev[0:BLOCK, :] = rows_of(3, 0, BLOCK)
    m_prev[BLOCK:, :] = rows_of(2, 128, 128)


def attend(info, pieces, w_mine, taps, gain, bias):
    low = lambda *shape: jax.ShapeDtypeStruct(shape, BF16)
    return pl.pallas_call(
        attend_kernel,
        out_shape=(
            low(FULL, WIDTH),
            low(FULL, COLS), low(FULL, COLS), low(FULL, COLS),
            low(FULL, COLS),
            low(BLOCK, COLS), low(BLOCK + 128, COLS), low(BLOCK + 128, COLS),
            jax.ShapeDtypeStruct((8, FULL), F32),
        ),
        in_specs=[pl.BlockSpec(memory_space=pltpu.SMEM)] + [vmem()] * 9,
        out_specs=[vmem()] * 9,
        scratch_shapes=[pltpu.VMEM((FULL + 8, COLS), F32)] * 3
        + [pltpu.VMEM((FULL, COLS), BF16)] * 3
        + [pltpu.VMEM((BLOCK, BLOCK), F32)],
        compiler_params=params(40),
        cost_estimate=cost(3e9, 8e6, 2e6),
        name="attend",
    )(info, *pieces, w_mine, taps, gain, bias)


def attend_back_kernel(
    first, last,
    info, g0, g_next, g_over, g_prev, g_under, normed, raw_q, raw_k, raw_v, mixed, lse_t,
    w_mine, taps, gain, bias, ffn_vectors, dw_in, small_in,
    d0, d_next, d_prev, dw_out, small_out, *scratch,
):
    if last:
        pack_out, scratch = scratch[0], scratch[1:]
    pad_q, pad_k, pad_v, q_s, k_s, v_s, g_s, dq_s, dk_s, dv_s, d_all, below = scratch
    here, length = info[0], info[1]
    blocks = (length + BLOCK - 1) // BLOCK
    masks = head_masks()

    for piece, start, ahead, shift, size in (
        (g0, 0, 0, 0, BLOCK),
        (g_next, 0, 3, 0, BLOCK),
        (g_over, 0, 2, 0, 128),
        (g_prev, 0, 1, 0, BLOCK),
        (g_under, 0, 2, 128, 128),
    ):
        at = pl.multiple_of(lax.rem(here + ahead, GROUPS) * BLOCK + shift, 128)
        g_s[pl.ds(at, size), :] = piece[start : start + size, :]

    row = lax.broadcasted_iota(jnp.int32, (BLOCK, BLOCK), 0)
    col = lax.broadcasted_iota(jnp.int32, (BLOCK, BLOCK), 1)
    below[...] = jnp.where(row <= col, 0.0, -1e30).astype(F32)
    for pad, raw in ((pad_q, raw_q), (pad_k, raw_k), (pad_v, raw_v)):
        pad[0:8, :] = jnp.zeros((8, COLS), F32)
    for total in (dq_s, dk_s, dv_s):
        total[...] = jnp.zeros((FULL + 8, COLS), F32)

    for b in range(GROUPS):

        @pl.when(b < blocks)
        def _(b=b):
            at = slice(b * BLOCK, (b + 1) * BLOCK)
            for pad, raw in ((pad_q, raw_q), (pad_k, raw_k), (pad_v, raw_v)):
                pad[8 + b * BLOCK : 8 + (b + 1) * BLOCK, :] = raw[at, :].astype(F32)
            q_s[at, :] = (conv_rows(pad_q, taps, 0, b * BLOCK).astype(BF16).astype(F32) * 0.125).astype(BF16)
            k_s[at, :] = conv_rows(pad_k, taps, 3, b * BLOCK).astype(BF16)
            v_s[at, :] = conv_rows(pad_v, taps, 6, b * BLOCK).astype(BF16)
            g_here = g_s[at, :]
            both = jnp.transpose(g_here.astype(F32) * mixed[at, :].astype(F32))
            dq_total = jnp.zeros((BLOCK, COLS), F32)
            for h in range(HEADS_HERE):
                mask_low = masks[h].astype(BF16)
                q_h = q_s[at, :] * mask_low
                g_h = g_here * mask_low
                row_dot = jnp.sum(both[h * HDIM : (h + 1) * HDIM, :], axis=0, keepdims=True)
                log_row = lse_t[h : h + 1, at]
                dq_h = jnp.zeros((BLOCK, COLS), F32)
                for j in range(b + 1):
                    keys = slice(j * BLOCK, (j + 1) * BLOCK)
                    scores = dot(k_s[keys, :], q_h, NT)
                    if j == b:
                        scores = scores + below[...]
                    probs = jnp.exp(scores - log_row)
                    grad_probs = dot(v_s[keys, :], g_h, NT)
                    grad_scores = (probs * (grad_probs - row_dot)).astype(BF16)
                    dv_s[keys, :] += dot(probs.astype(BF16), g_h, NN)
                    dk_s[keys, :] += dot(grad_scores, q_h, NN)
                    dq_h += dot(grad_scores, k_s[keys, :], TN)
                dq_total += dq_h * masks[h]
            dq_s[at, :] = dq_total * 0.125

    if first:
        dw_out[...] = jnp.zeros_like(dw_out)
        small_out[...] = jnp.zeros_like(small_out)
    else:
        dw_out[...] = dw_in[...]
        small_out[...] = small_in[...]

    for b in range(GROUPS):

        @pl.when(b < blocks)
        def _(b=b):
            start = b * BLOCK
            at = slice(start, start + BLOCK)
            parts = []
            for n, (pad, grad) in enumerate(((pad_q, dq_s), (pad_k, dk_s), (pad_v, dv_s))):
                now = grad[at, :]
                value = taps[3 * n : 3 * n + 1, :] * now
                for m in (1, 2):
                    value += taps[3 * n + m : 3 * n + m + 1, :] * grad[start + m : start + m + BLOCK, :]
                parts.append(value.astype(BF16))
                for m in range(3):
                    shifted = pad[8 + start - m : 8 + start - m + BLOCK, :]
                    small_out[3 * n + m : 3 * n + m + 1, 0:COLS] += jnp.sum(
                        shifted * now, axis=0, keepdims=True
                    )
            joined = jnp.concatenate(parts, axis=1)
            d_all[at, :] = joined
            small_out[9:10, 0 : 3 * COLS] += jnp.sum(joined.astype(F32), axis=0, keepdims=True)
            dw_out[...] += dot(joined, normed[at, :], TN)

        @pl.when(b >= blocks)
        def _(b=b):
            d_all[b * BLOCK : (b + 1) * BLOCK, :] = jnp.zeros((BLOCK, 3 * COLS), BF16)

    def rows_of(ahead, shift, size):
        at = pl.multiple_of(lax.rem(here + ahead, GROUPS) * BLOCK + shift, 128)
        return d_all[pl.ds(at, size), :]

    d0[...] = rows_of(0, 0, BLOCK)
    d_next[0:BLOCK, :] = rows_of(1, 0, BLOCK)
    d_next[BLOCK:, :] = rows_of(2, 0, 128)
    d_prev[0:BLOCK, :] = rows_of(3, 0, BLOCK)
    d_prev[BLOCK:, :] = rows_of(2, 128, 128)

    if last:
        sums = small_out[9:10, 0 : 3 * COLS]
        high = sums.astype(BF16)
        rest = (sums - high.astype(F32)).astype(BF16)
        grad_bias = dot(jnp.broadcast_to(high, (8, 3 * COLS)), w_mine[...], NN)[0:1, :]
        grad_bias += dot(jnp.broadcast_to(rest, (8, 3 * COLS)), w_mine[...], NN)[0:1, :]
        grad_normed = jnp.sum(w_mine[...].astype(F32) * dw_out[...], axis=0, keepdims=True)
        grad_gain = (grad_normed - bias[...] * grad_bias) / gain[...]
        pack_out[0 : 3 * COLS, :] = dw_out[...].astype(BF16)
        tail = jnp.concatenate(
            [
                small_out[0:9, :],
                grad_gain,
                grad_bias,
                ffn_vectors[0:2, :],
                jnp.zeros((3, WIDTH), F32),
            ],
            axis=0,
        )
        pack_out[3 * COLS : 3 * COLS + 16, :] = tail.astype(BF16)
        pack_out[3 * COLS + 16 :, :] = jnp.zeros((PACK_ROWS - 3 * COLS - 16, WIDTH), BF16)


def attend_back(first, last, info, grads, saved, w_mine, taps, gain, bias, ffn_vectors, dw, small):
    low = lambda *shape: jax.ShapeDtypeStruct(shape, BF16)
    full = lambda *shape: jax.ShapeDtypeStruct(shape, F32)
    out_shape = [
        low(BLOCK, 3 * COLS), low(BLOCK + 128, 3 * COLS), low(BLOCK + 128, 3 * COLS),
        full(3 * COLS, WIDTH), full(16, WIDTH),
    ]
    if last:
        out_shape.append(low(PACK_ROWS, WIDTH))
    return pl.pallas_call(
        functools.partial(attend_back_kernel, first, last),
        out_shape=out_shape,
        in_specs=[pl.BlockSpec(memory_space=pltpu.SMEM)] + [vmem()] * 18,
        out_specs=[vmem()] * len(out_shape),
        scratch_shapes=[pltpu.VMEM((FULL + 8, COLS), F32)] * 3
        + [pltpu.VMEM((FULL, COLS), BF16)] * 4
        + [pltpu.VMEM((FULL + 8, COLS), F32)] * 3
        + [pltpu.VMEM((FULL, 3 * COLS), BF16)]
        + [pltpu.VMEM((BLOCK, BLOCK), F32)],
        compiler_params=params(48),
        cost_estimate=cost(5e9, 1.2e7, 2e6),
        name="attend_back",
    )(info, *grads, *saved, w_mine, taps, gain, bias, ffn_vectors, dw, small)


def ffn_kernel(
    info, x, cotangent, *refs,
):
    pieces, refs = refs[: 5 * SEQS], refs[5 * SEQS :]
    (
        w_out, gain, bias, w_up, w_down,
        layer_output, grad_middle, g0, g_next, g_prev,
        send, keep, send_out, keep_out, vectors,
        middle, normed, low_grad, total_out, total_grad, sq_s, gh_s, branch, dw_out, mixed_s,
    ) = refs
    step = pl.program_id(0)
    here, core = info[0], info[1]

    def w_out_rows(ahead):
        at = pl.multiple_of(lax.rem(here + ahead, GROUPS) * COLS, 64)
        return pl.ds(at, COLS)

    @pl.when(step == 0)
    def _():
        for s in range(SEQS):
            at = slice(s * BLOCK, (s + 1) * BLOCK)
            m0, m_next, m_over, m_prev, m_under = pieces[5 * s : 5 * s + 5]
            mixed_s[0, at, :] = m0[...]
            mixed_s[3, at, :] = m_next[0:BLOCK, :]
            mixed_s[2, s * BLOCK : s * BLOCK + 128, :] = m_over[...]
            mixed_s[2, s * BLOCK + 128 : (s + 1) * BLOCK, :] = m_under[...]
            mixed_s[1, at, :] = m_prev[0:BLOCK, :]
            value = x[s].astype(F32)
            for k in range(GROUPS):
                value += dot(mixed_s[k, at, :], w_out[w_out_rows(k), :], NN)
            middle[at, :] = value
            unit, _ = unit_rows(value)
            normed[at, :] = (unit * gain[...] + bias[...]).astype(BF16)
            position = here * BLOCK + lax.broadcasted_iota(jnp.int32, (BLOCK, 1), 0)
            keep_row = position < info[2 + s]
            low_grad[at, :] = jnp.where(keep_row, cotangent[s].astype(F32), 0.0).astype(BF16)
            total_out[at, :] = jnp.zeros((BLOCK, WIDTH), F32)
            total_grad[at, :] = jnp.zeros((BLOCK, WIDTH), F32)

    for s in range(SEQS):
        at = slice(s * BLOCK, (s + 1) * BLOCK)
        hidden = jnp.maximum(dot(normed[at, :], w_up[...], NN), 0.0)
        squared = (hidden * hidden).astype(BF16)
        sq_s[at, :] = squared
        total_out[at, :] += dot(squared, w_down[...], NN)
        back = dot(low_grad[at, :], w_down[...], NT)
        grad_hidden = (back * 2.0 * hidden).astype(BF16)
        gh_s[at, :] = grad_hidden
        total_grad[at, :] += dot(grad_hidden, w_up[...], NT)
    grad_up = dot(gh_s[...], normed[...], TN).astype(BF16)
    grad_down = dot(sq_s[...], low_grad[...], TN).astype(BF16)

    @pl.when(step < 3)
    def _():
        send[0] = grad_up
        send[1] = grad_down

    @pl.when(step >= 3)
    def _():
        keep[0] = grad_up
        keep[1] = grad_down

    @pl.when(step == 5)
    def _():
        sum_gain = jnp.zeros((1, WIDTH), F32)
        sum_bias = jnp.zeros((1, WIDTH), F32)
        for s in range(SEQS):
            at = slice(s * BLOCK, (s + 1) * BLOCK)
            position = here * BLOCK + lax.broadcasted_iota(jnp.int32, (BLOCK, 1), 0)
            keep_row = position < info[2 + s]
            layer_output[s] = jnp.where(keep_row, middle[at, :] + total_out[at, :], 0.0).astype(BF16)
            unit, inverse = unit_rows(middle[at, :])
            grad_normed = total_grad[at, :]
            scaled = grad_normed * gain[...]
            mean_grad = jnp.mean(scaled, axis=-1, keepdims=True)
            mean_dot = jnp.mean(scaled * unit, axis=-1, keepdims=True)
            value = low_grad[at, :].astype(F32) + inverse * (scaled - mean_grad - unit * mean_dot)
            sum_gain += jnp.sum(grad_normed * unit, axis=0, keepdims=True)
            sum_bias += jnp.sum(grad_normed, axis=0, keepdims=True)
            grad_middle[s] = value
            branch[at, :] = value.astype(BF16)
            low = branch[at, :]
            g0[s] = dot(low, w_out[w_out_rows(0), :], NT).astype(BF16)
            g_next[s, 0:BLOCK, :] = dot(low, w_out[w_out_rows(1), :], NT).astype(BF16)
            over = dot(low, w_out[w_out_rows(2), :], NT).astype(BF16)
            g_next[s, BLOCK:, :] = over[0:128]
            g_prev[s, BLOCK:, :] = over[128:]
            g_prev[s, 0:BLOCK, :] = dot(low, w_out[w_out_rows(3), :], NT).astype(BF16)
        vectors[...] = jnp.concatenate(
            [sum_gain, sum_bias, jnp.zeros((6, WIDTH), F32)], axis=0
        )
        for k in range(GROUPS):
            dw_out[w_out_rows(k), :] = dot(mixed_s[k], branch[...], TN).astype(BF16)
        half = WIDTH // 2
        keep_out[...] = dw_out[pl.ds(pl.multiple_of(core * half, 128), half), :]
        send_out[...] = dw_out[pl.ds(pl.multiple_of((1 - core) * half, 128), half), :]


def ffn(info, x, cotangent, pieces, w_out, gain, bias, w_up, w_down):
    low = lambda *shape: jax.ShapeDtypeStruct(shape, BF16)
    full = lambda *shape: jax.ShapeDtypeStruct(shape, F32)
    rows = SEQS * BLOCK
    steps = FF // CHUNK
    half = steps // 2

    def chunk(i, sc):
        side = jnp.where(i < half, 1 - sc[1], sc[1])
        return side * half + lax.rem(i, half)

    whole = lambda shape: pl.BlockSpec(shape, lambda i, sc: (0,) * len(shape))
    piece_shapes = [p.shape for p in pieces]
    grid_spec = pltpu.PrefetchScalarGridSpec(
        num_scalar_prefetch=1,
        grid=(steps,),
        in_specs=[whole((SEQS, BLOCK, WIDTH)), whole((SEQS, BLOCK, WIDTH))]
        + [whole(s) for s in piece_shapes]
        + [
            whole((WIDTH, WIDTH)), whole((1, WIDTH)), whole((1, WIDTH)),
            pl.BlockSpec((WIDTH, CHUNK), lambda i, sc: (0, chunk(i, sc))),
            pl.BlockSpec((CHUNK, WIDTH), lambda i, sc: (chunk(i, sc), 0)),
        ],
        out_specs=[
            whole((SEQS, BLOCK, WIDTH)), whole((SEQS, BLOCK, WIDTH)),
            whole((SEQS, BLOCK, COLS)), whole((SEQS, BLOCK + 128, COLS)), whole((SEQS, BLOCK + 128, COLS)),
            pl.BlockSpec((2, CHUNK, WIDTH), lambda i, sc: (0, jnp.minimum(i, half - 1), 0)),
            pl.BlockSpec((2, CHUNK, WIDTH), lambda i, sc: (0, jnp.maximum(i - half, 0), 0)),
            whole((WIDTH // 2, WIDTH)), whole((WIDTH // 2, WIDTH)),
            whole((8, WIDTH)),
        ],
        scratch_shapes=[
            pltpu.VMEM((rows, WIDTH), F32),
            pltpu.VMEM((rows, WIDTH), BF16),
            pltpu.VMEM((rows, WIDTH), BF16),
            pltpu.VMEM((rows, WIDTH), F32),
            pltpu.VMEM((rows, WIDTH), F32),
            pltpu.VMEM((rows, CHUNK), BF16),
            pltpu.VMEM((rows, CHUNK), BF16),
            pltpu.VMEM((rows, WIDTH), BF16),
            pltpu.VMEM((WIDTH, WIDTH), BF16),
            pltpu.VMEM((GROUPS, rows, COLS), BF16),
        ],
    )
    return pl.pallas_call(
        ffn_kernel,
        grid_spec=grid_spec,
        out_shape=(
            low(SEQS, BLOCK, WIDTH), full(SEQS, BLOCK, WIDTH),
            low(SEQS, BLOCK, COLS), low(SEQS, BLOCK + 128, COLS), low(SEQS, BLOCK + 128, COLS),
            low(2, FF // 2, WIDTH), low(2, FF // 2, WIDTH),
            low(WIDTH // 2, WIDTH), low(WIDTH // 2, WIDTH),
            full(8, WIDTH),
        ),
        compiler_params=params(60),
        cost_estimate=cost(2.4e10, 3e7),
        name="ffn",
    )(info, x, cotangent, *pieces, w_out, gain, bias, w_up, w_down)


def input_kernel(s, info, x, grad_middle, d0, d_next, d_over, d_prev, d_under, w_groups, gain, *rest):
    out = rest[-1]
    here = info[0]

    def w_of(ahead):
        return w_groups[lax.rem(here + ahead, GROUPS)]

    unit, inverse = unit_rows(x[0].astype(F32))
    over = jnp.concatenate([d_over[...], d_under[...]], axis=0)
    grad_normed = dot(d0[...], w_of(0), NN)
    grad_normed += dot(d_next[0:BLOCK, :], w_of(3), NN)
    grad_normed += dot(d_prev[0:BLOCK, :], w_of(1), NN)
    grad_normed += dot(over, w_of(2), NN)
    scaled = grad_normed * gain[...]
    mean_grad = jnp.mean(scaled, axis=-1, keepdims=True)
    mean_dot = jnp.mean(scaled * unit, axis=-1, keepdims=True)
    out[0] = grad_middle[0] + inverse * (scaled - mean_grad - unit * mean_dot)


def input_grad_of(s, info, x, grad_middle, pieces, w_groups, gain, earlier):
    one = lambda: pl.BlockSpec((1, BLOCK, WIDTH), lambda i, sc: (s, 0, 0))
    whole = lambda shape: pl.BlockSpec(shape, lambda i, sc: (0,) * len(shape))
    extra = [] if earlier is None else [earlier]
    return pl.pallas_call(
        functools.partial(input_kernel, s),
        grid_spec=pltpu.PrefetchScalarGridSpec(
            num_scalar_prefetch=1,
            grid=(1,),
            in_specs=[one(), one()]
            + [whole(p.shape) for p in pieces]
            + [whole(w_groups.shape), whole((1, WIDTH))]
            + [pl.BlockSpec(memory_space=pl.ANY)] * len(extra),
            out_specs=one(),
        ),
        out_shape=jax.ShapeDtypeStruct((SEQS, BLOCK, WIDTH), F32),
        input_output_aliases={} if earlier is None else {10: 0},
        compiler_params=params(40),
        cost_estimate=cost(1e9, 6e6),
        name="input_grad",
    )(info, x, grad_middle, *pieces, w_groups, gain, *extra)


def place_kernel(info, up_a, down_a, out_a, up_b, down_b, out_b, grad_up, grad_down, grad_out):
    mine = (pl.program_id(0) // 3) == info[1]

    @pl.when(mine)
    def _():
        grad_up[...] = jnp.transpose(up_a[...].astype(F32))
        grad_down[...] = down_a[...].astype(F32)
        grad_out[...] = out_a[...].astype(F32)

    @pl.when(jnp.logical_not(mine))
    def _():
        grad_up[...] = jnp.transpose(up_b[...].astype(F32))
        grad_down[...] = down_b[...].astype(F32)
        grad_out[...] = out_b[...].astype(F32)


def place(info, own, other):
    half = FF // CHUNK // 2

    def spec(rows, base, is_own):
        def index(i, sc):
            mine = (i // half) == sc[1] if is_own else (i // half) != sc[1]
            first = jnp.where(i < half, 0, half - 1)
            return (base + jnp.where(mine, lax.rem(i, half), first), 0)

        return pl.BlockSpec((rows, WIDTH), index)

    def three(is_own):
        return [spec(CHUNK, 0, is_own), spec(CHUNK, half, is_own), spec(128, 24, is_own)]

    return pl.pallas_call(
        place_kernel,
        grid_spec=pltpu.PrefetchScalarGridSpec(
            num_scalar_prefetch=1,
            grid=(2 * half,),
            in_specs=three(True) + three(False),
            out_specs=[
                pl.BlockSpec((WIDTH, CHUNK), lambda i, sc: (0, i)),
                pl.BlockSpec((CHUNK, WIDTH), lambda i, sc: (i, 0)),
                pl.BlockSpec((128, WIDTH), lambda i, sc: (i, 0)),
            ],
        ),
        out_shape=(
            jax.ShapeDtypeStruct((WIDTH, FF), F32),
            jax.ShapeDtypeStruct((FF, WIDTH), F32),
            jax.ShapeDtypeStruct((WIDTH, WIDTH), F32),
        ),
        compiler_params=params(40),
        cost_estimate=cost(1e6, 3.2e7),
        name="place",
    )(info, own, own, own, other, other, other)


def shift(array, axis, by):
    return lax.ppermute(array, axis, [(i, (i + by) % GROUPS) for i in range(GROUPS)])


def gather_rows(rows):
    ahead = shift(rows, "head", -1)
    behind = shift(rows, "head", 1)
    over_lo = shift(ahead[:128], "head", -1)
    over_hi = shift(behind[128:], "head", 1)
    return rows, ahead, over_lo, over_hi, behind


def exchange(own, to_next, to_prev):
    from_prev = shift(to_next, "head", 1)
    from_next = shift(to_prev, "head", -1)
    over = shift(from_prev[BLOCK:], "head", 1)
    under = shift(from_next[BLOCK:], "head", -1)
    return own, from_prev, over, from_next, under


def swap_cores(array):
    return lax.ppermute(array, "core", [(0, 1), (1, 0)])


def add_low(*terms):
    total = terms[0].astype(F32)
    for term in terms[1:]:
        total = total + term.astype(F32)
    return total.astype(BF16)


def scatter_sum(array, axis):
    me = lax.axis_index(axis)
    quarters = array.reshape(GROUPS, array.shape[0] // GROUPS, *array.shape[1:])
    pick = lambda k: lax.dynamic_index_in_dim(quarters, lax.rem(me + k, GROUPS), 0, False)
    return add_low(pick(0), *(shift(pick(k), axis, k) for k in (1, 2, 3)))


def gather_all(array, axis):
    me = lax.axis_index(axis)
    parts = [array] + [shift(array, axis, -k) for k in (1, 2, 3)]
    out = jnp.zeros((GROUPS, *array.shape), array.dtype)
    for k, part in enumerate(parts):
        out = lax.dynamic_update_index_in_dim(out, part, lax.rem(me + k, GROUPS), 0)
    return out.reshape(GROUPS * array.shape[0], *array.shape[1:])


def per_device(
    layer_input, lengths, cotangent, w_query, w_key, w_value, conv_query, conv_key, conv_value,
    w_out, w_up, w_down, gain_attn, bias_attn, gain_ffn, bias_ffn,
):
    here = lax.axis_index("head").astype(jnp.int32)
    core = lax.axis_index("core").astype(jnp.int32)
    gathered = [gather_rows(layer_input[s]) for s in range(SEQS)]

    w_groups = jnp.concatenate(
        [w.T.reshape(GROUPS, COLS, WIDTH) for w in (w_query, w_key, w_value)], axis=1
    )
    w_mine = lax.dynamic_index_in_dim(w_groups, here, 0, False)
    taps = lax.dynamic_slice_in_dim(
        jnp.concatenate([conv_query, conv_key, conv_value], axis=0), here * COLS, COLS, 1
    )
    gain_a, bias_a, gain_f, bias_f = (
        v.reshape(1, WIDTH) for v in (gain_attn, bias_attn, gain_ffn, bias_ffn)
    )
    infos = [jnp.stack([here, lengths[s]]) for s in range(SEQS)]
    info_all = jnp.concatenate([jnp.stack([here, core]), lengths])

    saved, pieces = [], []
    for s in range(SEQS):
        normed, raw_q, raw_k, raw_v, mixed, m0, m_next, m_prev, lse_t = attend(
            infos[s], gathered[s], w_mine, taps, gain_a, bias_a
        )
        saved.append((normed, raw_q, raw_k, raw_v, mixed, lse_t))
        pieces.extend(exchange(m0, m_next, m_prev))

    (
        layer_output, grad_middle, g0, g_next, g_prev, send, keep, send_out, keep_out, vectors,
    ) = ffn(info_all, layer_input, cotangent, pieces, w_out, gain_f, bias_f, w_up, w_down)

    half_sum = jnp.concatenate(
        [
            add_low(keep, swap_cores(send)).reshape(FF, WIDTH),
            add_low(keep_out, swap_cores(send_out)),
        ],
        axis=0,
    )
    half_sum = lax.psum(half_sum, ("x", "z", "head"))
    grad_up, grad_down, grad_out = place(info_all, half_sum, swap_cores(half_sum))

    dw = jnp.zeros((3 * COLS, WIDTH), F32)
    small = jnp.zeros((16, WIDTH), F32)
    input_grad = None
    for s in range(SEQS):
        grads = exchange(g0[s], g_next[s], g_prev[s])
        results = attend_back(
            s == 0, s == SEQS - 1, infos[s], grads, saved[s], w_mine, taps, gain_a, bias_a, vectors, dw, small
        )
        d0, d_next, d_prev, dw, small = results[:5]
        input_grad = input_grad_of(
            s, info_all, layer_input, grad_middle, exchange(d0, d_next, d_prev), w_groups, gain_a, input_grad
        )
    pack = results[5]

    half = PACK_ROWS // 2
    part = add_low(
        lax.dynamic_slice_in_dim(pack, core * half, half, 0),
        swap_cores(lax.dynamic_slice_in_dim(pack, (1 - core) * half, half, 0)),
    )
    part = scatter_sum(scatter_sum(part, "x"), "z")
    part = gather_all(gather_all(part, "z"), "x")
    part = gather_all(part[None], "head")
    other = swap_cores(part)
    pair = jnp.stack([part, other], axis=1)
    pair = jnp.where(core == 0, pair, pair[:, ::-1])
    whole = pair.reshape(GROUPS, PACK_ROWS, WIDTH).astype(F32)

    def weight(n):
        return whole[:, n * COLS : (n + 1) * COLS, :].reshape(WIDTH, WIDTH).T

    def conv(n):
        rows = whole[:, 3 * COLS + 3 * n : 3 * COLS + 3 * n + 3, 0:COLS]
        return jnp.transpose(rows, (1, 0, 2)).reshape(3, WIDTH)

    vector = jnp.sum(whole[:, 3 * COLS + 9 : 3 * COLS + 13, :], axis=0)
    return (
        layer_output,
        input_grad,
        weight(0), weight(1), weight(2),
        conv(0), conv(1), conv(2),
        grad_out, grad_up, grad_down,
        vector[0], vector[1], vector[2], vector[3],
    )


def solution(mesh):
    fine = Mesh(mesh.devices.reshape(4, 4, 2, GROUPS), ("x", "z", "core", "head"))
    dp = ("x", "z", "core")
    rows = P(dp, "head", None)
    return jax.shard_map(
        per_device,
        mesh=fine,
        in_specs=(rows, P(dp), rows) + (P(),) * 13,
        out_specs=(rows, rows) + (P(),) * 13,
        check_vma=False,
    )
```

```python
import functools

import jax
import jax.numpy as jnp
from jax import lax
from jax.experimental import pallas as pl
from jax.experimental.pallas import tpu as pltpu
from jax.sharding import Mesh
from jax.sharding import PartitionSpec as P

HDIM = 64
GROUPS = 4
BLOCK = 256
FULL = 1024
WIDTH = 768
COLS = 192
FF = 3072
SEQS = 3
CHUNK = 512
HEADS_HERE = 3
PACK_ROWS = 640
F32 = jnp.float32
BF16 = jnp.bfloat16
NN = (((1,), (0,)), ((), ()))
NT = (((1,), (1,)), ((), ()))
TN = (((0,), (0,)), ((), ()))


def dot(left, right, dims):
    return lax.dot_general(left, right, dims, preferred_element_type=F32)


def cost(flops, nbytes, transcendentals=0):
    return pl.CostEstimate(
        flops=int(flops), bytes_accessed=int(nbytes), transcendentals=int(transcendentals)
    )


def vmem():
    return pl.BlockSpec(memory_space=pltpu.VMEM)


def params(mib):
    return pltpu.CompilerParams(vmem_limit_bytes=mib << 20)


def unit_rows(rows):
    average = jnp.mean(rows, axis=-1, keepdims=True)
    centred = rows - average
    variance = jnp.mean(centred * centred, axis=-1, keepdims=True)
    inverse = lax.rsqrt(variance + 1e-05)
    return centred * inverse, inverse


def head_masks():
    lane = lax.broadcasted_iota(jnp.int32, (1, COLS), 1)
    return [
        jnp.where((lane >= h * HDIM) & (lane < (h + 1) * HDIM), 1.0, 0.0).astype(F32)
        for h in range(HEADS_HERE)
    ]


def conv_rows(raw_f, taps, tap_row, start):
    total = taps[tap_row : tap_row + 1, :] * raw_f[8 + start : 8 + start + BLOCK, :]
    for m in (1, 2):
        total += (
            taps[tap_row + m : tap_row + m + 1, :]
            * raw_f[8 + start - m : 8 + start - m + BLOCK, :]
        )
    return total


def attend_kernel(
    info, x0, x1, x2_lo, x2_hi, x3, w_mine, taps, gain, bias,
    normed, raw_q, raw_k, raw_v, mixed, lse_t,
    pad_q, pad_k, pad_v, q_s, k_s, v_s, below,
):
    here, length = info[0], info[1]
    blocks = (length + BLOCK - 1) // BLOCK
    masks = head_masks()

    for piece, ahead, shift, size in (
        (x0, 0, 0, BLOCK), (x1, 1, 0, BLOCK), (x2_lo, 2, 0, 128), (x2_hi, 2, 128, 128), (x3, 3, 0, BLOCK)
    ):
        home = lax.rem(here + ahead, GROUPS)

        @pl.when(home < blocks)
        def _(piece=piece, home=home, shift=shift, size=size):
            unit, _ = unit_rows(piece[0].astype(F32))
            low = (unit * gain[...] + bias[...]).astype(BF16)
            at = pl.multiple_of(home * BLOCK + shift, 128)
            normed[pl.ds(at, size), :] = low
            for n, (raw, pad) in enumerate(((raw_q, pad_q), (raw_k, pad_k), (raw_v, pad_v))):
                value = dot(low, w_mine[n * COLS : (n + 1) * COLS, :], NT).astype(BF16)
                raw[pl.ds(at, size), :] = value
                pad[pl.ds(at + 8, size), :] = value.astype(F32)

    for pad in (pad_q, pad_k, pad_v):
        pad[0:8, :] = jnp.zeros((8, COLS), F32)
    row = lax.broadcasted_iota(jnp.int32, (BLOCK, BLOCK), 0)
    col = lax.broadcasted_iota(jnp.int32, (BLOCK, BLOCK), 1)
    below[...] = jnp.where(col <= row, 0.0, -1e30).astype(F32)

    for b in range(GROUPS):

        @pl.when(b < blocks)
        def _(b=b):
            at = slice(b * BLOCK, (b + 1) * BLOCK)
            q_s[at, :] = (conv_rows(pad_q, taps, 0, b * BLOCK).astype(BF16).astype(F32) * 0.125).astype(BF16)
            k_s[at, :] = conv_rows(pad_k, taps, 3, b * BLOCK).astype(BF16)
            v_s[at, :] = conv_rows(pad_v, taps, 6, b * BLOCK).astype(BF16)
            lane = lax.broadcasted_iota(jnp.int32, (BLOCK, 128), 1)
            total_out = jnp.zeros((BLOCK, COLS), F32)
            logs = jnp.zeros((BLOCK, 128), F32)
            for h in range(HEADS_HERE):
                q_h = q_s[at, :] * masks[h].astype(BF16)
                diag = dot(q_h, k_s[at, :], NT) + below[...]
                top = jnp.max(diag, axis=-1, keepdims=True)
                if b:
                    left = dot(q_h, k_s[0 : b * BLOCK, :], NT)
                    top = jnp.maximum(top, jnp.max(left, axis=-1, keepdims=True))
                    expo_left = jnp.exp(left - top)
                expo = jnp.exp(diag - top)
                total = jnp.sum(expo, axis=-1, keepdims=True)
                out = dot(expo.astype(BF16), v_s[at, :], NN)
                if b:
                    total += jnp.sum(expo_left, axis=-1, keepdims=True)
                    out += dot(expo_left.astype(BF16), v_s[0 : b * BLOCK, :], NN)
                total_out = total_out + (out * masks[h]) * (1.0 / total)
                logs = jnp.where(lane == h, top + jnp.log(total), logs)
            mixed[b] = jnp.transpose(total_out).astype(BF16)
            lse_t[:, at] = jnp.transpose(logs)[0:8, :]

        @pl.when(b >= blocks)
        def _(b=b):
            mixed[b] = jnp.zeros((COLS, BLOCK), BF16)


def attend(s, info, gathered, w_mine, taps, gain, bias):
    low = lambda *shape: jax.ShapeDtypeStruct(shape, BF16)
    one = lambda rows: pl.BlockSpec((1, rows, WIDTH), lambda i, sc: (s, 0, 0))
    whole = lambda *shape: pl.BlockSpec(shape, lambda i, sc: (0,) * len(shape))
    return pl.pallas_call(
        attend_kernel,
        grid_spec=pltpu.PrefetchScalarGridSpec(
            num_scalar_prefetch=1,
            grid=(1,),
            in_specs=[one(p.shape[1]) for p in gathered]
            + [whole(3 * COLS, WIDTH), whole(9, COLS), whole(1, WIDTH), whole(1, WIDTH)],
            out_specs=[whole(FULL, WIDTH)]
            + [whole(FULL, COLS)] * 3
            + [whole(GROUPS, COLS, BLOCK), whole(8, FULL)],
            scratch_shapes=[pltpu.VMEM((FULL + 8, COLS), F32)] * 3
            + [pltpu.VMEM((FULL, COLS), BF16)] * 3
            + [pltpu.VMEM((BLOCK, BLOCK), F32)],
        ),
        out_shape=(
            low(FULL, WIDTH),
            low(FULL, COLS), low(FULL, COLS), low(FULL, COLS),
            low(GROUPS, COLS, BLOCK),
            jax.ShapeDtypeStruct((8, FULL), F32),
        ),
        compiler_params=params(60),
        cost_estimate=cost(3e9, 8e6, 2e6),
        name="attend",
    )(info, *gathered, w_mine, taps, gain, bias)


def attend_back_kernel(
    first, last,
    info, g_s, normed, raw_q, raw_k, raw_v, mixed, lse_t,
    w_mine, taps, gain, bias, ffn_vectors, dw_in, small_in,
    d_all, dw_out, small_out, *scratch,
):
    if last:
        keep, send, pack, scratch = *scratch[:2], scratch[-1], scratch[2:-1]
    pad_q, pad_k, pad_v, q_s, k_s, v_s, dq_s, dk_s, dv_s, below = scratch
    length, core = info[1], info[2]
    blocks = (length + BLOCK - 1) // BLOCK
    masks = head_masks()

    row = lax.broadcasted_iota(jnp.int32, (BLOCK, BLOCK), 0)
    col = lax.broadcasted_iota(jnp.int32, (BLOCK, BLOCK), 1)
    below[...] = jnp.where(row <= col, 0.0, -1e30).astype(F32)
    for pad, raw in ((pad_q, raw_q), (pad_k, raw_k), (pad_v, raw_v)):
        pad[0:8, :] = jnp.zeros((8, COLS), F32)
    for total in (dq_s, dk_s, dv_s):
        total[...] = jnp.zeros((FULL + 8, COLS), F32)

    for b in range(GROUPS):

        @pl.when(b < blocks)
        def _(b=b):
            at = slice(b * BLOCK, (b + 1) * BLOCK)
            for pad, raw in ((pad_q, raw_q), (pad_k, raw_k), (pad_v, raw_v)):
                pad[8 + b * BLOCK : 8 + (b + 1) * BLOCK, :] = raw[at, :].astype(F32)
            q_s[at, :] = (conv_rows(pad_q, taps, 0, b * BLOCK).astype(BF16).astype(F32) * 0.125).astype(BF16)
            k_s[at, :] = conv_rows(pad_k, taps, 3, b * BLOCK).astype(BF16)
            v_s[at, :] = conv_rows(pad_v, taps, 6, b * BLOCK).astype(BF16)
            both = g_s[b].astype(F32) * mixed[b].astype(F32)
            dq_total = jnp.zeros((BLOCK, COLS), F32)
            for h in range(HEADS_HERE):
                q_h = q_s[at, :] * masks[h].astype(BF16)
                own = slice(h * HDIM, (h + 1) * HDIM)
                blank = lambda n: [jnp.zeros((n * HDIM, BLOCK), BF16)] if n else []
                g_h = jnp.concatenate(blank(h) + [g_s[b, own, :]] + blank(HEADS_HERE - 1 - h), axis=0)
                row_dot = jnp.sum(both[own, :], axis=0, keepdims=True)
                log_row = lse_t[h : h + 1, at]
                dq_h = jnp.zeros((BLOCK, COLS), F32)
                for j in range(b + 1):
                    keys = slice(j * BLOCK, (j + 1) * BLOCK)
                    scores = dot(k_s[keys, :], q_h, NT)
                    if j == b:
                        scores = scores + below[...]
                    probs = jnp.exp(scores - log_row)
                    grad_probs = dot(v_s[keys, :], g_h, NN)
                    grad_scores = (probs * (grad_probs - row_dot)).astype(BF16)
                    dv_s[keys, :] += dot(probs.astype(BF16), g_h, NT)
                    dk_s[keys, :] += dot(grad_scores, q_h, NN)
                    dq_h += dot(grad_scores, k_s[keys, :], TN)
                dq_total += dq_h * masks[h]
            dq_s[at, :] = dq_total * 0.125

    if first:
        dw_out[...] = jnp.zeros_like(dw_out)
        small_out[...] = jnp.zeros_like(small_out)
    else:
        dw_out[...] = dw_in[...]
        small_out[...] = small_in[...]

    for b in range(GROUPS):

        @pl.when(b < blocks)
        def _(b=b):
            start = b * BLOCK
            at = slice(start, start + BLOCK)
            for n, (pad, grad) in enumerate(((pad_q, dq_s), (pad_k, dk_s), (pad_v, dv_s))):
                now = grad[at, :]
                value = taps[3 * n : 3 * n + 1, :] * now
                for m in (1, 2):
                    value += taps[3 * n + m : 3 * n + m + 1, :] * grad[start + m : start + m + BLOCK, :]
                value = value.astype(BF16).astype(F32)
                d_all[b, n * COLS : (n + 1) * COLS, :] = jnp.transpose(value).astype(BF16)
                small_out[9 + n : 10 + n, 0:COLS] += jnp.sum(value, axis=0, keepdims=True)
                for m in range(3):
                    shifted = pad[8 + start - m : 8 + start - m + BLOCK, :]
                    small_out[3 * n + m : 3 * n + m + 1, 0:COLS] += jnp.sum(
                        shifted * now, axis=0, keepdims=True
                    )
            dw_out[...] += dot(d_all[b], normed[at, :], NN)

        @pl.when(b >= blocks)
        def _(b=b):
            d_all[b] = jnp.zeros((3 * COLS, BLOCK), BF16)

    if last:
        grad_bias = jnp.zeros((1, WIDTH), F32)
        for n in range(3):
            sums = small_out[9 + n : 10 + n, 0:COLS]
            high = sums.astype(BF16)
            rest = (sums - high.astype(F32)).astype(BF16)
            for term in (high, rest):
                wide = jnp.broadcast_to(term.astype(F32), (16, COLS)).astype(BF16)
                grad_bias += dot(wide, w_mine[n * COLS : (n + 1) * COLS, :], NN)[0:1, :]
        grad_normed = jnp.sum(w_mine[...].astype(F32) * dw_out[...], axis=0, keepdims=True)
        grad_gain = (grad_normed - bias[...] * grad_bias) / gain[...]
        pack[0 : 3 * COLS, :] = dw_out[...].astype(BF16)
        tail = jnp.concatenate(
            [
                small_out[0:9, :],
                grad_gain,
                grad_bias,
                ffn_vectors[0:2, :],
                jnp.zeros((3, WIDTH), F32),
            ],
            axis=0,
        )
        pack[3 * COLS : 3 * COLS + 16, :] = tail.astype(BF16)
        pack[3 * COLS + 16 :, :] = jnp.zeros((PACK_ROWS - 3 * COLS - 16, WIDTH), BF16)
        half = PACK_ROWS // 2
        keep[...] = pack[pl.ds(pl.multiple_of(core * half, 64), half), :]
        send[...] = pack[pl.ds(pl.multiple_of((1 - core) * half, 64), half), :]


def attend_back(first, last, info, grad_mixed, saved, w_mine, taps, gain, bias, ffn_vectors, dw, small):
    low = lambda *shape: jax.ShapeDtypeStruct(shape, BF16)
    full = lambda *shape: jax.ShapeDtypeStruct(shape, F32)
    out_shape = [low(GROUPS, 3 * COLS, BLOCK), full(3 * COLS, WIDTH), full(16, WIDTH)]
    scratch = (
        [pltpu.VMEM((FULL + 8, COLS), F32)] * 3
        + [pltpu.VMEM((FULL, COLS), BF16)] * 3
        + [pltpu.VMEM((FULL + 8, COLS), F32)] * 3
        + [pltpu.VMEM((BLOCK, BLOCK), F32)]
    )
    if last:
        out_shape += [low(PACK_ROWS // 2, WIDTH)] * 2
        scratch.append(pltpu.VMEM((PACK_ROWS, WIDTH), BF16))
    return pl.pallas_call(
        functools.partial(attend_back_kernel, first, last),
        out_shape=out_shape,
        in_specs=[pl.BlockSpec(memory_space=pltpu.SMEM)] + [vmem()] * 14,
        out_specs=[vmem()] * len(out_shape),
        scratch_shapes=scratch,
        compiler_params=params(60),
        cost_estimate=cost(1e6, 1e5),
        name="attend_back",
    )(info, grad_mixed, *saved, w_mine, taps, gain, bias, ffn_vectors, dw, small)


def ffn_kernel(
    info, x, cotangent, mixed_0, mixed_1, mixed_2, w_out, gain, bias, w_up, w_down,
    layer_output, grad_middle, g_0, g_1, g_2, grad_up, grad_down, grad_out, vectors,
    middle, normed, low_grad, total_out, total_grad, sq_s, gh_s, branch,
):
    step = pl.program_id(0)
    position = info[0] * BLOCK + lax.broadcasted_iota(jnp.int32, (BLOCK, 1), 0)
    parts = [slice(s * BLOCK, (s + 1) * BLOCK) for s in range(SEQS)]
    mixed = (mixed_0, mixed_1, mixed_2)

    @pl.when(step == 0)
    def _():
        for s, at in enumerate(parts):
            value = x[s].astype(F32) + dot(mixed[s][...], w_out[...], TN)
            middle[at, :] = value
            unit, _ = unit_rows(value)
            normed[at, :] = (unit * gain[...] + bias[...]).astype(BF16)
            keep_row = position < info[2 + s]
            low_grad[at, :] = jnp.where(keep_row, cotangent[s].astype(F32), 0.0).astype(BF16)
            total_out[at, :] = jnp.zeros((BLOCK, WIDTH), F32)
            total_grad[at, :] = jnp.zeros((BLOCK, WIDTH), F32)

    for at in parts:
        hidden = jnp.maximum(dot(normed[at, :], w_up[...], NN), 0.0)
        squared = (hidden * hidden).astype(BF16)
        sq_s[at, :] = squared
        back = dot(low_grad[at, :], w_down[...], NT)
        grad_hidden = (back * 2.0 * hidden).astype(BF16)
        gh_s[at, :] = grad_hidden
        total_out[at, :] += dot(squared, w_down[...], NN)
        total_grad[at, :] += dot(grad_hidden, w_up[...], NT)
    grad_up[...] = dot(gh_s[...], normed[...], TN).astype(BF16)
    grad_down[...] = dot(sq_s[...], low_grad[...], TN).astype(BF16)

    @pl.when(step == FF // CHUNK - 1)
    def _():
        sum_gain = jnp.zeros((1, WIDTH), F32)
        sum_bias = jnp.zeros((1, WIDTH), F32)
        total = jnp.zeros((WIDTH, WIDTH), F32)
        for s, (at, g) in enumerate(zip(parts, (g_0, g_1, g_2))):
            keep_row = position < info[2 + s]
            layer_output[s] = jnp.where(keep_row, middle[at, :] + total_out[at, :], 0.0).astype(BF16)
            unit, inverse = unit_rows(middle[at, :])
            grad_normed = total_grad[at, :]
            scaled = grad_normed * gain[...]
            mean_grad = jnp.mean(scaled, axis=-1, keepdims=True)
            mean_dot = jnp.mean(scaled * unit, axis=-1, keepdims=True)
            value = low_grad[at, :].astype(F32) + inverse * (scaled - mean_grad - unit * mean_dot)
            sum_gain += jnp.sum(grad_normed * unit, axis=0, keepdims=True)
            sum_bias += jnp.sum(grad_normed, axis=0, keepdims=True)
            grad_middle[s] = value
            low = value.astype(BF16)
            g[...] = dot(w_out[...], low, NT).astype(BF16)
            total += dot(mixed[s][...], low, NN)
        grad_out[...] = total.astype(BF16)
        vectors[...] = jnp.concatenate(
            [sum_gain, sum_bias, jnp.zeros((6, WIDTH), F32)], axis=0
        )


def ffn(info, x, cotangent, mixed, w_out, gain, bias, w_up, w_down):
    low = lambda *shape: jax.ShapeDtypeStruct(shape, BF16)
    full = lambda *shape: jax.ShapeDtypeStruct(shape, F32)
    rows = SEQS * BLOCK
    whole = lambda *shape: pl.BlockSpec(shape, lambda i, sc: (0,) * len(shape))
    down = lambda: pl.BlockSpec((CHUNK, WIDTH), lambda i, sc: (i, 0))
    return pl.pallas_call(
        ffn_kernel,
        grid_spec=pltpu.PrefetchScalarGridSpec(
            num_scalar_prefetch=1,
            grid=(FF // CHUNK,),
            in_specs=[whole(SEQS, BLOCK, WIDTH)] * 2
            + [whole(WIDTH, BLOCK)] * SEQS
            + [
                whole(WIDTH, WIDTH), whole(1, WIDTH), whole(1, WIDTH),
                pl.BlockSpec((WIDTH, CHUNK), lambda i, sc: (0, i)),
                down(),
            ],
            out_specs=[whole(SEQS, BLOCK, WIDTH)] * 2
            + [whole(WIDTH, BLOCK)] * SEQS
            + [down(), down(), whole(WIDTH, WIDTH), whole(8, WIDTH)],
            scratch_shapes=[
                pltpu.VMEM((rows, WIDTH), F32),
                pltpu.VMEM((rows, WIDTH), BF16),
                pltpu.VMEM((rows, WIDTH), BF16),
                pltpu.VMEM((rows, WIDTH), F32),
                pltpu.VMEM((rows, WIDTH), F32),
                pltpu.VMEM((rows, CHUNK), BF16),
                pltpu.VMEM((rows, CHUNK), BF16),
                pltpu.VMEM((rows, WIDTH), BF16),
            ],
        ),
        out_shape=(
            low(SEQS, BLOCK, WIDTH), full(SEQS, BLOCK, WIDTH),
            low(WIDTH, BLOCK), low(WIDTH, BLOCK), low(WIDTH, BLOCK),
            low(FF, WIDTH), low(FF, WIDTH), low(WIDTH, WIDTH),
            full(8, WIDTH),
        ),
        compiler_params=params(60),
        cost_estimate=cost(2.4e10, 3e7),
        name="ffn",
    )(info, x, cotangent, *mixed, w_out, gain, bias, w_up, w_down)


def input_kernel(x, grad_middle, pieces, w_groups, gain, *rest):
    out = rest[-1]
    unit, inverse = unit_rows(x[0].astype(F32))
    grad_normed = dot(pieces[...], w_groups[...], TN)
    scaled = grad_normed * gain[...]
    mean_grad = jnp.mean(scaled, axis=-1, keepdims=True)
    mean_dot = jnp.mean(scaled * unit, axis=-1, keepdims=True)
    out[0] = grad_middle[0] + inverse * (scaled - mean_grad - unit * mean_dot)


def input_grad_of(s, x, grad_middle, pieces, w_groups, gain, earlier):
    one = lambda: pl.BlockSpec((1, BLOCK, WIDTH), lambda i: (s, 0, 0))
    whole = lambda *shape: pl.BlockSpec(shape, lambda i: (0,) * len(shape))
    extra = [] if earlier is None else [earlier]
    return pl.pallas_call(
        input_kernel,
        grid=(1,),
        in_specs=[one(), one(), whole(*pieces.shape), whole(*w_groups.shape), whole(1, WIDTH)]
        + [pl.BlockSpec(memory_space=pl.ANY)] * len(extra),
        out_specs=one(),
        out_shape=jax.ShapeDtypeStruct((SEQS, BLOCK, WIDTH), F32),
        input_output_aliases={} if earlier is None else {5: 0},
        compiler_params=params(60),
        cost_estimate=cost(1e6, 1e5),
        name="input_grad",
    )(x, grad_middle, pieces, w_groups, gain, *extra)


def place_kernel(up, down, out, grad_up, grad_down, grad_out):
    grad_up[...] = jnp.transpose(up[...].astype(F32))
    grad_down[...] = down[...].astype(F32)
    grad_out[...] = out[...].astype(F32)


def place(up, down, out):
    steps = FF // CHUNK
    rows = lambda n: pl.BlockSpec((n, WIDTH), lambda i: (i, 0))
    return pl.pallas_call(
        place_kernel,
        grid=(steps,),
        in_specs=[rows(CHUNK), rows(CHUNK), rows(WIDTH // steps)],
        out_specs=[pl.BlockSpec((WIDTH, CHUNK), lambda i: (0, i)), rows(CHUNK), rows(WIDTH // steps)],
        out_shape=(
            jax.ShapeDtypeStruct((WIDTH, FF), F32),
            jax.ShapeDtypeStruct((FF, WIDTH), F32),
            jax.ShapeDtypeStruct((WIDTH, WIDTH), F32),
        ),
        compiler_params=params(60),
        cost_estimate=cost(1e6, 3.2e7),
        name="place",
    )(up, down, out)


def shift(array, axis, by):
    return lax.ppermute(array, axis, [(i, (i + by) % GROUPS) for i in range(GROUPS)])


def gather_rows(rows):
    ahead = shift(rows, "head", -1)
    behind = shift(rows, "head", 1)
    over_lo = shift(ahead[:, :128], "head", -1)
    over_hi = shift(behind[:, 128:], "head", 1)
    return rows, ahead, over_lo, over_hi, behind


def trade(array, axes):
    return lax.all_to_all(array, axes, 0, 0, tiled=True)


def swap_cores(array):
    return lax.ppermute(array, "core", [(0, 1), (1, 0)])


def add_low(*terms):
    total = terms[0].astype(F32)
    for term in terms[1:]:
        total = total + term.astype(F32)
    return total.astype(BF16)


def per_device(
    layer_input, lengths, cotangent, w_query, w_key, w_value, conv_query, conv_key, conv_value,
    w_out, w_up, w_down, gain_attn, bias_attn, gain_ffn, bias_ffn,
):
    here = lax.axis_index("head").astype(jnp.int32)
    core = lax.axis_index("core").astype(jnp.int32)
    gathered = gather_rows(layer_input)

    w_groups = jnp.concatenate(
        [w.T.reshape(GROUPS, COLS, WIDTH) for w in (w_query, w_key, w_value)], axis=1
    )
    w_mine = lax.dynamic_index_in_dim(w_groups, here, 0, False)
    taps = lax.dynamic_slice_in_dim(
        jnp.concatenate([conv_query, conv_key, conv_value], axis=0), here * COLS, COLS, 1
    )
    gain_a, bias_a, gain_f, bias_f = (
        v.reshape(1, WIDTH) for v in (gain_attn, bias_attn, gain_ffn, bias_ffn)
    )
    infos = [jnp.stack([here, lengths[s], core]) for s in range(SEQS)]

    saved, mixed_rows = [], []
    for s in range(SEQS):
        normed, raw_q, raw_k, raw_v, mixed, lse_t = attend(
            s, infos[s], gathered, w_mine, taps, gain_a, bias_a
        )
        saved.append((normed, raw_q, raw_k, raw_v, mixed, lse_t))
        mixed_rows.append(trade(mixed, "head").reshape(WIDTH, BLOCK))
    layer_output, grad_middle, *grad_mixed, up, down, out, ffn_vectors = ffn(
        jnp.concatenate([jnp.stack([here, core]), lengths]),
        layer_input, cotangent, mixed_rows, w_out, gain_f, bias_f, w_up, w_down,
    )
    grad_up, grad_down, grad_out = place(*lax.psum((up, down, out), ("x", "z", "core", "head")))

    def attention_grads(grad_mixed, saved, grad_middle, ffn_vectors):
        dw = jnp.zeros((3 * COLS, WIDTH), F32)
        small = jnp.zeros((16, WIDTH), F32)
        input_grad = None
        w_rows = w_groups.reshape(GROUPS * 3 * COLS, WIDTH)
        traded = [trade(g.reshape(GROUPS, COLS, BLOCK), "head") for g in grad_mixed]
        pieces = []
        for s in range(SEQS):
            grad = traded[s]
            if s == 2:
                grad, pieces[0] = lax.optimization_barrier((grad, pieces[0]))
            results = attend_back(
                s == 0, s == SEQS - 1, infos[s], grad, saved[s], w_mine, taps, gain_a, bias_a, ffn_vectors, dw, small
            )
            dw, small = results[1:3]
            pieces.append(trade(results[0], "head").reshape(GROUPS * 3 * COLS, BLOCK))
        for s in range(SEQS):
            input_grad = input_grad_of(s, layer_input, grad_middle, pieces[s], w_rows, gain_a, input_grad)
        keep, send = results[3:]

        half = PACK_ROWS // 2
        part = add_low(keep, swap_cores(send)).reshape(16, half // 16, WIDTH)
        part = add_low(*trade(part, ("x", "z")))
        part = trade(jnp.broadcast_to(part[None], (64, half // 16, WIDTH)), ("x", "z", "head"))
        other = swap_cores(part)
        pair = jnp.where(core == 0, jnp.stack([part, other]), jnp.stack([other, part]))
        whole = pair.reshape(2, 16, GROUPS, half // 16, WIDTH).transpose(2, 0, 1, 3, 4)
        whole = whole.reshape(GROUPS, PACK_ROWS, WIDTH).astype(F32)

        def weight(n):
            return whole[:, n * COLS : (n + 1) * COLS, :].reshape(WIDTH, WIDTH).T

        def conv(n):
            taps_of = whole[:, 3 * COLS + 3 * n : 3 * COLS + 3 * n + 3, 0:COLS]
            return jnp.transpose(taps_of, (1, 0, 2)).reshape(3, WIDTH)

        vector = jnp.sum(whole[:, 3 * COLS + 9 : 3 * COLS + 13, :], axis=0)
        return (
            input_grad, weight(0), weight(1), weight(2), conv(0), conv(1), conv(2),
            vector[0], vector[1], vector[2], vector[3],
        )

    operands = (grad_mixed, saved, grad_middle, ffn_vectors)
    blank = lambda *args: jax.tree.map(
        lambda a: jnp.zeros(a.shape, a.dtype), jax.eval_shape(attention_grads, *args)
    )
    later = lax.cond(lengths[0] > 0, attention_grads, blank, *operands)
    return (layer_output, *later[:7], grad_out, grad_up, grad_down, *later[7:])


def solution(mesh):
    fine = Mesh(mesh.devices.reshape(4, 4, 2, GROUPS), ("x", "z", "core", "head"))
    dp = ("x", "z", "core")
    rows = P(dp, "head", None)
    return jax.shard_map(
        per_device,
        mesh=fine,
        in_specs=(rows, P(dp), rows) + (P(),) * 13,
        out_specs=(rows, rows) + (P(),) * 13,
        check_vma=False,
    )
```

```python
import functools

import jax
import jax.numpy as jnp
from jax import lax
from jax.experimental import pallas as pl
from jax.experimental.pallas import tpu as pltpu
from jax.sharding import Mesh
from jax.sharding import PartitionSpec as P

HDIM = 64
GROUPS = 4
BLOCK = 256
FULL = 1024
WIDTH = 768
COLS = 192
FF = 3072
SEQS = 3
CHUNK = 512
HEADS_HERE = 3
PACK_ROWS = 640
F32 = jnp.float32
BF16 = jnp.bfloat16
NN = (((1,), (0,)), ((), ()))
NT = (((1,), (1,)), ((), ()))
TN = (((0,), (0,)), ((), ()))


def dot(left, right, dims):
    return lax.dot_general(left, right, dims, preferred_element_type=F32)


def cost(flops, nbytes, transcendentals=0):
    return pl.CostEstimate(
        flops=int(flops), bytes_accessed=int(nbytes), transcendentals=int(transcendentals)
    )


def vmem():
    return pl.BlockSpec(memory_space=pltpu.VMEM)


def params(mib):
    return pltpu.CompilerParams(vmem_limit_bytes=mib << 20)


def unit_rows(rows):
    average = jnp.mean(rows, axis=-1, keepdims=True)
    centred = rows - average
    variance = jnp.mean(centred * centred, axis=-1, keepdims=True)
    inverse = lax.rsqrt(variance + 1e-05)
    return centred * inverse, inverse


def head_masks():
    lane = lax.broadcasted_iota(jnp.int32, (1, COLS), 1)
    return [
        jnp.where((lane >= h * HDIM) & (lane < (h + 1) * HDIM), 1.0, 0.0).astype(F32)
        for h in range(HEADS_HERE)
    ]


def conv_rows(raw_f, taps, tap_row, start):
    total = taps[tap_row : tap_row + 1, :] * raw_f[8 + start : 8 + start + BLOCK, :]
    for m in (1, 2):
        total += (
            taps[tap_row + m : tap_row + m + 1, :]
            * raw_f[8 + start - m : 8 + start - m + BLOCK, :]
        )
    return total


def attend_kernel(
    info, x0, x1, x2_lo, x2_hi, x3, w_mine, taps, gain, bias,
    normed, raw_q, raw_k, raw_v, mixed, lse_t,
    pad_q, pad_k, pad_v, q_s, k_s, v_s, below,
):
    here, length = info[0], info[1]
    blocks = (length + BLOCK - 1) // BLOCK
    masks = head_masks()

    for piece, ahead, shift, size in (
        (x0, 0, 0, BLOCK), (x1, 1, 0, BLOCK), (x2_lo, 2, 0, 128), (x2_hi, 2, 128, 128), (x3, 3, 0, BLOCK)
    ):
        home = lax.rem(here + ahead, GROUPS)

        @pl.when(home < blocks)
        def _(piece=piece, home=home, shift=shift, size=size):
            unit, _ = unit_rows(piece[0].astype(F32))
            low = (unit * gain[...] + bias[...]).astype(BF16)
            at = pl.multiple_of(home * BLOCK + shift, 128)
            normed[pl.ds(at, size), :] = low
            for n, (raw, pad) in enumerate(((raw_q, pad_q), (raw_k, pad_k), (raw_v, pad_v))):
                value = dot(low, w_mine[n * COLS : (n + 1) * COLS, :], NT).astype(BF16)
                raw[pl.ds(at, size), :] = value
                pad[pl.ds(at + 8, size), :] = value.astype(F32)

    for pad in (pad_q, pad_k, pad_v):
        pad[0:8, :] = jnp.zeros((8, COLS), F32)
    row = lax.broadcasted_iota(jnp.int32, (BLOCK, BLOCK), 0)
    col = lax.broadcasted_iota(jnp.int32, (BLOCK, BLOCK), 1)
    below[...] = jnp.where(col <= row, 0.0, -1e30).astype(F32)

    for b in range(GROUPS):

        @pl.when(b < blocks)
        def _(b=b):
            at = slice(b * BLOCK, (b + 1) * BLOCK)
            q_s[at, :] = (conv_rows(pad_q, taps, 0, b * BLOCK).astype(BF16).astype(F32) * 0.125).astype(BF16)
            k_s[at, :] = conv_rows(pad_k, taps, 3, b * BLOCK).astype(BF16)
            v_s[at, :] = conv_rows(pad_v, taps, 6, b * BLOCK).astype(BF16)
            lane = lax.broadcasted_iota(jnp.int32, (BLOCK, 128), 1)
            total_out = jnp.zeros((BLOCK, COLS), F32)
            logs = jnp.zeros((BLOCK, 128), F32)
            for h in range(HEADS_HERE):
                q_h = q_s[at, :] * masks[h].astype(BF16)
                diag = dot(q_h, k_s[at, :], NT) + below[...]
                top = jnp.max(diag, axis=-1, keepdims=True)
                if b:
                    left = dot(q_h, k_s[0 : b * BLOCK, :], NT)
                    top = jnp.maximum(top, jnp.max(left, axis=-1, keepdims=True))
                    expo_left = jnp.exp(left - top)
                expo = jnp.exp(diag - top)
                total = jnp.sum(expo, axis=-1, keepdims=True)
                out = dot(expo.astype(BF16), v_s[at, :], NN)
                if b:
                    total += jnp.sum(expo_left, axis=-1, keepdims=True)
                    out += dot(expo_left.astype(BF16), v_s[0 : b * BLOCK, :], NN)
                total_out = total_out + (out * masks[h]) * (1.0 / total)
                logs = jnp.where(lane == h, top + jnp.log(total), logs)
            mixed[b] = jnp.transpose(total_out).astype(BF16)
            lse_t[:, at] = jnp.transpose(logs)[0:8, :]

        @pl.when(b >= blocks)
        def _(b=b):
            mixed[b] = jnp.zeros((COLS, BLOCK), BF16)


def attend(s, info, gathered, w_mine, taps, gain, bias):
    low = lambda *shape: jax.ShapeDtypeStruct(shape, BF16)
    one = lambda rows: pl.BlockSpec((1, rows, WIDTH), lambda i, sc: (s, 0, 0))
    whole = lambda *shape: pl.BlockSpec(shape, lambda i, sc: (0,) * len(shape))
    return pl.pallas_call(
        attend_kernel,
        grid_spec=pltpu.PrefetchScalarGridSpec(
            num_scalar_prefetch=1,
            grid=(1,),
            in_specs=[one(p.shape[1]) for p in gathered]
            + [whole(3 * COLS, WIDTH), whole(9, COLS), whole(1, WIDTH), whole(1, WIDTH)],
            out_specs=[whole(FULL, WIDTH)]
            + [whole(FULL, COLS)] * 3
            + [whole(GROUPS, COLS, BLOCK), whole(8, FULL)],
            scratch_shapes=[pltpu.VMEM((FULL + 8, COLS), F32)] * 3
            + [pltpu.VMEM((FULL, COLS), BF16)] * 3
            + [pltpu.VMEM((BLOCK, BLOCK), F32)],
        ),
        out_shape=(
            low(FULL, WIDTH),
            low(FULL, COLS), low(FULL, COLS), low(FULL, COLS),
            low(GROUPS, COLS, BLOCK),
            jax.ShapeDtypeStruct((8, FULL), F32),
        ),
        compiler_params=params(60),
        cost_estimate=cost(3e9, 8e6, 2e6),
        name="attend",
    )(info, *gathered, w_mine, taps, gain, bias)


def attend_back_kernel(
    first, last,
    info, g_s, normed, raw_q, raw_k, raw_v, mixed, lse_t,
    w_mine, taps, gain, bias, ffn_vectors, dw_in, small_in,
    d_all, dw_out, small_out, *scratch,
):
    if last:
        keep, send, pack, scratch = *scratch[:2], scratch[-1], scratch[2:-1]
    pad_q, pad_k, pad_v, q_s, k_s, v_s, dq_s, dk_s, dv_s, below, p_all, ds_all = scratch
    length, core = info[1], info[2]
    blocks = (length + BLOCK - 1) // BLOCK
    masks = head_masks()

    row = lax.broadcasted_iota(jnp.int32, (BLOCK, BLOCK), 0)
    col = lax.broadcasted_iota(jnp.int32, (BLOCK, BLOCK), 1)
    below[...] = jnp.where(row <= col, 0.0, -1e30).astype(F32)
    for pad, raw in ((pad_q, raw_q), (pad_k, raw_k), (pad_v, raw_v)):
        pad[0:8, :] = jnp.zeros((8, COLS), F32)
    for total in (dq_s, dk_s, dv_s):
        total[...] = jnp.zeros((FULL + 8, COLS), F32)

    for b in range(GROUPS):

        @pl.when(b < blocks)
        def _(b=b):
            at = slice(b * BLOCK, (b + 1) * BLOCK)
            for pad, raw in ((pad_q, raw_q), (pad_k, raw_k), (pad_v, raw_v)):
                pad[8 + b * BLOCK : 8 + (b + 1) * BLOCK, :] = raw[at, :].astype(F32)
            q_s[at, :] = (conv_rows(pad_q, taps, 0, b * BLOCK).astype(BF16).astype(F32) * 0.125).astype(BF16)
            k_s[at, :] = conv_rows(pad_k, taps, 3, b * BLOCK).astype(BF16)
            v_s[at, :] = conv_rows(pad_v, taps, 6, b * BLOCK).astype(BF16)
            both = g_s[b].astype(F32) * mixed[b].astype(F32)
            reach = slice(0, (b + 1) * BLOCK)
            dq_total = jnp.zeros((BLOCK, COLS), F32)
            q_heads, g_heads = [], []
            for h in range(HEADS_HERE):
                lanes = slice(h * BLOCK, (h + 1) * BLOCK)
                q_h = q_s[at, :] * masks[h].astype(BF16)
                own = slice(h * HDIM, (h + 1) * HDIM)
                blank = lambda n: [jnp.zeros((n * HDIM, BLOCK), BF16)] if n else []
                g_h = jnp.concatenate(blank(h) + [g_s[b, own, :]] + blank(HEADS_HERE - 1 - h), axis=0)
                q_heads.append(q_h)
                g_heads.append(g_h)
                row_dot = jnp.sum(both[own, :], axis=0, keepdims=True)
                log_row = lse_t[h : h + 1, at]
                for j in range(b + 1):
                    keys = slice(j * BLOCK, (j + 1) * BLOCK)
                    scores = dot(k_s[keys, :], q_h, NT)
                    if j == b:
                        scores = scores + below[...]
                    probs = jnp.exp(scores - log_row)
                    grad_probs = dot(v_s[keys, :], g_h, NN)
                    p_all[keys, lanes] = probs.astype(BF16)
                    ds_all[keys, lanes] = (probs * (grad_probs - row_dot)).astype(BF16)
                dq_total += dot(ds_all[reach, lanes], k_s[reach, :], TN) * masks[h]
            dq_s[at, :] = dq_total * 0.125
            dv_s[reach, :] += dot(p_all[reach, :], jnp.concatenate(g_heads, axis=1), NT)
            dk_s[reach, :] += dot(ds_all[reach, :], jnp.concatenate(q_heads, axis=0), NN)

    if first:
        dw_out[...] = jnp.zeros_like(dw_out)
        small_out[...] = jnp.zeros_like(small_out)
    else:
        dw_out[...] = dw_in[...]
        small_out[...] = small_in[...]

    for b in range(GROUPS):

        @pl.when(b < blocks)
        def _(b=b):
            start = b * BLOCK
            at = slice(start, start + BLOCK)
            for n, (pad, grad) in enumerate(((pad_q, dq_s), (pad_k, dk_s), (pad_v, dv_s))):
                now = grad[at, :]
                value = taps[3 * n : 3 * n + 1, :] * now
                for m in (1, 2):
                    value += taps[3 * n + m : 3 * n + m + 1, :] * grad[start + m : start + m + BLOCK, :]
                value = value.astype(BF16).astype(F32)
                d_all[b, n * COLS : (n + 1) * COLS, :] = jnp.transpose(value).astype(BF16)
                small_out[9 + n : 10 + n, 0:COLS] += jnp.sum(value, axis=0, keepdims=True)
                for m in range(3):
                    shifted = pad[8 + start - m : 8 + start - m + BLOCK, :]
                    small_out[3 * n + m : 3 * n + m + 1, 0:COLS] += jnp.sum(
                        shifted * now, axis=0, keepdims=True
                    )
            dw_out[...] += dot(d_all[b], normed[at, :], NN)

        @pl.when(b >= blocks)
        def _(b=b):
            d_all[b] = jnp.zeros((3 * COLS, BLOCK), BF16)

    if last:
        grad_bias = jnp.zeros((1, WIDTH), F32)
        for n in range(3):
            sums = small_out[9 + n : 10 + n, 0:COLS]
            high = sums.astype(BF16)
            rest = (sums - high.astype(F32)).astype(BF16)
            for term in (high, rest):
                wide = jnp.broadcast_to(term.astype(F32), (16, COLS)).astype(BF16)
                grad_bias += dot(wide, w_mine[n * COLS : (n + 1) * COLS, :], NN)[0:1, :]
        grad_normed = jnp.sum(w_mine[...].astype(F32) * dw_out[...], axis=0, keepdims=True)
        grad_gain = (grad_normed - bias[...] * grad_bias) / gain[...]
        pack[0 : 3 * COLS, :] = dw_out[...].astype(BF16)
        tail = jnp.concatenate(
            [
                small_out[0:9, :],
                grad_gain,
                grad_bias,
                ffn_vectors[0:2, :],
                jnp.zeros((3, WIDTH), F32),
            ],
            axis=0,
        )
        pack[3 * COLS : 3 * COLS + 16, :] = tail.astype(BF16)
        pack[3 * COLS + 16 :, :] = jnp.zeros((PACK_ROWS - 3 * COLS - 16, WIDTH), BF16)
        half = PACK_ROWS // 2
        keep[...] = pack[pl.ds(pl.multiple_of(core * half, 64), half), :]
        send[...] = pack[pl.ds(pl.multiple_of((1 - core) * half, 64), half), :]


def attend_back(s, info, grad_mixed, saved, w_mine, taps, gain, bias, ffn_vectors, dw, small):
    low = lambda *shape: jax.ShapeDtypeStruct(shape, BF16)
    full = lambda *shape: jax.ShapeDtypeStruct(shape, F32)
    first, last = s == 0, s == SEQS - 1
    out_shape = [low(GROUPS, 3 * COLS, BLOCK), full(3 * COLS, WIDTH), full(16, WIDTH)]
    scratch = (
        [pltpu.VMEM((FULL + 8, COLS), F32)] * 3
        + [pltpu.VMEM((FULL, COLS), BF16)] * 3
        + [pltpu.VMEM((FULL + 8, COLS), F32)] * 3
        + [pltpu.VMEM((BLOCK, BLOCK), F32)]
        + [pltpu.VMEM((FULL, HEADS_HERE * BLOCK), BF16)] * 2
    )
    if last:
        out_shape += [low(PACK_ROWS // 2, WIDTH)] * 2
        scratch.append(pltpu.VMEM((PACK_ROWS, WIDTH), BF16))
    return pl.pallas_call(
        functools.partial(attend_back_kernel, first, last),
        out_shape=out_shape,
        grid=(1,),
        in_specs=[
            pl.BlockSpec(memory_space=pltpu.SMEM),
            pl.BlockSpec((GROUPS, COLS, BLOCK), lambda i: (0, s, 0)),
        ]
        + [vmem()] * 13,
        out_specs=[vmem()] * len(out_shape),
        scratch_shapes=scratch,
        compiler_params=params(60),
        cost_estimate=cost(1e6, 1e5),
        name="attend_back",
    )(info, grad_mixed, *saved, w_mine, taps, gain, bias, ffn_vectors, dw, small)


def ffn_kernel(
    info, x, cotangent, mixed_0, mixed_1, mixed_2, w_out, gain, bias, w_up, w_down,
    layer_output, grad_middle, grad_mixed, send, keep, send_out, keep_out, vectors,
    middle, normed, low_grad, total_out, total_grad, sq_s, gh_s, dw_out,
):
    step = pl.program_id(0)
    position = info[0] * BLOCK + lax.broadcasted_iota(jnp.int32, (BLOCK, 1), 0)
    parts = [slice(s * BLOCK, (s + 1) * BLOCK) for s in range(SEQS)]
    mixed = (mixed_0, mixed_1, mixed_2)

    @pl.when(step == 0)
    def _():
        for s, at in enumerate(parts):
            value = x[s].astype(F32) + dot(mixed[s][...], w_out[...], TN)
            middle[at, :] = value
            unit, _ = unit_rows(value)
            normed[at, :] = (unit * gain[...] + bias[...]).astype(BF16)
            keep_row = position < info[2 + s]
            low_grad[at, :] = jnp.where(keep_row, cotangent[s].astype(F32), 0.0).astype(BF16)
            total_out[at, :] = jnp.zeros((BLOCK, WIDTH), F32)
            total_grad[at, :] = jnp.zeros((BLOCK, WIDTH), F32)

    for at in parts:
        hidden = jnp.maximum(dot(normed[at, :], w_up[...], NN), 0.0)
        squared = (hidden * hidden).astype(BF16)
        sq_s[at, :] = squared
        back = dot(low_grad[at, :], w_down[...], NT)
        grad_hidden = (back * 2.0 * hidden).astype(BF16)
        gh_s[at, :] = grad_hidden
        total_out[at, :] += dot(squared, w_down[...], NN)
        total_grad[at, :] += dot(grad_hidden, w_up[...], NT)
    grad_up = dot(gh_s[...], normed[...], TN).astype(BF16)
    grad_down = dot(sq_s[...], low_grad[...], TN).astype(BF16)
    steps = FF // CHUNK

    @pl.when(step < steps // 2)
    def _():
        send[0] = grad_up
        send[1] = grad_down

    @pl.when(step >= steps // 2)
    def _():
        keep[0] = grad_up
        keep[1] = grad_down

    @pl.when(step == FF // CHUNK - 1)
    def _():
        sum_gain = jnp.zeros((1, WIDTH), F32)
        sum_bias = jnp.zeros((1, WIDTH), F32)
        total = jnp.zeros((WIDTH, WIDTH), F32)
        for s, at in enumerate(parts):
            keep_row = position < info[2 + s]
            layer_output[s] = jnp.where(keep_row, middle[at, :] + total_out[at, :], 0.0).astype(BF16)
            unit, inverse = unit_rows(middle[at, :])
            grad_normed = total_grad[at, :]
            scaled = grad_normed * gain[...]
            mean_grad = jnp.mean(scaled, axis=-1, keepdims=True)
            mean_dot = jnp.mean(scaled * unit, axis=-1, keepdims=True)
            value = low_grad[at, :].astype(F32) + inverse * (scaled - mean_grad - unit * mean_dot)
            sum_gain += jnp.sum(grad_normed * unit, axis=0, keepdims=True)
            sum_bias += jnp.sum(grad_normed, axis=0, keepdims=True)
            grad_middle[s] = value
            low = value.astype(BF16)
            value = dot(w_out[...], low, NT).astype(BF16)
            for k in range(GROUPS):
                grad_mixed[k, s * COLS : (s + 1) * COLS, :] = value[k * COLS : (k + 1) * COLS]
            total += dot(mixed[s][...], low, NN)
        dw_out[...] = total.astype(BF16)
        half = WIDTH // 2
        keep_out[...] = dw_out[pl.ds(pl.multiple_of(info[1] * half, 128), half), :]
        send_out[...] = dw_out[pl.ds(pl.multiple_of((1 - info[1]) * half, 128), half), :]
        vectors[...] = jnp.concatenate(
            [sum_gain, sum_bias, jnp.zeros((6, WIDTH), F32)], axis=0
        )


def ffn(info, x, cotangent, mixed, w_out, gain, bias, w_up, w_down):
    low = lambda *shape: jax.ShapeDtypeStruct(shape, BF16)
    full = lambda *shape: jax.ShapeDtypeStruct(shape, F32)
    rows = SEQS * BLOCK
    steps = FF // CHUNK
    half = steps // 2
    whole = lambda *shape: pl.BlockSpec(shape, lambda i, sc: (0,) * len(shape))

    def chunk(i, sc):
        return jnp.where(i < half, 1 - sc[1], sc[1]) * half + lax.rem(i, half)

    return pl.pallas_call(
        ffn_kernel,
        grid_spec=pltpu.PrefetchScalarGridSpec(
            num_scalar_prefetch=1,
            grid=(steps,),
            in_specs=[whole(SEQS, BLOCK, WIDTH)] * 2
            + [whole(WIDTH, BLOCK)] * SEQS
            + [
                whole(WIDTH, WIDTH), whole(1, WIDTH), whole(1, WIDTH),
                pl.BlockSpec((WIDTH, CHUNK), lambda i, sc: (0, chunk(i, sc))),
                pl.BlockSpec((CHUNK, WIDTH), lambda i, sc: (chunk(i, sc), 0)),
            ],
            out_specs=[whole(SEQS, BLOCK, WIDTH)] * 2
            + [
                whole(GROUPS, SEQS * COLS, BLOCK),
                pl.BlockSpec((2, CHUNK, WIDTH), lambda i, sc: (0, jnp.minimum(i, half - 1), 0)),
                pl.BlockSpec((2, CHUNK, WIDTH), lambda i, sc: (0, jnp.maximum(i - half, 0), 0)),
                whole(WIDTH // 2, WIDTH), whole(WIDTH // 2, WIDTH), whole(8, WIDTH),
            ],
            scratch_shapes=[
                pltpu.VMEM((rows, WIDTH), F32),
                pltpu.VMEM((rows, WIDTH), BF16),
                pltpu.VMEM((rows, WIDTH), BF16),
                pltpu.VMEM((rows, WIDTH), F32),
                pltpu.VMEM((rows, WIDTH), F32),
                pltpu.VMEM((rows, CHUNK), BF16),
                pltpu.VMEM((rows, CHUNK), BF16),
                pltpu.VMEM((WIDTH, WIDTH), BF16),
            ],
        ),
        out_shape=(
            low(SEQS, BLOCK, WIDTH), full(SEQS, BLOCK, WIDTH),
            low(GROUPS, SEQS * COLS, BLOCK),
            low(2, FF // 2, WIDTH), low(2, FF // 2, WIDTH),
            low(WIDTH // 2, WIDTH), low(WIDTH // 2, WIDTH),
            full(8, WIDTH),
        ),
        compiler_params=params(60),
        cost_estimate=cost(2.4e10, 3e7),
        name="ffn",
    )(info, x, cotangent, *mixed, w_out, gain, bias, w_up, w_down)


def input_kernel(x, grad_middle, pieces, w_groups, gain, *rest):
    out = rest[-1]
    unit, inverse = unit_rows(x[0].astype(F32))
    grad_normed = dot(pieces[...], w_groups[...], TN)
    scaled = grad_normed * gain[...]
    mean_grad = jnp.mean(scaled, axis=-1, keepdims=True)
    mean_dot = jnp.mean(scaled * unit, axis=-1, keepdims=True)
    out[0] = grad_middle[0] + inverse * (scaled - mean_grad - unit * mean_dot)


def input_grad_of(s, x, grad_middle, pieces, w_groups, gain, earlier):
    one = lambda: pl.BlockSpec((1, BLOCK, WIDTH), lambda i: (s, 0, 0))
    whole = lambda *shape: pl.BlockSpec(shape, lambda i: (0,) * len(shape))
    extra = [] if earlier is None else [earlier]
    return pl.pallas_call(
        input_kernel,
        grid=(1,),
        in_specs=[one(), one(), whole(*pieces.shape), whole(*w_groups.shape), whole(1, WIDTH)]
        + [pl.BlockSpec(memory_space=pl.ANY)] * len(extra),
        out_specs=one(),
        out_shape=jax.ShapeDtypeStruct((SEQS, BLOCK, WIDTH), F32),
        input_output_aliases={} if earlier is None else {5: 0},
        compiler_params=params(60),
        cost_estimate=cost(1e6, 1e5),
        name="input_grad",
    )(x, grad_middle, pieces, w_groups, gain, *extra)


def place_kernel(info, up, down, out, *rest):
    grad_up, grad_down, grad_out = rest[-3:]
    grad_up[...] = jnp.transpose(up[...].astype(F32))
    grad_down[...] = down[...].astype(F32)
    grad_out[...] = out[...].astype(F32)


def place(side, half_sum, earlier):
    half = FF // CHUNK // 2
    rows = lambda n, base: pl.BlockSpec((n, WIDTH), lambda i, sc: (base + i, 0))
    own = lambda n: pl.BlockSpec((n, WIDTH), lambda i, sc: (sc[0] * half + i, 0))
    out_rows = WIDTH // 2 // half
    return pl.pallas_call(
        place_kernel,
        grid_spec=pltpu.PrefetchScalarGridSpec(
            num_scalar_prefetch=1,
            grid=(half,),
            in_specs=[rows(CHUNK, 0), rows(CHUNK, half), rows(out_rows, FF // out_rows)]
            + [pl.BlockSpec(memory_space=pl.ANY)] * len(earlier),
            out_specs=[
                pl.BlockSpec((WIDTH, CHUNK), lambda i, sc: (0, sc[0] * half + i)), own(CHUNK), own(out_rows)
            ],
        ),
        out_shape=(
            jax.ShapeDtypeStruct((WIDTH, FF), F32),
            jax.ShapeDtypeStruct((FF, WIDTH), F32),
            jax.ShapeDtypeStruct((WIDTH, WIDTH), F32),
        ),
        input_output_aliases={4 + n: n for n in range(len(earlier))},
        compiler_params=params(60),
        cost_estimate=cost(1e6, 1.6e7),
        name="place",
    )(side.reshape(1), half_sum, half_sum, half_sum, *earlier)


def unpack_kernel(info, own, other, grad_q, grad_k, grad_v, tails, rows):
    half = PACK_ROWS // 2
    size = half // 16

    def fill(pieces, base):
        for y in range(GROUPS):
            for n in range(16):
                rows[y, base + n * size : base + (n + 1) * size, :] = pieces[n * GROUPS + y].astype(F32)

    @pl.when(info[0] == 0)
    def _():
        fill(own, 0)
        fill(other, half)

    @pl.when(info[0] != 0)
    def _():
        fill(other, 0)
        fill(own, half)

    for n, grad in enumerate((grad_q, grad_k, grad_v)):
        part = jnp.concatenate([rows[y, n * COLS : (n + 1) * COLS, :] for y in range(GROUPS)], axis=0)
        grad[...] = jnp.transpose(part)
    for y in range(GROUPS):
        tails[y] = rows[y, 3 * COLS : 3 * COLS + 16, :]


def unpack(core, own, other):
    full = lambda *shape: jax.ShapeDtypeStruct(shape, F32)
    return pl.pallas_call(
        unpack_kernel,
        in_specs=[pl.BlockSpec(memory_space=pltpu.SMEM), vmem(), vmem()],
        out_specs=[vmem()] * 4,
        out_shape=(full(WIDTH, WIDTH), full(WIDTH, WIDTH), full(WIDTH, WIDTH), full(GROUPS, 16, WIDTH)),
        scratch_shapes=[pltpu.VMEM((GROUPS, PACK_ROWS, WIDTH), F32)],
        compiler_params=params(60),
        cost_estimate=cost(1e6, 1e5),
        name="unpack",
    )(core.reshape(1), own, other)


def shift(array, axis, by):
    return lax.ppermute(array, axis, [(i, (i + by) % GROUPS) for i in range(GROUPS)])


def gather_rows(rows):
    ahead = shift(rows, "head", -1)
    behind = shift(rows, "head", 1)
    over_lo = shift(ahead[:, :128], "head", -1)
    over_hi = shift(behind[:, 128:], "head", 1)
    return rows, ahead, over_lo, over_hi, behind


def trade(array, axes):
    return lax.all_to_all(array, axes, 0, 0, tiled=True)


def swap_cores(array):
    return lax.ppermute(array, "core", [(0, 1), (1, 0)])


def add_low(*terms):
    total = terms[0].astype(F32)
    for term in terms[1:]:
        total = total + term.astype(F32)
    return total.astype(BF16)


def per_device(
    layer_input, lengths, cotangent, w_query, w_key, w_value, conv_query, conv_key, conv_value,
    w_out, w_up, w_down, gain_attn, bias_attn, gain_ffn, bias_ffn,
):
    here = lax.axis_index("head").astype(jnp.int32)
    core = lax.axis_index("core").astype(jnp.int32)
    gathered = gather_rows(layer_input)

    w_groups = jnp.concatenate(
        [w.T.reshape(GROUPS, COLS, WIDTH) for w in (w_query, w_key, w_value)], axis=1
    )
    w_mine = lax.dynamic_index_in_dim(w_groups, here, 0, False)
    taps = lax.dynamic_slice_in_dim(
        jnp.concatenate([conv_query, conv_key, conv_value], axis=0), here * COLS, COLS, 1
    )
    gain_a, bias_a, gain_f, bias_f = (
        v.reshape(1, WIDTH) for v in (gain_attn, bias_attn, gain_ffn, bias_ffn)
    )
    infos = [jnp.stack([here, lengths[s], core]) for s in range(SEQS)]

    saved, mixed_rows = [], []
    for s in range(SEQS):
        normed, raw_q, raw_k, raw_v, mixed, lse_t = attend(
            s, infos[s], gathered, w_mine, taps, gain_a, bias_a
        )
        saved.append((normed, raw_q, raw_k, raw_v, mixed, lse_t))
        mixed_rows.append(trade(mixed, "head").reshape(WIDTH, BLOCK))
    layer_output, grad_middle, grad_mixed, send, keep, send_out, keep_out, ffn_vectors = ffn(
        jnp.concatenate([jnp.stack([here, core]), lengths]),
        layer_input, cotangent, mixed_rows, w_out, gain_f, bias_f, w_up, w_down,
    )

    half_sum = jnp.concatenate(
        [
            add_low(keep, swap_cores(send)).reshape(FF, WIDTH),
            add_low(keep_out, swap_cores(send_out)),
        ],
        axis=0,
    )
    half_sum, grad_mixed = lax.optimization_barrier((half_sum, trade(grad_mixed, "head")))
    half_sum = lax.psum(half_sum, ("x", "z", "head"))

    def attention_grads(grad_mixed, saved, grad_middle, ffn_vectors):
        dw = jnp.zeros((3 * COLS, WIDTH), F32)
        small = jnp.zeros((16, WIDTH), F32)
        input_grad = None
        w_rows = w_groups.reshape(GROUPS * 3 * COLS, WIDTH)
        pieces = []
        for s in range(SEQS):
            if s == 2:
                dw, pieces[0] = lax.optimization_barrier((dw, pieces[0]))
            results = attend_back(
                s, infos[s], grad_mixed, saved[s], w_mine, taps, gain_a, bias_a, ffn_vectors, dw, small
            )
            dw, small = results[1:3]
            pieces.append(trade(results[0], "head").reshape(GROUPS * 3 * COLS, BLOCK))
        keep, send = results[3:]
        keep, send, pieces[1] = lax.optimization_barrier((keep, send, pieces[1]))
        for s in range(SEQS):
            input_grad = input_grad_of(s, layer_input, grad_middle, pieces[s], w_rows, gain_a, input_grad)

        half = PACK_ROWS // 2
        part = add_low(keep, swap_cores(send)).reshape(16, half // 16, WIDTH)
        part = add_low(*trade(part, ("x", "z")))
        part = trade(jnp.broadcast_to(part[None], (64, half // 16, WIDTH)), ("x", "z", "head"))
        grad_q, grad_k, grad_v, tails = unpack(core, part, swap_cores(part))
        conv = lambda n: jnp.transpose(tails[:, 3 * n : 3 * n + 3, 0:COLS], (1, 0, 2)).reshape(3, WIDTH)
        vector = jnp.sum(tails[:, 9:13, :], axis=0)
        return (
            input_grad, grad_q, grad_k, grad_v, conv(0), conv(1), conv(2),
            vector[0], vector[1], vector[2], vector[3],
        )

    operands = (grad_mixed, saved, grad_middle, ffn_vectors)
    blank = lambda *args: jax.tree.map(
        lambda a: jnp.zeros(a.shape, a.dtype), jax.eval_shape(attention_grads, *args)
    )
    later = lax.cond(lengths[0] > 0, attention_grads, blank, *operands)
    half_sum, later = lax.optimization_barrier((half_sum, later))
    grads = place(core, half_sum, ())
    grad_up, grad_down, grad_out = place(1 - core, swap_cores(half_sum), grads)
    return (layer_output, *later[:7], grad_out, grad_up, grad_down, *later[7:])


def solution(mesh):
    fine = Mesh(mesh.devices.reshape(4, 4, 2, GROUPS), ("x", "z", "core", "head"))
    dp = ("x", "z", "core")
    rows = P(dp, "head", None)
    return jax.shard_map(
        per_device,
        mesh=fine,
        in_specs=(rows, P(dp), rows) + (P(),) * 13,
        out_specs=(rows, rows) + (P(),) * 13,
        check_vma=False,
    )
```

```python
import functools

import jax
import jax.numpy as jnp
from jax import lax
from jax.experimental import pallas as pl
from jax.experimental.pallas import tpu as pltpu
from jax.sharding import Mesh
from jax.sharding import PartitionSpec as P

HDIM = 64
GROUPS = 4
BLOCK = 256
FULL = 1024
WIDTH = 768
COLS = 192
FF = 3072
SEQS = 3
CHUNK = 512
HEADS_HERE = 3
PACK_ROWS = 640
F32 = jnp.float32
BF16 = jnp.bfloat16
NN = (((1,), (0,)), ((), ()))
NT = (((1,), (1,)), ((), ()))
TN = (((0,), (0,)), ((), ()))


def dot(left, right, dims):
    return lax.dot_general(left, right, dims, preferred_element_type=F32)


def cost(flops, nbytes, transcendentals=0):
    return pl.CostEstimate(
        flops=int(flops), bytes_accessed=int(nbytes), transcendentals=int(transcendentals)
    )


def vmem():
    return pl.BlockSpec(memory_space=pltpu.VMEM)


def params(mib):
    return pltpu.CompilerParams(vmem_limit_bytes=mib << 20)


def unit_rows(rows):
    average = jnp.mean(rows, axis=-1, keepdims=True)
    centred = rows - average
    variance = jnp.mean(centred * centred, axis=-1, keepdims=True)
    inverse = lax.rsqrt(variance + 1e-05)
    return centred * inverse, inverse


def head_masks():
    lane = lax.broadcasted_iota(jnp.int32, (1, COLS), 1)
    return [
        jnp.where((lane >= h * HDIM) & (lane < (h + 1) * HDIM), 1.0, 0.0).astype(F32)
        for h in range(HEADS_HERE)
    ]


def conv_rows(raw_f, taps, tap_row, start):
    total = taps[tap_row : tap_row + 1, :] * raw_f[8 + start : 8 + start + BLOCK, :]
    for m in (1, 2):
        total += (
            taps[tap_row + m : tap_row + m + 1, :]
            * raw_f[8 + start - m : 8 + start - m + BLOCK, :]
        )
    return total


def attend_kernel(first, info, *refs):
    count = 5 if first else GROUPS
    pieces, refs = refs[:count], refs[count:]
    w_mine, taps, gain, bias = refs[:4]
    refs = refs[4:] if first else refs[10:]
    normed, raw_q, raw_k, raw_v, mixed, lse_t = refs[:6]
    pad_q, pad_k, pad_v, q_s, k_s, v_s, below = refs[6:]
    here = info[0]
    length = info[1] if first else info[2 + pl.program_id(0)]
    blocks = (length + BLOCK - 1) // BLOCK
    masks = head_masks()
    if first:
        homes = [(lax.rem(here + ahead, GROUPS), shift) for ahead, shift in ((0, 0), (1, 0), (2, 0), (2, 128), (3, 0))]
    else:
        homes = [(k, 0) for k in range(GROUPS)]

    for piece, (home, shift) in zip(pieces, homes):

        @pl.when(home < blocks)
        def _(piece=piece, home=home, shift=shift):
            rows = piece[...].reshape(piece.shape[-2], WIDTH).astype(F32)
            size = rows.shape[0]
            unit, _ = unit_rows(rows)
            low = (unit * gain[...] + bias[...]).astype(BF16)
            at = home * BLOCK + shift
            at = pl.multiple_of(at, 128) if first else at
            normed[0, pl.ds(at, size), :] = low
            for n, (raw, pad) in enumerate(((raw_q, pad_q), (raw_k, pad_k), (raw_v, pad_v))):
                value = dot(low, w_mine[n * COLS : (n + 1) * COLS, :], NT).astype(BF16)
                raw[0, pl.ds(at, size), :] = value
                pad[pl.ds(at + 8, size), :] = value.astype(F32)

    for pad in (pad_q, pad_k, pad_v):
        pad[0:8, :] = jnp.zeros((8, COLS), F32)
    row = lax.broadcasted_iota(jnp.int32, (BLOCK, BLOCK), 0)
    col = lax.broadcasted_iota(jnp.int32, (BLOCK, BLOCK), 1)
    below[...] = jnp.where(col <= row, 0.0, -1e30).astype(F32)

    for b in range(GROUPS):

        @pl.when(b < blocks)
        def _(b=b):
            at = slice(b * BLOCK, (b + 1) * BLOCK)
            q_s[at, :] = (conv_rows(pad_q, taps, 0, b * BLOCK).astype(BF16).astype(F32) * 0.125).astype(BF16)
            k_s[at, :] = conv_rows(pad_k, taps, 3, b * BLOCK).astype(BF16)
            v_s[at, :] = conv_rows(pad_v, taps, 6, b * BLOCK).astype(BF16)
            lane = lax.broadcasted_iota(jnp.int32, (BLOCK, 128), 1)
            total_out = jnp.zeros((BLOCK, COLS), F32)
            logs = jnp.zeros((BLOCK, 128), F32)
            for h in range(HEADS_HERE):
                q_h = q_s[at, :] * masks[h].astype(BF16)
                diag = dot(q_h, k_s[at, :], NT) + below[...]
                top = jnp.max(diag, axis=-1, keepdims=True)
                if b:
                    left = dot(q_h, k_s[0 : b * BLOCK, :], NT)
                    top = jnp.maximum(top, jnp.max(left, axis=-1, keepdims=True))
                    expo_left = jnp.exp(left - top)
                expo = jnp.exp(diag - top)
                total = jnp.sum(expo, axis=-1, keepdims=True)
                out = dot(expo.astype(BF16), v_s[at, :], NN)
                if b:
                    total += jnp.sum(expo_left, axis=-1, keepdims=True)
                    out += dot(expo_left.astype(BF16), v_s[0 : b * BLOCK, :], NN)
                total_out = total_out + (out * masks[h]) * (1.0 / total)
                logs = jnp.where(lane == h, top + jnp.log(total), logs)
            mixed[b] = jnp.transpose(total_out).astype(BF16)
            lse_t[0, :, at] = jnp.transpose(logs)[0:8, :]

        @pl.when(b >= blocks)
        def _(b=b):
            mixed[b] = jnp.zeros((COLS, BLOCK), BF16)


def attend(first, info, pieces, w_mine, taps, gain, bias, earlier=()):
    base = 0 if first else 1
    whole = lambda *shape: pl.BlockSpec(shape, lambda i, sc: (0,) * len(shape))
    mine = lambda *shape: pl.BlockSpec((1, *shape), lambda i, sc: (base + i,) + (0,) * len(shape))
    if first:
        piece_specs = [whole(*p.shape) for p in pieces]
    else:
        piece_specs = [
            pl.BlockSpec((1, 1, BLOCK, WIDTH), lambda i, sc, k=k: (k, i, 0, 0)) for k in range(GROUPS)
        ]
        pieces = [pieces] * GROUPS
    full = lambda dtype, *shape: jax.ShapeDtypeStruct((SEQS, *shape), dtype)
    return pl.pallas_call(
        functools.partial(attend_kernel, first),
        grid_spec=pltpu.PrefetchScalarGridSpec(
            num_scalar_prefetch=1,
            grid=(1 if first else SEQS - 1,),
            in_specs=piece_specs
            + [whole(3 * COLS, WIDTH), whole(9, COLS), whole(1, WIDTH), whole(1, WIDTH)]
            + [pl.BlockSpec(memory_space=pl.ANY)] * len(earlier),
            out_specs=[mine(FULL, WIDTH)]
            + [mine(FULL, COLS)] * 3
            + [pl.BlockSpec((GROUPS, COLS, BLOCK), lambda i, sc: (0, base + i, 0)), mine(8, FULL)],
            scratch_shapes=[pltpu.VMEM((FULL + 8, COLS), F32)] * 3
            + [pltpu.VMEM((FULL, COLS), BF16)] * 3
            + [pltpu.VMEM((BLOCK, BLOCK), F32)],
        ),
        out_shape=(
            full(BF16, FULL, WIDTH),
            full(BF16, FULL, COLS), full(BF16, FULL, COLS), full(BF16, FULL, COLS),
            jax.ShapeDtypeStruct((GROUPS, SEQS * COLS, BLOCK), BF16),
            full(F32, 8, FULL),
        ),
        input_output_aliases={1 + len(pieces) + 4 + n: n for n in range(len(earlier))},
        compiler_params=params(60),
        cost_estimate=cost(3e9, 8e6, 2e6),
        name="attend",
    )(info, *pieces, w_mine, taps, gain, bias, *earlier)


def attend_back_kernel(
    info, g_s, normed, raw_q, raw_k, raw_v, mixed, lse_t,
    w_mine, taps, gain, bias, ffn_vectors,
    d_own, d_next, d_prev, keep, send,
    dw_out, small_out, d_all, pack,
    pad_q, pad_k, pad_v, q_s, k_s, v_s, dq_s, dk_s, dv_s, below, p_all, ds_all,
):
    step = pl.program_id(0)
    here, core, length = info[0], info[1], info[2 + step]
    blocks = (length + BLOCK - 1) // BLOCK
    masks = head_masks()

    row = lax.broadcasted_iota(jnp.int32, (BLOCK, BLOCK), 0)
    col = lax.broadcasted_iota(jnp.int32, (BLOCK, BLOCK), 1)
    below[...] = jnp.where(row <= col, 0.0, -1e30).astype(F32)
    for pad, raw in ((pad_q, raw_q), (pad_k, raw_k), (pad_v, raw_v)):
        pad[0:8, :] = jnp.zeros((8, COLS), F32)
    for total in (dq_s, dk_s, dv_s):
        total[...] = jnp.zeros((FULL + 8, COLS), F32)

    for b in range(GROUPS):

        @pl.when(b < blocks)
        def _(b=b):
            at = slice(b * BLOCK, (b + 1) * BLOCK)
            for pad, raw in ((pad_q, raw_q), (pad_k, raw_k), (pad_v, raw_v)):
                pad[8 + b * BLOCK : 8 + (b + 1) * BLOCK, :] = raw[0, at, :].astype(F32)
            q_s[at, :] = (conv_rows(pad_q, taps, 0, b * BLOCK).astype(BF16).astype(F32) * 0.125).astype(BF16)
            k_s[at, :] = conv_rows(pad_k, taps, 3, b * BLOCK).astype(BF16)
            v_s[at, :] = conv_rows(pad_v, taps, 6, b * BLOCK).astype(BF16)
            both = g_s[b].astype(F32) * mixed[b].astype(F32)
            reach = slice(0, (b + 1) * BLOCK)
            dq_total = jnp.zeros((BLOCK, COLS), F32)
            q_heads, g_heads = [], []
            for h in range(HEADS_HERE):
                lanes = slice(h * BLOCK, (h + 1) * BLOCK)
                q_h = q_s[at, :] * masks[h].astype(BF16)
                own = slice(h * HDIM, (h + 1) * HDIM)
                blank = lambda n: [jnp.zeros((n * HDIM, BLOCK), BF16)] if n else []
                g_h = jnp.concatenate(blank(h) + [g_s[b, own, :]] + blank(HEADS_HERE - 1 - h), axis=0)
                q_heads.append(q_h)
                g_heads.append(g_h)
                row_dot = jnp.sum(both[own, :], axis=0, keepdims=True)
                log_row = lse_t[0, h : h + 1, at]
                for j in range(b + 1):
                    keys = slice(j * BLOCK, (j + 1) * BLOCK)
                    scores = dot(k_s[keys, :], q_h, NT)
                    if j == b:
                        scores = scores + below[...]
                    probs = jnp.exp(scores - log_row)
                    grad_probs = dot(v_s[keys, :], g_h, NN)
                    p_all[keys, lanes] = probs.astype(BF16)
                    ds_all[keys, lanes] = (probs * (grad_probs - row_dot)).astype(BF16)
                dq_total += dot(ds_all[reach, lanes], k_s[reach, :], TN) * masks[h]
            dq_s[at, :] = dq_total * 0.125
            dv_s[reach, :] += dot(p_all[reach, :], jnp.concatenate(g_heads, axis=1), NT)
            dk_s[reach, :] += dot(ds_all[reach, :], jnp.concatenate(q_heads, axis=0), NN)

    @pl.when(step == 0)
    def _():
        dw_out[...] = jnp.zeros_like(dw_out)
        small_out[...] = jnp.zeros_like(small_out)

    for b in range(GROUPS):

        @pl.when(b < blocks)
        def _(b=b):
            start = b * BLOCK
            at = slice(start, start + BLOCK)
            for n, (pad, grad) in enumerate(((pad_q, dq_s), (pad_k, dk_s), (pad_v, dv_s))):
                now = grad[at, :]
                value = taps[3 * n : 3 * n + 1, :] * now
                for m in (1, 2):
                    value += taps[3 * n + m : 3 * n + m + 1, :] * grad[start + m : start + m + BLOCK, :]
                value = value.astype(BF16).astype(F32)
                d_all[b, n * COLS : (n + 1) * COLS, :] = jnp.transpose(value).astype(BF16)
                small_out[9 + n : 10 + n, 0:COLS] += jnp.sum(value, axis=0, keepdims=True)
                for m in range(3):
                    shifted = pad[8 + start - m : 8 + start - m + BLOCK, :]
                    small_out[3 * n + m : 3 * n + m + 1, 0:COLS] += jnp.sum(
                        shifted * now, axis=0, keepdims=True
                    )
            dw_out[...] += dot(d_all[b], normed[0, at, :], NN)

        @pl.when(b >= blocks)
        def _(b=b):
            d_all[b] = jnp.zeros((3 * COLS, BLOCK), BF16)

    far = lax.rem(here + 2, GROUPS)
    d_own[0] = d_all[here]
    d_next[0, 0 : 3 * COLS, :] = d_all[lax.rem(here + 1, GROUPS)]
    d_next[0, 3 * COLS :, :] = d_all[far, 0 : 3 * COLS // 2, :]
    d_prev[0, 0 : 3 * COLS, :] = d_all[lax.rem(here + 3, GROUPS)]
    d_prev[0, 3 * COLS :, :] = d_all[far, 3 * COLS // 2 :, :]

    @pl.when(step == SEQS - 1)
    def _():
        grad_bias = jnp.zeros((1, WIDTH), F32)
        for n in range(3):
            sums = small_out[9 + n : 10 + n, 0:COLS]
            high = sums.astype(BF16)
            rest = (sums - high.astype(F32)).astype(BF16)
            for term in (high, rest):
                wide = jnp.broadcast_to(term.astype(F32), (16, COLS)).astype(BF16)
                grad_bias += dot(wide, w_mine[n * COLS : (n + 1) * COLS, :], NN)[0:1, :]
        grad_normed = jnp.sum(w_mine[...].astype(F32) * dw_out[...], axis=0, keepdims=True)
        grad_gain = (grad_normed - bias[...] * grad_bias) / gain[...]
        pack[0 : 3 * COLS, :] = dw_out[...].astype(BF16)
        tail = jnp.concatenate(
            [
                small_out[0:9, :],
                grad_gain,
                grad_bias,
                ffn_vectors[0:2, :],
                jnp.zeros((3, WIDTH), F32),
            ],
            axis=0,
        )
        pack[3 * COLS : 3 * COLS + 16, :] = tail.astype(BF16)
        pack[3 * COLS + 16 :, :] = jnp.zeros((PACK_ROWS - 3 * COLS - 16, WIDTH), BF16)
        half = PACK_ROWS // 2
        keep[...] = pack[pl.ds(pl.multiple_of(core * half, 64), half), :]
        send[...] = pack[pl.ds(pl.multiple_of((1 - core) * half, 64), half), :]


def attend_back(info, grad_mixed, saved, w_mine, taps, gain, bias, ffn_vectors):
    low = lambda *shape: jax.ShapeDtypeStruct(shape, BF16)
    whole = lambda *shape: pl.BlockSpec(shape, lambda i, sc: (0,) * len(shape))
    mine = lambda *shape: pl.BlockSpec((1, *shape), lambda i, sc: (i,) + (0,) * len(shape))
    across = pl.BlockSpec((GROUPS, COLS, BLOCK), lambda i, sc: (0, i, 0))
    long_rows = 3 * COLS * 3 // 2
    return pl.pallas_call(
        attend_back_kernel,
        grid_spec=pltpu.PrefetchScalarGridSpec(
            num_scalar_prefetch=1,
            grid=(SEQS,),
            in_specs=[across, mine(FULL, WIDTH)]
            + [mine(FULL, COLS)] * 3
            + [across, mine(8, FULL)]
            + [whole(3 * COLS, WIDTH), whole(9, COLS), whole(1, WIDTH), whole(1, WIDTH), whole(8, WIDTH)],
            out_specs=[mine(3 * COLS, BLOCK), mine(long_rows, BLOCK), mine(long_rows, BLOCK)]
            + [whole(PACK_ROWS // 2, WIDTH)] * 2,
            scratch_shapes=[
                pltpu.VMEM((3 * COLS, WIDTH), F32),
                pltpu.VMEM((16, WIDTH), F32),
                pltpu.VMEM((GROUPS, 3 * COLS, BLOCK), BF16),
                pltpu.VMEM((PACK_ROWS, WIDTH), BF16),
            ]
            + [pltpu.VMEM((FULL + 8, COLS), F32)] * 3
            + [pltpu.VMEM((FULL, COLS), BF16)] * 3
            + [pltpu.VMEM((FULL + 8, COLS), F32)] * 3
            + [pltpu.VMEM((BLOCK, BLOCK), F32)]
            + [pltpu.VMEM((FULL, HEADS_HERE * BLOCK), BF16)] * 2,
        ),
        out_shape=(
            low(SEQS, 3 * COLS, BLOCK), low(SEQS, long_rows, BLOCK), low(SEQS, long_rows, BLOCK),
            low(PACK_ROWS // 2, WIDTH), low(PACK_ROWS // 2, WIDTH),
        ),
        compiler_params=params(60),
        cost_estimate=cost(1e6, 1e5),
        name="attend_back",
    )(info, grad_mixed, *saved, w_mine, taps, gain, bias, ffn_vectors)


def ffn_kernel(
    info, x, cotangent, mixed, w_out, gain, bias, w_up, w_down,
    middle, low_grad, total_out, total_grad, send, keep,
    normed, sq_s, gh_s,
):
    step = pl.program_id(0)
    position = info[0] * BLOCK + lax.broadcasted_iota(jnp.int32, (BLOCK, 1), 0)

    @pl.when(step == 0)
    def _():
        for s in range(SEQS):
            at = slice(s * BLOCK, (s + 1) * BLOCK)
            heads = jnp.concatenate([mixed[k, s * COLS : (s + 1) * COLS, :] for k in range(GROUPS)], axis=0)
            value = x[s].astype(F32) + dot(heads, w_out[...], TN)
            middle[s] = value
            unit, _ = unit_rows(value)
            normed[at, :] = (unit * gain[...] + bias[...]).astype(BF16)
            keep_row = position < info[2 + s]
            low_grad[s] = jnp.where(keep_row, cotangent[s].astype(F32), 0.0).astype(BF16)
            total_out[s] = jnp.zeros((BLOCK, WIDTH), F32)
            total_grad[s] = jnp.zeros((BLOCK, WIDTH), F32)

    for s in range(SEQS):
        at = slice(s * BLOCK, (s + 1) * BLOCK)
        hidden = jnp.maximum(dot(normed[at, :], w_up[...], NN), 0.0)
        squared = (hidden * hidden).astype(BF16)
        sq_s[at, :] = squared
        back = dot(low_grad[s], w_down[...], NT)
        grad_hidden = (back * 2.0 * hidden).astype(BF16)
        gh_s[at, :] = grad_hidden
        total_out[s] += dot(squared, w_down[...], NN)
        total_grad[s] += dot(grad_hidden, w_up[...], NT)
    grad_up = dot(gh_s[...], normed[...], TN).astype(BF16)
    grad_down = dot(sq_s[...], low_grad[...].reshape(SEQS * BLOCK, WIDTH), TN).astype(BF16)
    steps = FF // CHUNK

    @pl.when(step < steps // 2)
    def _():
        send[0] = grad_up
        send[1] = grad_down

    @pl.when(step >= steps // 2)
    def _():
        keep[0] = grad_up
        keep[1] = grad_down


def ffn(info, x, cotangent, mixed, w_out, gain, bias, w_up, w_down):
    low = lambda *shape: jax.ShapeDtypeStruct(shape, BF16)
    full = lambda *shape: jax.ShapeDtypeStruct(shape, F32)
    rows = SEQS * BLOCK
    steps = FF // CHUNK
    half = steps // 2
    whole = lambda *shape: pl.BlockSpec(shape, lambda i, sc: (0,) * len(shape))

    def chunk(i, sc):
        return jnp.where(i < half, 1 - sc[1], sc[1]) * half + lax.rem(i, half)

    return pl.pallas_call(
        ffn_kernel,
        grid_spec=pltpu.PrefetchScalarGridSpec(
            num_scalar_prefetch=1,
            grid=(steps,),
            in_specs=[whole(SEQS, BLOCK, WIDTH)] * 2
            + [
                whole(GROUPS, SEQS * COLS, BLOCK),
                whole(WIDTH, WIDTH), whole(1, WIDTH), whole(1, WIDTH),
                pl.BlockSpec((WIDTH, CHUNK), lambda i, sc: (0, chunk(i, sc))),
                pl.BlockSpec((CHUNK, WIDTH), lambda i, sc: (chunk(i, sc), 0)),
            ],
            out_specs=[whole(SEQS, BLOCK, WIDTH)] * 4
            + [
                pl.BlockSpec((2, CHUNK, WIDTH), lambda i, sc: (0, jnp.minimum(i, half - 1), 0)),
                pl.BlockSpec((2, CHUNK, WIDTH), lambda i, sc: (0, jnp.maximum(i - half, 0), 0)),
            ],
            scratch_shapes=[
                pltpu.VMEM((rows, WIDTH), BF16),
                pltpu.VMEM((rows, CHUNK), BF16),
                pltpu.VMEM((rows, CHUNK), BF16),
            ],
        ),
        out_shape=(
            full(SEQS, BLOCK, WIDTH), low(SEQS, BLOCK, WIDTH),
            full(SEQS, BLOCK, WIDTH), full(SEQS, BLOCK, WIDTH),
            low(2, FF // 2, WIDTH), low(2, FF // 2, WIDTH),
        ),
        compiler_params=params(60),
        cost_estimate=cost(2.4e10, 3e7),
        name="ffn",
    )(info, x, cotangent, mixed, w_out, gain, bias, w_up, w_down)


def ffn_rows_kernel(
    info, middle, low_grad, total_out, total_grad, mixed, w_out, gain,
    layer_output, grad_middle, grad_mixed, send_out, keep_out, vectors,
    dw_out,
):
    step = pl.program_id(0)

    @pl.when(step == 0)
    def _():
        dw_out[...] = jnp.zeros_like(dw_out)
        vectors[...] = jnp.zeros_like(vectors)

    position = info[0] * BLOCK + lax.broadcasted_iota(jnp.int32, (BLOCK, 1), 0)
    layer_output[0] = jnp.where(position < info[2 + step], middle[0] + total_out[0], 0.0).astype(BF16)
    unit, inverse = unit_rows(middle[0])
    grad_normed = total_grad[0]
    scaled = grad_normed * gain[...]
    mean_grad = jnp.mean(scaled, axis=-1, keepdims=True)
    mean_dot = jnp.mean(scaled * unit, axis=-1, keepdims=True)
    value = low_grad[0].astype(F32) + inverse * (scaled - mean_grad - unit * mean_dot)
    vectors[0:1, :] += jnp.sum(grad_normed * unit, axis=0, keepdims=True)
    vectors[1:2, :] += jnp.sum(grad_normed, axis=0, keepdims=True)
    grad_middle[0] = value
    low = value.astype(BF16)
    heads_grad = dot(w_out[...], low, NT).astype(BF16)
    for k in range(GROUPS):
        grad_mixed[k] = heads_grad[k * COLS : (k + 1) * COLS]
    heads = jnp.concatenate([mixed[k] for k in range(GROUPS)], axis=0)
    dw_out[...] += dot(heads, low, NN)

    @pl.when(step == SEQS - 1)
    def _():
        half = WIDTH // 2
        keep_out[...] = dw_out[pl.ds(pl.multiple_of(info[1] * half, 128), half), :].astype(BF16)
        send_out[...] = dw_out[pl.ds(pl.multiple_of((1 - info[1]) * half, 128), half), :].astype(BF16)


def ffn_rows(info, middle, low_grad, total_out, total_grad, mixed, w_out, gain):
    low = lambda *shape: jax.ShapeDtypeStruct(shape, BF16)
    full = lambda *shape: jax.ShapeDtypeStruct(shape, F32)
    whole = lambda *shape: pl.BlockSpec(shape, lambda i, sc: (0,) * len(shape))
    mine = lambda: pl.BlockSpec((1, BLOCK, WIDTH), lambda i, sc: (i, 0, 0))
    across = lambda: pl.BlockSpec((GROUPS, COLS, BLOCK), lambda i, sc: (0, i, 0))
    return pl.pallas_call(
        ffn_rows_kernel,
        grid_spec=pltpu.PrefetchScalarGridSpec(
            num_scalar_prefetch=1,
            grid=(SEQS,),
            in_specs=[mine(), mine(), mine(), mine(), across(), whole(WIDTH, WIDTH), whole(1, WIDTH)],
            out_specs=[mine(), mine(), across()] + [whole(WIDTH // 2, WIDTH)] * 2 + [whole(8, WIDTH)],
            scratch_shapes=[pltpu.VMEM((WIDTH, WIDTH), F32)],
        ),
        out_shape=(
            low(SEQS, BLOCK, WIDTH), full(SEQS, BLOCK, WIDTH), low(GROUPS, SEQS * COLS, BLOCK),
            low(WIDTH // 2, WIDTH), low(WIDTH // 2, WIDTH), full(8, WIDTH),
        ),
        compiler_params=params(60),
        cost_estimate=cost(3e9, 1.5e7),
        name="ffn_rows",
    )(info, middle, low_grad, total_out, total_grad, mixed, w_out, gain)


def input_kernel(info, x, grad_middle, own, behind, over, ahead, under, w_groups, gain, out):
    here = info[0]
    w_of = lambda k: w_groups[lax.rem(here + k, GROUPS)]
    unit, inverse = unit_rows(x[0].astype(F32))
    grad_normed = dot(own[0], w_of(0), TN)
    grad_normed += dot(ahead[0], w_of(1), TN)
    grad_normed += dot(jnp.concatenate([over[0], under[0]], axis=0), w_of(2), TN)
    grad_normed += dot(behind[0], w_of(3), TN)
    scaled = grad_normed * gain[...]
    mean_grad = jnp.mean(scaled, axis=-1, keepdims=True)
    mean_dot = jnp.mean(scaled * unit, axis=-1, keepdims=True)
    out[0] = grad_middle[0] + inverse * (scaled - mean_grad - unit * mean_dot)


def input_grad_of(info, x, grad_middle, pieces, w_groups, gain):
    mine = lambda rows, lanes: pl.BlockSpec((1, rows, lanes), lambda i, sc: (i, 0, 0))
    whole = lambda *shape: pl.BlockSpec(shape, lambda i, sc: (0,) * len(shape))
    piece = mine(3 * COLS, BLOCK)
    half = mine(3 * COLS // 2, BLOCK)
    return pl.pallas_call(
        input_kernel,
        grid_spec=pltpu.PrefetchScalarGridSpec(
            num_scalar_prefetch=1,
            grid=(SEQS,),
            in_specs=[mine(BLOCK, WIDTH)] * 2
            + [piece, piece, half, piece, half, whole(*w_groups.shape), whole(1, WIDTH)],
            out_specs=mine(BLOCK, WIDTH),
        ),
        out_shape=jax.ShapeDtypeStruct((SEQS, BLOCK, WIDTH), F32),
        compiler_params=params(60),
        cost_estimate=cost(1e6, 1e5),
        name="input_grad",
    )(info, x, grad_middle, *pieces, w_groups, gain)


def place_kernel(info, up, down, out, *rest):
    grad_up, grad_down, grad_out = rest[-3:]
    grad_up[...] = jnp.transpose(up[...].astype(F32))
    grad_down[...] = down[...].astype(F32)
    grad_out[...] = out[...].astype(F32)


def place(side, up_down, out, earlier):
    half = FF // CHUNK // 2
    rows = lambda n, base: pl.BlockSpec((n, WIDTH), lambda i, sc: (base + i, 0))
    own = lambda n: pl.BlockSpec((n, WIDTH), lambda i, sc: (sc[0] * half + i, 0))
    out_rows = WIDTH // 2 // half
    return pl.pallas_call(
        place_kernel,
        grid_spec=pltpu.PrefetchScalarGridSpec(
            num_scalar_prefetch=1,
            grid=(half,),
            in_specs=[rows(CHUNK, 0), rows(CHUNK, half), rows(out_rows, 0)]
            + [pl.BlockSpec(memory_space=pl.ANY)] * len(earlier),
            out_specs=[
                pl.BlockSpec((WIDTH, CHUNK), lambda i, sc: (0, sc[0] * half + i)), own(CHUNK), own(out_rows)
            ],
        ),
        out_shape=(
            jax.ShapeDtypeStruct((WIDTH, FF), F32),
            jax.ShapeDtypeStruct((FF, WIDTH), F32),
            jax.ShapeDtypeStruct((WIDTH, WIDTH), F32),
        ),
        input_output_aliases={4 + n: n for n in range(len(earlier))},
        compiler_params=params(60),
        cost_estimate=cost(1e6, 1.6e7),
        name="place",
    )(side.reshape(1), up_down, up_down, out, *earlier)


def unpack_kernel(info, own, other, grad_q, grad_k, grad_v, tails, rows):
    half = PACK_ROWS // 2
    size = half // 16

    def fill(pieces, base):
        for y in range(GROUPS):
            for n in range(16):
                rows[y, base + n * size : base + (n + 1) * size, :] = pieces[n * GROUPS + y].astype(F32)

    @pl.when(info[0] == 0)
    def _():
        fill(own, 0)
        fill(other, half)

    @pl.when(info[0] != 0)
    def _():
        fill(other, 0)
        fill(own, half)

    for n, grad in enumerate((grad_q, grad_k, grad_v)):
        part = jnp.concatenate([rows[y, n * COLS : (n + 1) * COLS, :] for y in range(GROUPS)], axis=0)
        grad[...] = jnp.transpose(part)
    for y in range(GROUPS):
        tails[y] = rows[y, 3 * COLS : 3 * COLS + 16, :]


def unpack(core, own, other):
    full = lambda *shape: jax.ShapeDtypeStruct(shape, F32)
    return pl.pallas_call(
        unpack_kernel,
        in_specs=[pl.BlockSpec(memory_space=pltpu.SMEM), vmem(), vmem()],
        out_specs=[vmem()] * 4,
        out_shape=(full(WIDTH, WIDTH), full(WIDTH, WIDTH), full(WIDTH, WIDTH), full(GROUPS, 16, WIDTH)),
        scratch_shapes=[pltpu.VMEM((GROUPS, PACK_ROWS, WIDTH), F32)],
        compiler_params=params(60),
        cost_estimate=cost(1e6, 1e5),
        name="unpack",
    )(core.reshape(1), own, other)


def shift(array, axis, by):
    return lax.ppermute(array, axis, [(i, (i + by) % GROUPS) for i in range(GROUPS)])


def gather_rows(rows):
    ahead = shift(rows, "head", -1)
    behind = shift(rows, "head", 1)
    over_lo = shift(ahead[:128], "head", -1)
    over_hi = shift(behind[128:], "head", 1)
    return rows, ahead, over_lo, over_hi, behind


def near_exchange(to_next, to_prev):
    return shift(to_next, "head", 1), shift(to_prev, "head", -1)


def far_exchange(from_prev, from_next, size):
    return shift(from_prev[:, size:], "head", 1), shift(from_next[:, size:], "head", -1)


def trade(array, axes):
    return lax.all_to_all(array, axes, 0, 0, tiled=True)


def swap_cores(array):
    return lax.ppermute(array, "core", [(0, 1), (1, 0)])


def add_low(*terms):
    total = terms[0].astype(F32)
    for term in terms[1:]:
        total = total + term.astype(F32)
    return total.astype(BF16)


def per_device(
    layer_input, lengths, cotangent, w_query, w_key, w_value, conv_query, conv_key, conv_value,
    w_out, w_up, w_down, gain_attn, bias_attn, gain_ffn, bias_ffn,
):
    here = lax.axis_index("head").astype(jnp.int32)
    core = lax.axis_index("core").astype(jnp.int32)
    first_rows = gather_rows(layer_input[0])
    other_rows = lax.all_gather(layer_input[1:], "head", axis=0)

    w_groups = jnp.concatenate(
        [w.T.reshape(GROUPS, COLS, WIDTH) for w in (w_query, w_key, w_value)], axis=1
    )
    w_mine = lax.dynamic_index_in_dim(w_groups, here, 0, False)
    taps = lax.dynamic_slice_in_dim(
        jnp.concatenate([conv_query, conv_key, conv_value], axis=0), here * COLS, COLS, 1
    )
    gain_a, bias_a, gain_f, bias_f = (
        v.reshape(1, WIDTH) for v in (gain_attn, bias_attn, gain_ffn, bias_ffn)
    )
    info = jnp.concatenate([jnp.stack([here, core]), lengths])
    info_attend = jnp.concatenate([here.reshape(1), lengths])

    saved = attend(True, info_attend, first_rows, w_mine, taps, gain_a, bias_a)
    saved = attend(False, info_attend, other_rows, w_mine, taps, gain_a, bias_a, saved)
    mixed_rows = trade(saved[4], "head")
    middle, low_grad, total_out, total_grad, send, keep = ffn(
        info, layer_input, cotangent, mixed_rows, w_out, gain_f, bias_f, w_up, w_down
    )
    layer_output, grad_middle, grad_mixed, send_out, keep_out, ffn_vectors = ffn_rows(
        info, middle, low_grad, total_out, total_grad, mixed_rows, w_out, gain_f
    )

    half_sum = (
        add_low(keep, swap_cores(send)).reshape(FF, WIDTH),
        add_low(keep_out, swap_cores(send_out)),
    )
    half_sum, grad_mixed = lax.optimization_barrier((half_sum, trade(grad_mixed, "head")))
    half_sum = lax.psum(half_sum, ("x", "z", "head"))

    def attention_grads(grad_mixed, saved, grad_middle, ffn_vectors):
        d_own, d_next, d_prev, keep, send = attend_back(
            info, grad_mixed, saved, w_mine, taps, gain_a, bias_a, ffn_vectors
        )
        behind, ahead = near_exchange(d_next, d_prev)

        half = PACK_ROWS // 2
        part = add_low(keep, swap_cores(send)).reshape(16, half // 16, WIDTH)
        part = add_low(*trade(part, ("x", "z")))
        part, behind, ahead = lax.optimization_barrier((part, behind, ahead))
        over, under = far_exchange(behind, ahead, 3 * COLS)
        part = trade(jnp.broadcast_to(part[None], (64, half // 16, WIDTH)), ("x", "z", "head"))
        input_grad = input_grad_of(
            info, layer_input, grad_middle, (d_own, behind, over, ahead, under), w_groups, gain_a
        )
        grad_q, grad_k, grad_v, tails = unpack(core, part, swap_cores(part))
        conv = lambda n: jnp.transpose(tails[:, 3 * n : 3 * n + 3, 0:COLS], (1, 0, 2)).reshape(3, WIDTH)
        vector = jnp.sum(tails[:, 9:13, :], axis=0)
        return (
            input_grad, grad_q, grad_k, grad_v, conv(0), conv(1), conv(2),
            vector[0], vector[1], vector[2], vector[3],
        )

    operands = (grad_mixed, saved, grad_middle, ffn_vectors)
    blank = lambda *args: jax.tree.map(
        lambda a: jnp.zeros(a.shape, a.dtype), jax.eval_shape(attention_grads, *args)
    )
    later = lax.cond(lengths[0] > 0, attention_grads, blank, *operands)
    half_sum, later = lax.optimization_barrier((half_sum, later))
    grads = place(core, *half_sum, ())
    grad_up, grad_down, grad_out = place(1 - core, *(swap_cores(part) for part in half_sum), grads)
    return (layer_output, *later[:7], grad_out, grad_up, grad_down, *later[7:])


def solution(mesh):
    fine = Mesh(mesh.devices.reshape(4, 4, 2, GROUPS), ("x", "z", "core", "head"))
    dp = ("x", "z", "core")
    rows = P(dp, "head", None)
    return jax.shard_map(
        per_device,
        mesh=fine,
        in_specs=(rows, P(dp), rows) + (P(),) * 13,
        out_specs=(rows, rows) + (P(),) * 13,
        check_vma=False,
    )
```

```python
import functools

import jax
import jax.numpy as jnp
from jax import lax
from jax.experimental import pallas as pl
from jax.experimental.pallas import tpu as pltpu
from jax.sharding import Mesh
from jax.sharding import PartitionSpec as P

HDIM = 64
GROUPS = 4
BLOCK = 256
FULL = 1024
WIDTH = 768
COLS = 192
FF = 3072
SEQS = 3
CHUNK = 512
HEADS_HERE = 3
PACK_ROWS = 640
F32 = jnp.float32
BF16 = jnp.bfloat16
NN = (((1,), (0,)), ((), ()))
NT = (((1,), (1,)), ((), ()))
TN = (((0,), (0,)), ((), ()))


def dot(left, right, dims):
    return lax.dot_general(left, right, dims, preferred_element_type=F32)


def cost(flops, nbytes, transcendentals=0):
    return pl.CostEstimate(
        flops=int(flops), bytes_accessed=int(nbytes), transcendentals=int(transcendentals)
    )


def vmem():
    return pl.BlockSpec(memory_space=pltpu.VMEM)


def params(mib):
    return pltpu.CompilerParams(vmem_limit_bytes=mib << 20)


def unit_rows(rows):
    average = jnp.mean(rows, axis=-1, keepdims=True)
    centred = rows - average
    variance = jnp.mean(centred * centred, axis=-1, keepdims=True)
    inverse = lax.rsqrt(variance + 1e-05)
    return centred * inverse, inverse


def head_masks():
    lane = lax.broadcasted_iota(jnp.int32, (1, COLS), 1)
    return [
        jnp.where((lane >= h * HDIM) & (lane < (h + 1) * HDIM), 1.0, 0.0).astype(F32)
        for h in range(HEADS_HERE)
    ]


def conv_rows(raw_f, taps, tap_row, start):
    total = taps[tap_row : tap_row + 1, :] * raw_f[8 + start : 8 + start + BLOCK, :]
    for m in (1, 2):
        total += (
            taps[tap_row + m : tap_row + m + 1, :]
            * raw_f[8 + start - m : 8 + start - m + BLOCK, :]
        )
    return total


def attend_kernel(first, info, *refs):
    count = 5 if first else GROUPS
    pieces, refs = refs[:count], refs[count:]
    w_mine, taps, gain, bias = refs[:4]
    refs = refs[4:] if first else refs[10:]
    normed, raw_q, raw_k, raw_v, mixed, lse_t, to_rows = refs[:7]
    pad_q, pad_k, pad_v, q_s, k_s, v_s, below = refs[7:]
    here = info[0]
    length = info[2] if first else info[3 + pl.program_id(0)]
    blocks = (length + BLOCK - 1) // BLOCK
    masks = head_masks()
    if first:
        homes = [(lax.rem(here + ahead, GROUPS), shift) for ahead, shift in ((0, 0), (1, 0), (2, 0), (2, 128), (3, 0))]
    else:
        homes = [(k, 0) for k in range(GROUPS)]

    for piece, (home, shift) in zip(pieces, homes):

        @pl.when(home < blocks)
        def _(piece=piece, home=home, shift=shift):
            rows = piece[...].reshape(piece.shape[-2], WIDTH).astype(F32)
            size = rows.shape[0]
            unit, _ = unit_rows(rows)
            low = (unit * gain[...] + bias[...]).astype(BF16)
            at = home * BLOCK + shift
            at = pl.multiple_of(at, 128) if first else at
            normed[0, pl.ds(at, size), :] = low
            for n, (raw, pad) in enumerate(((raw_q, pad_q), (raw_k, pad_k), (raw_v, pad_v))):
                value = dot(low, w_mine[n * COLS : (n + 1) * COLS, :], NT).astype(BF16)
                raw[0, pl.ds(at, size), :] = value
                pad[pl.ds(at + 8, size), :] = value.astype(F32)

    for pad in (pad_q, pad_k, pad_v):
        pad[0:8, :] = jnp.zeros((8, COLS), F32)
    row = lax.broadcasted_iota(jnp.int32, (BLOCK, BLOCK), 0)
    col = lax.broadcasted_iota(jnp.int32, (BLOCK, BLOCK), 1)
    below[...] = jnp.where(col <= row, 0.0, -1e30).astype(F32)

    for b in range(GROUPS):

        @pl.when(b < blocks)
        def _(b=b):
            at = slice(b * BLOCK, (b + 1) * BLOCK)
            q_s[at, :] = (conv_rows(pad_q, taps, 0, b * BLOCK).astype(BF16).astype(F32) * 0.125).astype(BF16)
            k_s[at, :] = conv_rows(pad_k, taps, 3, b * BLOCK).astype(BF16)
            v_s[at, :] = conv_rows(pad_v, taps, 6, b * BLOCK).astype(BF16)
            lane = lax.broadcasted_iota(jnp.int32, (BLOCK, 128), 1)
            total_out = jnp.zeros((BLOCK, COLS), F32)
            logs = jnp.zeros((BLOCK, 128), F32)
            for h in range(HEADS_HERE):
                q_h = q_s[at, :] * masks[h].astype(BF16)
                diag = dot(q_h, k_s[at, :], NT) + below[...]
                top = jnp.max(diag, axis=-1, keepdims=True)
                if b:
                    left = dot(q_h, k_s[0 : b * BLOCK, :], NT)
                    top = jnp.maximum(top, jnp.max(left, axis=-1, keepdims=True))
                    expo_left = jnp.exp(left - top)
                expo = jnp.exp(diag - top)
                total = jnp.sum(expo, axis=-1, keepdims=True)
                out = dot(expo.astype(BF16), v_s[at, :], NN)
                if b:
                    total += jnp.sum(expo_left, axis=-1, keepdims=True)
                    out += dot(expo_left.astype(BF16), v_s[0 : b * BLOCK, :], NN)
                total_out = total_out + (out * masks[h]) * (1.0 / total)
                logs = jnp.where(lane == h, top + jnp.log(total), logs)
            result = jnp.transpose(total_out).astype(BF16)
            mixed[b] = result
            to_rows[b] = result
            lse_t[0, :, at] = jnp.transpose(logs)[0:8, :]

        @pl.when(b >= blocks)
        def _(b=b):
            mixed[b] = jnp.zeros((COLS, BLOCK), BF16)
            to_rows[b] = jnp.zeros((COLS, BLOCK), BF16)


def attend(first, info, pieces, w_mine, taps, gain, bias, earlier=()):
    base = 0 if first else 1
    whole = lambda *shape: pl.BlockSpec(shape, lambda i, sc: (0,) * len(shape))
    mine = lambda *shape: pl.BlockSpec((1, *shape), lambda i, sc: (base + i,) + (0,) * len(shape))
    if first:
        piece_specs = [whole(*p.shape) for p in pieces]
    else:
        piece_specs = [
            pl.BlockSpec((1, 1, BLOCK, WIDTH), lambda i, sc, k=k: (k, i, 0, 0)) for k in range(GROUPS)
        ]
        pieces = [pieces] * GROUPS
    full = lambda dtype, *shape: jax.ShapeDtypeStruct((SEQS, *shape), dtype)
    return pl.pallas_call(
        functools.partial(attend_kernel, first),
        grid_spec=pltpu.PrefetchScalarGridSpec(
            num_scalar_prefetch=1,
            grid=(1 if first else SEQS - 1,),
            in_specs=piece_specs
            + [whole(3 * COLS, WIDTH), whole(9, COLS), whole(1, WIDTH), whole(1, WIDTH)]
            + [pl.BlockSpec(memory_space=pl.ANY)] * len(earlier),
            out_specs=[mine(FULL, WIDTH)]
            + [mine(FULL, COLS)] * 3
            + [
                pl.BlockSpec((GROUPS, COLS, BLOCK), lambda i, sc: (0, base + i, 0)),
                mine(8, FULL),
                pl.BlockSpec((GROUPS, COLS, BLOCK), lambda i, sc: (0, i, 0)),
            ],
            scratch_shapes=[pltpu.VMEM((FULL + 8, COLS), F32)] * 3
            + [pltpu.VMEM((FULL, COLS), BF16)] * 3
            + [pltpu.VMEM((BLOCK, BLOCK), F32)],
        ),
        out_shape=(
            full(BF16, FULL, WIDTH),
            full(BF16, FULL, COLS), full(BF16, FULL, COLS), full(BF16, FULL, COLS),
            jax.ShapeDtypeStruct((GROUPS, SEQS * COLS, BLOCK), BF16),
            full(F32, 8, FULL),
            jax.ShapeDtypeStruct((GROUPS, (1 if first else SEQS - 1) * COLS, BLOCK), BF16),
        ),
        input_output_aliases={1 + len(pieces) + 4 + n: n for n in range(len(earlier))},
        compiler_params=params(60),
        cost_estimate=cost(3e9, 8e6, 2e6),
        name="attend",
    )(info, *pieces, w_mine, taps, gain, bias, *earlier)


def attend_back_kernel(
    info, g_s, normed, raw_q, raw_k, raw_v, mixed, lse_t,
    w_mine, taps, gain, bias, ffn_vectors,
    d_own, d_next, d_prev, keep, send,
    dw_out, small_out, d_all, pack,
    pad_q, pad_k, pad_v, q_s, k_s, v_s, dq_s, dk_s, dv_s, below, p_all, ds_all,
):
    step = pl.program_id(0)
    here, core, length = info[0], info[1], info[2 + step]
    blocks = (length + BLOCK - 1) // BLOCK
    masks = head_masks()

    row = lax.broadcasted_iota(jnp.int32, (BLOCK, BLOCK), 0)
    col = lax.broadcasted_iota(jnp.int32, (BLOCK, BLOCK), 1)
    below[...] = jnp.where(row <= col, 0.0, -1e30).astype(F32)
    for pad, raw in ((pad_q, raw_q), (pad_k, raw_k), (pad_v, raw_v)):
        pad[0:8, :] = jnp.zeros((8, COLS), F32)
    for total in (dq_s, dk_s, dv_s):
        total[...] = jnp.zeros((FULL + 8, COLS), F32)

    for b in range(GROUPS):

        @pl.when(b < blocks)
        def _(b=b):
            at = slice(b * BLOCK, (b + 1) * BLOCK)
            for pad, raw in ((pad_q, raw_q), (pad_k, raw_k), (pad_v, raw_v)):
                pad[8 + b * BLOCK : 8 + (b + 1) * BLOCK, :] = raw[0, at, :].astype(F32)
            q_s[at, :] = (conv_rows(pad_q, taps, 0, b * BLOCK).astype(BF16).astype(F32) * 0.125).astype(BF16)
            k_s[at, :] = conv_rows(pad_k, taps, 3, b * BLOCK).astype(BF16)
            v_s[at, :] = conv_rows(pad_v, taps, 6, b * BLOCK).astype(BF16)
            both = g_s[b].astype(F32) * mixed[b].astype(F32)
            reach = slice(0, (b + 1) * BLOCK)
            dq_total = jnp.zeros((BLOCK, COLS), F32)
            q_heads, g_heads = [], []
            for h in range(HEADS_HERE):
                lanes = slice(h * BLOCK, (h + 1) * BLOCK)
                q_h = q_s[at, :] * masks[h].astype(BF16)
                own = slice(h * HDIM, (h + 1) * HDIM)
                blank = lambda n: [jnp.zeros((n * HDIM, BLOCK), BF16)] if n else []
                g_h = jnp.concatenate(blank(h) + [g_s[b, own, :]] + blank(HEADS_HERE - 1 - h), axis=0)
                q_heads.append(q_h)
                g_heads.append(g_h)
                row_dot = jnp.sum(both[own, :], axis=0, keepdims=True)
                log_row = lse_t[0, h : h + 1, at]
                for j in range(b + 1):
                    keys = slice(j * BLOCK, (j + 1) * BLOCK)
                    scores = dot(k_s[keys, :], q_h, NT)
                    if j == b:
                        scores = scores + below[...]
                    probs = jnp.exp(scores - log_row)
                    grad_probs = dot(v_s[keys, :], g_h, NN)
                    p_all[keys, lanes] = probs.astype(BF16)
                    ds_all[keys, lanes] = (probs * (grad_probs - row_dot)).astype(BF16)
                dq_total += dot(ds_all[reach, lanes], k_s[reach, :], TN) * masks[h]
            dq_s[at, :] = dq_total * 0.125
            dv_s[reach, :] += dot(p_all[reach, :], jnp.concatenate(g_heads, axis=1), NT)
            dk_s[reach, :] += dot(ds_all[reach, :], jnp.concatenate(q_heads, axis=0), NN)

    @pl.when(step == 0)
    def _():
        dw_out[...] = jnp.zeros_like(dw_out)
        small_out[...] = jnp.zeros_like(small_out)

    for b in range(GROUPS):

        @pl.when(b < blocks)
        def _(b=b):
            start = b * BLOCK
            at = slice(start, start + BLOCK)
            for n, (pad, grad) in enumerate(((pad_q, dq_s), (pad_k, dk_s), (pad_v, dv_s))):
                now = grad[at, :]
                value = taps[3 * n : 3 * n + 1, :] * now
                for m in (1, 2):
                    value += taps[3 * n + m : 3 * n + m + 1, :] * grad[start + m : start + m + BLOCK, :]
                value = value.astype(BF16).astype(F32)
                d_all[b, n * COLS : (n + 1) * COLS, :] = jnp.transpose(value).astype(BF16)
                small_out[9 + n : 10 + n, 0:COLS] += jnp.sum(value, axis=0, keepdims=True)
                for m in range(3):
                    shifted = pad[8 + start - m : 8 + start - m + BLOCK, :]
                    small_out[3 * n + m : 3 * n + m + 1, 0:COLS] += jnp.sum(
                        shifted * now, axis=0, keepdims=True
                    )
            dw_out[...] += dot(d_all[b], normed[0, at, :], NN)

        @pl.when(b >= blocks)
        def _(b=b):
            d_all[b] = jnp.zeros((3 * COLS, BLOCK), BF16)

    far = lax.rem(here + 2, GROUPS)
    d_own[0] = d_all[here]
    d_next[0, 0 : 3 * COLS, :] = d_all[lax.rem(here + 1, GROUPS)]
    d_next[0, 3 * COLS :, :] = d_all[far, 0 : 3 * COLS // 2, :]
    d_prev[0, 0 : 3 * COLS, :] = d_all[lax.rem(here + 3, GROUPS)]
    d_prev[0, 3 * COLS :, :] = d_all[far, 3 * COLS // 2 :, :]

    @pl.when(step == SEQS - 1)
    def _():
        grad_bias = jnp.zeros((1, WIDTH), F32)
        for n in range(3):
            sums = small_out[9 + n : 10 + n, 0:COLS]
            high = sums.astype(BF16)
            rest = (sums - high.astype(F32)).astype(BF16)
            for term in (high, rest):
                wide = jnp.broadcast_to(term.astype(F32), (16, COLS)).astype(BF16)
                grad_bias += dot(wide, w_mine[n * COLS : (n + 1) * COLS, :], NN)[0:1, :]
        grad_normed = jnp.sum(w_mine[...].astype(F32) * dw_out[...], axis=0, keepdims=True)
        grad_gain = (grad_normed - bias[...] * grad_bias) / gain[...]
        pack[0 : 3 * COLS, :] = dw_out[...].astype(BF16)
        tail = jnp.concatenate(
            [
                small_out[0:9, :],
                grad_gain,
                grad_bias,
                ffn_vectors[0:2, :],
                jnp.zeros((3, WIDTH), F32),
            ],
            axis=0,
        )
        pack[3 * COLS : 3 * COLS + 16, :] = tail.astype(BF16)
        pack[3 * COLS + 16 :, :] = jnp.zeros((PACK_ROWS - 3 * COLS - 16, WIDTH), BF16)
        half = WIDTH // 2
        keep[...] = pack[:, pl.ds(pl.multiple_of(core * half, 128), half)]
        send[...] = pack[:, pl.ds(pl.multiple_of((1 - core) * half, 128), half)]


def attend_back(info, grad_mixed, saved, w_mine, taps, gain, bias, ffn_vectors):
    low = lambda *shape: jax.ShapeDtypeStruct(shape, BF16)
    whole = lambda *shape: pl.BlockSpec(shape, lambda i, sc: (0,) * len(shape))
    mine = lambda *shape: pl.BlockSpec((1, *shape), lambda i, sc: (i,) + (0,) * len(shape))
    across = pl.BlockSpec((GROUPS, COLS, BLOCK), lambda i, sc: (0, i, 0))
    long_rows = 3 * COLS * 3 // 2
    return pl.pallas_call(
        attend_back_kernel,
        grid_spec=pltpu.PrefetchScalarGridSpec(
            num_scalar_prefetch=1,
            grid=(SEQS,),
            in_specs=[across, mine(FULL, WIDTH)]
            + [mine(FULL, COLS)] * 3
            + [across, mine(8, FULL)]
            + [whole(3 * COLS, WIDTH), whole(9, COLS), whole(1, WIDTH), whole(1, WIDTH), whole(8, WIDTH)],
            out_specs=[mine(3 * COLS, BLOCK), mine(long_rows, BLOCK), mine(long_rows, BLOCK)]
            + [whole(PACK_ROWS, WIDTH // 2)] * 2,
            scratch_shapes=[
                pltpu.VMEM((3 * COLS, WIDTH), F32),
                pltpu.VMEM((16, WIDTH), F32),
                pltpu.VMEM((GROUPS, 3 * COLS, BLOCK), BF16),
                pltpu.VMEM((PACK_ROWS, WIDTH), BF16),
            ]
            + [pltpu.VMEM((FULL + 8, COLS), F32)] * 3
            + [pltpu.VMEM((FULL, COLS), BF16)] * 3
            + [pltpu.VMEM((FULL + 8, COLS), F32)] * 3
            + [pltpu.VMEM((BLOCK, BLOCK), F32)]
            + [pltpu.VMEM((FULL, HEADS_HERE * BLOCK), BF16)] * 2,
        ),
        out_shape=(
            low(SEQS, 3 * COLS, BLOCK), low(SEQS, long_rows, BLOCK), low(SEQS, long_rows, BLOCK),
            low(PACK_ROWS, WIDTH // 2), low(PACK_ROWS, WIDTH // 2),
        ),
        compiler_params=params(60),
        cost_estimate=cost(1e6, 1e5),
        name="attend_back",
    )(info, grad_mixed, *saved, w_mine, taps, gain, bias, ffn_vectors)


def ffn_kernel(
    info, x_0, x_1, x_2, c_0, c_1, c_2, mixed_0, mixed_1, w_out, gain, bias, w_up, w_down,
    layer_output, grad_middle, grad_mixed, squared_out, grad_hidden_out, normed, low_grad,
    send_out, keep_out, vectors,
    middle, total_out, total_grad, dw_out,
):
    step = pl.program_id(0)
    position = info[0] * BLOCK + lax.broadcasted_iota(jnp.int32, (BLOCK, 1), 0)
    parts = [slice(s * BLOCK, (s + 1) * BLOCK) for s in range(SEQS)]

    def heads_of(s):
        source, at = (mixed_0, 0) if s == 0 else (mixed_1, (s - 1) * COLS)
        return jnp.concatenate([source[k, at : at + COLS, :] for k in range(GROUPS)], axis=0)

    @pl.when(step == 0)
    def _():
        for s, (at, x, c) in enumerate(zip(parts, (x_0, x_1, x_2), (c_0, c_1, c_2))):
            value = x[0].astype(F32) + dot(heads_of(s), w_out[...], TN)
            middle[at, :] = value
            unit, _ = unit_rows(value)
            normed[at, :] = (unit * gain[...] + bias[...]).astype(BF16)
            low_grad[at, :] = jnp.where(position < info[2 + s], c[0].astype(F32), 0.0).astype(BF16)
            total_out[at, :] = jnp.zeros((BLOCK, WIDTH), F32)
            total_grad[at, :] = jnp.zeros((BLOCK, WIDTH), F32)

    for at in parts:
        hidden = jnp.maximum(dot(normed[at, :], w_up[...], NN), 0.0)
        squared = (hidden * hidden).astype(BF16)
        squared_out[at, :] = squared
        back = dot(low_grad[at, :], w_down[...], NT)
        grad_hidden = (back * 2.0 * hidden).astype(BF16)
        grad_hidden_out[at, :] = grad_hidden
        total_out[at, :] += dot(squared, w_down[...], NN)
        total_grad[at, :] += dot(grad_hidden, w_up[...], NT)

    @pl.when(step == FF // CHUNK - 1)
    def _():
        vectors[...] = jnp.zeros_like(vectors)
        dw_out[...] = jnp.zeros_like(dw_out)
        for s, at in enumerate(parts):
            result = jnp.where(position < info[2 + s], middle[at, :] + total_out[at, :], 0.0)
            layer_output[info[5 + s]] = result.astype(BF16)
            unit, inverse = unit_rows(middle[at, :])
            grad_normed = total_grad[at, :]
            scaled = grad_normed * gain[...]
            mean_grad = jnp.mean(scaled, axis=-1, keepdims=True)
            mean_dot = jnp.mean(scaled * unit, axis=-1, keepdims=True)
            value = low_grad[at, :].astype(F32) + inverse * (scaled - mean_grad - unit * mean_dot)
            vectors[0:1, :] += jnp.sum(grad_normed * unit, axis=0, keepdims=True)
            vectors[1:2, :] += jnp.sum(grad_normed, axis=0, keepdims=True)
            grad_middle[s] = value
            low = value.astype(BF16)
            heads_grad = dot(w_out[...], low, NT).astype(BF16)
            for k in range(GROUPS):
                grad_mixed[k, s * COLS : (s + 1) * COLS, :] = heads_grad[k * COLS : (k + 1) * COLS]
            dw_out[...] += dot(heads_of(s), low, NN)
        half = WIDTH // 2
        keep_out[...] = dw_out[pl.ds(pl.multiple_of(info[1] * half, 128), half), :].astype(BF16)
        send_out[...] = dw_out[pl.ds(pl.multiple_of((1 - info[1]) * half, 128), half), :].astype(BF16)


def ffn(info, x, cotangent, mixed, w_out, gain, bias, w_up, w_down):
    low = lambda *shape: jax.ShapeDtypeStruct(shape, BF16)
    full = lambda *shape: jax.ShapeDtypeStruct(shape, F32)
    rows = SEQS * BLOCK
    whole = lambda *shape: pl.BlockSpec(shape, lambda i, sc: (0,) * len(shape))
    nth = lambda s: pl.BlockSpec((1, BLOCK, WIDTH), lambda i, sc: (sc[5 + s], 0, 0))
    across = lambda n: pl.BlockSpec((n, CHUNK), lambda i, sc: (0, i))
    return pl.pallas_call(
        ffn_kernel,
        grid_spec=pltpu.PrefetchScalarGridSpec(
            num_scalar_prefetch=1,
            grid=(FF // CHUNK,),
            in_specs=[nth(s) for s in range(SEQS)] * 2
            + [
                whole(GROUPS, COLS, BLOCK), whole(GROUPS, (SEQS - 1) * COLS, BLOCK),
                whole(WIDTH, WIDTH), whole(1, WIDTH), whole(1, WIDTH),
                across(WIDTH),
                pl.BlockSpec((CHUNK, WIDTH), lambda i, sc: (i, 0)),
            ],
            out_specs=[
                whole(SEQS, BLOCK, WIDTH), whole(SEQS, BLOCK, WIDTH), whole(GROUPS, SEQS * COLS, BLOCK),
                across(rows), across(rows), whole(rows, WIDTH), whole(rows, WIDTH),
                whole(WIDTH // 2, WIDTH), whole(WIDTH // 2, WIDTH), whole(8, WIDTH),
            ],
            scratch_shapes=[pltpu.VMEM((rows, WIDTH), F32)] * 3 + [pltpu.VMEM((WIDTH, WIDTH), F32)],
        ),
        out_shape=(
            low(SEQS, BLOCK, WIDTH), full(SEQS, BLOCK, WIDTH), low(GROUPS, SEQS * COLS, BLOCK),
            low(rows, FF), low(rows, FF), low(rows, WIDTH), low(rows, WIDTH),
            low(WIDTH // 2, WIDTH), low(WIDTH // 2, WIDTH), full(8, WIDTH),
        ),
        compiler_params=params(60),
        cost_estimate=cost(2e10, 3e7),
        name="ffn",
    )(info, x, x, x, cotangent, cotangent, cotangent, *mixed, w_out, gain, bias, w_up, w_down)


def weight_kernel(info, squared, grad_hidden, normed, low_grad, *rest):
    grad_up = dot(grad_hidden[...], normed[...], TN)
    grad_down = dot(squared[...], low_grad[...], TN)
    if len(rest) == 1:
        (out,) = rest
    else:
        came, keep_out, came_out, out, sum_out = rest
        grad_up += came[0].astype(F32)
        grad_down += came[1].astype(F32)

        @pl.when(pl.program_id(0) == 0)
        def _():
            sum_out[...] = (keep_out[...].astype(F32) + came_out[...].astype(F32)).astype(BF16)

    out[0] = grad_up.astype(BF16)
    out[1] = grad_down.astype(BF16)


def weight_grads(side, squared, grad_hidden, normed, low_grad, others=()):
    low = lambda *shape: jax.ShapeDtypeStruct(shape, BF16)
    rows = SEQS * BLOCK
    half = FF // CHUNK // 2
    whole = lambda *shape: pl.BlockSpec(shape, lambda i, sc: (0,) * len(shape))
    across = pl.BlockSpec((rows, CHUNK), lambda i, sc: (0, sc[0] * half + i))
    both = pl.BlockSpec((2, CHUNK, WIDTH), lambda i, sc: (0, i, 0))
    out = whole(WIDTH // 2, WIDTH)
    return pl.pallas_call(
        weight_kernel,
        grid_spec=pltpu.PrefetchScalarGridSpec(
            num_scalar_prefetch=1,
            grid=(half,),
            in_specs=[across, across, whole(rows, WIDTH), whole(rows, WIDTH)] + ([both, out, out] if others else []),
            out_specs=[both] + ([out] if others else []),
        ),
        out_shape=[low(2, FF // 2, WIDTH)] + ([low(WIDTH // 2, WIDTH)] if others else []),
        compiler_params=params(60),
        cost_estimate=cost(3.6e9, 1.3e7),
        name="weight_grads",
    )(side.reshape(1), squared, grad_hidden, normed, low_grad, *others)


def input_kernel(info, x, grad_middle, own, behind, over, ahead, under, w_groups, gain, out):
    here = info[0]
    w_of = lambda k: w_groups[lax.rem(here + k, GROUPS)]
    unit, inverse = unit_rows(x[0].astype(F32))
    grad_normed = dot(own[0], w_of(0), TN)
    grad_normed += dot(ahead[0], w_of(1), TN)
    grad_normed += dot(jnp.concatenate([over[0], under[0]], axis=0), w_of(2), TN)
    grad_normed += dot(behind[0], w_of(3), TN)
    scaled = grad_normed * gain[...]
    mean_grad = jnp.mean(scaled, axis=-1, keepdims=True)
    mean_dot = jnp.mean(scaled * unit, axis=-1, keepdims=True)
    out[0] = grad_middle[0] + inverse * (scaled - mean_grad - unit * mean_dot)


def input_grad_of(info, x, grad_middle, pieces, w_groups, gain):
    mine = lambda rows, lanes: pl.BlockSpec((1, rows, lanes), lambda i, sc: (i, 0, 0))
    whole = lambda *shape: pl.BlockSpec(shape, lambda i, sc: (0,) * len(shape))
    placed = pl.BlockSpec((1, BLOCK, WIDTH), lambda i, sc: (sc[5 + i], 0, 0))
    piece = mine(3 * COLS, BLOCK)
    half = mine(3 * COLS // 2, BLOCK)
    return pl.pallas_call(
        input_kernel,
        grid_spec=pltpu.PrefetchScalarGridSpec(
            num_scalar_prefetch=1,
            grid=(SEQS,),
            in_specs=[placed, mine(BLOCK, WIDTH)]
            + [piece, piece, half, piece, half, whole(*w_groups.shape), whole(1, WIDTH)],
            out_specs=placed,
        ),
        out_shape=jax.ShapeDtypeStruct((SEQS, BLOCK, WIDTH), F32),
        compiler_params=params(60),
        cost_estimate=cost(1e6, 1e5),
        name="input_grad",
    )(info, x, grad_middle, *pieces, w_groups, gain)


def place_kernel(info, up, down, out, *rest):
    grad_up, grad_down, grad_out = rest[-3:]
    grad_up[...] = jnp.transpose(up[...].astype(F32))
    grad_down[...] = down[...].astype(F32)
    grad_out[...] = out[...].astype(F32)


def place(side, up_down, out, earlier):
    half = FF // CHUNK // 2
    rows = lambda n, base: pl.BlockSpec((n, WIDTH), lambda i, sc: (base + i, 0))
    own = lambda n: pl.BlockSpec((n, WIDTH), lambda i, sc: (sc[0] * half + i, 0))
    out_rows = WIDTH // 2 // half
    return pl.pallas_call(
        place_kernel,
        grid_spec=pltpu.PrefetchScalarGridSpec(
            num_scalar_prefetch=1,
            grid=(half,),
            in_specs=[rows(CHUNK, 0), rows(CHUNK, half), rows(out_rows, 0)]
            + [pl.BlockSpec(memory_space=pl.ANY)] * len(earlier),
            out_specs=[
                pl.BlockSpec((WIDTH, CHUNK), lambda i, sc: (0, sc[0] * half + i)), own(CHUNK), own(out_rows)
            ],
        ),
        out_shape=(
            jax.ShapeDtypeStruct((WIDTH, FF), F32),
            jax.ShapeDtypeStruct((FF, WIDTH), F32),
            jax.ShapeDtypeStruct((WIDTH, WIDTH), F32),
        ),
        input_output_aliases={4 + n: n for n in range(len(earlier))},
        compiler_params=params(60),
        cost_estimate=cost(1e6, 1.6e7),
        name="place",
    )(side.reshape(1), up_down, up_down, out, *earlier)


def unpack_kernel(info, own, other, grad_q, grad_k, grad_v, tails, rows):
    size = PACK_ROWS // 16
    half = WIDTH // 2

    def fill(pieces, base):
        for y in range(GROUPS):
            for n in range(16):
                rows[y, n * size : (n + 1) * size, base : base + half] = pieces[n * GROUPS + y].astype(F32)

    @pl.when(info[0] == 0)
    def _():
        fill(own, 0)
        fill(other, half)

    @pl.when(info[0] != 0)
    def _():
        fill(other, 0)
        fill(own, half)

    for n, grad in enumerate((grad_q, grad_k, grad_v)):
        part = jnp.concatenate([rows[y, n * COLS : (n + 1) * COLS, :] for y in range(GROUPS)], axis=0)
        grad[...] = jnp.transpose(part)
    for y in range(GROUPS):
        tails[y] = rows[y, 3 * COLS : 3 * COLS + 16, :]


def unpack(core, own, other):
    full = lambda *shape: jax.ShapeDtypeStruct(shape, F32)
    return pl.pallas_call(
        unpack_kernel,
        in_specs=[pl.BlockSpec(memory_space=pltpu.SMEM), vmem(), vmem()],
        out_specs=[vmem()] * 4,
        out_shape=(full(WIDTH, WIDTH), full(WIDTH, WIDTH), full(WIDTH, WIDTH), full(GROUPS, 16, WIDTH)),
        scratch_shapes=[pltpu.VMEM((GROUPS, PACK_ROWS, WIDTH), F32)],
        compiler_params=params(60),
        cost_estimate=cost(1e6, 1e5),
        name="unpack",
    )(core.reshape(1), own, other)


def shift(array, axis, by):
    return lax.ppermute(array, axis, [(i, (i + by) % GROUPS) for i in range(GROUPS)])


def gather_rows(rows):
    ahead = shift(rows, "head", -1)
    behind = shift(rows, "head", 1)
    over_lo = shift(ahead[:128], "head", -1)
    over_hi = shift(behind[128:], "head", 1)
    return rows, ahead, over_lo, over_hi, behind


def near_exchange(to_next, to_prev):
    return shift(to_next, "head", 1), shift(to_prev, "head", -1)


def far_exchange(from_prev, from_next, size):
    return shift(from_prev[:, size:], "head", 1), shift(from_next[:, size:], "head", -1)


def trade(array, axes):
    return lax.all_to_all(array, axes, 0, 0, tiled=True)


def swap_cores(array):
    return lax.ppermute(array, "core", [(0, 1), (1, 0)])


def add_low(*terms):
    total = terms[0].astype(F32)
    for term in terms[1:]:
        total = total + term.astype(F32)
    return total.astype(BF16)


def per_device(
    layer_input, lengths, cotangent, w_query, w_key, w_value, conv_query, conv_key, conv_value,
    w_out, w_up, w_down, gain_attn, bias_attn, gain_ffn, bias_ffn,
):
    here = lax.axis_index("head").astype(jnp.int32)
    core = lax.axis_index("core").astype(jnp.int32)
    first = jnp.where(
        (lengths[0] >= lengths[1]) & (lengths[0] >= lengths[2]), 0, jnp.where(lengths[1] >= lengths[2], 1, 2)
    )
    order = jnp.stack([first, jnp.where(first == 0, 1, 0), jnp.where(first == 2, 1, 2)]).astype(jnp.int32)
    pick = lambda n: lax.dynamic_index_in_dim(layer_input, order[n], 0, False)
    first_rows = gather_rows(pick(0))
    other_rows = lax.all_gather(jnp.stack([pick(1), pick(2)]), "head", axis=0)
    sorted_lengths = jnp.stack([jnp.max(lengths), lengths[order[1]], lengths[order[2]]])
    info = jnp.concatenate([jnp.stack([here, core]), sorted_lengths, order])

    w_groups = jnp.concatenate(
        [w.T.reshape(GROUPS, COLS, WIDTH) for w in (w_query, w_key, w_value)], axis=1
    )
    w_mine = lax.dynamic_index_in_dim(w_groups, here, 0, False)
    taps = lax.dynamic_slice_in_dim(
        jnp.concatenate([conv_query, conv_key, conv_value], axis=0), here * COLS, COLS, 1
    )
    gain_a, bias_a, gain_f, bias_f = (
        v.reshape(1, WIDTH) for v in (gain_attn, bias_attn, gain_ffn, bias_ffn)
    )
    *saved, mixed = attend(True, info, first_rows, w_mine, taps, gain_a, bias_a)
    mixed_rows = [trade(mixed, "head")]
    *saved, mixed = attend(False, info, other_rows, w_mine, taps, gain_a, bias_a, saved)
    mixed_rows.append(trade(mixed, "head"))
    (
        layer_output, grad_middle, grad_mixed, squared, grad_hidden, normed_ffn, low_grad, send_out, keep_out,
        ffn_vectors,
    ) = ffn(info, layer_input, cotangent, mixed_rows, w_out, gain_f, bias_f, w_up, w_down)

    rows_of = (squared, grad_hidden, normed_ffn, low_grad)
    (send,) = weight_grads(1 - core, *rows_of)
    came, came_out = swap_cores(send), swap_cores(send_out)
    up_down, out = weight_grads(core, *rows_of, (came, keep_out, came_out))
    half_sum, grad_mixed = lax.optimization_barrier(
        ((up_down.reshape(FF, WIDTH), out), trade(grad_mixed, "head"))
    )
    half_sum = lax.psum(half_sum, ("x", "z", "head"))

    def attention_grads(grad_mixed, saved, grad_middle, ffn_vectors):
        d_own, d_next, d_prev, keep, send = attend_back(
            info, grad_mixed, saved, w_mine, taps, gain_a, bias_a, ffn_vectors
        )
        behind, ahead = near_exchange(d_next, d_prev)

        part = add_low(keep, swap_cores(send)).reshape(16, PACK_ROWS // 16, WIDTH // 2)
        part = add_low(*trade(part, ("x", "z")))
        part, behind, ahead = lax.optimization_barrier((part, behind, ahead))
        over, under = far_exchange(behind, ahead, 3 * COLS)
        part = trade(jnp.broadcast_to(part[None], (64, *part.shape)), ("x", "z", "head"))
        input_grad = input_grad_of(
            info, layer_input, grad_middle, (d_own, behind, over, ahead, under), w_groups, gain_a
        )
        grad_q, grad_k, grad_v, tails = unpack(core, part, swap_cores(part))
        conv = lambda n: jnp.transpose(tails[:, 3 * n : 3 * n + 3, 0:COLS], (1, 0, 2)).reshape(3, WIDTH)
        vector = jnp.sum(tails[:, 9:13, :], axis=0)
        return (
            input_grad, grad_q, grad_k, grad_v, conv(0), conv(1), conv(2),
            vector[0], vector[1], vector[2], vector[3],
        )

    operands = (grad_mixed, saved, grad_middle, ffn_vectors)
    blank = lambda *args: jax.tree.map(
        lambda a: jnp.zeros(a.shape, a.dtype), jax.eval_shape(attention_grads, *args)
    )
    later = lax.cond(lengths[0] > 0, attention_grads, blank, *operands)
    half_sum, later = lax.optimization_barrier((half_sum, later))
    grads = place(core, *half_sum, ())
    grad_up, grad_down, grad_out = place(1 - core, *(swap_cores(part) for part in half_sum), grads)
    return (layer_output, *later[:7], grad_out, grad_up, grad_down, *later[7:])


def solution(mesh):
    fine = Mesh(mesh.devices.reshape(4, 4, 2, GROUPS), ("x", "z", "core", "head"))
    dp = ("x", "z", "core")
    rows = P(dp, "head", None)
    return jax.shard_map(
        per_device,
        mesh=fine,
        in_specs=(rows, P(dp), rows) + (P(),) * 13,
        out_specs=(rows, rows) + (P(),) * 13,
        check_vma=False,
    )
```

```python
import functools

import jax
import jax.numpy as jnp
from jax import lax
from jax.experimental import pallas as pl
from jax.experimental.pallas import tpu as pltpu
from jax.sharding import Mesh
from jax.sharding import PartitionSpec as P

HDIM = 64
GROUPS = 4
BLOCK = 256
FULL = 1024
WIDTH = 768
COLS = 192
FF = 3072
SEQS = 3
CHUNK = 512
SMALL = 256
HEADS_HERE = 3
PACK_ROWS = 640
F32 = jnp.float32
BF16 = jnp.bfloat16
NN = (((1,), (0,)), ((), ()))
NT = (((1,), (1,)), ((), ()))
TN = (((0,), (0,)), ((), ()))


def dot(left, right, dims):
    return lax.dot_general(left, right, dims, preferred_element_type=F32)


def cost(flops, nbytes, transcendentals=0):
    return pl.CostEstimate(
        flops=int(flops), bytes_accessed=int(nbytes), transcendentals=int(transcendentals)
    )


def vmem():
    return pl.BlockSpec(memory_space=pltpu.VMEM)


def params(mib):
    return pltpu.CompilerParams(vmem_limit_bytes=mib << 20)


def unit_rows(rows):
    average = jnp.mean(rows, axis=-1, keepdims=True)
    centred = rows - average
    variance = jnp.mean(centred * centred, axis=-1, keepdims=True)
    inverse = lax.rsqrt(variance + 1e-05)
    return centred * inverse, inverse


def head_masks():
    lane = lax.broadcasted_iota(jnp.int32, (1, COLS), 1)
    return [
        jnp.where((lane >= h * HDIM) & (lane < (h + 1) * HDIM), 1.0, 0.0).astype(F32)
        for h in range(HEADS_HERE)
    ]


def conv_rows(raw_f, taps, tap_row, start):
    total = taps[tap_row : tap_row + 1, :] * raw_f[8 + start : 8 + start + BLOCK, :]
    for m in (1, 2):
        total += (
            taps[tap_row + m : tap_row + m + 1, :]
            * raw_f[8 + start - m : 8 + start - m + BLOCK, :]
        )
    return total


def prepare_kernel(lengths, rows, first_rows, other_rows, info, sems):
    a, b, c = lengths[0], lengths[1], lengths[2]
    first = jnp.where((a >= b) & (a >= c), 0, jnp.where(b >= c, 1, 2))
    second = jnp.where(first == 0, 1, 0)
    third = jnp.where(first == 2, 1, 2)
    copies = [
        pltpu.make_async_copy(rows.at[first], first_rows, sems.at[0]),
        pltpu.make_async_copy(rows.at[second], other_rows.at[0], sems.at[1]),
        pltpu.make_async_copy(rows.at[third], other_rows.at[1], sems.at[2]),
    ]
    for copy in copies:
        copy.start()
    info[0] = lax.axis_index("head").astype(jnp.int32)
    info[1] = lax.axis_index("core").astype(jnp.int32)
    for n, s in enumerate((first, second, third)):
        info[2 + n] = jnp.where(s == 0, a, jnp.where(s == 1, b, c))
        info[5 + n] = s
    for copy in copies:
        copy.wait()


def prepare(lengths, rows):
    anywhere = pl.BlockSpec(memory_space=pl.ANY)
    scalars = pl.BlockSpec(memory_space=pltpu.SMEM)
    return pl.pallas_call(
        prepare_kernel,
        in_specs=[scalars, anywhere],
        out_specs=[anywhere, anywhere, scalars],
        out_shape=(
            jax.ShapeDtypeStruct((BLOCK, WIDTH), BF16),
            jax.ShapeDtypeStruct((SEQS - 1, BLOCK, WIDTH), BF16),
            jax.ShapeDtypeStruct((8,), jnp.int32),
        ),
        scratch_shapes=[pltpu.SemaphoreType.DMA((SEQS,))],
        compiler_params=params(60),
        cost_estimate=cost(1e3, 2.4e6),
        name="prepare",
    )(lengths, rows)


def attend_kernel(first, info, *refs):
    count = 5 if first else GROUPS
    pieces, refs = refs[:count], refs[count:]
    w_mine, taps, gain, bias = refs[:4]
    refs = refs[4:] if first else refs[10:]
    normed, raw_q, raw_k, raw_v, mixed, lse_t, to_rows = refs[:7]
    pad_q, pad_k, pad_v, q_s, k_s, v_s, below = refs[7:]
    here = info[0]
    length = info[2] if first else info[3 + pl.program_id(0)]
    blocks = (length + BLOCK - 1) // BLOCK
    masks = head_masks()
    if first:
        homes = [(lax.rem(here + ahead, GROUPS), shift) for ahead, shift in ((0, 0), (1, 0), (2, 0), (2, 128), (3, 0))]
    else:
        homes = [(k, 0) for k in range(GROUPS)]

    for piece, (home, shift) in zip(pieces, homes):

        @pl.when(home < blocks)
        def _(piece=piece, home=home, shift=shift):
            rows = piece[...].reshape(piece.shape[-2], WIDTH).astype(F32)
            size = rows.shape[0]
            unit, _ = unit_rows(rows)
            low = (unit * gain[...] + bias[...]).astype(BF16)
            at = home * BLOCK + shift
            at = pl.multiple_of(at, 128) if first else at
            normed[0, pl.ds(at, size), :] = low
            for n, (raw, pad) in enumerate(((raw_q, pad_q), (raw_k, pad_k), (raw_v, pad_v))):
                value = dot(low, w_mine[n * COLS : (n + 1) * COLS, :], NT).astype(BF16)
                raw[0, pl.ds(at, size), :] = value
                pad[pl.ds(at + 8, size), :] = value.astype(F32)

    for pad in (pad_q, pad_k, pad_v):
        pad[0:8, :] = jnp.zeros((8, COLS), F32)
    row = lax.broadcasted_iota(jnp.int32, (BLOCK, BLOCK), 0)
    col = lax.broadcasted_iota(jnp.int32, (BLOCK, BLOCK), 1)
    below[...] = jnp.where(col <= row, 0.0, -1e30).astype(F32)

    for b in range(GROUPS):

        @pl.when(b < blocks)
        def _(b=b):
            at = slice(b * BLOCK, (b + 1) * BLOCK)
            q_s[at, :] = (conv_rows(pad_q, taps, 0, b * BLOCK).astype(BF16).astype(F32) * 0.125).astype(BF16)
            k_s[at, :] = conv_rows(pad_k, taps, 3, b * BLOCK).astype(BF16)
            v_s[at, :] = conv_rows(pad_v, taps, 6, b * BLOCK).astype(BF16)
            lane = lax.broadcasted_iota(jnp.int32, (BLOCK, 128), 1)
            total_out = jnp.zeros((BLOCK, COLS), F32)
            logs = jnp.zeros((BLOCK, 128), F32)
            for h in range(HEADS_HERE):
                q_h = q_s[at, :] * masks[h].astype(BF16)
                diag = dot(q_h, k_s[at, :], NT) + below[...]
                top = jnp.max(diag, axis=-1, keepdims=True)
                if b:
                    left = dot(q_h, k_s[0 : b * BLOCK, :], NT)
                    top = jnp.maximum(top, jnp.max(left, axis=-1, keepdims=True))
                    expo_left = jnp.exp(left - top)
                expo = jnp.exp(diag - top)
                total = jnp.sum(expo, axis=-1, keepdims=True)
                out = dot(expo.astype(BF16), v_s[at, :], NN)
                if b:
                    total += jnp.sum(expo_left, axis=-1, keepdims=True)
                    out += dot(expo_left.astype(BF16), v_s[0 : b * BLOCK, :], NN)
                total_out = total_out + (out * masks[h]) * (1.0 / total)
                logs = jnp.where(lane == h, top + jnp.log(total), logs)
            result = jnp.transpose(total_out).astype(BF16)
            mixed[b] = result
            to_rows[b] = result
            lse_t[0, :, at] = jnp.transpose(logs)[0:8, :]

        @pl.when(b >= blocks)
        def _(b=b):
            mixed[b] = jnp.zeros((COLS, BLOCK), BF16)
            to_rows[b] = jnp.zeros((COLS, BLOCK), BF16)


def attend(first, info, pieces, w_mine, taps, gain, bias, earlier=()):
    base = 0 if first else 1
    whole = lambda *shape: pl.BlockSpec(shape, lambda i, sc: (0,) * len(shape))
    mine = lambda *shape: pl.BlockSpec((1, *shape), lambda i, sc: (base + i,) + (0,) * len(shape))
    if first:
        piece_specs = [whole(*p.shape) for p in pieces]
    else:
        piece_specs = [
            pl.BlockSpec((1, 1, BLOCK, WIDTH), lambda i, sc, k=k: (k, i, 0, 0)) for k in range(GROUPS)
        ]
        pieces = [pieces] * GROUPS
    full = lambda dtype, *shape: jax.ShapeDtypeStruct((SEQS, *shape), dtype)
    return pl.pallas_call(
        functools.partial(attend_kernel, first),
        grid_spec=pltpu.PrefetchScalarGridSpec(
            num_scalar_prefetch=1,
            grid=(1 if first else SEQS - 1,),
            in_specs=piece_specs
            + [whole(3 * COLS, WIDTH), whole(9, COLS), whole(1, WIDTH), whole(1, WIDTH)]
            + [pl.BlockSpec(memory_space=pl.ANY)] * len(earlier),
            out_specs=[mine(FULL, WIDTH)]
            + [mine(FULL, COLS)] * 3
            + [
                pl.BlockSpec((GROUPS, COLS, BLOCK), lambda i, sc: (0, base + i, 0)),
                mine(8, FULL),
                pl.BlockSpec((GROUPS, COLS, BLOCK), lambda i, sc: (0, i, 0)),
            ],
            scratch_shapes=[pltpu.VMEM((FULL + 8, COLS), F32)] * 3
            + [pltpu.VMEM((FULL, COLS), BF16)] * 3
            + [pltpu.VMEM((BLOCK, BLOCK), F32)],
        ),
        out_shape=(
            full(BF16, FULL, WIDTH),
            full(BF16, FULL, COLS), full(BF16, FULL, COLS), full(BF16, FULL, COLS),
            jax.ShapeDtypeStruct((GROUPS, SEQS * COLS, BLOCK), BF16),
            full(F32, 8, FULL),
            jax.ShapeDtypeStruct((GROUPS, (1 if first else SEQS - 1) * COLS, BLOCK), BF16),
        ),
        input_output_aliases={1 + len(pieces) + 4 + n: n for n in range(len(earlier))},
        compiler_params=params(60),
        cost_estimate=cost(3e9, 8e6, 2e6),
        name="attend",
    )(info, *pieces, w_mine, taps, gain, bias, *earlier)


def attend_back_kernel(
    info, g_first, g_others, normed, raw_q, raw_k, raw_v, mixed, lse_t,
    w_mine, taps, gain, bias, ffn_vectors,
    d_own, d_next, d_prev, keep, send,
    dw_out, small_out, d_all, pack, g_s,
    pad_q, pad_k, pad_v, q_s, k_s, v_s, dq_s, dk_s, dv_s, below, p_all, ds_all,
):
    step = pl.program_id(0)
    here, core, length = info[0], info[1], info[2 + step]

    @pl.when(step == 0)
    def _():
        g_s[...] = g_first[...]

    @pl.when(step > 0)
    def _():
        g_s[...] = g_others[...]

    blocks = (length + BLOCK - 1) // BLOCK
    masks = head_masks()

    row = lax.broadcasted_iota(jnp.int32, (BLOCK, BLOCK), 0)
    col = lax.broadcasted_iota(jnp.int32, (BLOCK, BLOCK), 1)
    below[...] = jnp.where(row <= col, 0.0, -1e30).astype(F32)
    for pad, raw in ((pad_q, raw_q), (pad_k, raw_k), (pad_v, raw_v)):
        pad[0:8, :] = jnp.zeros((8, COLS), F32)
    for total in (dq_s, dk_s, dv_s):
        total[...] = jnp.zeros((FULL + 8, COLS), F32)

    for b in range(GROUPS):

        @pl.when(b < blocks)
        def _(b=b):
            at = slice(b * BLOCK, (b + 1) * BLOCK)
            for pad, raw in ((pad_q, raw_q), (pad_k, raw_k), (pad_v, raw_v)):
                pad[8 + b * BLOCK : 8 + (b + 1) * BLOCK, :] = raw[0, at, :].astype(F32)
            q_s[at, :] = (conv_rows(pad_q, taps, 0, b * BLOCK).astype(BF16).astype(F32) * 0.125).astype(BF16)
            k_s[at, :] = conv_rows(pad_k, taps, 3, b * BLOCK).astype(BF16)
            v_s[at, :] = conv_rows(pad_v, taps, 6, b * BLOCK).astype(BF16)
            both = g_s[b].astype(F32) * mixed[b].astype(F32)
            reach = slice(0, (b + 1) * BLOCK)
            dq_total = jnp.zeros((BLOCK, COLS), F32)
            q_heads, g_heads = [], []
            for h in range(HEADS_HERE):
                lanes = slice(h * BLOCK, (h + 1) * BLOCK)
                q_h = q_s[at, :] * masks[h].astype(BF16)
                own = slice(h * HDIM, (h + 1) * HDIM)
                blank = lambda n: [jnp.zeros((n * HDIM, BLOCK), BF16)] if n else []
                g_h = jnp.concatenate(blank(h) + [g_s[b, own, :]] + blank(HEADS_HERE - 1 - h), axis=0)
                q_heads.append(q_h)
                g_heads.append(g_h)
                row_dot = jnp.sum(both[own, :], axis=0, keepdims=True)
                log_row = lse_t[0, h : h + 1, at]
                for j in range(b + 1):
                    keys = slice(j * BLOCK, (j + 1) * BLOCK)
                    scores = dot(k_s[keys, :], q_h, NT)
                    if j == b:
                        scores = scores + below[...]
                    probs = jnp.exp(scores - log_row)
                    grad_probs = dot(v_s[keys, :], g_h, NN)
                    p_all[keys, lanes] = probs.astype(BF16)
                    ds_all[keys, lanes] = (probs * (grad_probs - row_dot)).astype(BF16)
                dq_total += dot(ds_all[reach, lanes], k_s[reach, :], TN) * masks[h]
            dq_s[at, :] = dq_total * 0.125
            dv_s[reach, :] += dot(p_all[reach, :], jnp.concatenate(g_heads, axis=1), NT)
            dk_s[reach, :] += dot(ds_all[reach, :], jnp.concatenate(q_heads, axis=0), NN)

    @pl.when(step == 0)
    def _():
        dw_out[...] = jnp.zeros_like(dw_out)
        small_out[...] = jnp.zeros_like(small_out)

    for b in range(GROUPS):

        @pl.when(b < blocks)
        def _(b=b):
            start = b * BLOCK
            at = slice(start, start + BLOCK)
            for n, (pad, grad) in enumerate(((pad_q, dq_s), (pad_k, dk_s), (pad_v, dv_s))):
                now = grad[at, :]
                value = taps[3 * n : 3 * n + 1, :] * now
                for m in (1, 2):
                    value += taps[3 * n + m : 3 * n + m + 1, :] * grad[start + m : start + m + BLOCK, :]
                value = value.astype(BF16).astype(F32)
                d_all[b, n * COLS : (n + 1) * COLS, :] = jnp.transpose(value).astype(BF16)
                small_out[9 + n : 10 + n, 0:COLS] += jnp.sum(value, axis=0, keepdims=True)
                for m in range(3):
                    shifted = pad[8 + start - m : 8 + start - m + BLOCK, :]
                    small_out[3 * n + m : 3 * n + m + 1, 0:COLS] += jnp.sum(
                        shifted * now, axis=0, keepdims=True
                    )
            dw_out[...] += dot(d_all[b], normed[0, at, :], NN)

        @pl.when(b >= blocks)
        def _(b=b):
            d_all[b] = jnp.zeros((3 * COLS, BLOCK), BF16)

    far = lax.rem(here + 2, GROUPS)
    d_own[0] = d_all[here]
    d_next[0, 0 : 3 * COLS, :] = d_all[lax.rem(here + 1, GROUPS)]
    d_next[0, 3 * COLS :, :] = d_all[far, 0 : 3 * COLS // 2, :]
    d_prev[0, 0 : 3 * COLS, :] = d_all[lax.rem(here + 3, GROUPS)]
    d_prev[0, 3 * COLS :, :] = d_all[far, 3 * COLS // 2 :, :]

    @pl.when(step == SEQS - 1)
    def _():
        grad_bias = jnp.zeros((1, WIDTH), F32)
        for n in range(3):
            sums = small_out[9 + n : 10 + n, 0:COLS]
            high = sums.astype(BF16)
            rest = (sums - high.astype(F32)).astype(BF16)
            for term in (high, rest):
                wide = jnp.broadcast_to(term.astype(F32), (16, COLS)).astype(BF16)
                grad_bias += dot(wide, w_mine[n * COLS : (n + 1) * COLS, :], NN)[0:1, :]
        grad_normed = jnp.sum(w_mine[...].astype(F32) * dw_out[...], axis=0, keepdims=True)
        grad_gain = (grad_normed - bias[...] * grad_bias) / gain[...]
        pack[0 : 3 * COLS, :] = dw_out[...].astype(BF16)
        tail = jnp.concatenate(
            [
                small_out[0:9, :],
                grad_gain,
                grad_bias,
                ffn_vectors[0:2, :],
                jnp.zeros((3, WIDTH), F32),
            ],
            axis=0,
        )
        pack[3 * COLS : 3 * COLS + 16, :] = tail.astype(BF16)
        pack[3 * COLS + 16 :, :] = jnp.zeros((PACK_ROWS - 3 * COLS - 16, WIDTH), BF16)
        half = WIDTH // 2
        keep[...] = pack[:, pl.ds(pl.multiple_of(core * half, 128), half)]
        send[...] = pack[:, pl.ds(pl.multiple_of((1 - core) * half, 128), half)]


def attend_back(info, grad_mixed, saved, w_mine, taps, gain, bias, ffn_vectors):
    low = lambda *shape: jax.ShapeDtypeStruct(shape, BF16)
    whole = lambda *shape: pl.BlockSpec(shape, lambda i, sc: (0,) * len(shape))
    mine = lambda *shape: pl.BlockSpec((1, *shape), lambda i, sc: (i,) + (0,) * len(shape))
    across = pl.BlockSpec((GROUPS, COLS, BLOCK), lambda i, sc: (0, i, 0))
    long_rows = 3 * COLS * 3 // 2
    return pl.pallas_call(
        attend_back_kernel,
        grid_spec=pltpu.PrefetchScalarGridSpec(
            num_scalar_prefetch=1,
            grid=(SEQS,),
            in_specs=[
                whole(GROUPS, COLS, BLOCK),
                pl.BlockSpec((GROUPS, COLS, BLOCK), lambda i, sc: (0, jnp.maximum(i - 1, 0), 0)),
                mine(FULL, WIDTH),
            ]
            + [mine(FULL, COLS)] * 3
            + [across, mine(8, FULL)]
            + [whole(3 * COLS, WIDTH), whole(9, COLS), whole(1, WIDTH), whole(1, WIDTH), whole(8, WIDTH)],
            out_specs=[mine(3 * COLS, BLOCK), mine(long_rows, BLOCK), mine(long_rows, BLOCK)]
            + [whole(PACK_ROWS, WIDTH // 2)] * 2,
            scratch_shapes=[
                pltpu.VMEM((3 * COLS, WIDTH), F32),
                pltpu.VMEM((16, WIDTH), F32),
                pltpu.VMEM((GROUPS, 3 * COLS, BLOCK), BF16),
                pltpu.VMEM((PACK_ROWS, WIDTH), BF16),
                pltpu.VMEM((GROUPS, COLS, BLOCK), BF16),
            ]
            + [pltpu.VMEM((FULL + 8, COLS), F32)] * 3
            + [pltpu.VMEM((FULL, COLS), BF16)] * 3
            + [pltpu.VMEM((FULL + 8, COLS), F32)] * 3
            + [pltpu.VMEM((BLOCK, BLOCK), F32)]
            + [pltpu.VMEM((FULL, HEADS_HERE * BLOCK), BF16)] * 2,
        ),
        out_shape=(
            low(SEQS, 3 * COLS, BLOCK), low(SEQS, long_rows, BLOCK), low(SEQS, long_rows, BLOCK),
            low(PACK_ROWS, WIDTH // 2), low(PACK_ROWS, WIDTH // 2),
        ),
        compiler_params=params(60),
        cost_estimate=cost(1e6, 1e5),
        name="attend_back",
    )(info, *grad_mixed, *saved, w_mine, taps, gain, bias, ffn_vectors)


def ffn_kernel(first, info, *refs):
    count = 1 if first else SEQS - 1
    base = 0 if first else 1
    x, cotangent, refs = refs[:count], refs[count : 2 * count], refs[2 * count :]
    mixed, w_out, gain, bias, w_up, w_down = refs[:6]
    refs = refs[6:]
    if not first:
        mixed_first, branch_first, vectors_first = refs[:3]
        refs = refs[3:]
    layer_output, grad_middle, grad_mixed, squared_out, grad_hidden_out, normed, low_grad, branch, vectors = refs[:9]
    if not first:
        send_out, keep_out = refs[9:11]
    middle, total_out, total_grad, dw_out = refs[-4:]
    step = pl.program_id(0)
    position = info[0] * BLOCK + lax.broadcasted_iota(jnp.int32, (BLOCK, 1), 0)
    parts = [slice(s * BLOCK, (s + 1) * BLOCK) for s in range(count)]

    def heads_of(source, s):
        return jnp.concatenate([source[k, s * COLS : (s + 1) * COLS, :] for k in range(GROUPS)], axis=0)

    @pl.when(step == 0)
    def _():
        for s, at in enumerate(parts):
            value = x[s][0].astype(F32) + dot(heads_of(mixed, s), w_out[...], TN)
            middle[at, :] = value
            unit, _ = unit_rows(value)
            normed[at, :] = (unit * gain[...] + bias[...]).astype(BF16)
            keep_row = position < info[2 + base + s]
            low_grad[at, :] = jnp.where(keep_row, cotangent[s][0].astype(F32), 0.0).astype(BF16)
            total_out[at, :] = jnp.zeros((BLOCK, WIDTH), F32)
            total_grad[at, :] = jnp.zeros((BLOCK, WIDTH), F32)

    for at in parts:
        hidden = jnp.maximum(dot(normed[at, :], w_up[...], NN), 0.0)
        squared = (hidden * hidden).astype(BF16)
        squared_out[at, :] = squared
        back = dot(low_grad[at, :], w_down[...], NT)
        grad_hidden = (back * 2.0 * hidden).astype(BF16)
        grad_hidden_out[at, :] = grad_hidden
        total_out[at, :] += dot(squared, w_down[...], NN)
        total_grad[at, :] += dot(grad_hidden, w_up[...], NT)

    @pl.when(step == FF // CHUNK - 1)
    def _():
        if first:
            vectors[...] = jnp.zeros_like(vectors)
        else:
            vectors[...] = vectors_first[...]
            dw_out[...] = dot(heads_of(mixed_first, 0), branch_first[...], NN)
        for s, at in enumerate(parts):
            keep_row = position < info[2 + base + s]
            layer_output[s] = jnp.where(keep_row, middle[at, :] + total_out[at, :], 0.0).astype(BF16)
            unit, inverse = unit_rows(middle[at, :])
            grad_normed = total_grad[at, :]
            scaled = grad_normed * gain[...]
            mean_grad = jnp.mean(scaled, axis=-1, keepdims=True)
            mean_dot = jnp.mean(scaled * unit, axis=-1, keepdims=True)
            value = low_grad[at, :].astype(F32) + inverse * (scaled - mean_grad - unit * mean_dot)
            vectors[0:1, :] += jnp.sum(grad_normed * unit, axis=0, keepdims=True)
            vectors[1:2, :] += jnp.sum(grad_normed, axis=0, keepdims=True)
            grad_middle[s] = value
            low = value.astype(BF16)
            branch[at, :] = low
            heads_grad = dot(w_out[...], low, NT).astype(BF16)
            for k in range(GROUPS):
                grad_mixed[k, s * COLS : (s + 1) * COLS, :] = heads_grad[k * COLS : (k + 1) * COLS]
            if not first:
                dw_out[...] += dot(heads_of(mixed, s), low, NN)
        if not first:
            half = WIDTH // 2
            keep_out[...] = dw_out[pl.ds(pl.multiple_of(info[1] * half, 128), half), :].astype(BF16)
            send_out[...] = dw_out[pl.ds(pl.multiple_of((1 - info[1]) * half, 128), half), :].astype(BF16)


def ffn(first, info, x, cotangent, mixed, w_out, gain, bias, w_up, w_down, earlier=()):
    count = 1 if first else SEQS - 1
    base = 0 if first else 1
    low = lambda *shape: jax.ShapeDtypeStruct(shape, BF16)
    full = lambda *shape: jax.ShapeDtypeStruct(shape, F32)
    rows = count * BLOCK
    whole = lambda *shape: pl.BlockSpec(shape, lambda i, sc: (0,) * len(shape))
    nth = lambda s: pl.BlockSpec((1, BLOCK, WIDTH), lambda i, sc: (sc[5 + base + s], 0, 0))
    across = lambda n: pl.BlockSpec((n, CHUNK), lambda i, sc: (0, i))
    halves = [] if first else [low(WIDTH // 2, WIDTH)] * 2
    return pl.pallas_call(
        functools.partial(ffn_kernel, first),
        grid_spec=pltpu.PrefetchScalarGridSpec(
            num_scalar_prefetch=1,
            grid=(FF // CHUNK,),
            in_specs=[nth(s) for s in range(count)] * 2
            + [
                whole(GROUPS, count * COLS, BLOCK), whole(WIDTH, WIDTH), whole(1, WIDTH), whole(1, WIDTH),
                across(WIDTH),
                pl.BlockSpec((CHUNK, WIDTH), lambda i, sc: (i, 0)),
            ]
            + [whole(*a.shape) for a in earlier],
            out_specs=[
                whole(count, BLOCK, WIDTH), whole(count, BLOCK, WIDTH), whole(GROUPS, count * COLS, BLOCK),
                across(rows), across(rows), whole(rows, WIDTH), whole(rows, WIDTH), whole(rows, WIDTH),
                whole(8, WIDTH),
            ]
            + [whole(*a.shape) for a in halves],
            scratch_shapes=[pltpu.VMEM((rows, WIDTH), F32)] * 3 + [pltpu.VMEM((WIDTH, WIDTH), F32)],
        ),
        out_shape=[
            low(count, BLOCK, WIDTH), full(count, BLOCK, WIDTH), low(GROUPS, count * COLS, BLOCK),
            low(rows, FF), low(rows, FF), low(rows, WIDTH), low(rows, WIDTH), low(rows, WIDTH),
            full(8, WIDTH),
        ]
        + halves,
        compiler_params=params(60),
        cost_estimate=cost(7e9 * count, 1.8e7),
        name="ffn",
    )(info, *[x] * count, *[cotangent] * count, mixed, w_out, gain, bias, w_up, w_down, *earlier)


def weight_kernel(info, *refs):
    squared, grad_hidden, normed, low_grad = (
        jnp.concatenate([refs[2 * n][...], refs[2 * n + 1][...]], axis=0) for n in range(4)
    )
    rest = refs[8:]
    grad_up = dot(grad_hidden, normed, TN)
    grad_down = dot(squared, low_grad, TN)
    if len(rest) > 1:
        grad_up += rest[0][0].astype(F32)
        grad_down += rest[0][1].astype(F32)
    if len(rest) > 2:
        keep_out, came_out, sum_out = rest[1], rest[2], rest[4]

        @pl.when(pl.program_id(0) == 0)
        def _():
            sum_out[...] = (keep_out[...].astype(F32) + came_out[...].astype(F32)).astype(BF16)

    out = rest[3] if len(rest) > 2 else rest[-1]
    out[0] = grad_up.astype(BF16)
    out[1] = grad_down.astype(BF16)


def weight_grads(quarter, rows_of, came=(), outs=()):
    low = lambda *shape: jax.ShapeDtypeStruct(shape, BF16)
    steps = FF // 4 // SMALL
    whole = lambda *shape: pl.BlockSpec(shape, lambda i, sc: (0,) * len(shape))
    across = lambda a: pl.BlockSpec((a.shape[0], SMALL), lambda i, sc: (0, sc[0] * steps + i))
    both = pl.BlockSpec((2, SMALL, WIDTH), lambda i, sc: (0, i, 0))
    out = whole(WIDTH // 2, WIDTH)
    wide, narrow = rows_of[:4], rows_of[4:]
    return pl.pallas_call(
        weight_kernel,
        grid_spec=pltpu.PrefetchScalarGridSpec(
            num_scalar_prefetch=1,
            grid=(steps,),
            in_specs=[across(a) for a in wide]
            + [whole(*a.shape) for a in narrow]
            + [both for _ in came]
            + [out for _ in outs],
            out_specs=[both] + ([out] if outs else []),
        ),
        out_shape=[low(2, FF // 4, WIDTH)] + ([low(WIDTH // 2, WIDTH)] if outs else []),
        compiler_params=params(60),
        cost_estimate=cost(1.8e9, 7e6),
        name="weight_grads",
    )(quarter.reshape(1), *rows_of, *came, *outs)


def input_kernel(
    info, x, middle_first, middle_others, output_first, output_others, own, behind, over, ahead, under, w_groups, gain,
    out, layer_output, grad_middle,
):
    @pl.when(pl.program_id(0) == 0)
    def _():
        grad_middle[...] = middle_first[0]
        layer_output[...] = output_first[...]

    @pl.when(pl.program_id(0) > 0)
    def _():
        grad_middle[...] = middle_others[0]
        layer_output[...] = output_others[...]

    here = info[0]
    w_of = lambda k: w_groups[lax.rem(here + k, GROUPS)]
    unit, inverse = unit_rows(x[0].astype(F32))
    grad_normed = dot(own[0], w_of(0), TN)
    grad_normed += dot(ahead[0], w_of(1), TN)
    grad_normed += dot(jnp.concatenate([over[0], under[0]], axis=0), w_of(2), TN)
    grad_normed += dot(behind[0], w_of(3), TN)
    scaled = grad_normed * gain[...]
    mean_grad = jnp.mean(scaled, axis=-1, keepdims=True)
    mean_dot = jnp.mean(scaled * unit, axis=-1, keepdims=True)
    out[0] = grad_middle[...] + inverse * (scaled - mean_grad - unit * mean_dot)


def input_grad_of(info, x, grad_middle, layer_output, pieces, w_groups, gain):
    mine = lambda rows, lanes: pl.BlockSpec((1, rows, lanes), lambda i, sc: (i, 0, 0))
    whole = lambda *shape: pl.BlockSpec(shape, lambda i, sc: (0,) * len(shape))
    placed = pl.BlockSpec((1, BLOCK, WIDTH), lambda i, sc: (sc[5 + i], 0, 0))
    two = [whole(1, BLOCK, WIDTH), pl.BlockSpec((1, BLOCK, WIDTH), lambda i, sc: (jnp.maximum(i - 1, 0), 0, 0))]
    piece = mine(3 * COLS, BLOCK)
    half = mine(3 * COLS // 2, BLOCK)
    return pl.pallas_call(
        input_kernel,
        grid_spec=pltpu.PrefetchScalarGridSpec(
            num_scalar_prefetch=1,
            grid=(SEQS,),
            in_specs=[placed, *two, *two, piece, piece, half, piece, half, whole(*w_groups.shape), whole(1, WIDTH)],
            out_specs=[placed, placed],
            scratch_shapes=[pltpu.VMEM((BLOCK, WIDTH), F32)],
        ),
        out_shape=(
            jax.ShapeDtypeStruct((SEQS, BLOCK, WIDTH), F32),
            jax.ShapeDtypeStruct((SEQS, BLOCK, WIDTH), BF16),
        ),
        compiler_params=params(60),
        cost_estimate=cost(1e6, 1e5),
        name="input_grad",
    )(info, x, *grad_middle, *layer_output, *pieces, w_groups, gain)


def place_kernel(info, up, down, out, *rest):
    grad_up, grad_down, grad_out = rest[-3:]
    grad_up[...] = jnp.transpose(up[0].astype(F32))
    grad_down[...] = down[0].astype(F32)
    grad_out[...] = out[...].astype(F32)


def place(side, quarters, out, earlier):
    steps = FF // 4 // SMALL
    rows = lambda which: pl.BlockSpec((1, SMALL, WIDTH), lambda i, sc: (which, i, 0))
    out_rows = WIDTH // 4 // steps
    for n, quarter in enumerate(quarters):
        own = lambda r, n=n: pl.BlockSpec((r, WIDTH), lambda i, sc: ((sc[0] * 2 + n) * steps + i, 0))
        earlier = pl.pallas_call(
            place_kernel,
            grid_spec=pltpu.PrefetchScalarGridSpec(
                num_scalar_prefetch=1,
                grid=(steps,),
                in_specs=[
                    rows(0), rows(1), pl.BlockSpec((out_rows, WIDTH), lambda i, sc, n=n: (n * steps + i, 0))
                ]
                + [pl.BlockSpec(memory_space=pl.ANY)] * len(earlier),
                out_specs=[
                    pl.BlockSpec((WIDTH, SMALL), lambda i, sc, n=n: (0, (sc[0] * 2 + n) * steps + i)),
                    own(SMALL), own(out_rows),
                ],
            ),
            out_shape=(
                jax.ShapeDtypeStruct((WIDTH, FF), F32),
                jax.ShapeDtypeStruct((FF, WIDTH), F32),
                jax.ShapeDtypeStruct((WIDTH, WIDTH), F32),
            ),
            input_output_aliases={4 + m: m for m in range(len(earlier))},
            compiler_params=params(60),
            cost_estimate=cost(1e6, 8e6),
            name="place",
        )(side.reshape(1), quarter, quarter, out, *earlier)
    return earlier


def unpack_kernel(info, own, other, grad_q, grad_k, grad_v, tails, rows):
    size = PACK_ROWS // 16
    half = WIDTH // 2

    def fill(pieces, base):
        for y in range(GROUPS):
            for n in range(16):
                rows[y, n * size : (n + 1) * size, base : base + half] = pieces[n * GROUPS + y].astype(F32)

    @pl.when(info[0] == 0)
    def _():
        fill(own, 0)
        fill(other, half)

    @pl.when(info[0] != 0)
    def _():
        fill(other, 0)
        fill(own, half)

    for n, grad in enumerate((grad_q, grad_k, grad_v)):
        part = jnp.concatenate([rows[y, n * COLS : (n + 1) * COLS, :] for y in range(GROUPS)], axis=0)
        grad[...] = jnp.transpose(part)
    for y in range(GROUPS):
        tails[y] = rows[y, 3 * COLS : 3 * COLS + 16, :]


def unpack(core, own, other):
    full = lambda *shape: jax.ShapeDtypeStruct(shape, F32)
    return pl.pallas_call(
        unpack_kernel,
        in_specs=[pl.BlockSpec(memory_space=pltpu.SMEM), vmem(), vmem()],
        out_specs=[vmem()] * 4,
        out_shape=(full(WIDTH, WIDTH), full(WIDTH, WIDTH), full(WIDTH, WIDTH), full(GROUPS, 16, WIDTH)),
        scratch_shapes=[pltpu.VMEM((GROUPS, PACK_ROWS, WIDTH), F32)],
        compiler_params=params(60),
        cost_estimate=cost(1e6, 1e5),
        name="unpack",
    )(core.reshape(1), own, other)


def shift(array, axis, by):
    return lax.ppermute(array, axis, [(i, (i + by) % GROUPS) for i in range(GROUPS)])


def gather_rows(rows):
    ahead = shift(rows, "head", -1)
    behind = shift(rows, "head", 1)
    over_lo = shift(ahead[:128], "head", -1)
    over_hi = shift(behind[128:], "head", 1)
    return rows, ahead, over_lo, over_hi, behind


def near_exchange(to_next, to_prev):
    return shift(to_next, "head", 1), shift(to_prev, "head", -1)


def far_exchange(from_prev, from_next, size):
    return shift(from_prev[:, size:], "head", 1), shift(from_next[:, size:], "head", -1)


def trade(array, axes):
    return lax.all_to_all(array, axes, 0, 0, tiled=True)


def swap_cores(array):
    return lax.ppermute(array, "core", [(0, 1), (1, 0)])


def add_low(*terms):
    total = terms[0].astype(F32)
    for term in terms[1:]:
        total = total + term.astype(F32)
    return total.astype(BF16)


def per_device(
    layer_input, lengths, cotangent, w_query, w_key, w_value, conv_query, conv_key, conv_value,
    w_out, w_up, w_down, gain_attn, bias_attn, gain_ffn, bias_ffn,
):
    here = lax.axis_index("head").astype(jnp.int32)
    core = lax.axis_index("core").astype(jnp.int32)
    first_rows, other_rows, info = prepare(lengths, layer_input)
    first_rows = gather_rows(first_rows)
    other_rows = lax.all_gather(other_rows, "head", axis=0)

    w_groups = jnp.concatenate(
        [w.T.reshape(GROUPS, COLS, WIDTH) for w in (w_query, w_key, w_value)], axis=1
    )
    w_mine = lax.dynamic_index_in_dim(w_groups, here, 0, False)
    taps = lax.dynamic_slice_in_dim(
        jnp.concatenate([conv_query, conv_key, conv_value], axis=0), here * COLS, COLS, 1
    )
    gain_a, bias_a, gain_f, bias_f = (
        v.reshape(1, WIDTH) for v in (gain_attn, bias_attn, gain_ffn, bias_ffn)
    )
    *saved, mixed_first = attend(True, info, first_rows, w_mine, taps, gain_a, bias_a)
    mixed_first = trade(mixed_first, "head")
    *saved, mixed_others = attend(False, info, other_rows, w_mine, taps, gain_a, bias_a, saved)
    mixed_first, mixed_others = lax.optimization_barrier((mixed_first, mixed_others))
    mixed_others = trade(mixed_others, "head")
    weights = (w_out, gain_f, bias_f, w_up, w_down)
    output_a, middle_a, grad_a, *rows_a, branch_a, vectors_a = ffn(
        True, info, layer_input, cotangent, mixed_first, *weights
    )
    mixed_others, grad_a = lax.optimization_barrier((mixed_others, grad_a))
    output_b, middle_b, grad_b, *rows_b, _, ffn_vectors, send_out, keep_out = ffn(
        False, info, layer_input, cotangent, mixed_others, *weights, (mixed_first, branch_a, vectors_a)
    )
    rows_a, grad_a = lax.optimization_barrier((rows_a, trade(grad_a, "head")))

    rows_of = [a for pair in zip(rows_a, rows_b) for a in pair]
    sent = [weight_grads((1 - core) * 2 + n, rows_of)[0] for n in range(2)]
    came_out = swap_cores(send_out)
    came = [swap_cores(part) for part in sent]
    (part_0,) = weight_grads(core * 2, rows_of, (came[0],))
    part_1, out = weight_grads(core * 2 + 1, rows_of, (came[1],), (keep_out, came_out))
    half_sum = lax.psum((part_0, part_1, out), ("x", "z", "head"))

    def attention_grads(grad_mixed, saved, grad_middle, layer_output, ffn_vectors):
        grad_mixed = (grad_mixed[0], trade(grad_mixed[1], "head"))
        d_own, d_next, d_prev, keep, send = attend_back(
            info, grad_mixed, saved, w_mine, taps, gain_a, bias_a, ffn_vectors
        )
        behind, ahead = near_exchange(d_next, d_prev)

        part = add_low(keep, swap_cores(send)).reshape(16, PACK_ROWS // 16, WIDTH // 2)
        part = add_low(*trade(part, ("x", "z")))
        part, behind, ahead = lax.optimization_barrier((part, behind, ahead))
        over, under = far_exchange(behind, ahead, 3 * COLS)
        part = trade(jnp.broadcast_to(part[None], (64, *part.shape)), ("x", "z", "head"))
        input_grad, layer_output = input_grad_of(
            info, layer_input, grad_middle, layer_output, (d_own, behind, over, ahead, under), w_groups, gain_a
        )
        grad_q, grad_k, grad_v, tails = unpack(core, part, swap_cores(part))
        conv = lambda n: jnp.transpose(tails[:, 3 * n : 3 * n + 3, 0:COLS], (1, 0, 2)).reshape(3, WIDTH)
        vector = jnp.sum(tails[:, 9:13, :], axis=0)
        return (
            layer_output, input_grad, grad_q, grad_k, grad_v, conv(0), conv(1), conv(2),
            vector[0], vector[1], vector[2], vector[3],
        )

    operands = ((grad_a, grad_b), saved, (middle_a, middle_b), (output_a, output_b), ffn_vectors)
    blank = lambda *args: jax.tree.map(
        lambda a: jnp.zeros(a.shape, a.dtype), jax.eval_shape(attention_grads, *args)
    )
    later = lax.cond(lengths[0] > 0, attention_grads, blank, *operands)
    half_sum, later = lax.optimization_barrier((half_sum, later))
    grads = place(core, half_sum[:2], half_sum[2], ())
    swapped = [swap_cores(part) for part in half_sum]
    grad_up, grad_down, grad_out = place(1 - core, swapped[:2], swapped[2], grads)
    return (*later[:8], grad_out, grad_up, grad_down, *later[8:])


def solution(mesh):
    fine = Mesh(mesh.devices.reshape(4, 4, 2, GROUPS), ("x", "z", "core", "head"))
    dp = ("x", "z", "core")
    rows = P(dp, "head", None)
    return jax.shard_map(
        per_device,
        mesh=fine,
        in_specs=(rows, P(dp), rows) + (P(),) * 13,
        out_specs=(rows, rows) + (P(),) * 13,
        check_vma=False,
    )
```

```python
import functools

import jax
import jax.numpy as jnp
from jax import lax
from jax.experimental import pallas as pl
from jax.experimental.pallas import tpu as pltpu
from jax.sharding import Mesh
from jax.sharding import PartitionSpec as P

HDIM = 64
GROUPS = 4
BLOCK = 256
FULL = 1024
WIDTH = 768
COLS = 192
FF = 3072
SEQS = 3
CHUNK = 512
HEADS_HERE = 3
PACK_ROWS = 640
F32 = jnp.float32
BF16 = jnp.bfloat16
NN = (((1,), (0,)), ((), ()))
NT = (((1,), (1,)), ((), ()))
TN = (((0,), (0,)), ((), ()))


def dot(left, right, dims):
    return lax.dot_general(left, right, dims, preferred_element_type=F32)


def cost(flops, nbytes, transcendentals=0):
    return pl.CostEstimate(
        flops=int(flops), bytes_accessed=int(nbytes), transcendentals=int(transcendentals)
    )


def vmem():
    return pl.BlockSpec(memory_space=pltpu.VMEM)


def params(mib):
    return pltpu.CompilerParams(vmem_limit_bytes=mib << 20)


def unit_rows(rows):
    average = jnp.mean(rows, axis=-1, keepdims=True)
    centred = rows - average
    variance = jnp.mean(centred * centred, axis=-1, keepdims=True)
    inverse = lax.rsqrt(variance + 1e-05)
    return centred * inverse, inverse


def head_masks():
    lane = lax.broadcasted_iota(jnp.int32, (1, COLS), 1)
    return [
        jnp.where((lane >= h * HDIM) & (lane < (h + 1) * HDIM), 1.0, 0.0).astype(F32)
        for h in range(HEADS_HERE)
    ]


def conv_rows(raw_f, taps, tap_row, start):
    total = taps[tap_row : tap_row + 1, :] * raw_f[8 + start : 8 + start + BLOCK, :]
    for m in (1, 2):
        total += (
            taps[tap_row + m : tap_row + m + 1, :]
            * raw_f[8 + start - m : 8 + start - m + BLOCK, :]
        )
    return total


def order_of(lengths):
    a, b, c = lengths[0], lengths[1], lengths[2]
    first = jnp.where((a >= b) & (a >= c), 0, jnp.where(b >= c, 1, 2)).astype(jnp.int32)
    second = jnp.where(first == 0, 1, 0).astype(jnp.int32)
    third = jnp.where(first == 2, 1, 2).astype(jnp.int32)
    return first, second, third


def prepare_kernel(lengths, row_0, row_1, row_2, first_rows, other_rows, info):
    first_rows[...] = row_0[0]
    other_rows[0] = row_1[0]
    other_rows[1] = row_2[0]
    info[0] = lax.axis_index("head").astype(jnp.int32)
    info[1] = lax.axis_index("core").astype(jnp.int32)
    a, b, c = lengths[0], lengths[1], lengths[2]
    for n, s in enumerate(order_of(lengths)):
        info[2 + n] = jnp.where(s == 0, a, jnp.where(s == 1, b, c))
        info[5 + n] = s


def prepare(lengths, rows):
    nth = lambda n: pl.BlockSpec((1, BLOCK, WIDTH), lambda i, sc: (order_of(sc)[n], 0, 0))
    whole = lambda *shape: pl.BlockSpec(shape, lambda i, sc: (0,) * len(shape))
    return pl.pallas_call(
        prepare_kernel,
        grid_spec=pltpu.PrefetchScalarGridSpec(
            num_scalar_prefetch=1,
            grid=(1,),
            in_specs=[nth(0), nth(1), nth(2)],
            out_specs=[
                whole(BLOCK, WIDTH), whole(SEQS - 1, BLOCK, WIDTH), pl.BlockSpec(memory_space=pltpu.SMEM)
            ],
        ),
        out_shape=(
            jax.ShapeDtypeStruct((BLOCK, WIDTH), BF16),
            jax.ShapeDtypeStruct((SEQS - 1, BLOCK, WIDTH), BF16),
            jax.ShapeDtypeStruct((8,), jnp.int32),
        ),
        compiler_params=params(60),
        cost_estimate=cost(1e3, 2.4e6),
        name="prepare",
    )(lengths, rows, rows, rows)


def attend_kernel(first, info, *refs):
    count = 5 if first else GROUPS
    pieces, refs = refs[:count], refs[count:]
    w_mine, taps, gain, bias = refs[:4]
    refs = refs[4:] if first else refs[10:]
    normed, raw_q, raw_k, raw_v, mixed, lse_t, to_rows = refs[:7]
    pad_q, pad_k, pad_v, q_s, k_s, v_s, below = refs[7:]
    here = info[0]
    length = info[2] if first else info[3 + pl.program_id(0)]
    blocks = (length + BLOCK - 1) // BLOCK
    masks = head_masks()
    if first:
        homes = [(lax.rem(here + ahead, GROUPS), shift) for ahead, shift in ((0, 0), (1, 0), (2, 0), (2, 128), (3, 0))]
    else:
        homes = [(k, 0) for k in range(GROUPS)]

    for piece, (home, shift) in zip(pieces, homes):

        @pl.when(home < blocks)
        def _(piece=piece, home=home, shift=shift):
            rows = piece[...].reshape(piece.shape[-2], WIDTH).astype(F32)
            size = rows.shape[0]
            unit, _ = unit_rows(rows)
            low = (unit * gain[...] + bias[...]).astype(BF16)
            at = home * BLOCK + shift
            at = pl.multiple_of(at, 128) if first else at
            normed[0, pl.ds(at, size), :] = low
            for n, (raw, pad) in enumerate(((raw_q, pad_q), (raw_k, pad_k), (raw_v, pad_v))):
                value = dot(low, w_mine[n * COLS : (n + 1) * COLS, :], NT).astype(BF16)
                raw[0, pl.ds(at, size), :] = value
                pad[pl.ds(at + 8, size), :] = value.astype(F32)

    for pad in (pad_q, pad_k, pad_v):
        pad[0:8, :] = jnp.zeros((8, COLS), F32)
    row = lax.broadcasted_iota(jnp.int32, (BLOCK, BLOCK), 0)
    col = lax.broadcasted_iota(jnp.int32, (BLOCK, BLOCK), 1)
    below[...] = jnp.where(col <= row, 0.0, -1e30).astype(F32)

    for b in range(GROUPS):

        @pl.when(b < blocks)
        def _(b=b):
            at = slice(b * BLOCK, (b + 1) * BLOCK)
            q_s[at, :] = (conv_rows(pad_q, taps, 0, b * BLOCK).astype(BF16).astype(F32) * 0.125).astype(BF16)
            k_s[at, :] = conv_rows(pad_k, taps, 3, b * BLOCK).astype(BF16)
            v_s[at, :] = conv_rows(pad_v, taps, 6, b * BLOCK).astype(BF16)
            lane = lax.broadcasted_iota(jnp.int32, (BLOCK, 128), 1)
            total_out = jnp.zeros((BLOCK, COLS), F32)
            logs = jnp.zeros((BLOCK, 128), F32)
            for h in range(HEADS_HERE):
                q_h = q_s[at, :] * masks[h].astype(BF16)
                diag = dot(q_h, k_s[at, :], NT) + below[...]
                top = jnp.max(diag, axis=-1, keepdims=True)
                if b:
                    left = dot(q_h, k_s[0 : b * BLOCK, :], NT)
                    top = jnp.maximum(top, jnp.max(left, axis=-1, keepdims=True))
                    expo_left = jnp.exp(left - top)
                expo = jnp.exp(diag - top)
                total = jnp.sum(expo, axis=-1, keepdims=True)
                out = dot(expo.astype(BF16), v_s[at, :], NN)
                if b:
                    total += jnp.sum(expo_left, axis=-1, keepdims=True)
                    out += dot(expo_left.astype(BF16), v_s[0 : b * BLOCK, :], NN)
                total_out = total_out + (out * masks[h]) * (1.0 / total)
                logs = jnp.where(lane == h, top + jnp.log(total), logs)
            result = jnp.transpose(total_out).astype(BF16)
            mixed[b] = result
            to_rows[b] = result
            lse_t[0, :, at] = jnp.transpose(logs)[0:8, :]

        @pl.when(b >= blocks)
        def _(b=b):
            mixed[b] = jnp.zeros((COLS, BLOCK), BF16)
            to_rows[b] = jnp.zeros((COLS, BLOCK), BF16)


def attend(first, info, pieces, w_mine, taps, gain, bias, earlier=()):
    base = 0 if first else 1
    whole = lambda *shape: pl.BlockSpec(shape, lambda i, sc: (0,) * len(shape))
    mine = lambda *shape: pl.BlockSpec((1, *shape), lambda i, sc: (base + i,) + (0,) * len(shape))
    if first:
        piece_specs = [whole(*p.shape) for p in pieces]
    else:
        piece_specs = [
            pl.BlockSpec((1, 1, BLOCK, WIDTH), lambda i, sc, k=k: (k, i, 0, 0)) for k in range(GROUPS)
        ]
        pieces = [pieces] * GROUPS
    full = lambda dtype, *shape: jax.ShapeDtypeStruct((SEQS, *shape), dtype)
    return pl.pallas_call(
        functools.partial(attend_kernel, first),
        grid_spec=pltpu.PrefetchScalarGridSpec(
            num_scalar_prefetch=1,
            grid=(1 if first else SEQS - 1,),
            in_specs=piece_specs
            + [whole(3 * COLS, WIDTH), whole(9, COLS), whole(1, WIDTH), whole(1, WIDTH)]
            + [pl.BlockSpec(memory_space=pl.ANY)] * len(earlier),
            out_specs=[mine(FULL, WIDTH)]
            + [mine(FULL, COLS)] * 3
            + [
                pl.BlockSpec((GROUPS, COLS, BLOCK), lambda i, sc: (0, base + i, 0)),
                mine(8, FULL),
                pl.BlockSpec((GROUPS, COLS, BLOCK), lambda i, sc: (0, i, 0)),
            ],
            scratch_shapes=[pltpu.VMEM((FULL + 8, COLS), F32)] * 3
            + [pltpu.VMEM((FULL, COLS), BF16)] * 3
            + [pltpu.VMEM((BLOCK, BLOCK), F32)],
        ),
        out_shape=(
            full(BF16, FULL, WIDTH),
            full(BF16, FULL, COLS), full(BF16, FULL, COLS), full(BF16, FULL, COLS),
            jax.ShapeDtypeStruct((GROUPS, SEQS * COLS, BLOCK), BF16),
            full(F32, 8, FULL),
            jax.ShapeDtypeStruct((GROUPS, (1 if first else SEQS - 1) * COLS, BLOCK), BF16),
        ),
        input_output_aliases={1 + len(pieces) + 4 + n: n for n in range(len(earlier))},
        compiler_params=params(60),
        cost_estimate=cost(3e9, 8e6, 2e6),
        name="attend",
    )(info, *pieces, w_mine, taps, gain, bias, *earlier)


def attend_back_kernel(
    info, g_s, normed, raw_q, raw_k, raw_v, mixed, lse_t,
    w_mine, taps, gain, bias, ffn_vectors,
    d_own, d_next, d_prev, keep, send,
    dw_out, small_out, d_all, pack,
    pad_q, pad_k, pad_v, q_s, k_s, v_s, dq_s, dk_s, dv_s, below, p_all, ds_all,
):
    step = pl.program_id(0)
    here, core, length = info[0], info[1], info[2 + step]

    blocks = (length + BLOCK - 1) // BLOCK
    masks = head_masks()

    row = lax.broadcasted_iota(jnp.int32, (BLOCK, BLOCK), 0)
    col = lax.broadcasted_iota(jnp.int32, (BLOCK, BLOCK), 1)
    below[...] = jnp.where(row <= col, 0.0, -1e30).astype(F32)
    for pad, raw in ((pad_q, raw_q), (pad_k, raw_k), (pad_v, raw_v)):
        pad[0:8, :] = jnp.zeros((8, COLS), F32)
    for total in (dq_s, dk_s, dv_s):
        total[...] = jnp.zeros((FULL + 8, COLS), F32)

    for b in range(GROUPS):

        @pl.when(b < blocks)
        def _(b=b):
            at = slice(b * BLOCK, (b + 1) * BLOCK)
            for pad, raw in ((pad_q, raw_q), (pad_k, raw_k), (pad_v, raw_v)):
                pad[8 + b * BLOCK : 8 + (b + 1) * BLOCK, :] = raw[0, at, :].astype(F32)
            q_s[at, :] = (conv_rows(pad_q, taps, 0, b * BLOCK).astype(BF16).astype(F32) * 0.125).astype(BF16)
            k_s[at, :] = conv_rows(pad_k, taps, 3, b * BLOCK).astype(BF16)
            v_s[at, :] = conv_rows(pad_v, taps, 6, b * BLOCK).astype(BF16)
            both = g_s[b].astype(F32) * mixed[b].astype(F32)
            reach = slice(0, (b + 1) * BLOCK)
            dq_total = jnp.zeros((BLOCK, COLS), F32)
            q_heads, g_heads = [], []
            for h in range(HEADS_HERE):
                lanes = slice(h * BLOCK, (h + 1) * BLOCK)
                q_h = q_s[at, :] * masks[h].astype(BF16)
                own = slice(h * HDIM, (h + 1) * HDIM)
                blank = lambda n: [jnp.zeros((n * HDIM, BLOCK), BF16)] if n else []
                g_h = jnp.concatenate(blank(h) + [g_s[b, own, :]] + blank(HEADS_HERE - 1 - h), axis=0)
                q_heads.append(q_h)
                g_heads.append(g_h)
                row_dot = jnp.sum(both[own, :], axis=0, keepdims=True)
                log_row = lse_t[0, h : h + 1, at]
                for j in range(b + 1):
                    keys = slice(j * BLOCK, (j + 1) * BLOCK)
                    scores = dot(k_s[keys, :], q_h, NT)
                    if j == b:
                        scores = scores + below[...]
                    probs = jnp.exp(scores - log_row)
                    grad_probs = dot(v_s[keys, :], g_h, NN)
                    p_all[keys, lanes] = probs.astype(BF16)
                    ds_all[keys, lanes] = (probs * (grad_probs - row_dot)).astype(BF16)
                dq_total += dot(ds_all[reach, lanes], k_s[reach, :], TN) * masks[h]
            dq_s[at, :] = dq_total * 0.125
            dv_s[reach, :] += dot(p_all[reach, :], jnp.concatenate(g_heads, axis=1), NT)
            dk_s[reach, :] += dot(ds_all[reach, :], jnp.concatenate(q_heads, axis=0), NN)

    @pl.when(step == 0)
    def _():
        dw_out[...] = jnp.zeros_like(dw_out)
        small_out[...] = jnp.zeros_like(small_out)

    for b in range(GROUPS):

        @pl.when(b < blocks)
        def _(b=b):
            start = b * BLOCK
            at = slice(start, start + BLOCK)
            for n, (pad, grad) in enumerate(((pad_q, dq_s), (pad_k, dk_s), (pad_v, dv_s))):
                now = grad[at, :]
                value = taps[3 * n : 3 * n + 1, :] * now
                for m in (1, 2):
                    value += taps[3 * n + m : 3 * n + m + 1, :] * grad[start + m : start + m + BLOCK, :]
                value = value.astype(BF16).astype(F32)
                d_all[b, n * COLS : (n + 1) * COLS, :] = jnp.transpose(value).astype(BF16)
                small_out[9 + n : 10 + n, 0:COLS] += jnp.sum(value, axis=0, keepdims=True)
                for m in range(3):
                    shifted = pad[8 + start - m : 8 + start - m + BLOCK, :]
                    small_out[3 * n + m : 3 * n + m + 1, 0:COLS] += jnp.sum(
                        shifted * now, axis=0, keepdims=True
                    )
            dw_out[...] += dot(d_all[b], normed[0, at, :], NN)

        @pl.when(b >= blocks)
        def _(b=b):
            d_all[b] = jnp.zeros((3 * COLS, BLOCK), BF16)

    far = lax.rem(here + 2, GROUPS)
    d_own[0] = d_all[here]
    d_next[0, 0 : 3 * COLS, :] = d_all[lax.rem(here + 1, GROUPS)]
    d_next[0, 3 * COLS :, :] = d_all[far, 0 : 3 * COLS // 2, :]
    d_prev[0, 0 : 3 * COLS, :] = d_all[lax.rem(here + 3, GROUPS)]
    d_prev[0, 3 * COLS :, :] = d_all[far, 3 * COLS // 2 :, :]

    @pl.when(step == SEQS - 1)
    def _():
        grad_bias = jnp.zeros((1, WIDTH), F32)
        for n in range(3):
            sums = small_out[9 + n : 10 + n, 0:COLS]
            high = sums.astype(BF16)
            rest = (sums - high.astype(F32)).astype(BF16)
            for term in (high, rest):
                wide = jnp.broadcast_to(term.astype(F32), (16, COLS)).astype(BF16)
                grad_bias += dot(wide, w_mine[n * COLS : (n + 1) * COLS, :], NN)[0:1, :]
        grad_normed = jnp.sum(w_mine[...].astype(F32) * dw_out[...], axis=0, keepdims=True)
        grad_gain = (grad_normed - bias[...] * grad_bias) / gain[...]
        pack[0 : 3 * COLS, :] = dw_out[...].astype(BF16)
        tail = jnp.concatenate(
            [
                small_out[0:9, :],
                grad_gain,
                grad_bias,
                ffn_vectors[0:2, :],
                jnp.zeros((3, WIDTH), F32),
            ],
            axis=0,
        )
        pack[3 * COLS : 3 * COLS + 16, :] = tail.astype(BF16)
        pack[3 * COLS + 16 :, :] = jnp.zeros((PACK_ROWS - 3 * COLS - 16, WIDTH), BF16)
        half = WIDTH // 2
        keep[...] = pack[:, pl.ds(pl.multiple_of(core * half, 128), half)]
        send[...] = pack[:, pl.ds(pl.multiple_of((1 - core) * half, 128), half)]


def attend_back(info, grad_mixed, saved, w_mine, taps, gain, bias, ffn_vectors):
    low = lambda *shape: jax.ShapeDtypeStruct(shape, BF16)
    whole = lambda *shape: pl.BlockSpec(shape, lambda i, sc: (0,) * len(shape))
    mine = lambda *shape: pl.BlockSpec((1, *shape), lambda i, sc: (i,) + (0,) * len(shape))
    across = pl.BlockSpec((GROUPS, COLS, BLOCK), lambda i, sc: (0, i, 0))
    long_rows = 3 * COLS * 3 // 2
    return pl.pallas_call(
        attend_back_kernel,
        grid_spec=pltpu.PrefetchScalarGridSpec(
            num_scalar_prefetch=1,
            grid=(SEQS,),
            in_specs=[
                pl.BlockSpec((GROUPS, COLS, BLOCK), lambda i, sc: (0, lax.rem(i + 2, SEQS), 0)),
                mine(FULL, WIDTH),
            ]
            + [mine(FULL, COLS)] * 3
            + [across, mine(8, FULL)]
            + [whole(3 * COLS, WIDTH), whole(9, COLS), whole(1, WIDTH), whole(1, WIDTH), whole(8, WIDTH)],
            out_specs=[mine(3 * COLS, BLOCK), mine(long_rows, BLOCK), mine(long_rows, BLOCK)]
            + [whole(PACK_ROWS, WIDTH // 2)] * 2,
            scratch_shapes=[
                pltpu.VMEM((3 * COLS, WIDTH), F32),
                pltpu.VMEM((16, WIDTH), F32),
                pltpu.VMEM((GROUPS, 3 * COLS, BLOCK), BF16),
                pltpu.VMEM((PACK_ROWS, WIDTH), BF16),
            ]
            + [pltpu.VMEM((FULL + 8, COLS), F32)] * 3
            + [pltpu.VMEM((FULL, COLS), BF16)] * 3
            + [pltpu.VMEM((FULL + 8, COLS), F32)] * 3
            + [pltpu.VMEM((BLOCK, BLOCK), F32)]
            + [pltpu.VMEM((FULL, HEADS_HERE * BLOCK), BF16)] * 2,
        ),
        out_shape=(
            low(SEQS, 3 * COLS, BLOCK), low(SEQS, long_rows, BLOCK), low(SEQS, long_rows, BLOCK),
            low(PACK_ROWS, WIDTH // 2), low(PACK_ROWS, WIDTH // 2),
        ),
        compiler_params=params(60),
        cost_estimate=cost(1e6, 1e5),
        name="attend_back",
    )(info, grad_mixed, *saved, w_mine, taps, gain, bias, ffn_vectors)


def ffn_kernel(first, info, *refs):
    count = 1 if first else SEQS - 1
    base = 0 if first else 1
    x, cotangent, refs = refs[:count], refs[count : 2 * count], refs[2 * count :]
    mixed, w_out, gain, bias, w_up, w_down = refs[:6]
    refs = refs[6:]
    if first:
        layer_output, grad_middle, grad_mixed, sq_first, gh_first, normed, low_grad, branch, vectors = refs[:9]
        middle, total_out, total_grad = refs[9:]
    else:
        mixed_first, branch_first, vectors_first, sq_first, gh_first, normed_first, low_first = refs[:7]
        layer_output, grad_middle, grad_mixed, send_up, send_down, keep_up, keep_down = refs[8:15]
        send_out, keep_out, vectors = refs[15:18]
        middle, total_out, total_grad, normed_all, low_all, sq_all, gh_all, dw_out = refs[18:]
    step = pl.program_id(0)
    position = info[0] * BLOCK + lax.broadcasted_iota(jnp.int32, (BLOCK, 1), 0)
    parts = [slice(s * BLOCK, (s + 1) * BLOCK) for s in range(count)]
    if first:
        normed_of, low_of, sq_of, gh_of = normed, low_grad, sq_first, gh_first
        places = parts
    else:
        normed_of, low_of, sq_of, gh_of = normed_all, low_all, sq_all, gh_all
        places = [slice((s + 1) * BLOCK, (s + 2) * BLOCK) for s in range(count)]

    def heads_of(source, s):
        return jnp.concatenate([source[k, s * COLS : (s + 1) * COLS, :] for k in range(GROUPS)], axis=0)

    @pl.when(step == 0)
    def _():
        for s, (at, to) in enumerate(zip(parts, places)):
            value = x[s][0].astype(F32) + dot(heads_of(mixed, s), w_out[...], TN)
            middle[at, :] = value
            unit, _ = unit_rows(value)
            normed_of[to, :] = (unit * gain[...] + bias[...]).astype(BF16)
            keep_row = position < info[2 + base + s]
            low_of[to, :] = jnp.where(keep_row, cotangent[s][0].astype(F32), 0.0).astype(BF16)
            total_out[at, :] = jnp.zeros((BLOCK, WIDTH), F32)
            total_grad[at, :] = jnp.zeros((BLOCK, WIDTH), F32)
        if not first:
            normed_all[0:BLOCK, :] = normed_first[...]
            low_all[0:BLOCK, :] = low_first[...]

    for at, to in zip(parts, places):
        hidden = jnp.maximum(dot(normed_of[to, :], w_up[...], NN), 0.0)
        squared = (hidden * hidden).astype(BF16)
        sq_of[to, :] = squared
        back = dot(low_of[to, :], w_down[...], NT)
        grad_hidden = (back * 2.0 * hidden).astype(BF16)
        gh_of[to, :] = grad_hidden
        total_out[at, :] += dot(squared, w_down[...], NN)
        total_grad[at, :] += dot(grad_hidden, w_up[...], NT)

    steps = FF // CHUNK
    if not first:
        sq_all[0:BLOCK, :] = sq_first[...]
        gh_all[0:BLOCK, :] = gh_first[...]
        grad_up = dot(gh_all[...], normed_all[...], TN).astype(BF16)
        grad_down = dot(sq_all[...], low_all[...], TN).astype(BF16)

        @pl.when(step < steps // 2)
        def _():
            send_up[...] = grad_up
            send_down[...] = grad_down

        @pl.when(step >= steps // 2)
        def _():
            keep_up[...] = grad_up
            keep_down[...] = grad_down

    @pl.when(step == steps - 1)
    def _():
        if first:
            vectors[...] = jnp.zeros_like(vectors)
        else:
            vectors[...] = vectors_first[...]
            dw_out[...] = dot(heads_of(mixed_first, 0), branch_first[...], NN)
        for s, (at, to) in enumerate(zip(parts, places)):
            keep_row = position < info[2 + base + s]
            layer_output[s] = jnp.where(keep_row, middle[at, :] + total_out[at, :], 0.0).astype(BF16)
            unit, inverse = unit_rows(middle[at, :])
            grad_normed = total_grad[at, :]
            scaled = grad_normed * gain[...]
            mean_grad = jnp.mean(scaled, axis=-1, keepdims=True)
            mean_dot = jnp.mean(scaled * unit, axis=-1, keepdims=True)
            value = low_of[to, :].astype(F32) + inverse * (scaled - mean_grad - unit * mean_dot)
            vectors[0:1, :] += jnp.sum(grad_normed * unit, axis=0, keepdims=True)
            vectors[1:2, :] += jnp.sum(grad_normed, axis=0, keepdims=True)
            grad_middle[s] = value
            low = value.astype(BF16)
            if first:
                branch[...] = low
            else:
                dw_out[...] += dot(heads_of(mixed, s), low, NN)
            heads_grad = dot(w_out[...], low, NT).astype(BF16)
            for k in range(GROUPS):
                grad_mixed[k, s * COLS : (s + 1) * COLS, :] = heads_grad[k * COLS : (k + 1) * COLS]
        if not first:
            half = WIDTH // 2
            keep_out[...] = dw_out[pl.ds(pl.multiple_of(info[1] * half, 128), half), :].astype(BF16)
            send_out[...] = dw_out[pl.ds(pl.multiple_of((1 - info[1]) * half, 128), half), :].astype(BF16)


def ffn(first, info, x, cotangent, mixed, w_out, gain, bias, w_up, w_down, earlier=()):
    count = 1 if first else SEQS - 1
    base = 0 if first else 1
    low = lambda *shape: jax.ShapeDtypeStruct(shape, BF16)
    full = lambda *shape: jax.ShapeDtypeStruct(shape, F32)
    rows = count * BLOCK
    steps = FF // CHUNK
    half = steps // 2
    whole = lambda *shape: pl.BlockSpec(shape, lambda i, sc: (0,) * len(shape))
    nth = lambda s: pl.BlockSpec((1, BLOCK, WIDTH), lambda i, sc: (sc[5 + base + s], 0, 0))

    def chunk(i, sc):
        return jnp.where(i < half, 1 - sc[1], sc[1]) * half + lax.rem(i, half)

    across = lambda n: pl.BlockSpec((n, CHUNK), lambda i, sc: (0, chunk(i, sc)))
    early = pl.BlockSpec((CHUNK, WIDTH), lambda i, sc: (jnp.minimum(i, half - 1), 0))
    late = pl.BlockSpec((CHUNK, WIDTH), lambda i, sc: (jnp.maximum(i - half, 0), 0))
    grads = pl.BlockSpec((GROUPS, count * COLS, BLOCK), lambda i, sc: (0, SEQS - 1 if first else 0, 0))
    scratch = [pltpu.VMEM((rows, WIDTH), F32)] * 3
    if first:
        extra_specs = []
        out_specs = [across(rows)] * 2 + [whole(rows, WIDTH)] * 3 + [whole(8, WIDTH)]
        out_shape = [low(rows, FF)] * 2 + [low(rows, WIDTH)] * 3 + [full(8, WIDTH)]
        aliases = {}
    else:
        extra_specs = (
            [whole(GROUPS, COLS, BLOCK), whole(BLOCK, WIDTH), whole(8, WIDTH)]
            + [across(BLOCK)] * 2
            + [whole(BLOCK, WIDTH)] * 2
            + [pl.BlockSpec(memory_space=pl.ANY)]
        )
        out_specs = [early] * 2 + [late] * 2 + [whole(WIDTH // 2, WIDTH)] * 2 + [whole(8, WIDTH)]
        out_shape = [low(FF // 2, WIDTH)] * 4 + [low(WIDTH // 2, WIDTH)] * 2 + [full(8, WIDTH)]
        scratch += (
            [pltpu.VMEM((SEQS * BLOCK, WIDTH), BF16)] * 2
            + [pltpu.VMEM((SEQS * BLOCK, CHUNK), BF16)] * 2
            + [pltpu.VMEM((WIDTH, WIDTH), F32)]
        )
        aliases = {1 + 2 * count + 6 + 7: 2}
    return pl.pallas_call(
        functools.partial(ffn_kernel, first),
        grid_spec=pltpu.PrefetchScalarGridSpec(
            num_scalar_prefetch=1,
            grid=(steps,),
            in_specs=[nth(s) for s in range(count)] * 2
            + [
                whole(GROUPS, count * COLS, BLOCK), whole(WIDTH, WIDTH), whole(1, WIDTH), whole(1, WIDTH),
                across(WIDTH),
                pl.BlockSpec((CHUNK, WIDTH), lambda i, sc: (chunk(i, sc), 0)),
            ]
            + extra_specs,
            out_specs=[whole(count, BLOCK, WIDTH), whole(count, BLOCK, WIDTH), grads] + out_specs,
            scratch_shapes=scratch,
        ),
        out_shape=[low(count, BLOCK, WIDTH), full(count, BLOCK, WIDTH), low(GROUPS, SEQS * COLS, BLOCK)] + out_shape,
        input_output_aliases=aliases,
        compiler_params=params(60),
        cost_estimate=cost(7e9 if first else 2.2e10, 2e7),
        name="ffn",
    )(info, *[x] * count, *[cotangent] * count, mixed, w_out, gain, bias, w_up, w_down, *earlier)


def input_kernel(
    info, x, middle_first, middle_others, output_first, output_others, own, behind, over, ahead, under, w_groups, gain,
    out, layer_output, grad_middle,
):
    @pl.when(pl.program_id(0) == 0)
    def _():
        grad_middle[...] = middle_first[0]
        layer_output[...] = output_first[...]

    @pl.when(pl.program_id(0) > 0)
    def _():
        grad_middle[...] = middle_others[0]
        layer_output[...] = output_others[...]

    here = info[0]
    w_of = lambda k: w_groups[lax.rem(here + k, GROUPS)]
    unit, inverse = unit_rows(x[0].astype(F32))
    grad_normed = dot(own[0], w_of(0), TN)
    grad_normed += dot(ahead[0], w_of(1), TN)
    grad_normed += dot(jnp.concatenate([over[0], under[0]], axis=0), w_of(2), TN)
    grad_normed += dot(behind[0], w_of(3), TN)
    scaled = grad_normed * gain[...]
    mean_grad = jnp.mean(scaled, axis=-1, keepdims=True)
    mean_dot = jnp.mean(scaled * unit, axis=-1, keepdims=True)
    out[0] = grad_middle[...] + inverse * (scaled - mean_grad - unit * mean_dot)


def input_grad_of(info, x, grad_middle, layer_output, pieces, w_groups, gain):
    mine = lambda rows, lanes: pl.BlockSpec((1, rows, lanes), lambda i, sc: (i, 0, 0))
    whole = lambda *shape: pl.BlockSpec(shape, lambda i, sc: (0,) * len(shape))
    placed = pl.BlockSpec((1, BLOCK, WIDTH), lambda i, sc: (sc[5 + i], 0, 0))
    two = [whole(1, BLOCK, WIDTH), pl.BlockSpec((1, BLOCK, WIDTH), lambda i, sc: (jnp.maximum(i - 1, 0), 0, 0))]
    piece = mine(3 * COLS, BLOCK)
    half = mine(3 * COLS // 2, BLOCK)
    return pl.pallas_call(
        input_kernel,
        grid_spec=pltpu.PrefetchScalarGridSpec(
            num_scalar_prefetch=1,
            grid=(SEQS,),
            in_specs=[placed, *two, *two, piece, piece, half, piece, half, whole(*w_groups.shape), whole(1, WIDTH)],
            out_specs=[placed, placed],
            scratch_shapes=[pltpu.VMEM((BLOCK, WIDTH), F32)],
        ),
        out_shape=(
            jax.ShapeDtypeStruct((SEQS, BLOCK, WIDTH), F32),
            jax.ShapeDtypeStruct((SEQS, BLOCK, WIDTH), BF16),
        ),
        compiler_params=params(60),
        cost_estimate=cost(1e6, 1e5),
        name="input_grad",
    )(info, x, *grad_middle, *layer_output, *pieces, w_groups, gain)


def place_kernel(info, up, down, out, *rest):
    grad_up, grad_down, grad_out = rest[-3:]
    grad_up[...] = jnp.transpose(up[...].astype(F32))
    grad_down[...] = down[...].astype(F32)
    grad_out[...] = out[...].astype(F32)


def place(side, up, down, out, earlier):
    half = FF // CHUNK // 2
    rows = lambda n: pl.BlockSpec((n, WIDTH), lambda i, sc: (i, 0))
    own = lambda n: pl.BlockSpec((n, WIDTH), lambda i, sc: (sc[0] * half + i, 0))
    out_rows = WIDTH // 2 // half
    return pl.pallas_call(
        place_kernel,
        grid_spec=pltpu.PrefetchScalarGridSpec(
            num_scalar_prefetch=1,
            grid=(half,),
            in_specs=[rows(CHUNK), rows(CHUNK), rows(out_rows)]
            + [pl.BlockSpec(memory_space=pl.ANY)] * len(earlier),
            out_specs=[
                pl.BlockSpec((WIDTH, CHUNK), lambda i, sc: (0, sc[0] * half + i)), own(CHUNK), own(out_rows)
            ],
        ),
        out_shape=(
            jax.ShapeDtypeStruct((WIDTH, FF), F32),
            jax.ShapeDtypeStruct((FF, WIDTH), F32),
            jax.ShapeDtypeStruct((WIDTH, WIDTH), F32),
        ),
        input_output_aliases={4 + n: n for n in range(len(earlier))},
        compiler_params=params(60),
        cost_estimate=cost(1e6, 1.6e7),
        name="place",
    )(side.reshape(1), up, down, out, *earlier)


def unpack_kernel(info, own, other, grad_q, grad_k, grad_v, tails, rows):
    size = PACK_ROWS // 16
    half = WIDTH // 2

    def fill(pieces, base):
        for y in range(GROUPS):
            for n in range(16):
                rows[y, n * size : (n + 1) * size, base : base + half] = pieces[n * GROUPS + y].astype(F32)

    @pl.when(info[0] == 0)
    def _():
        fill(own, 0)
        fill(other, half)

    @pl.when(info[0] != 0)
    def _():
        fill(other, 0)
        fill(own, half)

    for n, grad in enumerate((grad_q, grad_k, grad_v)):
        part = jnp.concatenate([rows[y, n * COLS : (n + 1) * COLS, :] for y in range(GROUPS)], axis=0)
        grad[...] = jnp.transpose(part)
    for y in range(GROUPS):
        tails[y] = rows[y, 3 * COLS : 3 * COLS + 16, :]


def unpack(core, own, other):
    full = lambda *shape: jax.ShapeDtypeStruct(shape, F32)
    return pl.pallas_call(
        unpack_kernel,
        in_specs=[pl.BlockSpec(memory_space=pltpu.SMEM), vmem(), vmem()],
        out_specs=[vmem()] * 4,
        out_shape=(full(WIDTH, WIDTH), full(WIDTH, WIDTH), full(WIDTH, WIDTH), full(GROUPS, 16, WIDTH)),
        scratch_shapes=[pltpu.VMEM((GROUPS, PACK_ROWS, WIDTH), F32)],
        compiler_params=params(60),
        cost_estimate=cost(1e6, 1e5),
        name="unpack",
    )(core.reshape(1), own, other)


def shift(array, axis, by):
    return lax.ppermute(array, axis, [(i, (i + by) % GROUPS) for i in range(GROUPS)])


def gather_rows(rows):
    ahead = shift(rows, "head", -1)
    behind = shift(rows, "head", 1)
    over_lo = shift(ahead[:128], "head", -1)
    over_hi = shift(behind[128:], "head", 1)
    return rows, ahead, over_lo, over_hi, behind


def near_exchange(to_next, to_prev):
    return shift(to_next, "head", 1), shift(to_prev, "head", -1)


def far_exchange(from_prev, from_next, size):
    return shift(from_prev[:, size:], "head", 1), shift(from_next[:, size:], "head", -1)


def trade(array, axes):
    return lax.all_to_all(array, axes, 0, 0, tiled=True)


def swap_cores(array):
    return lax.ppermute(array, "core", [(0, 1), (1, 0)])


def add_low(*terms):
    total = terms[0].astype(F32)
    for term in terms[1:]:
        total = total + term.astype(F32)
    return total.astype(BF16)


def per_device(
    layer_input, lengths, cotangent, w_query, w_key, w_value, conv_query, conv_key, conv_value,
    w_out, w_up, w_down, gain_attn, bias_attn, gain_ffn, bias_ffn,
):
    here = lax.axis_index("head").astype(jnp.int32)
    core = lax.axis_index("core").astype(jnp.int32)
    first_rows, other_rows, info = prepare(lengths, layer_input)
    first_rows = gather_rows(first_rows)
    other_rows = lax.all_gather(other_rows, "head", axis=0)

    w_groups = jnp.concatenate(
        [w.T.reshape(GROUPS, COLS, WIDTH) for w in (w_query, w_key, w_value)], axis=1
    )
    w_mine = lax.dynamic_index_in_dim(w_groups, here, 0, False)
    taps = lax.dynamic_slice_in_dim(
        jnp.concatenate([conv_query, conv_key, conv_value], axis=0), here * COLS, COLS, 1
    )
    gain_a, bias_a, gain_f, bias_f = (
        v.reshape(1, WIDTH) for v in (gain_attn, bias_attn, gain_ffn, bias_ffn)
    )
    *saved, mixed_first = attend(True, info, first_rows, w_mine, taps, gain_a, bias_a)
    mixed_first = trade(mixed_first, "head")
    *saved, mixed_others = attend(False, info, other_rows, w_mine, taps, gain_a, bias_a, saved)
    mixed_first, mixed_others = lax.optimization_barrier((mixed_first, mixed_others))
    mixed_others = trade(mixed_others, "head")
    weights = (w_out, gain_f, bias_f, w_up, w_down)
    output_a, middle_a, grad_a, *rows_a, branch_a, vectors_a = ffn(
        True, info, layer_input, cotangent, mixed_first, *weights
    )
    output_b, middle_b, grad_mixed, *halves, ffn_vectors = ffn(
        False, info, layer_input, cotangent, mixed_others, *weights,
        (mixed_first, branch_a, vectors_a, *rows_a, grad_a),
    )
    sent, kept = (halves[0], halves[1], halves[4]), (halves[2], halves[3], halves[5])

    half_sum = tuple(add_low(keep, swap_cores(send)) for keep, send in zip(kept, sent))
    half_sum, grad_mixed = lax.optimization_barrier((half_sum, trade(grad_mixed, "head")))
    half_sum = lax.psum(half_sum, ("x", "z", "head"))

    def attention_grads(grad_mixed, saved, grad_middle, layer_output, ffn_vectors):
        d_own, d_next, d_prev, keep, send = attend_back(
            info, grad_mixed, saved, w_mine, taps, gain_a, bias_a, ffn_vectors
        )
        behind, ahead = near_exchange(d_next, d_prev)

        part = add_low(keep, swap_cores(send)).reshape(16, PACK_ROWS // 16, WIDTH // 2)
        part = add_low(*trade(part, ("x", "z")))
        part, behind, ahead = lax.optimization_barrier((part, behind, ahead))
        over, under = far_exchange(behind, ahead, 3 * COLS)
        for axis in ("head", "z", "x"):
            if axis == "x":
                part, over, under = lax.optimization_barrier((part, over, under))
            part = trade(jnp.broadcast_to(part[None], (GROUPS, *part.shape)), axis)
        part = part.reshape(64, PACK_ROWS // 16, WIDTH // 2)
        input_grad, layer_output = input_grad_of(
            info, layer_input, grad_middle, layer_output, (d_own, behind, over, ahead, under), w_groups, gain_a
        )
        grad_q, grad_k, grad_v, tails = unpack(core, part, swap_cores(part))
        conv = lambda n: jnp.transpose(tails[:, 3 * n : 3 * n + 3, 0:COLS], (1, 0, 2)).reshape(3, WIDTH)
        vector = jnp.sum(tails[:, 9:13, :], axis=0)
        return (
            layer_output, input_grad, grad_q, grad_k, grad_v, conv(0), conv(1), conv(2),
            vector[0], vector[1], vector[2], vector[3],
        )

    operands = (grad_mixed, saved, (middle_a, middle_b), (output_a, output_b), ffn_vectors)
    blank = lambda *args: jax.tree.map(
        lambda a: jnp.zeros(a.shape, a.dtype), jax.eval_shape(attention_grads, *args)
    )
    later = lax.cond(lengths[0] > 0, attention_grads, blank, *operands)
    half_sum, later = lax.optimization_barrier((half_sum, later))
    grads = place(core, *half_sum, ())
    grad_up, grad_down, grad_out = place(1 - core, *(swap_cores(part) for part in half_sum), grads)
    return (*later[:8], grad_out, grad_up, grad_down, *later[8:])


def solution(mesh):
    fine = Mesh(mesh.devices.reshape(4, 4, 2, GROUPS), ("x", "z", "core", "head"))
    dp = ("x", "z", "core")
    rows = P(dp, "head", None)
    return jax.shard_map(
        per_device,
        mesh=fine,
        in_specs=(rows, P(dp), rows) + (P(),) * 13,
        out_specs=(rows, rows) + (P(),) * 13,
        check_vma=False,
    )
```

```python
import functools

import jax
import jax.numpy as jnp
from jax import lax
from jax.experimental import pallas as pl
from jax.experimental.pallas import tpu as pltpu
from jax.sharding import Mesh
from jax.sharding import PartitionSpec as P

HDIM = 64
GROUPS = 4
BLOCK = 256
FULL = 1024
WIDTH = 768
COLS = 192
FF = 3072
SEQS = 3
CHUNK = 512
HEADS_HERE = 3
PACK_ROWS = 640
F32 = jnp.float32
BF16 = jnp.bfloat16
NN = (((1,), (0,)), ((), ()))
NT = (((1,), (1,)), ((), ()))
TN = (((0,), (0,)), ((), ()))


def dot(left, right, dims):
    return lax.dot_general(left, right, dims, preferred_element_type=F32)


def cost(flops, nbytes, transcendentals=0):
    return pl.CostEstimate(
        flops=int(flops), bytes_accessed=int(nbytes), transcendentals=int(transcendentals)
    )


def vmem():
    return pl.BlockSpec(memory_space=pltpu.VMEM)


def params(mib):
    return pltpu.CompilerParams(vmem_limit_bytes=mib << 20)


def unit_rows(rows):
    average = jnp.mean(rows, axis=-1, keepdims=True)
    centred = rows - average
    variance = jnp.mean(centred * centred, axis=-1, keepdims=True)
    inverse = lax.rsqrt(variance + 1e-05)
    return centred * inverse, inverse


def head_masks():
    lane = lax.broadcasted_iota(jnp.int32, (1, COLS), 1)
    return [
        jnp.where((lane >= h * HDIM) & (lane < (h + 1) * HDIM), 1.0, 0.0).astype(F32)
        for h in range(HEADS_HERE)
    ]


def conv_rows(raw_f, taps, tap_row, start):
    total = taps[tap_row : tap_row + 1, :] * raw_f[8 + start : 8 + start + BLOCK, :]
    for m in (1, 2):
        total += (
            taps[tap_row + m : tap_row + m + 1, :]
            * raw_f[8 + start - m : 8 + start - m + BLOCK, :]
        )
    return total


def order_of(lengths):
    a, b, c = lengths[0], lengths[1], lengths[2]
    first = jnp.where((a >= b) & (a >= c), 0, jnp.where(b >= c, 1, 2)).astype(jnp.int32)
    second = jnp.where(first == 0, 1, 0).astype(jnp.int32)
    third = jnp.where(first == 2, 1, 2).astype(jnp.int32)
    return first, second, third


def prepare_kernel(lengths, row_0, row_1, row_2, first_rows, other_rows, info):
    first_rows[...] = row_0[0]
    other_rows[0] = row_1[0]
    other_rows[1] = row_2[0]
    info[0] = lax.axis_index("head").astype(jnp.int32)
    info[1] = lax.axis_index("core").astype(jnp.int32)
    a, b, c = lengths[0], lengths[1], lengths[2]
    for n, s in enumerate(order_of(lengths)):
        info[2 + n] = jnp.where(s == 0, a, jnp.where(s == 1, b, c))
        info[5 + n] = s


def prepare(lengths, rows):
    nth = lambda n: pl.BlockSpec((1, BLOCK, WIDTH), lambda i, sc: (order_of(sc)[n], 0, 0))
    whole = lambda *shape: pl.BlockSpec(shape, lambda i, sc: (0,) * len(shape))
    return pl.pallas_call(
        prepare_kernel,
        grid_spec=pltpu.PrefetchScalarGridSpec(
            num_scalar_prefetch=1,
            grid=(1,),
            in_specs=[nth(0), nth(1), nth(2)],
            out_specs=[
                whole(BLOCK, WIDTH), whole(SEQS - 1, BLOCK, WIDTH), pl.BlockSpec(memory_space=pltpu.SMEM)
            ],
        ),
        out_shape=(
            jax.ShapeDtypeStruct((BLOCK, WIDTH), BF16),
            jax.ShapeDtypeStruct((SEQS - 1, BLOCK, WIDTH), BF16),
            jax.ShapeDtypeStruct((8,), jnp.int32),
        ),
        compiler_params=params(60),
        cost_estimate=cost(1e3, 2.4e6),
        name="prepare",
    )(lengths, rows, rows, rows)


def attend_kernel(first, info, *refs):
    count = 5 if first else GROUPS
    pieces, refs = refs[:count], refs[count:]
    w_mine, taps, gain, bias = refs[:4]
    refs = refs[4:] if first else refs[10:]
    normed, raw_q, raw_k, raw_v, mixed, lse_t, to_rows = refs[:7]
    pad_q, pad_k, pad_v, q_s, k_s, v_s, below = refs[7:]
    here = info[0]
    length = info[2] if first else info[3 + pl.program_id(0)]
    blocks = (length + BLOCK - 1) // BLOCK
    masks = head_masks()
    if first:
        homes = [(lax.rem(here + ahead, GROUPS), shift) for ahead, shift in ((0, 0), (1, 0), (2, 0), (2, 128), (3, 0))]
    else:
        homes = [(k, 0) for k in range(GROUPS)]

    for piece, (home, shift) in zip(pieces, homes):

        @pl.when(home < blocks)
        def _(piece=piece, home=home, shift=shift):
            rows = piece[...].reshape(piece.shape[-2], WIDTH).astype(F32)
            size = rows.shape[0]
            unit, _ = unit_rows(rows)
            low = (unit * gain[...] + bias[...]).astype(BF16)
            at = home * BLOCK + shift
            at = pl.multiple_of(at, 128) if first else at
            normed[0, pl.ds(at, size), :] = low
            for n, (raw, pad) in enumerate(((raw_q, pad_q), (raw_k, pad_k), (raw_v, pad_v))):
                value = dot(low, w_mine[n * COLS : (n + 1) * COLS, :], NT).astype(BF16)
                raw[0, pl.ds(at, size), :] = value
                pad[pl.ds(at + 8, size), :] = value.astype(F32)

    for pad in (pad_q, pad_k, pad_v):
        pad[0:8, :] = jnp.zeros((8, COLS), F32)
    row = lax.broadcasted_iota(jnp.int32, (BLOCK, BLOCK), 0)
    col = lax.broadcasted_iota(jnp.int32, (BLOCK, BLOCK), 1)
    below[...] = jnp.where(col <= row, 0.0, -1e30).astype(F32)

    for b in range(GROUPS):

        @pl.when(b < blocks)
        def _(b=b):
            at = slice(b * BLOCK, (b + 1) * BLOCK)
            q_s[at, :] = (conv_rows(pad_q, taps, 0, b * BLOCK).astype(BF16).astype(F32) * 0.125).astype(BF16)
            k_s[at, :] = conv_rows(pad_k, taps, 3, b * BLOCK).astype(BF16)
            v_s[at, :] = conv_rows(pad_v, taps, 6, b * BLOCK).astype(BF16)
            lane = lax.broadcasted_iota(jnp.int32, (BLOCK, 128), 1)
            total_out = jnp.zeros((BLOCK, COLS), F32)
            logs = jnp.zeros((BLOCK, 128), F32)
            for h in range(HEADS_HERE):
                q_h = q_s[at, :] * masks[h].astype(BF16)
                diag = dot(q_h, k_s[at, :], NT) + below[...]
                top = jnp.max(diag, axis=-1, keepdims=True)
                if b:
                    left = dot(q_h, k_s[0 : b * BLOCK, :], NT)
                    top = jnp.maximum(top, jnp.max(left, axis=-1, keepdims=True))
                    expo_left = jnp.exp(left - top)
                expo = jnp.exp(diag - top)
                total = jnp.sum(expo, axis=-1, keepdims=True)
                out = dot(expo.astype(BF16), v_s[at, :], NN)
                if b:
                    total += jnp.sum(expo_left, axis=-1, keepdims=True)
                    out += dot(expo_left.astype(BF16), v_s[0 : b * BLOCK, :], NN)
                total_out = total_out + (out * masks[h]) * (1.0 / total)
                logs = jnp.where(lane == h, top + jnp.log(total), logs)
            result = jnp.transpose(total_out).astype(BF16)
            mixed[b] = result
            to_rows[b] = result
            lse_t[0, :, at] = jnp.transpose(logs)[0:8, :]

        @pl.when(b >= blocks)
        def _(b=b):
            mixed[b] = jnp.zeros((COLS, BLOCK), BF16)
            to_rows[b] = jnp.zeros((COLS, BLOCK), BF16)


def attend(first, info, pieces, w_mine, taps, gain, bias, earlier=()):
    base = 0 if first else 1
    whole = lambda *shape: pl.BlockSpec(shape, lambda i, sc: (0,) * len(shape))
    mine = lambda *shape: pl.BlockSpec((1, *shape), lambda i, sc: (base + i,) + (0,) * len(shape))
    if first:
        piece_specs = [whole(*p.shape) for p in pieces]
    else:
        piece_specs = [
            pl.BlockSpec((1, 1, BLOCK, WIDTH), lambda i, sc, k=k: (k, i, 0, 0)) for k in range(GROUPS)
        ]
        pieces = [pieces] * GROUPS
    full = lambda dtype, *shape: jax.ShapeDtypeStruct((SEQS, *shape), dtype)
    return pl.pallas_call(
        functools.partial(attend_kernel, first),
        grid_spec=pltpu.PrefetchScalarGridSpec(
            num_scalar_prefetch=1,
            grid=(1 if first else SEQS - 1,),
            in_specs=piece_specs
            + [whole(3 * COLS, WIDTH), whole(9, COLS), whole(1, WIDTH), whole(1, WIDTH)]
            + [pl.BlockSpec(memory_space=pl.ANY)] * len(earlier),
            out_specs=[mine(FULL, WIDTH)]
            + [mine(FULL, COLS)] * 3
            + [
                pl.BlockSpec((GROUPS, COLS, BLOCK), lambda i, sc: (0, base + i, 0)),
                mine(8, FULL),
                pl.BlockSpec((GROUPS, COLS, BLOCK), lambda i, sc: (0, i, 0)),
            ],
            scratch_shapes=[pltpu.VMEM((FULL + 8, COLS), F32)] * 3
            + [pltpu.VMEM((FULL, COLS), BF16)] * 3
            + [pltpu.VMEM((BLOCK, BLOCK), F32)],
        ),
        out_shape=(
            full(BF16, FULL, WIDTH),
            full(BF16, FULL, COLS), full(BF16, FULL, COLS), full(BF16, FULL, COLS),
            jax.ShapeDtypeStruct((GROUPS, SEQS * COLS, BLOCK), BF16),
            full(F32, 8, FULL),
            jax.ShapeDtypeStruct((GROUPS, (1 if first else SEQS - 1) * COLS, BLOCK), BF16),
        ),
        input_output_aliases={1 + len(pieces) + 4 + n: n for n in range(len(earlier))},
        compiler_params=params(60),
        cost_estimate=cost(3e9, 8e6, 2e6),
        name="attend",
    )(info, *pieces, w_mine, taps, gain, bias, *earlier)


def attend_back_kernel(
    info, g_s, normed, raw_q, raw_k, raw_v, mixed, lse_t,
    w_mine, taps, gain, bias, ffn_vectors,
    d_own, d_next, d_prev, keep, send,
    dw_out, small_out, d_all, pack,
    pad_q, pad_k, pad_v, q_s, k_s, v_s, dq_s, dk_s, dv_s, below, p_all, ds_all,
):
    step = pl.program_id(0)
    here, core, length = info[0], info[1], info[2 + step]

    blocks = (length + BLOCK - 1) // BLOCK
    masks = head_masks()

    row = lax.broadcasted_iota(jnp.int32, (BLOCK, BLOCK), 0)
    col = lax.broadcasted_iota(jnp.int32, (BLOCK, BLOCK), 1)
    below[...] = jnp.where(row <= col, 0.0, -1e30).astype(F32)
    for pad, raw in ((pad_q, raw_q), (pad_k, raw_k), (pad_v, raw_v)):
        pad[0:8, :] = jnp.zeros((8, COLS), F32)
    for total in (dq_s, dk_s, dv_s):
        total[...] = jnp.zeros((FULL + 8, COLS), F32)

    for b in range(GROUPS):

        @pl.when(b < blocks)
        def _(b=b):
            at = slice(b * BLOCK, (b + 1) * BLOCK)
            for pad, raw in ((pad_q, raw_q), (pad_k, raw_k), (pad_v, raw_v)):
                pad[8 + b * BLOCK : 8 + (b + 1) * BLOCK, :] = raw[0, at, :].astype(F32)
            q_s[at, :] = (conv_rows(pad_q, taps, 0, b * BLOCK).astype(BF16).astype(F32) * 0.125).astype(BF16)
            k_s[at, :] = conv_rows(pad_k, taps, 3, b * BLOCK).astype(BF16)
            v_s[at, :] = conv_rows(pad_v, taps, 6, b * BLOCK).astype(BF16)
            both = g_s[b].astype(F32) * mixed[b].astype(F32)
            reach = slice(0, (b + 1) * BLOCK)
            dq_total = jnp.zeros((BLOCK, COLS), F32)
            q_heads, g_heads = [], []
            for h in range(HEADS_HERE):
                lanes = slice(h * BLOCK, (h + 1) * BLOCK)
                q_h = q_s[at, :] * masks[h].astype(BF16)
                own = slice(h * HDIM, (h + 1) * HDIM)
                blank = lambda n: [jnp.zeros((n * HDIM, BLOCK), BF16)] if n else []
                g_h = jnp.concatenate(blank(h) + [g_s[b, own, :]] + blank(HEADS_HERE - 1 - h), axis=0)
                q_heads.append(q_h)
                g_heads.append(g_h)
                row_dot = jnp.sum(both[own, :], axis=0, keepdims=True)
                log_row = lse_t[0, h : h + 1, at]
                for j in range(b + 1):
                    keys = slice(j * BLOCK, (j + 1) * BLOCK)
                    scores = dot(k_s[keys, :], q_h, NT)
                    if j == b:
                        scores = scores + below[...]
                    probs = jnp.exp(scores - log_row)
                    grad_probs = dot(v_s[keys, :], g_h, NN)
                    p_all[keys, lanes] = probs.astype(BF16)
                    ds_all[keys, lanes] = (probs * (grad_probs - row_dot)).astype(BF16)
                dq_total += dot(ds_all[reach, lanes], k_s[reach, :], TN) * masks[h]
            dq_s[at, :] = dq_total * 0.125
            dv_s[reach, :] += dot(p_all[reach, :], jnp.concatenate(g_heads, axis=1), NT)
            dk_s[reach, :] += dot(ds_all[reach, :], jnp.concatenate(q_heads, axis=0), NN)

    @pl.when(step == 0)
    def _():
        dw_out[...] = jnp.zeros_like(dw_out)
        small_out[...] = jnp.zeros_like(small_out)

    for b in range(GROUPS):

        @pl.when(b < blocks)
        def _(b=b):
            start = b * BLOCK
            at = slice(start, start + BLOCK)
            for n, (pad, grad) in enumerate(((pad_q, dq_s), (pad_k, dk_s), (pad_v, dv_s))):
                now = grad[at, :]
                value = taps[3 * n : 3 * n + 1, :] * now
                for m in (1, 2):
                    value += taps[3 * n + m : 3 * n + m + 1, :] * grad[start + m : start + m + BLOCK, :]
                value = value.astype(BF16).astype(F32)
                d_all[b, n * COLS : (n + 1) * COLS, :] = jnp.transpose(value).astype(BF16)
                small_out[9 + n : 10 + n, 0:COLS] += jnp.sum(value, axis=0, keepdims=True)
                for m in range(3):
                    shifted = pad[8 + start - m : 8 + start - m + BLOCK, :]
                    small_out[3 * n + m : 3 * n + m + 1, 0:COLS] += jnp.sum(
                        shifted * now, axis=0, keepdims=True
                    )
            dw_out[...] += dot(d_all[b], normed[0, at, :], NN)

        @pl.when(b >= blocks)
        def _(b=b):
            d_all[b] = jnp.zeros((3 * COLS, BLOCK), BF16)

    far = lax.rem(here + 2, GROUPS)
    d_own[0] = d_all[here]
    d_next[0, 0 : 3 * COLS, :] = d_all[lax.rem(here + 1, GROUPS)]
    d_next[0, 3 * COLS :, :] = d_all[far, 0 : 3 * COLS // 2, :]
    d_prev[0, 0 : 3 * COLS, :] = d_all[lax.rem(here + 3, GROUPS)]
    d_prev[0, 3 * COLS :, :] = d_all[far, 3 * COLS // 2 :, :]

    @pl.when(step == SEQS - 1)
    def _():
        grad_bias = jnp.zeros((1, WIDTH), F32)
        for n in range(3):
            sums = small_out[9 + n : 10 + n, 0:COLS]
            high = sums.astype(BF16)
            rest = (sums - high.astype(F32)).astype(BF16)
            for term in (high, rest):
                wide = jnp.broadcast_to(term.astype(F32), (16, COLS)).astype(BF16)
                grad_bias += dot(wide, w_mine[n * COLS : (n + 1) * COLS, :], NN)[0:1, :]
        grad_normed = jnp.sum(w_mine[...].astype(F32) * dw_out[...], axis=0, keepdims=True)
        grad_gain = (grad_normed - bias[...] * grad_bias) / gain[...]
        pack[0 : 3 * COLS, :] = dw_out[...].astype(BF16)
        tail = jnp.concatenate(
            [
                small_out[0:9, :],
                grad_gain,
                grad_bias,
                ffn_vectors[0:2, :],
                jnp.zeros((3, WIDTH), F32),
            ],
            axis=0,
        )
        pack[3 * COLS : 3 * COLS + 16, :] = tail.astype(BF16)
        pack[3 * COLS + 16 :, :] = jnp.zeros((PACK_ROWS - 3 * COLS - 16, WIDTH), BF16)
        half = WIDTH // 2
        keep[...] = pack[:, pl.ds(pl.multiple_of(core * half, 128), half)]
        send[...] = pack[:, pl.ds(pl.multiple_of((1 - core) * half, 128), half)]


def attend_back(info, grad_mixed, saved, w_mine, taps, gain, bias, ffn_vectors):
    low = lambda *shape: jax.ShapeDtypeStruct(shape, BF16)
    whole = lambda *shape: pl.BlockSpec(shape, lambda i, sc: (0,) * len(shape))
    mine = lambda *shape: pl.BlockSpec((1, *shape), lambda i, sc: (i,) + (0,) * len(shape))
    across = pl.BlockSpec((GROUPS, COLS, BLOCK), lambda i, sc: (0, i, 0))
    long_rows = 3 * COLS * 3 // 2
    return pl.pallas_call(
        attend_back_kernel,
        grid_spec=pltpu.PrefetchScalarGridSpec(
            num_scalar_prefetch=1,
            grid=(SEQS,),
            in_specs=[
                pl.BlockSpec((GROUPS, COLS, BLOCK), lambda i, sc: (0, lax.rem(i + 2, SEQS), 0)),
                mine(FULL, WIDTH),
            ]
            + [mine(FULL, COLS)] * 3
            + [across, mine(8, FULL)]
            + [whole(3 * COLS, WIDTH), whole(9, COLS), whole(1, WIDTH), whole(1, WIDTH), whole(8, WIDTH)],
            out_specs=[mine(3 * COLS, BLOCK), mine(long_rows, BLOCK), mine(long_rows, BLOCK)]
            + [whole(PACK_ROWS, WIDTH // 2)] * 2,
            scratch_shapes=[
                pltpu.VMEM((3 * COLS, WIDTH), F32),
                pltpu.VMEM((16, WIDTH), F32),
                pltpu.VMEM((GROUPS, 3 * COLS, BLOCK), BF16),
                pltpu.VMEM((PACK_ROWS, WIDTH), BF16),
            ]
            + [pltpu.VMEM((FULL + 8, COLS), F32)] * 3
            + [pltpu.VMEM((FULL, COLS), BF16)] * 3
            + [pltpu.VMEM((FULL + 8, COLS), F32)] * 3
            + [pltpu.VMEM((BLOCK, BLOCK), F32)]
            + [pltpu.VMEM((FULL, HEADS_HERE * BLOCK), BF16)] * 2,
        ),
        out_shape=(
            low(SEQS, 3 * COLS, BLOCK), low(SEQS, long_rows, BLOCK), low(SEQS, long_rows, BLOCK),
            low(PACK_ROWS, WIDTH // 2), low(PACK_ROWS, WIDTH // 2),
        ),
        compiler_params=params(60),
        cost_estimate=cost(1e10, 2e7),
        name="attend_back",
    )(info, grad_mixed, *saved, w_mine, taps, gain, bias, ffn_vectors)


def heads_of(source, s):
    return jnp.concatenate([source[k, s * COLS : (s + 1) * COLS, :] for k in range(GROUPS)], axis=0)


def ffn_kernel(first, info, *refs):
    count = 1 if first else SEQS - 1
    base = 0 if first else 1
    x, cotangent, refs = refs[:count], refs[count : 2 * count], refs[2 * count :]
    mixed, w_out, gain, bias, w_up, w_down = refs[:6]
    refs = refs[6:]
    if first:
        middle, low_grad, total_out, total_grad, sq_of, gh_of, normed_of = refs
        places = [slice(0, BLOCK)]
    else:
        sq_first, gh_first, normed_first, low_first = refs[:4]
        middle, low_grad, total_out, total_grad, send_up, send_down, keep_up, keep_down = refs[4:12]
        normed_of, normed_t, low_all, sq_of, gh_of = refs[12:]
        places = [slice((s + 1) * BLOCK, (s + 2) * BLOCK) for s in range(count)]
    step = pl.program_id(0)

    @pl.when(step == 0)
    def _():
        position = info[0] * BLOCK + lax.broadcasted_iota(jnp.int32, (BLOCK, 1), 0)
        for s, to in enumerate(places):
            value = x[s][0].astype(F32) + dot(heads_of(mixed, s), w_out[...], TN)
            middle[s] = value
            unit, _ = unit_rows(value)
            normed_of[to, :] = (unit * gain[...] + bias[...]).astype(BF16)
            keep_row = position < info[2 + base + s]
            low_grad[s] = jnp.where(keep_row, cotangent[s][0].astype(F32), 0.0).astype(BF16)
            total_out[s] = jnp.zeros((BLOCK, WIDTH), F32)
            total_grad[s] = jnp.zeros((BLOCK, WIDTH), F32)
            if not first:
                low_all[to, :] = low_grad[s]
        if not first:
            normed_of[0:BLOCK, :] = normed_first[...]
            low_all[0:BLOCK, :] = low_first[0]
            normed_t[...] = jnp.transpose(normed_of[...].astype(F32)).astype(BF16)

    for s, to in enumerate(places):
        hidden = jnp.maximum(dot(normed_of[to, :], w_up[...], NN), 0.0)
        squared = (hidden * hidden).astype(BF16)
        sq_of[to, :] = squared
        back = dot(low_grad[s], w_down[...], NT)
        grad_hidden = (back * 2.0 * hidden).astype(BF16)
        gh_of[to, :] = grad_hidden
        total_out[s] += dot(squared, w_down[...], NN)
        total_grad[s] += dot(grad_hidden, w_up[...], NT)

    if not first:
        steps = FF // CHUNK
        sq_of[0:BLOCK, :] = sq_first[...]
        gh_of[0:BLOCK, :] = gh_first[...]
        grad_up = dot(normed_t[...], gh_of[...], NN).astype(BF16)
        grad_down = dot(sq_of[...], low_all[...], TN).astype(BF16)

        @pl.when(step < steps // 2)
        def _():
            send_up[...] = grad_up
            send_down[...] = grad_down

        @pl.when(step >= steps // 2)
        def _():
            keep_up[...] = grad_up
            keep_down[...] = grad_down


def ffn(first, info, x, cotangent, mixed, w_out, gain, bias, w_up, w_down, earlier=()):
    count = 1 if first else SEQS - 1
    base = 0 if first else 1
    low = lambda *shape: jax.ShapeDtypeStruct(shape, BF16)
    full = lambda *shape: jax.ShapeDtypeStruct(shape, F32)
    steps = FF // CHUNK
    half = steps // 2
    whole = lambda *shape: pl.BlockSpec(shape, lambda i, sc: (0,) * len(shape))
    nth = lambda s: pl.BlockSpec((1, BLOCK, WIDTH), lambda i, sc: (sc[5 + base + s], 0, 0))
    early = lambda i: jnp.minimum(i, half - 1)
    late = lambda i: jnp.maximum(i - half, 0)

    def chunk(i, sc):
        return jnp.where(i < half, 1 - sc[1], sc[1]) * half + lax.rem(i, half)

    across = lambda n: pl.BlockSpec((n, CHUNK), lambda i, sc: (0, chunk(i, sc)))
    rows = whole(count, BLOCK, WIDTH)
    if first:
        extra_specs = []
        out_specs = [across(BLOCK), across(BLOCK), whole(BLOCK, WIDTH)]
        out_shape = [low(BLOCK, FF), low(BLOCK, FF), low(BLOCK, WIDTH)]
        scratch = []
    else:
        extra_specs = [across(BLOCK), across(BLOCK), whole(BLOCK, WIDTH), whole(1, BLOCK, WIDTH)]
        out_specs = [
            pl.BlockSpec((WIDTH, CHUNK), lambda i, sc: (0, early(i))),
            pl.BlockSpec((CHUNK, WIDTH), lambda i, sc: (early(i), 0)),
            pl.BlockSpec((WIDTH, CHUNK), lambda i, sc: (0, late(i))),
            pl.BlockSpec((CHUNK, WIDTH), lambda i, sc: (late(i), 0)),
        ]
        out_shape = [low(WIDTH, FF // 2), low(FF // 2, WIDTH)] * 2
        all_rows = SEQS * BLOCK
        scratch = [
            pltpu.VMEM((all_rows, WIDTH), BF16), pltpu.VMEM((WIDTH, all_rows), BF16),
            pltpu.VMEM((all_rows, WIDTH), BF16),
            pltpu.VMEM((all_rows, CHUNK), BF16), pltpu.VMEM((all_rows, CHUNK), BF16),
        ]
    return pl.pallas_call(
        functools.partial(ffn_kernel, first),
        grid_spec=pltpu.PrefetchScalarGridSpec(
            num_scalar_prefetch=1,
            grid=(steps,),
            in_specs=[nth(s) for s in range(count)] * 2
            + [
                whole(GROUPS, count * COLS, BLOCK), whole(WIDTH, WIDTH), whole(1, WIDTH), whole(1, WIDTH),
                across(WIDTH),
                pl.BlockSpec((CHUNK, WIDTH), lambda i, sc: (chunk(i, sc), 0)),
            ]
            + extra_specs,
            out_specs=[rows] * 4 + out_specs,
            scratch_shapes=scratch,
        ),
        out_shape=[full(count, BLOCK, WIDTH), low(count, BLOCK, WIDTH)]
        + [full(count, BLOCK, WIDTH)] * 2
        + out_shape,
        compiler_params=params(60),
        cost_estimate=cost(7e9 if first else 2.2e10, 2e7),
        name="ffn",
    )(info, *[x] * count, *[cotangent] * count, mixed, w_out, gain, bias, w_up, w_down, *earlier)


def ffn_rows_kernel(first, info, *refs):
    count = 1 if first else SEQS - 1
    base = 0 if first else 1
    middle, low_grad, total_out, total_grad, w_out, gain = refs[:6]
    refs = refs[6:]
    if first:
        layer_output, grad_middle, grad_mixed, vectors, branch = refs
        vectors[...] = jnp.zeros_like(vectors)
    else:
        mixed_first, mixed, branch_first, vectors_first, _ = refs[:5]
        layer_output, grad_middle, grad_mixed, vectors, send_out, keep_out, dw_out = refs[5:]
        vectors[...] = vectors_first[...]
        dw_out[...] = dot(heads_of(mixed_first, 0), branch_first[...], NN)
    position = info[0] * BLOCK + lax.broadcasted_iota(jnp.int32, (BLOCK, 1), 0)
    for s in range(count):
        keep_row = position < info[2 + base + s]
        layer_output[s] = jnp.where(keep_row, middle[s] + total_out[s], 0.0).astype(BF16)
        unit, inverse = unit_rows(middle[s])
        grad_normed = total_grad[s]
        scaled = grad_normed * gain[...]
        mean_grad = jnp.mean(scaled, axis=-1, keepdims=True)
        mean_dot = jnp.mean(scaled * unit, axis=-1, keepdims=True)
        value = low_grad[s].astype(F32) + inverse * (scaled - mean_grad - unit * mean_dot)
        vectors[0:1, :] += jnp.sum(grad_normed * unit, axis=0, keepdims=True)
        vectors[1:2, :] += jnp.sum(grad_normed, axis=0, keepdims=True)
        grad_middle[s] = value
        low = value.astype(BF16)
        if first:
            branch[...] = low
        else:
            dw_out[...] += dot(heads_of(mixed, s), low, NN)
        heads_grad = dot(w_out[...], low, NT).astype(BF16)
        for k in range(GROUPS):
            grad_mixed[k, s * COLS : (s + 1) * COLS, :] = heads_grad[k * COLS : (k + 1) * COLS]
    if not first:
        half = WIDTH // 2
        keep_out[...] = dw_out[pl.ds(pl.multiple_of(info[1] * half, 128), half), :].astype(BF16)
        send_out[...] = dw_out[pl.ds(pl.multiple_of((1 - info[1]) * half, 128), half), :].astype(BF16)


def ffn_rows(first, info, rows, w_out, gain, earlier=()):
    count = 1 if first else SEQS - 1
    low = lambda *shape: jax.ShapeDtypeStruct(shape, BF16)
    full = lambda *shape: jax.ShapeDtypeStruct(shape, F32)
    whole = lambda *shape: pl.BlockSpec(shape, lambda i, sc: (0,) * len(shape))
    grads = pl.BlockSpec((GROUPS, count * COLS, BLOCK), lambda i, sc: (0, SEQS - 1 if first else 0, 0))
    seq_rows = whole(count, BLOCK, WIDTH)
    specs = [whole(*a.shape) for a in earlier[:-1]] + [pl.BlockSpec(memory_space=pl.ANY)] * min(len(earlier), 1)
    more = [low(BLOCK, WIDTH)] if first else [low(WIDTH // 2, WIDTH)] * 2
    return pl.pallas_call(
        functools.partial(ffn_rows_kernel, first),
        grid_spec=pltpu.PrefetchScalarGridSpec(
            num_scalar_prefetch=1,
            grid=(1,),
            in_specs=[seq_rows] * 4 + [whole(WIDTH, WIDTH), whole(1, WIDTH)] + specs,
            out_specs=[seq_rows, seq_rows, grads, whole(8, WIDTH)] + [whole(*a.shape) for a in more],
            scratch_shapes=[] if first else [pltpu.VMEM((WIDTH, WIDTH), F32)],
        ),
        out_shape=[
            low(count, BLOCK, WIDTH), full(count, BLOCK, WIDTH), low(GROUPS, SEQS * COLS, BLOCK), full(8, WIDTH)
        ]
        + more,
        input_output_aliases={} if first else {11: 2},
        compiler_params=params(60),
        cost_estimate=cost(1e9 * count, 6e6 * count),
        name="ffn_rows",
    )(info, *rows, w_out, gain, *earlier)


def add_kernel(*refs):
    for n in range(3):
        refs[6 + n][...] = (refs[n][...].astype(F32) + refs[3 + n][...].astype(F32)).astype(BF16)


def add_pairs(kept, came):
    steps = 6
    specs = [pl.BlockSpec((a.shape[0] // steps, a.shape[1]), lambda i: (i, 0)) for a in kept]
    return pl.pallas_call(
        add_kernel,
        grid=(steps,),
        in_specs=specs * 2,
        out_specs=specs,
        out_shape=[jax.ShapeDtypeStruct(a.shape, BF16) for a in kept],
        compiler_params=params(60),
        cost_estimate=cost(1e7, 1.7e7),
        name="add_pairs",
    )(*kept, *came)


def input_kernel(
    info, x, middle_first, middle_others, output_first, output_others, own, behind, over, ahead, under, w_groups, gain,
    out, layer_output, grad_middle,
):
    @pl.when(pl.program_id(0) == 0)
    def _():
        grad_middle[...] = middle_first[0]
        layer_output[...] = output_first[...]

    @pl.when(pl.program_id(0) > 0)
    def _():
        grad_middle[...] = middle_others[0]
        layer_output[...] = output_others[...]

    here = info[0]
    w_of = lambda k: w_groups[lax.rem(here + k, GROUPS)]
    unit, inverse = unit_rows(x[0].astype(F32))
    grad_normed = dot(own[0], w_of(0), TN)
    grad_normed += dot(ahead[0], w_of(1), TN)
    grad_normed += dot(jnp.concatenate([over[0], under[0]], axis=0), w_of(2), TN)
    grad_normed += dot(behind[0], w_of(3), TN)
    scaled = grad_normed * gain[...]
    mean_grad = jnp.mean(scaled, axis=-1, keepdims=True)
    mean_dot = jnp.mean(scaled * unit, axis=-1, keepdims=True)
    out[0] = grad_middle[...] + inverse * (scaled - mean_grad - unit * mean_dot)


def input_grad_of(info, x, grad_middle, layer_output, pieces, w_groups, gain):
    mine = lambda rows, lanes: pl.BlockSpec((1, rows, lanes), lambda i, sc: (i, 0, 0))
    whole = lambda *shape: pl.BlockSpec(shape, lambda i, sc: (0,) * len(shape))
    placed = pl.BlockSpec((1, BLOCK, WIDTH), lambda i, sc: (sc[5 + i], 0, 0))
    two = [whole(1, BLOCK, WIDTH), pl.BlockSpec((1, BLOCK, WIDTH), lambda i, sc: (jnp.maximum(i - 1, 0), 0, 0))]
    piece = mine(3 * COLS, BLOCK)
    half = mine(3 * COLS // 2, BLOCK)
    return pl.pallas_call(
        input_kernel,
        grid_spec=pltpu.PrefetchScalarGridSpec(
            num_scalar_prefetch=1,
            grid=(SEQS,),
            in_specs=[placed, *two, *two, piece, piece, half, piece, half, whole(*w_groups.shape), whole(1, WIDTH)],
            out_specs=[placed, placed],
            scratch_shapes=[pltpu.VMEM((BLOCK, WIDTH), F32)],
        ),
        out_shape=(
            jax.ShapeDtypeStruct((SEQS, BLOCK, WIDTH), F32),
            jax.ShapeDtypeStruct((SEQS, BLOCK, WIDTH), BF16),
        ),
        compiler_params=params(60),
        cost_estimate=cost(3e9, 1.5e7),
        name="input_grad",
    )(info, x, *grad_middle, *layer_output, *pieces, w_groups, gain)


def place_kernel(info, up, down, out, *rest):
    grad_up, grad_down, grad_out = rest[-3:]
    grad_up[...] = up[...].astype(F32)
    grad_down[...] = down[...].astype(F32)
    grad_out[...] = out[...].astype(F32)


def place(side, up, down, out, earlier):
    half = FF // CHUNK // 2
    rows = lambda n: pl.BlockSpec((n, WIDTH), lambda i, sc: (i, 0))
    own = lambda n: pl.BlockSpec((n, WIDTH), lambda i, sc: (sc[0] * half + i, 0))
    out_rows = WIDTH // 2 // half
    return pl.pallas_call(
        place_kernel,
        grid_spec=pltpu.PrefetchScalarGridSpec(
            num_scalar_prefetch=1,
            grid=(half,),
            in_specs=[pl.BlockSpec((WIDTH, CHUNK), lambda i, sc: (0, i)), rows(CHUNK), rows(out_rows)]
            + [pl.BlockSpec(memory_space=pl.ANY)] * len(earlier),
            out_specs=[
                pl.BlockSpec((WIDTH, CHUNK), lambda i, sc: (0, sc[0] * half + i)), own(CHUNK), own(out_rows)
            ],
        ),
        out_shape=(
            jax.ShapeDtypeStruct((WIDTH, FF), F32),
            jax.ShapeDtypeStruct((FF, WIDTH), F32),
            jax.ShapeDtypeStruct((WIDTH, WIDTH), F32),
        ),
        input_output_aliases={4 + n: n for n in range(len(earlier))},
        compiler_params=params(60),
        cost_estimate=cost(1e6, 1.6e7),
        name="place",
    )(side.reshape(1), up, down, out, *earlier)


def unpack_kernel(info, own, other, grad_q, grad_k, grad_v, tails, rows):
    size = PACK_ROWS // 16
    half = WIDTH // 2

    def fill(pieces, base):
        for y in range(GROUPS):
            for n in range(16):
                rows[y, n * size : (n + 1) * size, base : base + half] = pieces[n * GROUPS + y].astype(F32)

    @pl.when(info[0] == 0)
    def _():
        fill(own, 0)
        fill(other, half)

    @pl.when(info[0] != 0)
    def _():
        fill(other, 0)
        fill(own, half)

    for n, grad in enumerate((grad_q, grad_k, grad_v)):
        part = jnp.concatenate([rows[y, n * COLS : (n + 1) * COLS, :] for y in range(GROUPS)], axis=0)
        grad[...] = jnp.transpose(part)
    for y in range(GROUPS):
        tails[y] = rows[y, 3 * COLS : 3 * COLS + 16, :]


def unpack(core, own, other):
    full = lambda *shape: jax.ShapeDtypeStruct(shape, F32)
    return pl.pallas_call(
        unpack_kernel,
        in_specs=[pl.BlockSpec(memory_space=pltpu.SMEM), vmem(), vmem()],
        out_specs=[vmem()] * 4,
        out_shape=(full(WIDTH, WIDTH), full(WIDTH, WIDTH), full(WIDTH, WIDTH), full(GROUPS, 16, WIDTH)),
        scratch_shapes=[pltpu.VMEM((GROUPS, PACK_ROWS, WIDTH), F32)],
        compiler_params=params(60),
        cost_estimate=cost(1e6, 1e5),
        name="unpack",
    )(core.reshape(1), own, other)


def shift(array, axis, by):
    return lax.ppermute(array, axis, [(i, (i + by) % GROUPS) for i in range(GROUPS)])


def gather_rows(rows):
    ahead = shift(rows, "head", -1)
    behind = shift(rows, "head", 1)
    over_lo = shift(ahead[:128], "head", -1)
    over_hi = shift(behind[128:], "head", 1)
    return rows, ahead, over_lo, over_hi, behind


def near_exchange(to_next, to_prev):
    return shift(to_next, "head", 1), shift(to_prev, "head", -1)


def far_exchange(from_prev, from_next, size):
    return shift(from_prev[:, size:], "head", 1), shift(from_next[:, size:], "head", -1)


def trade(array, axes):
    return lax.all_to_all(array, axes, 0, 0, tiled=True)


def swap_cores(array):
    return lax.ppermute(array, "core", [(0, 1), (1, 0)])


def add_low(*terms):
    total = terms[0].astype(F32)
    for term in terms[1:]:
        total = total + term.astype(F32)
    return total.astype(BF16)


def per_device(
    layer_input, lengths, cotangent, w_query, w_key, w_value, conv_query, conv_key, conv_value,
    w_out, w_up, w_down, gain_attn, bias_attn, gain_ffn, bias_ffn,
):
    here = lax.axis_index("head").astype(jnp.int32)
    core = lax.axis_index("core").astype(jnp.int32)
    first_rows, other_rows, info = prepare(lengths, layer_input)
    first_rows = gather_rows(first_rows)
    other_rows = lax.all_gather(other_rows, "head", axis=0)

    w_groups = jnp.concatenate(
        [w.T.reshape(GROUPS, COLS, WIDTH) for w in (w_query, w_key, w_value)], axis=1
    )
    w_mine = lax.dynamic_index_in_dim(w_groups, here, 0, False)
    taps = lax.dynamic_slice_in_dim(
        jnp.concatenate([conv_query, conv_key, conv_value], axis=0), here * COLS, COLS, 1
    )
    gain_a, bias_a, gain_f, bias_f = (
        v.reshape(1, WIDTH) for v in (gain_attn, bias_attn, gain_ffn, bias_ffn)
    )
    *saved, mixed_first = attend(True, info, first_rows, w_mine, taps, gain_a, bias_a)
    mixed_first = trade(mixed_first, "head")
    *saved, mixed_others = attend(False, info, other_rows, w_mine, taps, gain_a, bias_a, saved)
    mixed_first, mixed_others = lax.optimization_barrier((mixed_first, mixed_others))
    mixed_others = trade(mixed_others, "head")
    weights = (w_out, gain_f, bias_f, w_up, w_down)
    *seq_a, sq_a, gh_a, normed_a = ffn(True, info, layer_input, cotangent, mixed_first, *weights)
    output_a, middle_a, grad_a, vectors_a, branch_a = ffn_rows(True, info, seq_a, w_out, gain_f)
    mixed_others, grad_a = lax.optimization_barrier((mixed_others, grad_a))
    *seq_b, send_up, send_down, keep_up, keep_down = ffn(
        False, info, layer_input, cotangent, mixed_others, *weights, (sq_a, gh_a, normed_a, seq_a[1])
    )
    output_b, middle_b, grad_mixed, ffn_vectors, send_out, keep_out = ffn_rows(
        False, info, seq_b, w_out, gain_f, (mixed_first, mixed_others, branch_a, vectors_a, grad_a)
    )

    came = [swap_cores(part) for part in (send_up, send_down, send_out)]
    half_sum = add_pairs((keep_up, keep_down, keep_out), came)
    half_sum = lax.psum(half_sum, ("x", "z", "head"))
    grad_mixed = trade(grad_mixed, "head")

    def attention_grads(grad_mixed, saved, grad_middle, layer_output, ffn_vectors):
        d_own, d_next, d_prev, keep, send = attend_back(
            info, grad_mixed, saved, w_mine, taps, gain_a, bias_a, ffn_vectors
        )

        part = add_low(keep, swap_cores(send)).reshape(16, PACK_ROWS // 16, WIDTH // 2)
        part = add_low(*trade(part, ("x", "z")))
        part, d_next, d_prev = lax.optimization_barrier((part, d_next, d_prev))
        behind, ahead = near_exchange(d_next, d_prev)
        over, under = far_exchange(behind, ahead, 3 * COLS)
        for axis in ("head", "z", "x"):
            part = trade(jnp.broadcast_to(part[None], (GROUPS, *part.shape)), axis)
        part = part.reshape(64, PACK_ROWS // 16, WIDTH // 2)
        input_grad, layer_output = input_grad_of(
            info, layer_input, grad_middle, layer_output, (d_own, behind, over, ahead, under), w_groups, gain_a
        )
        part, input_grad = lax.optimization_barrier((part, input_grad))
        grad_q, grad_k, grad_v, tails = unpack(core, part, swap_cores(part))
        conv = lambda n: jnp.transpose(tails[:, 3 * n : 3 * n + 3, 0:COLS], (1, 0, 2)).reshape(3, WIDTH)
        vector = jnp.sum(tails[:, 9:13, :], axis=0)
        return (
            layer_output, input_grad, grad_q, grad_k, grad_v, conv(0), conv(1), conv(2),
            vector[0], vector[1], vector[2], vector[3],
        )

    operands = (grad_mixed, saved, (middle_a, middle_b), (output_a, output_b), ffn_vectors)
    blank = lambda *args: jax.tree.map(
        lambda a: jnp.zeros(a.shape, a.dtype), jax.eval_shape(attention_grads, *args)
    )
    later = lax.cond(lengths[0] > 0, attention_grads, blank, *operands)
    half_sum, later = lax.optimization_barrier((half_sum, later))
    grads = place(core, *half_sum, ())
    grad_up, grad_down, grad_out = place(1 - core, *(swap_cores(part) for part in half_sum), grads)
    return (*later[:8], grad_out, grad_up, grad_down, *later[8:])


def solution(mesh):
    fine = Mesh(mesh.devices.reshape(4, 4, 2, GROUPS), ("x", "z", "core", "head"))
    dp = ("x", "z", "core")
    rows = P(dp, "head", None)
    return jax.shard_map(
        per_device,
        mesh=fine,
        in_specs=(rows, P(dp), rows) + (P(),) * 13,
        out_specs=(rows, rows) + (P(),) * 13,
        check_vma=False,
    )
```

```python
import functools

import jax
import jax.numpy as jnp
from jax import lax
from jax.experimental import pallas as pl
from jax.experimental.pallas import tpu as pltpu
from jax.sharding import Mesh
from jax.sharding import PartitionSpec as P

HDIM = 64
GROUPS = 4
BLOCK = 256
FULL = 1024
WIDTH = 768
COLS = 192
FF = 3072
SEQS = 3
CHUNK = 512
HEADS_HERE = 3
PACK_ROWS = 640
F32 = jnp.float32
BF16 = jnp.bfloat16
NN = (((1,), (0,)), ((), ()))
NT = (((1,), (1,)), ((), ()))
TN = (((0,), (0,)), ((), ()))


def dot(left, right, dims):
    return lax.dot_general(left, right, dims, preferred_element_type=F32)


def cost(flops, nbytes, transcendentals=0):
    return pl.CostEstimate(
        flops=int(flops), bytes_accessed=int(nbytes), transcendentals=int(transcendentals)
    )


def vmem():
    return pl.BlockSpec(memory_space=pltpu.VMEM)


def params(mib):
    return pltpu.CompilerParams(vmem_limit_bytes=mib << 20)


def unit_rows(rows):
    average = jnp.mean(rows, axis=-1, keepdims=True)
    centred = rows - average
    variance = jnp.mean(centred * centred, axis=-1, keepdims=True)
    inverse = lax.rsqrt(variance + 1e-05)
    return centred * inverse, inverse


def head_masks():
    lane = lax.broadcasted_iota(jnp.int32, (1, COLS), 1)
    return [
        jnp.where((lane >= h * HDIM) & (lane < (h + 1) * HDIM), 1.0, 0.0).astype(F32)
        for h in range(HEADS_HERE)
    ]


def conv_rows(raw_f, taps, tap_row, start):
    total = taps[tap_row : tap_row + 1, :] * raw_f[8 + start : 8 + start + BLOCK, :]
    for m in (1, 2):
        total += (
            taps[tap_row + m : tap_row + m + 1, :]
            * raw_f[8 + start - m : 8 + start - m + BLOCK, :]
        )
    return total


def order_of(lengths):
    a, b, c = lengths[0], lengths[1], lengths[2]
    first = jnp.where((a >= b) & (a >= c), 0, jnp.where(b >= c, 1, 2)).astype(jnp.int32)
    second = jnp.where(first == 0, 1, 0).astype(jnp.int32)
    third = jnp.where(first == 2, 1, 2).astype(jnp.int32)
    return first, second, third


def prepare_kernel(lengths, row_0, row_1, row_2, first_rows, other_rows, info):
    first_rows[...] = row_0[0]
    other_rows[0] = row_1[0]
    other_rows[1] = row_2[0]
    info[0] = lax.axis_index("head").astype(jnp.int32)
    info[1] = lax.axis_index("core").astype(jnp.int32)
    a, b, c = lengths[0], lengths[1], lengths[2]
    for n, s in enumerate(order_of(lengths)):
        info[2 + n] = jnp.where(s == 0, a, jnp.where(s == 1, b, c))
        info[5 + n] = s


def prepare(lengths, rows):
    nth = lambda n: pl.BlockSpec((1, BLOCK, WIDTH), lambda i, sc: (order_of(sc)[n], 0, 0))
    whole = lambda *shape: pl.BlockSpec(shape, lambda i, sc: (0,) * len(shape))
    return pl.pallas_call(
        prepare_kernel,
        grid_spec=pltpu.PrefetchScalarGridSpec(
            num_scalar_prefetch=1,
            grid=(1,),
            in_specs=[nth(0), nth(1), nth(2)],
            out_specs=[
                whole(BLOCK, WIDTH), whole(SEQS - 1, BLOCK, WIDTH), pl.BlockSpec(memory_space=pltpu.SMEM)
            ],
        ),
        out_shape=(
            jax.ShapeDtypeStruct((BLOCK, WIDTH), BF16),
            jax.ShapeDtypeStruct((SEQS - 1, BLOCK, WIDTH), BF16),
            jax.ShapeDtypeStruct((8,), jnp.int32),
        ),
        compiler_params=params(60),
        cost_estimate=cost(1e3, 2.4e6),
        name="prepare",
    )(lengths, rows, rows, rows)


def attend_kernel(first, info, *refs):
    count = 5 if first else GROUPS
    pieces, refs = refs[:count], refs[count:]
    w_mine, taps, gain, bias = refs[:4]
    refs = refs[4:] if first else refs[10:]
    normed, raw_q, raw_k, raw_v, mixed, lse_t, to_rows = refs[:7]
    pad_q, pad_k, pad_v, q_s, k_s, v_s, below = refs[7:]
    here = info[0]
    length = info[2] if first else info[3 + pl.program_id(0)]
    blocks = (length + BLOCK - 1) // BLOCK
    masks = head_masks()
    if first:
        homes = [(lax.rem(here + ahead, GROUPS), shift) for ahead, shift in ((0, 0), (1, 0), (2, 0), (2, 128), (3, 0))]
    else:
        homes = [(k, 0) for k in range(GROUPS)]

    for piece, (home, shift) in zip(pieces, homes):

        @pl.when(home < blocks)
        def _(piece=piece, home=home, shift=shift):
            rows = piece[...].reshape(piece.shape[-2], WIDTH).astype(F32)
            size = rows.shape[0]
            unit, _ = unit_rows(rows)
            low = (unit * gain[...] + bias[...]).astype(BF16)
            at = home * BLOCK + shift
            at = pl.multiple_of(at, 128) if first else at
            normed[0, pl.ds(at, size), :] = low
            for n, (raw, pad) in enumerate(((raw_q, pad_q), (raw_k, pad_k), (raw_v, pad_v))):
                value = dot(low, w_mine[n * COLS : (n + 1) * COLS, :], NT).astype(BF16)
                raw[0, pl.ds(at, size), :] = value
                pad[pl.ds(at + 8, size), :] = value.astype(F32)

    for pad in (pad_q, pad_k, pad_v):
        pad[0:8, :] = jnp.zeros((8, COLS), F32)
    row = lax.broadcasted_iota(jnp.int32, (BLOCK, BLOCK), 0)
    col = lax.broadcasted_iota(jnp.int32, (BLOCK, BLOCK), 1)
    below[...] = jnp.where(col <= row, 0.0, -1e30).astype(F32)

    for b in range(GROUPS):

        @pl.when(b < blocks)
        def _(b=b):
            at = slice(b * BLOCK, (b + 1) * BLOCK)
            q_s[at, :] = (conv_rows(pad_q, taps, 0, b * BLOCK).astype(BF16).astype(F32) * 0.125).astype(BF16)
            k_s[at, :] = conv_rows(pad_k, taps, 3, b * BLOCK).astype(BF16)
            v_s[at, :] = conv_rows(pad_v, taps, 6, b * BLOCK).astype(BF16)
            lane = lax.broadcasted_iota(jnp.int32, (BLOCK, 128), 1)
            total_out = jnp.zeros((BLOCK, COLS), F32)
            logs = jnp.zeros((BLOCK, 128), F32)
            for h in range(HEADS_HERE):
                q_h = q_s[at, :] * masks[h].astype(BF16)
                diag = dot(q_h, k_s[at, :], NT) + below[...]
                top = jnp.max(diag, axis=-1, keepdims=True)
                if b:
                    left = dot(q_h, k_s[0 : b * BLOCK, :], NT)
                    top = jnp.maximum(top, jnp.max(left, axis=-1, keepdims=True))
                    expo_left = jnp.exp(left - top)
                expo = jnp.exp(diag - top)
                total = jnp.sum(expo, axis=-1, keepdims=True)
                out = dot(expo.astype(BF16), v_s[at, :], NN)
                if b:
                    total += jnp.sum(expo_left, axis=-1, keepdims=True)
                    out += dot(expo_left.astype(BF16), v_s[0 : b * BLOCK, :], NN)
                total_out = total_out + (out * masks[h]) * (1.0 / total)
                logs = jnp.where(lane == h, top + jnp.log(total), logs)
            result = jnp.transpose(total_out).astype(BF16)
            mixed[b] = result
            to_rows[b] = result
            lse_t[0, :, at] = jnp.transpose(logs)[0:8, :]

        @pl.when(b >= blocks)
        def _(b=b):
            mixed[b] = jnp.zeros((COLS, BLOCK), BF16)
            to_rows[b] = jnp.zeros((COLS, BLOCK), BF16)


def attend(first, info, pieces, w_mine, taps, gain, bias, earlier=()):
    base = 0 if first else 1
    whole = lambda *shape: pl.BlockSpec(shape, lambda i, sc: (0,) * len(shape))
    mine = lambda *shape: pl.BlockSpec((1, *shape), lambda i, sc: (base + i,) + (0,) * len(shape))
    if first:
        piece_specs = [whole(*p.shape) for p in pieces]
    else:
        piece_specs = [
            pl.BlockSpec((1, 1, BLOCK, WIDTH), lambda i, sc, k=k: (k, i, 0, 0)) for k in range(GROUPS)
        ]
        pieces = [pieces] * GROUPS
    full = lambda dtype, *shape: jax.ShapeDtypeStruct((SEQS, *shape), dtype)
    return pl.pallas_call(
        functools.partial(attend_kernel, first),
        grid_spec=pltpu.PrefetchScalarGridSpec(
            num_scalar_prefetch=1,
            grid=(1 if first else SEQS - 1,),
            in_specs=piece_specs
            + [whole(3 * COLS, WIDTH), whole(9, COLS), whole(1, WIDTH), whole(1, WIDTH)]
            + [pl.BlockSpec(memory_space=pl.ANY)] * len(earlier),
            out_specs=[mine(FULL, WIDTH)]
            + [mine(FULL, COLS)] * 3
            + [
                pl.BlockSpec((GROUPS, COLS, BLOCK), lambda i, sc: (0, base + i, 0)),
                mine(8, FULL),
                pl.BlockSpec((GROUPS, COLS, BLOCK), lambda i, sc: (0, i, 0)),
            ],
            scratch_shapes=[pltpu.VMEM((FULL + 8, COLS), F32)] * 3
            + [pltpu.VMEM((FULL, COLS), BF16)] * 3
            + [pltpu.VMEM((BLOCK, BLOCK), F32)],
        ),
        out_shape=(
            full(BF16, FULL, WIDTH),
            full(BF16, FULL, COLS), full(BF16, FULL, COLS), full(BF16, FULL, COLS),
            jax.ShapeDtypeStruct((GROUPS, SEQS * COLS, BLOCK), BF16),
            full(F32, 8, FULL),
            jax.ShapeDtypeStruct((GROUPS, (1 if first else SEQS - 1) * COLS, BLOCK), BF16),
        ),
        input_output_aliases={1 + len(pieces) + 4 + n: n for n in range(len(earlier))},
        compiler_params=params(60),
        cost_estimate=cost(3e9, 8e6, 2e6),
        name="attend",
    )(info, *pieces, w_mine, taps, gain, bias, *earlier)


def attend_back_kernel(
    info, g_s, normed, raw_q, raw_k, raw_v, mixed, lse_t,
    w_mine, taps, gain, bias, ffn_vectors,
    d_own, d_next, d_prev, keep, send,
    dw_out, small_out, d_all, pack,
    pad_q, pad_k, pad_v, q_s, k_s, v_s, dq_s, dk_s, dv_s, below, p_all, ds_all,
):
    step = pl.program_id(0)
    here, core, length = info[0], info[1], info[2 + step]

    blocks = (length + BLOCK - 1) // BLOCK
    masks = head_masks()

    row = lax.broadcasted_iota(jnp.int32, (BLOCK, BLOCK), 0)
    col = lax.broadcasted_iota(jnp.int32, (BLOCK, BLOCK), 1)
    below[...] = jnp.where(row <= col, 0.0, -1e30).astype(F32)
    for pad, raw in ((pad_q, raw_q), (pad_k, raw_k), (pad_v, raw_v)):
        pad[0:8, :] = jnp.zeros((8, COLS), F32)
    for total in (dq_s, dk_s, dv_s):
        total[...] = jnp.zeros((FULL + 8, COLS), F32)

    for b in range(GROUPS):

        @pl.when(b < blocks)
        def _(b=b):
            at = slice(b * BLOCK, (b + 1) * BLOCK)
            for pad, raw in ((pad_q, raw_q), (pad_k, raw_k), (pad_v, raw_v)):
                pad[8 + b * BLOCK : 8 + (b + 1) * BLOCK, :] = raw[0, at, :].astype(F32)
            q_s[at, :] = (conv_rows(pad_q, taps, 0, b * BLOCK).astype(BF16).astype(F32) * 0.125).astype(BF16)
            k_s[at, :] = conv_rows(pad_k, taps, 3, b * BLOCK).astype(BF16)
            v_s[at, :] = conv_rows(pad_v, taps, 6, b * BLOCK).astype(BF16)
            both = g_s[b].astype(F32) * mixed[b].astype(F32)
            reach = slice(0, (b + 1) * BLOCK)
            dq_total = jnp.zeros((BLOCK, COLS), F32)
            q_heads, g_heads = [], []
            for h in range(HEADS_HERE):
                lanes = slice(h * BLOCK, (h + 1) * BLOCK)
                q_h = q_s[at, :] * masks[h].astype(BF16)
                own = slice(h * HDIM, (h + 1) * HDIM)
                blank = lambda n: [jnp.zeros((n * HDIM, BLOCK), BF16)] if n else []
                g_h = jnp.concatenate(blank(h) + [g_s[b, own, :]] + blank(HEADS_HERE - 1 - h), axis=0)
                q_heads.append(q_h)
                g_heads.append(g_h)
                row_dot = jnp.sum(both[own, :], axis=0, keepdims=True)
                log_row = lse_t[0, h : h + 1, at]
                for j in range(b + 1):
                    keys = slice(j * BLOCK, (j + 1) * BLOCK)
                    scores = dot(k_s[keys, :], q_h, NT)
                    if j == b:
                        scores = scores + below[...]
                    probs = jnp.exp(scores - log_row)
                    grad_probs = dot(v_s[keys, :], g_h, NN)
                    p_all[keys, lanes] = probs.astype(BF16)
                    ds_all[keys, lanes] = (probs * (grad_probs - row_dot)).astype(BF16)
                dq_total += dot(ds_all[reach, lanes], k_s[reach, :], TN) * masks[h]
            dq_s[at, :] = dq_total * 0.125
            dv_s[reach, :] += dot(p_all[reach, :], jnp.concatenate(g_heads, axis=1), NT)
            dk_s[reach, :] += dot(ds_all[reach, :], jnp.concatenate(q_heads, axis=0), NN)

    @pl.when(step == 0)
    def _():
        dw_out[...] = jnp.zeros_like(dw_out)
        small_out[...] = jnp.zeros_like(small_out)

    for b in range(GROUPS):

        @pl.when(b < blocks)
        def _(b=b):
            start = b * BLOCK
            at = slice(start, start + BLOCK)
            for n, (pad, grad) in enumerate(((pad_q, dq_s), (pad_k, dk_s), (pad_v, dv_s))):
                now = grad[at, :]
                value = taps[3 * n : 3 * n + 1, :] * now
                for m in (1, 2):
                    value += taps[3 * n + m : 3 * n + m + 1, :] * grad[start + m : start + m + BLOCK, :]
                value = value.astype(BF16).astype(F32)
                d_all[b, n * COLS : (n + 1) * COLS, :] = jnp.transpose(value).astype(BF16)
                small_out[9 + n : 10 + n, 0:COLS] += jnp.sum(value, axis=0, keepdims=True)
                for m in range(3):
                    shifted = pad[8 + start - m : 8 + start - m + BLOCK, :]
                    small_out[3 * n + m : 3 * n + m + 1, 0:COLS] += jnp.sum(
                        shifted * now, axis=0, keepdims=True
                    )
            dw_out[...] += dot(d_all[b], normed[0, at, :], NN)

        @pl.when(b >= blocks)
        def _(b=b):
            d_all[b] = jnp.zeros((3 * COLS, BLOCK), BF16)

    far = lax.rem(here + 2, GROUPS)
    d_own[0] = d_all[here]
    d_next[0, 0 : 3 * COLS, :] = d_all[lax.rem(here + 1, GROUPS)]
    d_next[0, 3 * COLS :, :] = d_all[far, 0 : 3 * COLS // 2, :]
    d_prev[0, 0 : 3 * COLS, :] = d_all[lax.rem(here + 3, GROUPS)]
    d_prev[0, 3 * COLS :, :] = d_all[far, 3 * COLS // 2 :, :]

    @pl.when(step == SEQS - 1)
    def _():
        grad_bias = jnp.zeros((1, WIDTH), F32)
        for n in range(3):
            sums = small_out[9 + n : 10 + n, 0:COLS]
            high = sums.astype(BF16)
            rest = (sums - high.astype(F32)).astype(BF16)
            for term in (high, rest):
                wide = jnp.broadcast_to(term.astype(F32), (16, COLS)).astype(BF16)
                grad_bias += dot(wide, w_mine[n * COLS : (n + 1) * COLS, :], NN)[0:1, :]
        grad_normed = jnp.sum(w_mine[...].astype(F32) * dw_out[...], axis=0, keepdims=True)
        grad_gain = (grad_normed - bias[...] * grad_bias) / gain[...]
        pack[0 : 3 * COLS, :] = dw_out[...].astype(BF16)
        tail = jnp.concatenate(
            [
                small_out[0:9, :],
                grad_gain,
                grad_bias,
                ffn_vectors[0:2, :],
                jnp.zeros((3, WIDTH), F32),
            ],
            axis=0,
        )
        pack[3 * COLS : 3 * COLS + 16, :] = tail.astype(BF16)
        pack[3 * COLS + 16 :, :] = jnp.zeros((PACK_ROWS - 3 * COLS - 16, WIDTH), BF16)
        half = WIDTH // 2
        keep[...] = pack[:, pl.ds(pl.multiple_of(core * half, 128), half)]
        send[...] = pack[:, pl.ds(pl.multiple_of((1 - core) * half, 128), half)]


def attend_back(info, grad_mixed, saved, w_mine, taps, gain, bias, ffn_vectors):
    low = lambda *shape: jax.ShapeDtypeStruct(shape, BF16)
    whole = lambda *shape: pl.BlockSpec(shape, lambda i, sc: (0,) * len(shape))
    mine = lambda *shape: pl.BlockSpec((1, *shape), lambda i, sc: (i,) + (0,) * len(shape))
    across = pl.BlockSpec((GROUPS, COLS, BLOCK), lambda i, sc: (0, i, 0))
    long_rows = 3 * COLS * 3 // 2
    return pl.pallas_call(
        attend_back_kernel,
        grid_spec=pltpu.PrefetchScalarGridSpec(
            num_scalar_prefetch=1,
            grid=(SEQS,),
            in_specs=[
                pl.BlockSpec((GROUPS, COLS, BLOCK), lambda i, sc: (0, lax.rem(i + 2, SEQS), 0)),
                mine(FULL, WIDTH),
            ]
            + [mine(FULL, COLS)] * 3
            + [across, mine(8, FULL)]
            + [whole(3 * COLS, WIDTH), whole(9, COLS), whole(1, WIDTH), whole(1, WIDTH), whole(8, WIDTH)],
            out_specs=[mine(3 * COLS, BLOCK), mine(long_rows, BLOCK), mine(long_rows, BLOCK)]
            + [whole(PACK_ROWS, WIDTH // 2)] * 2,
            scratch_shapes=[
                pltpu.VMEM((3 * COLS, WIDTH), F32),
                pltpu.VMEM((16, WIDTH), F32),
                pltpu.VMEM((GROUPS, 3 * COLS, BLOCK), BF16),
                pltpu.VMEM((PACK_ROWS, WIDTH), BF16),
            ]
            + [pltpu.VMEM((FULL + 8, COLS), F32)] * 3
            + [pltpu.VMEM((FULL, COLS), BF16)] * 3
            + [pltpu.VMEM((FULL + 8, COLS), F32)] * 3
            + [pltpu.VMEM((BLOCK, BLOCK), F32)]
            + [pltpu.VMEM((FULL, HEADS_HERE * BLOCK), BF16)] * 2,
        ),
        out_shape=(
            low(SEQS, 3 * COLS, BLOCK), low(SEQS, long_rows, BLOCK), low(SEQS, long_rows, BLOCK),
            low(PACK_ROWS, WIDTH // 2), low(PACK_ROWS, WIDTH // 2),
        ),
        compiler_params=params(60),
        cost_estimate=cost(1e10, 2e7),
        name="attend_back",
    )(info, grad_mixed, *saved, w_mine, taps, gain, bias, ffn_vectors)


def heads_of(source, s):
    return jnp.concatenate([source[k, s * COLS : (s + 1) * COLS, :] for k in range(GROUPS)], axis=0)


def ffn_kernel(first, info, *refs):
    count = 1 if first else SEQS - 1
    base = 0 if first else 1
    x, cotangent, refs = refs[:count], refs[count : 2 * count], refs[2 * count :]
    mixed, w_out, gain, bias, w_up, w_down = refs[:6]
    refs = refs[6:]
    steps = FF // CHUNK
    half = steps // 2
    if first:
        layer_output, grad_middle, grad_mixed, sq_out, gh_out, normed_of, low_of, branch, vectors = refs[:9]
        middle, total_out, total_grad = refs[9:]
        places = [slice(0, BLOCK)]
    else:
        mixed_first, branch_first, vectors_first, sq_first, gh_first, normed_first, low_first = refs[:7]
        layer_output, grad_middle, grad_mixed, sq_out, gh_out, normed_t, low_of, send_up, send_down = refs[8:17]
        send_out, keep_out, vectors = refs[17:20]
        middle, total_out, total_grad, normed_of, sq_all, gh_all, dw_out = refs[20:]
        places = [slice((s + 1) * BLOCK, (s + 2) * BLOCK) for s in range(count)]
    parts = [slice(s * BLOCK, (s + 1) * BLOCK) for s in range(count)]
    step = pl.program_id(0)
    position = info[0] * BLOCK + lax.broadcasted_iota(jnp.int32, (BLOCK, 1), 0)

    @pl.when(step == 0)
    def _():
        for s, (at, to) in enumerate(zip(parts, places)):
            value = x[s][0].astype(F32) + dot(heads_of(mixed, s), w_out[...], TN)
            middle[at, :] = value
            unit, _ = unit_rows(value)
            normed_of[to, :] = (unit * gain[...] + bias[...]).astype(BF16)
            keep_row = position < info[2 + base + s]
            low_of[to, :] = jnp.where(keep_row, cotangent[s][0].astype(F32), 0.0).astype(BF16)
            total_out[at, :] = jnp.zeros((BLOCK, WIDTH), F32)
            total_grad[at, :] = jnp.zeros((BLOCK, WIDTH), F32)
        if not first:
            normed_of[0:BLOCK, :] = normed_first[...]
            low_of[0:BLOCK, :] = low_first[...]
            normed_t[...] = jnp.transpose(normed_of[...].astype(F32)).astype(BF16)

    def rows_of_chunk(put):
        for at, to in zip(parts, places):
            hidden = jnp.maximum(dot(normed_of[to, :], w_up[...], NN), 0.0)
            squared = (hidden * hidden).astype(BF16)
            back = dot(low_of[to, :], w_down[...], NT)
            grad_hidden = (back * 2.0 * hidden).astype(BF16)
            put(to, squared, grad_hidden)
            total_out[at, :] += dot(squared, w_down[...], NN)
            total_grad[at, :] += dot(grad_hidden, w_up[...], NT)

    def finish(s):
        at, to = parts[s], places[s]
        keep_row = position < info[2 + base + s]
        layer_output[s] = jnp.where(keep_row, middle[at, :] + total_out[at, :], 0.0).astype(BF16)
        unit, inverse = unit_rows(middle[at, :])
        grad_normed = total_grad[at, :]
        scaled = grad_normed * gain[...]
        mean_grad = jnp.mean(scaled, axis=-1, keepdims=True)
        mean_dot = jnp.mean(scaled * unit, axis=-1, keepdims=True)
        value = low_of[to, :].astype(F32) + inverse * (scaled - mean_grad - unit * mean_dot)
        vectors[0:1, :] += jnp.sum(grad_normed * unit, axis=0, keepdims=True)
        vectors[1:2, :] += jnp.sum(grad_normed, axis=0, keepdims=True)
        grad_middle[s] = value
        low = value.astype(BF16)
        heads_grad = dot(w_out[...], low, NT).astype(BF16)
        for k in range(GROUPS):
            grad_mixed[k, s * COLS : (s + 1) * COLS, :] = heads_grad[k * COLS : (k + 1) * COLS]
        return low

    if first:

        def put(to, squared, grad_hidden):
            sq_out[to, :] = squared
            gh_out[to, :] = grad_hidden

        rows_of_chunk(put)

        @pl.when(step == steps - 1)
        def _():
            vectors[...] = jnp.zeros_like(vectors)
            branch[...] = finish(0)

        return

    @pl.when(step < half)
    def _():
        def put(to, squared, grad_hidden):
            sq_all[step, to, :] = squared
            gh_all[step, to, :] = grad_hidden

        rows_of_chunk(put)
        sq_all[step, 0:BLOCK, :] = sq_first[...]
        gh_all[step, 0:BLOCK, :] = gh_first[...]

    @pl.when((step >= half) & (step < steps))
    def _():
        def put(to, squared, grad_hidden):
            sq_out[to, :] = squared
            gh_out[to, :] = grad_hidden

        rows_of_chunk(put)
        sq_out[0:BLOCK, :] = sq_first[...]
        gh_out[0:BLOCK, :] = gh_first[...]

    def weights_of_chunk(n):
        send_up[...] = dot(normed_t[...], gh_all[n], NN).astype(BF16)
        send_down[...] = dot(sq_all[n], low_of[...], TN).astype(BF16)

    @pl.when(step == steps)
    def _():
        vectors[...] = vectors_first[...]
        weights_of_chunk(0)
        low = finish(0)
        dw_out[...] = dot(heads_of(mixed_first, 0), branch_first[...], NN) + dot(heads_of(mixed, 0), low, NN)

    @pl.when(step == steps + 1)
    def _():
        weights_of_chunk(1)
        low = finish(1)
        dw_out[...] += dot(heads_of(mixed, 1), low, NN)

    @pl.when(step == steps + 2)
    def _():
        weights_of_chunk(2)
        width = WIDTH // 2
        keep_out[...] = dw_out[pl.ds(pl.multiple_of(info[1] * width, 128), width), :].astype(BF16)
        send_out[...] = dw_out[pl.ds(pl.multiple_of((1 - info[1]) * width, 128), width), :].astype(BF16)


def ffn(first, info, x, cotangent, mixed, w_out, gain, bias, w_up, w_down, earlier=()):
    count = 1 if first else SEQS - 1
    base = 0 if first else 1
    low = lambda *shape: jax.ShapeDtypeStruct(shape, BF16)
    full = lambda *shape: jax.ShapeDtypeStruct(shape, F32)
    rows = count * BLOCK
    all_rows = SEQS * BLOCK
    steps = FF // CHUNK
    half = steps // 2
    whole = lambda *shape: pl.BlockSpec(shape, lambda i, sc: (0,) * len(shape))
    nth = lambda s: pl.BlockSpec((1, BLOCK, WIDTH), lambda i, sc: (sc[5 + base + s], 0, 0))

    def chunk(i, sc):
        i = jnp.minimum(i, steps - 1)
        return jnp.where(i < half, 1 - sc[1], sc[1]) * half + lax.rem(i, half)

    middle_steps = lambda i: jnp.clip(i - half, 0, half - 1)
    last_steps = lambda i: jnp.maximum(i - steps, 0)
    across = lambda n: pl.BlockSpec((n, CHUNK), lambda i, sc: (0, chunk(i, sc)))
    grads = pl.BlockSpec((GROUPS, count * COLS, BLOCK), lambda i, sc: (0, SEQS - 1 if first else 0, 0))
    scratch = [pltpu.VMEM((rows, WIDTH), F32)] * 3
    if first:
        extra_specs = []
        out_specs = [across(rows)] * 2 + [whole(rows, WIDTH)] * 3 + [whole(8, WIDTH)]
        out_shape = [low(rows, FF)] * 2 + [low(rows, WIDTH)] * 3 + [full(8, WIDTH)]
        aliases = {}
    else:
        extra_specs = (
            [whole(GROUPS, COLS, BLOCK), whole(BLOCK, WIDTH), whole(8, WIDTH)]
            + [across(BLOCK)] * 2
            + [whole(BLOCK, WIDTH)] * 2
            + [pl.BlockSpec(memory_space=pl.ANY)]
        )
        out_specs = (
            [pl.BlockSpec((all_rows, CHUNK), lambda i, sc: (0, middle_steps(i)))] * 2
            + [whole(WIDTH, all_rows), whole(all_rows, WIDTH)]
            + [
                pl.BlockSpec((WIDTH, CHUNK), lambda i, sc: (0, last_steps(i))),
                pl.BlockSpec((CHUNK, WIDTH), lambda i, sc: (last_steps(i), 0)),
            ]
            + [whole(WIDTH // 2, WIDTH)] * 2
            + [whole(8, WIDTH)]
        )
        out_shape = (
            [low(all_rows, FF // 2)] * 2
            + [low(WIDTH, all_rows), low(all_rows, WIDTH), low(WIDTH, FF // 2), low(FF // 2, WIDTH)]
            + [low(WIDTH // 2, WIDTH)] * 2
            + [full(8, WIDTH)]
        )
        scratch += (
            [pltpu.VMEM((all_rows, WIDTH), BF16)]
            + [pltpu.VMEM((half, all_rows, CHUNK), BF16)] * 2
            + [pltpu.VMEM((WIDTH, WIDTH), F32)]
        )
        aliases = {1 + 2 * count + 6 + 7: 2}
    return pl.pallas_call(
        functools.partial(ffn_kernel, first),
        grid_spec=pltpu.PrefetchScalarGridSpec(
            num_scalar_prefetch=1,
            grid=(steps if first else steps + half,),
            in_specs=[nth(s) for s in range(count)] * 2
            + [
                whole(GROUPS, count * COLS, BLOCK), whole(WIDTH, WIDTH), whole(1, WIDTH), whole(1, WIDTH),
                across(WIDTH),
                pl.BlockSpec((CHUNK, WIDTH), lambda i, sc: (chunk(i, sc), 0)),
            ]
            + extra_specs,
            out_specs=[whole(count, BLOCK, WIDTH), whole(count, BLOCK, WIDTH), grads] + out_specs,
            scratch_shapes=scratch,
        ),
        out_shape=[low(count, BLOCK, WIDTH), full(count, BLOCK, WIDTH), low(GROUPS, SEQS * COLS, BLOCK)] + out_shape,
        input_output_aliases=aliases,
        compiler_params=params(60),
        cost_estimate=cost(7e9 if first else 1.8e10, 2e7),
        name="ffn",
    )(info, *[x] * count, *[cotangent] * count, mixed, w_out, gain, bias, w_up, w_down, *earlier)


def weight_kernel(squared, grad_hidden, normed_t, low_grad, keep_out, came_up, came_down, came_out, up, down, out):
    up[...] = (dot(normed_t[...], grad_hidden[...], NN) + came_up[...].astype(F32)).astype(BF16)
    down[...] = (dot(squared[...], low_grad[...], TN) + came_down[...].astype(F32)).astype(BF16)
    out[...] = (keep_out[...].astype(F32) + came_out[...].astype(F32)).astype(BF16)


def weight_grads(squared, grad_hidden, normed_t, low_grad, keep_out, came_up, came_down, came_out):
    low = lambda *shape: jax.ShapeDtypeStruct(shape, BF16)
    all_rows = SEQS * BLOCK
    half = FF // CHUNK // 2
    whole = lambda *shape: pl.BlockSpec(shape, lambda i: (0,) * len(shape))
    across = lambda n: pl.BlockSpec((n, CHUNK), lambda i: (0, i))
    rows = lambda n: pl.BlockSpec((n, WIDTH), lambda i: (i, 0))
    out = rows(WIDTH // 2 // half)
    return pl.pallas_call(
        weight_kernel,
        grid=(half,),
        in_specs=[
            across(all_rows), across(all_rows), whole(WIDTH, all_rows), whole(all_rows, WIDTH),
            out, across(WIDTH), rows(CHUNK), out,
        ],
        out_specs=[across(WIDTH), rows(CHUNK), out],
        out_shape=(low(WIDTH, FF // 2), low(FF // 2, WIDTH), low(WIDTH // 2, WIDTH)),
        compiler_params=params(60),
        cost_estimate=cost(4e9, 1.8e7),
        name="weight_grads",
    )(squared, grad_hidden, normed_t, low_grad, keep_out, came_up, came_down, came_out)


def input_kernel(
    info, x, middle_first, middle_others, output_first, output_others, own, behind, over, ahead, under, w_groups, gain,
    out, layer_output, grad_middle,
):
    @pl.when(pl.program_id(0) == 0)
    def _():
        grad_middle[...] = middle_first[0]
        layer_output[...] = output_first[...]

    @pl.when(pl.program_id(0) > 0)
    def _():
        grad_middle[...] = middle_others[0]
        layer_output[...] = output_others[...]

    here = info[0]
    w_of = lambda k: w_groups[lax.rem(here + k, GROUPS)]
    unit, inverse = unit_rows(x[0].astype(F32))
    grad_normed = dot(own[0], w_of(0), TN)
    grad_normed += dot(ahead[0], w_of(1), TN)
    grad_normed += dot(jnp.concatenate([over[0], under[0]], axis=0), w_of(2), TN)
    grad_normed += dot(behind[0], w_of(3), TN)
    scaled = grad_normed * gain[...]
    mean_grad = jnp.mean(scaled, axis=-1, keepdims=True)
    mean_dot = jnp.mean(scaled * unit, axis=-1, keepdims=True)
    out[0] = grad_middle[...] + inverse * (scaled - mean_grad - unit * mean_dot)


def input_grad_of(info, x, grad_middle, layer_output, pieces, w_groups, gain):
    mine = lambda rows, lanes: pl.BlockSpec((1, rows, lanes), lambda i, sc: (i, 0, 0))
    whole = lambda *shape: pl.BlockSpec(shape, lambda i, sc: (0,) * len(shape))
    placed = pl.BlockSpec((1, BLOCK, WIDTH), lambda i, sc: (sc[5 + i], 0, 0))
    two = [whole(1, BLOCK, WIDTH), pl.BlockSpec((1, BLOCK, WIDTH), lambda i, sc: (jnp.maximum(i - 1, 0), 0, 0))]
    piece = mine(3 * COLS, BLOCK)
    half = mine(3 * COLS // 2, BLOCK)
    return pl.pallas_call(
        input_kernel,
        grid_spec=pltpu.PrefetchScalarGridSpec(
            num_scalar_prefetch=1,
            grid=(SEQS,),
            in_specs=[placed, *two, *two, piece, piece, half, piece, half, whole(*w_groups.shape), whole(1, WIDTH)],
            out_specs=[placed, placed],
            scratch_shapes=[pltpu.VMEM((BLOCK, WIDTH), F32)],
        ),
        out_shape=(
            jax.ShapeDtypeStruct((SEQS, BLOCK, WIDTH), F32),
            jax.ShapeDtypeStruct((SEQS, BLOCK, WIDTH), BF16),
        ),
        compiler_params=params(60),
        cost_estimate=cost(3e9, 1.5e7),
        name="input_grad",
    )(info, x, *grad_middle, *layer_output, *pieces, w_groups, gain)


def place_kernel(info, up, down, out, *rest):
    grad_up, grad_down, grad_out = rest[-3:]
    grad_up[...] = up[...].astype(F32)
    grad_down[...] = down[...].astype(F32)
    grad_out[...] = out[...].astype(F32)


def place(side, up, down, out, earlier):
    half = FF // CHUNK // 2
    rows = lambda n: pl.BlockSpec((n, WIDTH), lambda i, sc: (i, 0))
    own = lambda n: pl.BlockSpec((n, WIDTH), lambda i, sc: (sc[0] * half + i, 0))
    out_rows = WIDTH // 2 // half
    return pl.pallas_call(
        place_kernel,
        grid_spec=pltpu.PrefetchScalarGridSpec(
            num_scalar_prefetch=1,
            grid=(half,),
            in_specs=[pl.BlockSpec((WIDTH, CHUNK), lambda i, sc: (0, i)), rows(CHUNK), rows(out_rows)]
            + [pl.BlockSpec(memory_space=pl.ANY)] * len(earlier),
            out_specs=[
                pl.BlockSpec((WIDTH, CHUNK), lambda i, sc: (0, sc[0] * half + i)), own(CHUNK), own(out_rows)
            ],
        ),
        out_shape=(
            jax.ShapeDtypeStruct((WIDTH, FF), F32),
            jax.ShapeDtypeStruct((FF, WIDTH), F32),
            jax.ShapeDtypeStruct((WIDTH, WIDTH), F32),
        ),
        input_output_aliases={4 + n: n for n in range(len(earlier))},
        compiler_params=params(60),
        cost_estimate=cost(1e6, 1.6e7),
        name="place",
    )(side.reshape(1), up, down, out, *earlier)


def unpack_kernel(info, own, other, grad_q, grad_k, grad_v, tails, rows):
    size = PACK_ROWS // 16
    half = WIDTH // 2

    def fill(pieces, base):
        for y in range(GROUPS):
            for n in range(16):
                rows[y, n * size : (n + 1) * size, base : base + half] = pieces[n * GROUPS + y].astype(F32)

    @pl.when(info[0] == 0)
    def _():
        fill(own, 0)
        fill(other, half)

    @pl.when(info[0] != 0)
    def _():
        fill(other, 0)
        fill(own, half)

    for n, grad in enumerate((grad_q, grad_k, grad_v)):
        part = jnp.concatenate([rows[y, n * COLS : (n + 1) * COLS, :] for y in range(GROUPS)], axis=0)
        grad[...] = jnp.transpose(part)
    for y in range(GROUPS):
        tails[y] = rows[y, 3 * COLS : 3 * COLS + 16, :]


def unpack(core, own, other):
    full = lambda *shape: jax.ShapeDtypeStruct(shape, F32)
    return pl.pallas_call(
        unpack_kernel,
        in_specs=[pl.BlockSpec(memory_space=pltpu.SMEM), vmem(), vmem()],
        out_specs=[vmem()] * 4,
        out_shape=(full(WIDTH, WIDTH), full(WIDTH, WIDTH), full(WIDTH, WIDTH), full(GROUPS, 16, WIDTH)),
        scratch_shapes=[pltpu.VMEM((GROUPS, PACK_ROWS, WIDTH), F32)],
        compiler_params=params(60),
        cost_estimate=cost(1e6, 1e5),
        name="unpack",
    )(core.reshape(1), own, other)


def shift(array, axis, by):
    return lax.ppermute(array, axis, [(i, (i + by) % GROUPS) for i in range(GROUPS)])


def gather_rows(rows):
    ahead = shift(rows, "head", -1)
    behind = shift(rows, "head", 1)
    over_lo = shift(ahead[:128], "head", -1)
    over_hi = shift(behind[128:], "head", 1)
    return rows, ahead, over_lo, over_hi, behind


def near_exchange(to_next, to_prev):
    return shift(to_next, "head", 1), shift(to_prev, "head", -1)


def far_exchange(from_prev, from_next, size):
    return shift(from_prev[:, size:], "head", 1), shift(from_next[:, size:], "head", -1)


def trade(array, axes):
    return lax.all_to_all(array, axes, 0, 0, tiled=True)


def swap_cores(array):
    return lax.ppermute(array, "core", [(0, 1), (1, 0)])


def add_low(*terms):
    total = terms[0].astype(F32)
    for term in terms[1:]:
        total = total + term.astype(F32)
    return total.astype(BF16)


def per_device(
    layer_input, lengths, cotangent, w_query, w_key, w_value, conv_query, conv_key, conv_value,
    w_out, w_up, w_down, gain_attn, bias_attn, gain_ffn, bias_ffn,
):
    here = lax.axis_index("head").astype(jnp.int32)
    core = lax.axis_index("core").astype(jnp.int32)
    first_rows, other_rows, info = prepare(lengths, layer_input)
    first_rows = gather_rows(first_rows)
    other_rows = lax.all_gather(other_rows, "head", axis=0)

    w_groups = jnp.concatenate(
        [w.T.reshape(GROUPS, COLS, WIDTH) for w in (w_query, w_key, w_value)], axis=1
    )
    w_mine = lax.dynamic_index_in_dim(w_groups, here, 0, False)
    taps = lax.dynamic_slice_in_dim(
        jnp.concatenate([conv_query, conv_key, conv_value], axis=0), here * COLS, COLS, 1
    )
    gain_a, bias_a, gain_f, bias_f = (
        v.reshape(1, WIDTH) for v in (gain_attn, bias_attn, gain_ffn, bias_ffn)
    )
    *saved, mixed_first = attend(True, info, first_rows, w_mine, taps, gain_a, bias_a)
    mixed_first = trade(mixed_first, "head")
    *saved, mixed_others = attend(False, info, other_rows, w_mine, taps, gain_a, bias_a, saved)
    mixed_first, mixed_others = lax.optimization_barrier((mixed_first, mixed_others))
    mixed_others = trade(mixed_others, "head")
    weights = (w_out, gain_f, bias_f, w_up, w_down)
    output_a, middle_a, grad_a, *rows_a, branch_a, vectors_a = ffn(
        True, info, layer_input, cotangent, mixed_first, *weights
    )
    output_b, middle_b, grad_mixed, *own, send_up, send_down, send_out, keep_out, ffn_vectors = ffn(
        False, info, layer_input, cotangent, mixed_others, *weights,
        (mixed_first, branch_a, vectors_a, *rows_a, grad_a),
    )

    came = [swap_cores(part) for part in (send_up, send_down, send_out)]
    half_sum = weight_grads(*own, keep_out, *came)
    half_sum, grad_mixed = lax.optimization_barrier((half_sum, trade(grad_mixed, "head")))
    half_sum = lax.psum(half_sum, ("x", "z", "head"))

    def attention_grads(grad_mixed, saved, grad_middle, layer_output, ffn_vectors):
        d_own, d_next, d_prev, keep, send = attend_back(
            info, grad_mixed, saved, w_mine, taps, gain_a, bias_a, ffn_vectors
        )
        behind, ahead = near_exchange(d_next, d_prev)

        part = add_low(keep, swap_cores(send)).reshape(16, PACK_ROWS // 16, WIDTH // 2)
        part = add_low(*trade(part, ("x", "z")))
        part, behind, ahead = lax.optimization_barrier((part, behind, ahead))
        over, under = far_exchange(behind, ahead, 3 * COLS)
        for axis in ("head", "z", "x"):
            if axis == "x":
                part, over, under = lax.optimization_barrier((part, over, under))
            part = trade(jnp.broadcast_to(part[None], (GROUPS, *part.shape)), axis)
        part = part.reshape(64, PACK_ROWS // 16, WIDTH // 2)
        input_grad, layer_output = input_grad_of(
            info, layer_input, grad_middle, layer_output, (d_own, behind, over, ahead, under), w_groups, gain_a
        )
        part, input_grad = lax.optimization_barrier((part, input_grad))
        grad_q, grad_k, grad_v, tails = unpack(core, part, swap_cores(part))
        conv = lambda n: jnp.transpose(tails[:, 3 * n : 3 * n + 3, 0:COLS], (1, 0, 2)).reshape(3, WIDTH)
        vector = jnp.sum(tails[:, 9:13, :], axis=0)
        return (
            layer_output, input_grad, grad_q, grad_k, grad_v, conv(0), conv(1), conv(2),
            vector[0], vector[1], vector[2], vector[3],
        )

    operands = (grad_mixed, saved, (middle_a, middle_b), (output_a, output_b), ffn_vectors)
    blank = lambda *args: jax.tree.map(
        lambda a: jnp.zeros(a.shape, a.dtype), jax.eval_shape(attention_grads, *args)
    )
    later = lax.cond(lengths[0] > 0, attention_grads, blank, *operands)
    half_sum, later = lax.optimization_barrier((half_sum, later))
    grads = place(core, *half_sum, ())
    grad_up, grad_down, grad_out = place(1 - core, *(swap_cores(part) for part in half_sum), grads)
    return (*later[:8], grad_out, grad_up, grad_down, *later[8:])


def solution(mesh):
    fine = Mesh(mesh.devices.reshape(4, 4, 2, GROUPS), ("x", "z", "core", "head"))
    dp = ("x", "z", "core")
    rows = P(dp, "head", None)
    return jax.shard_map(
        per_device,
        mesh=fine,
        in_specs=(rows, P(dp), rows) + (P(),) * 13,
        out_specs=(rows, rows) + (P(),) * 13,
        check_vma=False,
    )
```

```python
import functools

import jax
import jax.numpy as jnp
from jax import lax
from jax.experimental import pallas as pl
from jax.experimental.pallas import tpu as pltpu
from jax.sharding import Mesh
from jax.sharding import PartitionSpec as P

HDIM = 64
GROUPS = 4
BLOCK = 256
FULL = 1024
WIDTH = 768
COLS = 192
FF = 3072
SEQS = 3
CHUNK = 512
HEADS_HERE = 3
PACK_ROWS = 640
F32 = jnp.float32
BF16 = jnp.bfloat16
NN = (((1,), (0,)), ((), ()))
NT = (((1,), (1,)), ((), ()))
TN = (((0,), (0,)), ((), ()))


def dot(left, right, dims):
    return lax.dot_general(left, right, dims, preferred_element_type=F32)


def cost(flops, nbytes, transcendentals=0):
    return pl.CostEstimate(
        flops=int(flops), bytes_accessed=int(nbytes), transcendentals=int(transcendentals)
    )


def vmem():
    return pl.BlockSpec(memory_space=pltpu.VMEM)


def params(mib):
    return pltpu.CompilerParams(vmem_limit_bytes=mib << 20)


def unit_rows(rows):
    average = jnp.mean(rows, axis=-1, keepdims=True)
    centred = rows - average
    variance = jnp.mean(centred * centred, axis=-1, keepdims=True)
    inverse = lax.rsqrt(variance + 1e-05)
    return centred * inverse, inverse


def head_masks():
    lane = lax.broadcasted_iota(jnp.int32, (1, COLS), 1)
    return [
        jnp.where((lane >= h * HDIM) & (lane < (h + 1) * HDIM), 1.0, 0.0).astype(F32)
        for h in range(HEADS_HERE)
    ]


def conv_rows(raw_f, taps, tap_row, start):
    total = taps[tap_row : tap_row + 1, :] * raw_f[8 + start : 8 + start + BLOCK, :]
    for m in (1, 2):
        total += (
            taps[tap_row + m : tap_row + m + 1, :]
            * raw_f[8 + start - m : 8 + start - m + BLOCK, :]
        )
    return total


def order_of(lengths):
    a, b, c = lengths[0], lengths[1], lengths[2]
    first = jnp.where((a >= b) & (a >= c), 0, jnp.where(b >= c, 1, 2)).astype(jnp.int32)
    second = jnp.where(first == 0, 1, 0).astype(jnp.int32)
    third = jnp.where(first == 2, 1, 2).astype(jnp.int32)
    return first, second, third


def prepare_kernel(lengths, row_0, row_1, row_2, first_rows, other_rows, info):
    first_rows[...] = row_0[0]
    other_rows[0] = row_1[0]
    other_rows[1] = row_2[0]
    info[0] = lax.axis_index("head").astype(jnp.int32)
    info[1] = lax.axis_index("core").astype(jnp.int32)
    a, b, c = lengths[0], lengths[1], lengths[2]
    for n, s in enumerate(order_of(lengths)):
        info[2 + n] = jnp.where(s == 0, a, jnp.where(s == 1, b, c))
        info[5 + n] = s


def prepare(lengths, rows):
    nth = lambda n: pl.BlockSpec((1, BLOCK, WIDTH), lambda i, sc: (order_of(sc)[n], 0, 0))
    whole = lambda *shape: pl.BlockSpec(shape, lambda i, sc: (0,) * len(shape))
    return pl.pallas_call(
        prepare_kernel,
        grid_spec=pltpu.PrefetchScalarGridSpec(
            num_scalar_prefetch=1,
            grid=(1,),
            in_specs=[nth(0), nth(1), nth(2)],
            out_specs=[
                whole(BLOCK, WIDTH), whole(SEQS - 1, BLOCK, WIDTH), pl.BlockSpec(memory_space=pltpu.SMEM)
            ],
        ),
        out_shape=(
            jax.ShapeDtypeStruct((BLOCK, WIDTH), BF16),
            jax.ShapeDtypeStruct((SEQS - 1, BLOCK, WIDTH), BF16),
            jax.ShapeDtypeStruct((8,), jnp.int32),
        ),
        compiler_params=params(60),
        cost_estimate=cost(1e3, 2.4e6),
        name="prepare",
    )(lengths, rows, rows, rows)


def attend_kernel(first, info, *refs):
    count = 5 if first else GROUPS
    pieces, refs = refs[:count], refs[count:]
    w_mine, taps, gain, bias = refs[:4]
    refs = refs[4:] if first else refs[10:]
    normed, raw_q, raw_k, raw_v, mixed, lse_t, to_rows = refs[:7]
    pad_q, pad_k, pad_v, q_s, k_s, v_s, below = refs[7:]
    here = info[0]
    length = info[2] if first else info[3 + pl.program_id(0)]
    blocks = (length + BLOCK - 1) // BLOCK
    masks = head_masks()
    if first:
        homes = [(lax.rem(here + ahead, GROUPS), shift) for ahead, shift in ((0, 0), (1, 0), (2, 0), (2, 128), (3, 0))]
    else:
        homes = [(k, 0) for k in range(GROUPS)]

    for piece, (home, shift) in zip(pieces, homes):

        @pl.when(home < blocks)
        def _(piece=piece, home=home, shift=shift):
            rows = piece[...].reshape(piece.shape[-2], WIDTH).astype(F32)
            size = rows.shape[0]
            unit, _ = unit_rows(rows)
            low = (unit * gain[...] + bias[...]).astype(BF16)
            at = home * BLOCK + shift
            at = pl.multiple_of(at, 128) if first else at
            normed[0, pl.ds(at, size), :] = low
            for n, (raw, pad) in enumerate(((raw_q, pad_q), (raw_k, pad_k), (raw_v, pad_v))):
                value = dot(low, w_mine[n * COLS : (n + 1) * COLS, :], NT).astype(BF16)
                raw[0, pl.ds(at, size), :] = value
                pad[pl.ds(at + 8, size), :] = value.astype(F32)

    for pad in (pad_q, pad_k, pad_v):
        pad[0:8, :] = jnp.zeros((8, COLS), F32)
    row = lax.broadcasted_iota(jnp.int32, (BLOCK, BLOCK), 0)
    col = lax.broadcasted_iota(jnp.int32, (BLOCK, BLOCK), 1)
    below[...] = jnp.where(col <= row, 0.0, -1e30).astype(F32)

    for b in range(GROUPS):

        @pl.when(b < blocks)
        def _(b=b):
            at = slice(b * BLOCK, (b + 1) * BLOCK)
            q_s[at, :] = (conv_rows(pad_q, taps, 0, b * BLOCK).astype(BF16).astype(F32) * 0.125).astype(BF16)
            k_s[at, :] = conv_rows(pad_k, taps, 3, b * BLOCK).astype(BF16)
            v_s[at, :] = conv_rows(pad_v, taps, 6, b * BLOCK).astype(BF16)
            lane = lax.broadcasted_iota(jnp.int32, (BLOCK, 128), 1)
            total_out = jnp.zeros((BLOCK, COLS), F32)
            logs = jnp.zeros((BLOCK, 128), F32)
            for h in range(HEADS_HERE):
                q_h = q_s[at, :] * masks[h].astype(BF16)
                diag = dot(q_h, k_s[at, :], NT) + below[...]
                top = jnp.max(diag, axis=-1, keepdims=True)
                if b:
                    left = dot(q_h, k_s[0 : b * BLOCK, :], NT)
                    top = jnp.maximum(top, jnp.max(left, axis=-1, keepdims=True))
                    expo_left = jnp.exp(left - top)
                expo = jnp.exp(diag - top)
                total = jnp.sum(expo, axis=-1, keepdims=True)
                out = dot(expo.astype(BF16), v_s[at, :], NN)
                if b:
                    total += jnp.sum(expo_left, axis=-1, keepdims=True)
                    out += dot(expo_left.astype(BF16), v_s[0 : b * BLOCK, :], NN)
                total_out = total_out + (out * masks[h]) * (1.0 / total)
                logs = jnp.where(lane == h, top + jnp.log(total), logs)
            result = jnp.transpose(total_out).astype(BF16)
            mixed[b] = result
            to_rows[b] = result
            lse_t[0, :, at] = jnp.transpose(logs)[0:8, :]

        @pl.when(b >= blocks)
        def _(b=b):
            mixed[b] = jnp.zeros((COLS, BLOCK), BF16)
            to_rows[b] = jnp.zeros((COLS, BLOCK), BF16)


def attend(first, info, pieces, w_mine, taps, gain, bias, earlier=()):
    base = 0 if first else 1
    whole = lambda *shape: pl.BlockSpec(shape, lambda i, sc: (0,) * len(shape))
    mine = lambda *shape: pl.BlockSpec((1, *shape), lambda i, sc: (base + i,) + (0,) * len(shape))
    if first:
        piece_specs = [whole(*p.shape) for p in pieces]
    else:
        piece_specs = [
            pl.BlockSpec((1, 1, BLOCK, WIDTH), lambda i, sc, k=k: (k, i, 0, 0)) for k in range(GROUPS)
        ]
        pieces = [pieces] * GROUPS
    full = lambda dtype, *shape: jax.ShapeDtypeStruct((SEQS, *shape), dtype)
    return pl.pallas_call(
        functools.partial(attend_kernel, first),
        grid_spec=pltpu.PrefetchScalarGridSpec(
            num_scalar_prefetch=1,
            grid=(1 if first else SEQS - 1,),
            in_specs=piece_specs
            + [whole(3 * COLS, WIDTH), whole(9, COLS), whole(1, WIDTH), whole(1, WIDTH)]
            + [pl.BlockSpec(memory_space=pl.ANY)] * len(earlier),
            out_specs=[mine(FULL, WIDTH)]
            + [mine(FULL, COLS)] * 3
            + [
                pl.BlockSpec((GROUPS, COLS, BLOCK), lambda i, sc: (0, base + i, 0)),
                mine(8, FULL),
                pl.BlockSpec((GROUPS, COLS, BLOCK), lambda i, sc: (0, i, 0)),
            ],
            scratch_shapes=[pltpu.VMEM((FULL + 8, COLS), F32)] * 3
            + [pltpu.VMEM((FULL, COLS), BF16)] * 3
            + [pltpu.VMEM((BLOCK, BLOCK), F32)],
        ),
        out_shape=(
            full(BF16, FULL, WIDTH),
            full(BF16, FULL, COLS), full(BF16, FULL, COLS), full(BF16, FULL, COLS),
            jax.ShapeDtypeStruct((GROUPS, SEQS * COLS, BLOCK), BF16),
            full(F32, 8, FULL),
            jax.ShapeDtypeStruct((GROUPS, (1 if first else SEQS - 1) * COLS, BLOCK), BF16),
        ),
        input_output_aliases={1 + len(pieces) + 4 + n: n for n in range(len(earlier))},
        compiler_params=params(60),
        cost_estimate=cost(3e9, 8e6, 2e6),
        name="attend",
    )(info, *pieces, w_mine, taps, gain, bias, *earlier)


def attend_back_kernel(
    info, g_s, normed, raw_q, raw_k, raw_v, mixed, lse_t,
    w_mine, taps, gain, bias, ffn_vectors,
    d_own, d_next, d_prev, keep, send,
    dw_out, small_out, d_all, pack,
    pad_q, pad_k, pad_v, q_s, k_s, v_s, dq_s, dk_s, dv_s, below, p_all, ds_all,
):
    step = pl.program_id(0)
    here, core, length = info[0], info[1], info[2 + step]

    blocks = (length + BLOCK - 1) // BLOCK
    masks = head_masks()

    row = lax.broadcasted_iota(jnp.int32, (BLOCK, BLOCK), 0)
    col = lax.broadcasted_iota(jnp.int32, (BLOCK, BLOCK), 1)
    below[...] = jnp.where(row <= col, 0.0, -1e30).astype(F32)
    for pad, raw in ((pad_q, raw_q), (pad_k, raw_k), (pad_v, raw_v)):
        pad[0:8, :] = jnp.zeros((8, COLS), F32)
    for total in (dq_s, dk_s, dv_s):
        total[...] = jnp.zeros((FULL + 8, COLS), F32)

    for b in range(GROUPS):

        @pl.when(b < blocks)
        def _(b=b):
            at = slice(b * BLOCK, (b + 1) * BLOCK)
            for pad, raw in ((pad_q, raw_q), (pad_k, raw_k), (pad_v, raw_v)):
                pad[8 + b * BLOCK : 8 + (b + 1) * BLOCK, :] = raw[0, at, :].astype(F32)
            q_s[at, :] = (conv_rows(pad_q, taps, 0, b * BLOCK).astype(BF16).astype(F32) * 0.125).astype(BF16)
            k_s[at, :] = conv_rows(pad_k, taps, 3, b * BLOCK).astype(BF16)
            v_s[at, :] = conv_rows(pad_v, taps, 6, b * BLOCK).astype(BF16)
            both = g_s[b].astype(F32) * mixed[b].astype(F32)
            reach = slice(0, (b + 1) * BLOCK)
            dq_total = jnp.zeros((BLOCK, COLS), F32)
            q_heads, g_heads = [], []
            for h in range(HEADS_HERE):
                lanes = slice(h * BLOCK, (h + 1) * BLOCK)
                q_h = q_s[at, :] * masks[h].astype(BF16)
                own = slice(h * HDIM, (h + 1) * HDIM)
                blank = lambda n: [jnp.zeros((n * HDIM, BLOCK), BF16)] if n else []
                g_h = jnp.concatenate(blank(h) + [g_s[b, own, :]] + blank(HEADS_HERE - 1 - h), axis=0)
                q_heads.append(q_h)
                g_heads.append(g_h)
                row_dot = jnp.sum(both[own, :], axis=0, keepdims=True)
                log_row = lse_t[0, h : h + 1, at]
                for j in range(b + 1):
                    keys = slice(j * BLOCK, (j + 1) * BLOCK)
                    scores = dot(k_s[keys, :], q_h, NT)
                    if j == b:
                        scores = scores + below[...]
                    probs = jnp.exp(scores - log_row)
                    grad_probs = dot(v_s[keys, :], g_h, NN)
                    p_all[keys, lanes] = probs.astype(BF16)
                    ds_all[keys, lanes] = (probs * (grad_probs - row_dot)).astype(BF16)
                dq_total += dot(ds_all[reach, lanes], k_s[reach, :], TN) * masks[h]
            dq_s[at, :] = dq_total * 0.125
            dv_s[reach, :] += dot(p_all[reach, :], jnp.concatenate(g_heads, axis=1), NT)
            dk_s[reach, :] += dot(ds_all[reach, :], jnp.concatenate(q_heads, axis=0), NN)

    @pl.when(step == 0)
    def _():
        dw_out[...] = jnp.zeros_like(dw_out)
        small_out[...] = jnp.zeros_like(small_out)

    for b in range(GROUPS):

        @pl.when(b < blocks)
        def _(b=b):
            start = b * BLOCK
            at = slice(start, start + BLOCK)
            for n, (pad, grad) in enumerate(((pad_q, dq_s), (pad_k, dk_s), (pad_v, dv_s))):
                now = grad[at, :]
                value = taps[3 * n : 3 * n + 1, :] * now
                for m in (1, 2):
                    value += taps[3 * n + m : 3 * n + m + 1, :] * grad[start + m : start + m + BLOCK, :]
                value = value.astype(BF16).astype(F32)
                d_all[b, n * COLS : (n + 1) * COLS, :] = jnp.transpose(value).astype(BF16)
                small_out[9 + n : 10 + n, 0:COLS] += jnp.sum(value, axis=0, keepdims=True)
                for m in range(3):
                    shifted = pad[8 + start - m : 8 + start - m + BLOCK, :]
                    small_out[3 * n + m : 3 * n + m + 1, 0:COLS] += jnp.sum(
                        shifted * now, axis=0, keepdims=True
                    )
            dw_out[...] += dot(d_all[b], normed[0, at, :], NN)

        @pl.when(b >= blocks)
        def _(b=b):
            d_all[b] = jnp.zeros((3 * COLS, BLOCK), BF16)

    far = lax.rem(here + 2, GROUPS)
    d_own[0] = d_all[here]
    d_next[0, 0 : 3 * COLS, :] = d_all[lax.rem(here + 1, GROUPS)]
    d_next[0, 3 * COLS :, :] = d_all[far, 0 : 3 * COLS // 2, :]
    d_prev[0, 0 : 3 * COLS, :] = d_all[lax.rem(here + 3, GROUPS)]
    d_prev[0, 3 * COLS :, :] = d_all[far, 3 * COLS // 2 :, :]

    @pl.when(step == SEQS - 1)
    def _():
        grad_bias = jnp.zeros((1, WIDTH), F32)
        for n in range(3):
            sums = small_out[9 + n : 10 + n, 0:COLS]
            high = sums.astype(BF16)
            rest = (sums - high.astype(F32)).astype(BF16)
            for term in (high, rest):
                wide = jnp.broadcast_to(term.astype(F32), (16, COLS)).astype(BF16)
                grad_bias += dot(wide, w_mine[n * COLS : (n + 1) * COLS, :], NN)[0:1, :]
        grad_normed = jnp.sum(w_mine[...].astype(F32) * dw_out[...], axis=0, keepdims=True)
        grad_gain = (grad_normed - bias[...] * grad_bias) / gain[...]
        pack[0 : 3 * COLS, :] = dw_out[...].astype(BF16)
        tail = jnp.concatenate(
            [
                small_out[0:9, :],
                grad_gain,
                grad_bias,
                ffn_vectors[0:2, :],
                jnp.zeros((3, WIDTH), F32),
            ],
            axis=0,
        )
        pack[3 * COLS : 3 * COLS + 16, :] = tail.astype(BF16)
        pack[3 * COLS + 16 :, :] = jnp.zeros((PACK_ROWS - 3 * COLS - 16, WIDTH), BF16)
        half = WIDTH // 2
        keep[...] = pack[:, pl.ds(pl.multiple_of(core * half, 128), half)]
        send[...] = pack[:, pl.ds(pl.multiple_of((1 - core) * half, 128), half)]


def attend_back(info, grad_mixed, saved, w_mine, taps, gain, bias, ffn_vectors):
    low = lambda *shape: jax.ShapeDtypeStruct(shape, BF16)
    whole = lambda *shape: pl.BlockSpec(shape, lambda i, sc: (0,) * len(shape))
    mine = lambda *shape: pl.BlockSpec((1, *shape), lambda i, sc: (i,) + (0,) * len(shape))
    across = pl.BlockSpec((GROUPS, COLS, BLOCK), lambda i, sc: (0, i, 0))
    long_rows = 3 * COLS * 3 // 2
    return pl.pallas_call(
        attend_back_kernel,
        grid_spec=pltpu.PrefetchScalarGridSpec(
            num_scalar_prefetch=1,
            grid=(SEQS,),
            in_specs=[
                pl.BlockSpec((GROUPS, COLS, BLOCK), lambda i, sc: (0, lax.rem(i + 2, SEQS), 0)),
                mine(FULL, WIDTH),
            ]
            + [mine(FULL, COLS)] * 3
            + [across, mine(8, FULL)]
            + [whole(3 * COLS, WIDTH), whole(9, COLS), whole(1, WIDTH), whole(1, WIDTH), whole(8, WIDTH)],
            out_specs=[mine(3 * COLS, BLOCK), mine(long_rows, BLOCK), mine(long_rows, BLOCK)]
            + [whole(PACK_ROWS, WIDTH // 2)] * 2,
            scratch_shapes=[
                pltpu.VMEM((3 * COLS, WIDTH), F32),
                pltpu.VMEM((16, WIDTH), F32),
                pltpu.VMEM((GROUPS, 3 * COLS, BLOCK), BF16),
                pltpu.VMEM((PACK_ROWS, WIDTH), BF16),
            ]
            + [pltpu.VMEM((FULL + 8, COLS), F32)] * 3
            + [pltpu.VMEM((FULL, COLS), BF16)] * 3
            + [pltpu.VMEM((FULL + 8, COLS), F32)] * 3
            + [pltpu.VMEM((BLOCK, BLOCK), F32)]
            + [pltpu.VMEM((FULL, HEADS_HERE * BLOCK), BF16)] * 2,
        ),
        out_shape=(
            low(SEQS, 3 * COLS, BLOCK), low(SEQS, long_rows, BLOCK), low(SEQS, long_rows, BLOCK),
            low(PACK_ROWS, WIDTH // 2), low(PACK_ROWS, WIDTH // 2),
        ),
        compiler_params=params(60),
        cost_estimate=cost(1e10, 2e7),
        name="attend_back",
    )(info, grad_mixed, *saved, w_mine, taps, gain, bias, ffn_vectors)


def heads_of(source, s):
    return jnp.concatenate([source[k, s * COLS : (s + 1) * COLS, :] for k in range(GROUPS)], axis=0)


def ffn_kernel(first, info, *refs):
    count = 1 if first else SEQS - 1
    base = 0 if first else 1
    x, cotangent, refs = refs[:count], refs[count : 2 * count], refs[2 * count :]
    mixed, w_out, gain, bias, w_up, w_down = refs[:6]
    refs = refs[6:]
    steps = FF // CHUNK
    if first:
        layer_output, grad_middle, grad_mixed, sq_out, gh_out, normed_of, low_of, branch, vectors = refs[:9]
        middle, total_out, total_grad = refs[9:]
        places = [slice(0, BLOCK)]
    else:
        mixed_first, branch_first, vectors_first, sq_first, gh_first, normed_first, low_first = refs[:7]
        layer_output, grad_middle, grad_mixed, grad_up, grad_down, grad_out, vectors = refs[8:15]
        middle, total_out, total_grad, normed_of, normed_t, low_of, sq_all, gh_all, dw_out = refs[15:]
        places = [slice((s + 1) * BLOCK, (s + 2) * BLOCK) for s in range(count)]
    parts = [slice(s * BLOCK, (s + 1) * BLOCK) for s in range(count)]
    step = pl.program_id(0)
    position = info[0] * BLOCK + lax.broadcasted_iota(jnp.int32, (BLOCK, 1), 0)

    @pl.when(step == 0)
    def _():
        for s, (at, to) in enumerate(zip(parts, places)):
            value = x[s][0].astype(F32) + dot(heads_of(mixed, s), w_out[...], TN)
            middle[at, :] = value
            unit, _ = unit_rows(value)
            normed_of[to, :] = (unit * gain[...] + bias[...]).astype(BF16)
            keep_row = position < info[2 + base + s]
            low_of[to, :] = jnp.where(keep_row, cotangent[s][0].astype(F32), 0.0).astype(BF16)
            total_out[at, :] = jnp.zeros((BLOCK, WIDTH), F32)
            total_grad[at, :] = jnp.zeros((BLOCK, WIDTH), F32)
        if not first:
            normed_of[0:BLOCK, :] = normed_first[...]
            low_of[0:BLOCK, :] = low_first[...]
            normed_t[...] = jnp.transpose(normed_of[...].astype(F32)).astype(BF16)

    def rows_of_chunk(put):
        for at, to in zip(parts, places):
            hidden = jnp.maximum(dot(normed_of[to, :], w_up[...], NN), 0.0)
            squared = (hidden * hidden).astype(BF16)
            back = dot(low_of[to, :], w_down[...], NT)
            grad_hidden = (back * 2.0 * hidden).astype(BF16)
            put(to, squared, grad_hidden)
            total_out[at, :] += dot(squared, w_down[...], NN)
            total_grad[at, :] += dot(grad_hidden, w_up[...], NT)

    def finish(s):
        at, to = parts[s], places[s]
        keep_row = position < info[2 + base + s]
        layer_output[s] = jnp.where(keep_row, middle[at, :] + total_out[at, :], 0.0).astype(BF16)
        unit, inverse = unit_rows(middle[at, :])
        grad_normed = total_grad[at, :]
        scaled = grad_normed * gain[...]
        mean_grad = jnp.mean(scaled, axis=-1, keepdims=True)
        mean_dot = jnp.mean(scaled * unit, axis=-1, keepdims=True)
        value = low_of[to, :].astype(F32) + inverse * (scaled - mean_grad - unit * mean_dot)
        vectors[0:1, :] += jnp.sum(grad_normed * unit, axis=0, keepdims=True)
        vectors[1:2, :] += jnp.sum(grad_normed, axis=0, keepdims=True)
        grad_middle[s] = value
        low = value.astype(BF16)
        heads_grad = dot(w_out[...], low, NT).astype(BF16)
        for k in range(GROUPS):
            grad_mixed[k, s * COLS : (s + 1) * COLS, :] = heads_grad[k * COLS : (k + 1) * COLS]
        return low

    if first:

        def put(to, squared, grad_hidden):
            sq_out[to, :] = squared
            gh_out[to, :] = grad_hidden

        rows_of_chunk(put)

        @pl.when(step == steps - 1)
        def _():
            vectors[...] = jnp.zeros_like(vectors)
            branch[...] = finish(0)

        return

    @pl.when(step < steps)
    def _():
        def put(to, squared, grad_hidden):
            sq_all[step, to, :] = squared
            gh_all[step, to, :] = grad_hidden

        rows_of_chunk(put)
        sq_all[step, 0:BLOCK, :] = sq_first[...]
        gh_all[step, 0:BLOCK, :] = gh_first[...]

    def weights_of_chunk(n):
        grad_up[...] = dot(normed_t[...], gh_all[n], NN).astype(BF16)
        grad_down[...] = dot(sq_all[n], low_of[...], TN).astype(BF16)

    @pl.when(step == steps)
    def _():
        vectors[...] = vectors_first[...]
        weights_of_chunk(0)
        low = finish(0)
        dw_out[...] = dot(heads_of(mixed_first, 0), branch_first[...], NN) + dot(heads_of(mixed, 0), low, NN)

    @pl.when(step == steps + 1)
    def _():
        weights_of_chunk(1)
        low = finish(1)
        dw_out[...] += dot(heads_of(mixed, 1), low, NN)

    @pl.when(step >= steps + 2)
    def _():
        weights_of_chunk(step - steps)
        grad_out[...] = dw_out[...].astype(BF16)


def ffn(first, info, x, cotangent, mixed, w_out, gain, bias, w_up, w_down, earlier=()):
    count = 1 if first else SEQS - 1
    base = 0 if first else 1
    low = lambda *shape: jax.ShapeDtypeStruct(shape, BF16)
    full = lambda *shape: jax.ShapeDtypeStruct(shape, F32)
    rows = count * BLOCK
    all_rows = SEQS * BLOCK
    steps = FF // CHUNK
    whole = lambda *shape: pl.BlockSpec(shape, lambda i, sc: (0,) * len(shape))
    nth = lambda s: pl.BlockSpec((1, BLOCK, WIDTH), lambda i, sc: (sc[5 + base + s], 0, 0))
    early = lambda i: jnp.minimum(i, steps - 1)
    late = lambda i: jnp.maximum(i - steps, 0)
    across = lambda n: pl.BlockSpec((n, CHUNK), lambda i, sc: (0, early(i)))
    grads = pl.BlockSpec((GROUPS, count * COLS, BLOCK), lambda i, sc: (0, SEQS - 1 if first else 0, 0))
    scratch = [pltpu.VMEM((rows, WIDTH), F32)] * 3
    if first:
        extra_specs = []
        out_specs = [across(rows)] * 2 + [whole(rows, WIDTH)] * 3 + [whole(8, WIDTH)]
        out_shape = [low(rows, FF)] * 2 + [low(rows, WIDTH)] * 3 + [full(8, WIDTH)]
        aliases = {}
    else:
        extra_specs = (
            [whole(GROUPS, COLS, BLOCK), whole(BLOCK, WIDTH), whole(8, WIDTH)]
            + [across(BLOCK)] * 2
            + [whole(BLOCK, WIDTH)] * 2
            + [pl.BlockSpec(memory_space=pl.ANY)]
        )
        out_specs = [
            pl.BlockSpec((WIDTH, CHUNK), lambda i, sc: (0, late(i))),
            pl.BlockSpec((CHUNK, WIDTH), lambda i, sc: (late(i), 0)),
            whole(WIDTH, WIDTH),
            whole(8, WIDTH),
        ]
        out_shape = [low(WIDTH, FF), low(FF, WIDTH), low(WIDTH, WIDTH), full(8, WIDTH)]
        scratch += (
            [pltpu.VMEM((all_rows, WIDTH), BF16), pltpu.VMEM((WIDTH, all_rows), BF16), pltpu.VMEM((all_rows, WIDTH), BF16)]
            + [pltpu.VMEM((steps, all_rows, CHUNK), BF16)] * 2
            + [pltpu.VMEM((WIDTH, WIDTH), F32)]
        )
        aliases = {1 + 2 * count + 6 + 7: 2}
    return pl.pallas_call(
        functools.partial(ffn_kernel, first),
        grid_spec=pltpu.PrefetchScalarGridSpec(
            num_scalar_prefetch=1,
            grid=(steps if first else 2 * steps,),
            in_specs=[nth(s) for s in range(count)] * 2
            + [
                whole(GROUPS, count * COLS, BLOCK), whole(WIDTH, WIDTH), whole(1, WIDTH), whole(1, WIDTH),
                across(WIDTH),
                pl.BlockSpec((CHUNK, WIDTH), lambda i, sc: (early(i), 0)),
            ]
            + extra_specs,
            out_specs=[whole(count, BLOCK, WIDTH), whole(count, BLOCK, WIDTH), grads] + out_specs,
            scratch_shapes=scratch,
        ),
        out_shape=[low(count, BLOCK, WIDTH), full(count, BLOCK, WIDTH), low(GROUPS, SEQS * COLS, BLOCK)] + out_shape,
        input_output_aliases=aliases,
        compiler_params=params(60),
        cost_estimate=cost(7e9 if first else 2.2e10, 2e7),
        name="ffn",
    )(info, *[x] * count, *[cotangent] * count, mixed, w_out, gain, bias, w_up, w_down, *earlier)


def input_kernel(
    info, x, middle_first, middle_others, output_first, output_others, own, behind, over, ahead, under, w_groups, gain,
    out, layer_output, grad_middle,
):
    @pl.when(pl.program_id(0) == 0)
    def _():
        grad_middle[...] = middle_first[0]
        layer_output[...] = output_first[...]

    @pl.when(pl.program_id(0) > 0)
    def _():
        grad_middle[...] = middle_others[0]
        layer_output[...] = output_others[...]

    here = info[0]
    w_of = lambda k: w_groups[lax.rem(here + k, GROUPS)]
    unit, inverse = unit_rows(x[0].astype(F32))
    grad_normed = dot(own[0], w_of(0), TN)
    grad_normed += dot(ahead[0], w_of(1), TN)
    grad_normed += dot(jnp.concatenate([over[0], under[0]], axis=0), w_of(2), TN)
    grad_normed += dot(behind[0], w_of(3), TN)
    scaled = grad_normed * gain[...]
    mean_grad = jnp.mean(scaled, axis=-1, keepdims=True)
    mean_dot = jnp.mean(scaled * unit, axis=-1, keepdims=True)
    out[0] = grad_middle[...] + inverse * (scaled - mean_grad - unit * mean_dot)


def input_grad_of(info, x, grad_middle, layer_output, pieces, w_groups, gain):
    mine = lambda rows, lanes: pl.BlockSpec((1, rows, lanes), lambda i, sc: (i, 0, 0))
    whole = lambda *shape: pl.BlockSpec(shape, lambda i, sc: (0,) * len(shape))
    placed = pl.BlockSpec((1, BLOCK, WIDTH), lambda i, sc: (sc[5 + i], 0, 0))
    two = [whole(1, BLOCK, WIDTH), pl.BlockSpec((1, BLOCK, WIDTH), lambda i, sc: (jnp.maximum(i - 1, 0), 0, 0))]
    piece = mine(3 * COLS, BLOCK)
    half = mine(3 * COLS // 2, BLOCK)
    return pl.pallas_call(
        input_kernel,
        grid_spec=pltpu.PrefetchScalarGridSpec(
            num_scalar_prefetch=1,
            grid=(SEQS,),
            in_specs=[placed, *two, *two, piece, piece, half, piece, half, whole(*w_groups.shape), whole(1, WIDTH)],
            out_specs=[placed, placed],
            scratch_shapes=[pltpu.VMEM((BLOCK, WIDTH), F32)],
        ),
        out_shape=(
            jax.ShapeDtypeStruct((SEQS, BLOCK, WIDTH), F32),
            jax.ShapeDtypeStruct((SEQS, BLOCK, WIDTH), BF16),
        ),
        compiler_params=params(60),
        cost_estimate=cost(3e9, 1.5e7),
        name="input_grad",
    )(info, x, *grad_middle, *layer_output, *pieces, w_groups, gain)


def place_kernel(up, down, out, grad_up, grad_down, grad_out):
    grad_up[...] = up[...].astype(F32)
    grad_down[...] = down[...].astype(F32)
    grad_out[...] = out[...].astype(F32)


def place(up, down, out):
    steps = FF // CHUNK
    rows = lambda n: pl.BlockSpec((n, WIDTH), lambda i: (i, 0))
    specs = [pl.BlockSpec((WIDTH, CHUNK), lambda i: (0, i)), rows(CHUNK), rows(WIDTH // steps)]
    return pl.pallas_call(
        place_kernel,
        grid=(steps,),
        in_specs=specs,
        out_specs=specs,
        out_shape=[jax.ShapeDtypeStruct(a.shape, F32) for a in (up, down, out)],
        compiler_params=params(60),
        cost_estimate=cost(1e6, 3.2e7),
        name="place",
    )(up, down, out)


def unpack_kernel(info, own, other, grad_q, grad_k, grad_v, tails, rows):
    size = PACK_ROWS // 16
    half = WIDTH // 2

    def fill(pieces, base):
        for y in range(GROUPS):
            for n in range(16):
                rows[y, n * size : (n + 1) * size, base : base + half] = pieces[n * GROUPS + y].astype(F32)

    @pl.when(info[0] == 0)
    def _():
        fill(own, 0)
        fill(other, half)

    @pl.when(info[0] != 0)
    def _():
        fill(other, 0)
        fill(own, half)

    for n, grad in enumerate((grad_q, grad_k, grad_v)):
        part = jnp.concatenate([rows[y, n * COLS : (n + 1) * COLS, :] for y in range(GROUPS)], axis=0)
        grad[...] = jnp.transpose(part)
    for y in range(GROUPS):
        tails[y] = rows[y, 3 * COLS : 3 * COLS + 16, :]


def unpack(core, own, other):
    full = lambda *shape: jax.ShapeDtypeStruct(shape, F32)
    return pl.pallas_call(
        unpack_kernel,
        in_specs=[pl.BlockSpec(memory_space=pltpu.SMEM), vmem(), vmem()],
        out_specs=[vmem()] * 4,
        out_shape=(full(WIDTH, WIDTH), full(WIDTH, WIDTH), full(WIDTH, WIDTH), full(GROUPS, 16, WIDTH)),
        scratch_shapes=[pltpu.VMEM((GROUPS, PACK_ROWS, WIDTH), F32)],
        compiler_params=params(60),
        cost_estimate=cost(1e6, 1e5),
        name="unpack",
    )(core.reshape(1), own, other)


def shift(array, axis, by):
    return lax.ppermute(array, axis, [(i, (i + by) % GROUPS) for i in range(GROUPS)])


def gather_rows(rows):
    ahead = shift(rows, "head", -1)
    behind = shift(rows, "head", 1)
    over_lo = shift(ahead[:128], "head", -1)
    over_hi = shift(behind[128:], "head", 1)
    return rows, ahead, over_lo, over_hi, behind


def near_exchange(to_next, to_prev):
    return shift(to_next, "head", 1), shift(to_prev, "head", -1)


def far_exchange(from_prev, from_next, size):
    return shift(from_prev[:, size:], "head", 1), shift(from_next[:, size:], "head", -1)


def trade(array, axes):
    return lax.all_to_all(array, axes, 0, 0, tiled=True)


def swap_cores(array):
    return lax.ppermute(array, "core", [(0, 1), (1, 0)])


def add_low(*terms):
    total = terms[0].astype(F32)
    for term in terms[1:]:
        total = total + term.astype(F32)
    return total.astype(BF16)


def per_device(
    layer_input, lengths, cotangent, w_query, w_key, w_value, conv_query, conv_key, conv_value,
    w_out, w_up, w_down, gain_attn, bias_attn, gain_ffn, bias_ffn,
):
    here = lax.axis_index("head").astype(jnp.int32)
    core = lax.axis_index("core").astype(jnp.int32)
    first_rows, other_rows, info = prepare(lengths, layer_input)
    first_rows = gather_rows(first_rows)
    other_rows = lax.all_gather(other_rows, "head", axis=0)

    w_groups = jnp.concatenate(
        [w.T.reshape(GROUPS, COLS, WIDTH) for w in (w_query, w_key, w_value)], axis=1
    )
    w_mine = lax.dynamic_index_in_dim(w_groups, here, 0, False)
    taps = lax.dynamic_slice_in_dim(
        jnp.concatenate([conv_query, conv_key, conv_value], axis=0), here * COLS, COLS, 1
    )
    gain_a, bias_a, gain_f, bias_f = (
        v.reshape(1, WIDTH) for v in (gain_attn, bias_attn, gain_ffn, bias_ffn)
    )
    *saved, mixed_first = attend(True, info, first_rows, w_mine, taps, gain_a, bias_a)
    mixed_first = trade(mixed_first, "head")
    *saved, mixed_others = attend(False, info, other_rows, w_mine, taps, gain_a, bias_a, saved)
    mixed_first, mixed_others = lax.optimization_barrier((mixed_first, mixed_others))
    mixed_others = trade(mixed_others, "head")
    weights = (w_out, gain_f, bias_f, w_up, w_down)
    output_a, middle_a, grad_a, *rows_a, branch_a, vectors_a = ffn(
        True, info, layer_input, cotangent, mixed_first, *weights
    )
    output_b, middle_b, grad_mixed, up, down, out, ffn_vectors = ffn(
        False, info, layer_input, cotangent, mixed_others, *weights,
        (mixed_first, branch_a, vectors_a, *rows_a, grad_a),
    )
    weight_sums = lax.psum((up, down, out), ("x", "z", "core", "head"))
    grad_mixed = trade(grad_mixed, "head")

    def attention_grads(grad_mixed, saved, grad_middle, layer_output, ffn_vectors):
        d_own, d_next, d_prev, keep, send = attend_back(
            info, grad_mixed, saved, w_mine, taps, gain_a, bias_a, ffn_vectors
        )
        behind, ahead = near_exchange(d_next, d_prev)

        part = add_low(keep, swap_cores(send)).reshape(16, PACK_ROWS // 16, WIDTH // 2)
        part = add_low(*trade(part, ("x", "z")))
        part, behind, ahead = lax.optimization_barrier((part, behind, ahead))
        over, under = far_exchange(behind, ahead, 3 * COLS)
        for axis in ("head", "z", "x"):
            if axis == "x":
                part, over, under = lax.optimization_barrier((part, over, under))
            part = trade(jnp.broadcast_to(part[None], (GROUPS, *part.shape)), axis)
        part = part.reshape(64, PACK_ROWS // 16, WIDTH // 2)
        input_grad, layer_output = input_grad_of(
            info, layer_input, grad_middle, layer_output, (d_own, behind, over, ahead, under), w_groups, gain_a
        )
        part, input_grad = lax.optimization_barrier((part, input_grad))
        grad_q, grad_k, grad_v, tails = unpack(core, part, swap_cores(part))
        conv = lambda n: jnp.transpose(tails[:, 3 * n : 3 * n + 3, 0:COLS], (1, 0, 2)).reshape(3, WIDTH)
        vector = jnp.sum(tails[:, 9:13, :], axis=0)
        return (
            layer_output, input_grad, grad_q, grad_k, grad_v, conv(0), conv(1), conv(2),
            vector[0], vector[1], vector[2], vector[3],
        )

    operands = (grad_mixed, saved, (middle_a, middle_b), (output_a, output_b), ffn_vectors)
    blank = lambda *args: jax.tree.map(
        lambda a: jnp.zeros(a.shape, a.dtype), jax.eval_shape(attention_grads, *args)
    )
    later = lax.cond(lengths[0] > 0, attention_grads, blank, *operands)
    weight_sums, later = lax.optimization_barrier((weight_sums, later))
    grad_up, grad_down, grad_out = place(*weight_sums)
    return (*later[:8], grad_out, grad_up, grad_down, *later[8:])


def solution(mesh):
    fine = Mesh(mesh.devices.reshape(4, 4, 2, GROUPS), ("x", "z", "core", "head"))
    dp = ("x", "z", "core")
    rows = P(dp, "head", None)
    return jax.shard_map(
        per_device,
        mesh=fine,
        in_specs=(rows, P(dp), rows) + (P(),) * 13,
        out_specs=(rows, rows) + (P(),) * 13,
        check_vma=False,
    )
```

```python
import functools

import jax
import jax.numpy as jnp
from jax import lax
from jax.experimental import pallas as pl
from jax.experimental.pallas import tpu as pltpu
from jax.sharding import Mesh
from jax.sharding import PartitionSpec as P

HDIM = 64
GROUPS = 4
BLOCK = 256
FULL = 1024
WIDTH = 768
COLS = 192
FF = 3072
SEQS = 3
CHUNK = 512
HEADS_HERE = 3
PACK_ROWS = 640
F32 = jnp.float32
BF16 = jnp.bfloat16
NN = (((1,), (0,)), ((), ()))
NT = (((1,), (1,)), ((), ()))
TN = (((0,), (0,)), ((), ()))


def dot(left, right, dims):
    return lax.dot_general(left, right, dims, preferred_element_type=F32)


def cost(flops, nbytes, transcendentals=0):
    return pl.CostEstimate(
        flops=int(flops), bytes_accessed=int(nbytes), transcendentals=int(transcendentals)
    )


def vmem():
    return pl.BlockSpec(memory_space=pltpu.VMEM)


def params(mib):
    return pltpu.CompilerParams(vmem_limit_bytes=mib << 20)


def unit_rows(rows):
    average = jnp.mean(rows, axis=-1, keepdims=True)
    centred = rows - average
    variance = jnp.mean(centred * centred, axis=-1, keepdims=True)
    inverse = lax.rsqrt(variance + 1e-05)
    return centred * inverse, inverse


def head_masks():
    lane = lax.broadcasted_iota(jnp.int32, (1, COLS), 1)
    return [
        jnp.where((lane >= h * HDIM) & (lane < (h + 1) * HDIM), 1.0, 0.0).astype(F32)
        for h in range(HEADS_HERE)
    ]


def conv_rows(raw_f, taps, tap_row, start):
    total = taps[tap_row : tap_row + 1, :] * raw_f[8 + start : 8 + start + BLOCK, :]
    for m in (1, 2):
        total += (
            taps[tap_row + m : tap_row + m + 1, :]
            * raw_f[8 + start - m : 8 + start - m + BLOCK, :]
        )
    return total


def order_of(lengths):
    a, b, c = lengths[0], lengths[1], lengths[2]
    first = jnp.where((a >= b) & (a >= c), 0, jnp.where(b >= c, 1, 2)).astype(jnp.int32)
    last = jnp.where((c <= a) & (c <= b), 2, jnp.where(b <= a, 1, 0)).astype(jnp.int32)
    return first, 3 - first - last, last


def prepare_kernel(lengths, row_0, row_1, row_2, out_0, out_1, out_2, info):
    for row, out in ((row_0, out_0), (row_1, out_1), (row_2, out_2)):
        out[...] = row[0]
    info[0] = lax.axis_index("head").astype(jnp.int32)
    info[1] = lax.axis_index("core").astype(jnp.int32)
    a, b, c = lengths[0], lengths[1], lengths[2]
    for n, s in enumerate(order_of(lengths)):
        info[2 + n] = jnp.where(s == 0, a, jnp.where(s == 1, b, c))
        info[5 + n] = s


def prepare(lengths, rows):
    nth = lambda n: pl.BlockSpec((1, BLOCK, WIDTH), lambda i, sc: (order_of(sc)[n], 0, 0))
    whole = lambda *shape: pl.BlockSpec(shape, lambda i, sc: (0,) * len(shape))
    return pl.pallas_call(
        prepare_kernel,
        grid_spec=pltpu.PrefetchScalarGridSpec(
            num_scalar_prefetch=1,
            grid=(1,),
            in_specs=[nth(0), nth(1), nth(2)],
            out_specs=[whole(BLOCK, WIDTH)] * SEQS + [pl.BlockSpec(memory_space=pltpu.SMEM)],
        ),
        out_shape=[jax.ShapeDtypeStruct((BLOCK, WIDTH), BF16)] * SEQS + [jax.ShapeDtypeStruct((8,), jnp.int32)],
        compiler_params=params(60),
        cost_estimate=cost(1e3, 2.4e6),
        name="prepare",
    )(lengths, rows, rows, rows)


def attend_kernel(seq, info, *refs):
    first = seq == 0
    count = 5 if first else GROUPS
    pieces, refs = refs[:count], refs[count:]
    w_mine, taps, gain, bias = refs[:4]
    refs = refs[4 + (0, 6, 7)[seq] :]
    normed, raw_q, raw_k, raw_v, mixed, lse_t, to_rows = refs[:7]
    pad_q, pad_k, pad_v, q_s, k_s, v_s, below = refs[7:]
    here = info[0]
    length = info[2 + seq]
    blocks = (length + BLOCK - 1) // BLOCK
    masks = head_masks()
    if first:
        homes = [(lax.rem(here + ahead, GROUPS), shift) for ahead, shift in ((0, 0), (1, 0), (2, 0), (2, 128), (3, 0))]
    else:
        homes = [(k, 0) for k in range(GROUPS)]

    for piece, (home, shift) in zip(pieces, homes):

        @pl.when(home < blocks)
        def _(piece=piece, home=home, shift=shift):
            rows = piece[...].reshape(piece.shape[-2], WIDTH).astype(F32)
            size = rows.shape[0]
            unit, _ = unit_rows(rows)
            low = (unit * gain[...] + bias[...]).astype(BF16)
            at = home * BLOCK + shift
            at = pl.multiple_of(at, 128) if first else at
            normed[0, pl.ds(at, size), :] = low
            for n, (raw, pad) in enumerate(((raw_q, pad_q), (raw_k, pad_k), (raw_v, pad_v))):
                value = dot(low, w_mine[n * COLS : (n + 1) * COLS, :], NT).astype(BF16)
                raw[0, pl.ds(at, size), :] = value
                pad[pl.ds(at + 8, size), :] = value.astype(F32)

    for pad in (pad_q, pad_k, pad_v):
        pad[0:8, :] = jnp.zeros((8, COLS), F32)
    row = lax.broadcasted_iota(jnp.int32, (BLOCK, BLOCK), 0)
    col = lax.broadcasted_iota(jnp.int32, (BLOCK, BLOCK), 1)
    below[...] = jnp.where(col <= row, 0.0, -1e30).astype(F32)

    for b in range(GROUPS):

        @pl.when(b < blocks)
        def _(b=b):
            at = slice(b * BLOCK, (b + 1) * BLOCK)
            q_s[at, :] = (conv_rows(pad_q, taps, 0, b * BLOCK).astype(BF16).astype(F32) * 0.125).astype(BF16)
            k_s[at, :] = conv_rows(pad_k, taps, 3, b * BLOCK).astype(BF16)
            v_s[at, :] = conv_rows(pad_v, taps, 6, b * BLOCK).astype(BF16)
            lane = lax.broadcasted_iota(jnp.int32, (BLOCK, 128), 1)
            total_out = jnp.zeros((BLOCK, COLS), F32)
            logs = jnp.zeros((BLOCK, 128), F32)
            for h in range(HEADS_HERE):
                q_h = q_s[at, :] * masks[h].astype(BF16)
                diag = dot(q_h, k_s[at, :], NT) + below[...]
                top = jnp.max(diag, axis=-1, keepdims=True)
                if b:
                    left = dot(q_h, k_s[0 : b * BLOCK, :], NT)
                    top = jnp.maximum(top, jnp.max(left, axis=-1, keepdims=True))
                    expo_left = jnp.exp(left - top)
                expo = jnp.exp(diag - top)
                total = jnp.sum(expo, axis=-1, keepdims=True)
                out = dot(expo.astype(BF16), v_s[at, :], NN)
                if b:
                    total += jnp.sum(expo_left, axis=-1, keepdims=True)
                    out += dot(expo_left.astype(BF16), v_s[0 : b * BLOCK, :], NN)
                total_out = total_out + (out * masks[h]) * (1.0 / total)
                logs = jnp.where(lane == h, top + jnp.log(total), logs)
            result = jnp.transpose(total_out).astype(BF16)
            mixed[b] = result
            to_rows[b] = result
            lse_t[0, :, at] = jnp.transpose(logs)[0:8, :]

        @pl.when(b >= blocks)
        def _(b=b):
            mixed[b] = jnp.zeros((COLS, BLOCK), BF16)
            to_rows[b] = jnp.zeros((COLS, BLOCK), BF16)


def attend(seq, info, pieces, w_mine, taps, gain, bias, earlier=()):
    whole = lambda *shape: pl.BlockSpec(shape, lambda i, sc: (0,) * len(shape))
    mine = lambda *shape: pl.BlockSpec((1, *shape), lambda i, sc: (seq,) + (0,) * len(shape))
    heads = lambda n: pl.BlockSpec((GROUPS, COLS, BLOCK), lambda i, sc: (0, n, 0))
    if seq == 0:
        piece_specs = [whole(*p.shape) for p in pieces]
    else:
        piece_specs = [pl.BlockSpec((BLOCK, WIDTH), lambda i, sc, k=k: (k, 0)) for k in range(GROUPS)]
        pieces = [pieces] * GROUPS
    full = lambda dtype, *shape: jax.ShapeDtypeStruct((SEQS, *shape), dtype)
    return pl.pallas_call(
        functools.partial(attend_kernel, seq),
        grid_spec=pltpu.PrefetchScalarGridSpec(
            num_scalar_prefetch=1,
            grid=(1,),
            in_specs=piece_specs
            + [whole(3 * COLS, WIDTH), whole(9, COLS), whole(1, WIDTH), whole(1, WIDTH)]
            + [pl.BlockSpec(memory_space=pl.ANY)] * len(earlier),
            out_specs=[mine(FULL, WIDTH)]
            + [mine(FULL, COLS)] * 3
            + [heads(seq), mine(8, FULL), heads(max(seq - 1, 0))],
            scratch_shapes=[pltpu.VMEM((FULL + 8, COLS), F32)] * 3
            + [pltpu.VMEM((FULL, COLS), BF16)] * 3
            + [pltpu.VMEM((BLOCK, BLOCK), F32)],
        ),
        out_shape=(
            full(BF16, FULL, WIDTH),
            full(BF16, FULL, COLS), full(BF16, FULL, COLS), full(BF16, FULL, COLS),
            jax.ShapeDtypeStruct((GROUPS, SEQS * COLS, BLOCK), BF16),
            full(F32, 8, FULL),
            jax.ShapeDtypeStruct((GROUPS, (SEQS - 1 if seq else 1) * COLS, BLOCK), BF16),
        ),
        input_output_aliases={1 + len(pieces) + 4 + n: n for n in range(len(earlier))},
        compiler_params=params(60),
        cost_estimate=cost(3e9, 8e6, 2e6),
        name="attend",
    )(info, *pieces, w_mine, taps, gain, bias, *earlier)


def attend_back_kernel(
    info, g_s, normed, raw_q, raw_k, raw_v, mixed, lse_t,
    w_mine, taps, gain, bias, ffn_vectors,
    d_own, d_next, d_prev, keep, send,
    dw_out, small_out, d_all, pack,
    pad_q, pad_k, pad_v, q_s, k_s, v_s, dq_s, dk_s, dv_s, below, p_all, ds_all,
):
    step = pl.program_id(0)
    here, core, length = info[0], info[1], info[2 + step]

    blocks = (length + BLOCK - 1) // BLOCK
    masks = head_masks()

    row = lax.broadcasted_iota(jnp.int32, (BLOCK, BLOCK), 0)
    col = lax.broadcasted_iota(jnp.int32, (BLOCK, BLOCK), 1)
    below[...] = jnp.where(row <= col, 0.0, -1e30).astype(F32)
    for pad, raw in ((pad_q, raw_q), (pad_k, raw_k), (pad_v, raw_v)):
        pad[0:8, :] = jnp.zeros((8, COLS), F32)
    for total in (dq_s, dk_s, dv_s):
        total[...] = jnp.zeros((FULL + 8, COLS), F32)

    for b in range(GROUPS):

        @pl.when(b < blocks)
        def _(b=b):
            at = slice(b * BLOCK, (b + 1) * BLOCK)
            for pad, raw in ((pad_q, raw_q), (pad_k, raw_k), (pad_v, raw_v)):
                pad[8 + b * BLOCK : 8 + (b + 1) * BLOCK, :] = raw[0, at, :].astype(F32)
            q_s[at, :] = (conv_rows(pad_q, taps, 0, b * BLOCK).astype(BF16).astype(F32) * 0.125).astype(BF16)
            k_s[at, :] = conv_rows(pad_k, taps, 3, b * BLOCK).astype(BF16)
            v_s[at, :] = conv_rows(pad_v, taps, 6, b * BLOCK).astype(BF16)
            both = g_s[b].astype(F32) * mixed[b].astype(F32)
            reach = slice(0, (b + 1) * BLOCK)
            dq_total = jnp.zeros((BLOCK, COLS), F32)
            q_heads, g_heads = [], []
            for h in range(HEADS_HERE):
                lanes = slice(h * BLOCK, (h + 1) * BLOCK)
                q_h = q_s[at, :] * masks[h].astype(BF16)
                own = slice(h * HDIM, (h + 1) * HDIM)
                blank = lambda n: [jnp.zeros((n * HDIM, BLOCK), BF16)] if n else []
                g_h = jnp.concatenate(blank(h) + [g_s[b, own, :]] + blank(HEADS_HERE - 1 - h), axis=0)
                q_heads.append(q_h)
                g_heads.append(g_h)
                row_dot = jnp.sum(both[own, :], axis=0, keepdims=True)
                log_row = lse_t[0, h : h + 1, at]
                for j in range(b + 1):
                    keys = slice(j * BLOCK, (j + 1) * BLOCK)
                    scores = dot(k_s[keys, :], q_h, NT)
                    if j == b:
                        scores = scores + below[...]
                    probs = jnp.exp(scores - log_row)
                    grad_probs = dot(v_s[keys, :], g_h, NN)
                    p_all[keys, lanes] = probs.astype(BF16)
                    ds_all[keys, lanes] = (probs * (grad_probs - row_dot)).astype(BF16)
                dq_total += dot(ds_all[reach, lanes], k_s[reach, :], TN) * masks[h]
            dq_s[at, :] = dq_total * 0.125
            dv_s[reach, :] += dot(p_all[reach, :], jnp.concatenate(g_heads, axis=1), NT)
            dk_s[reach, :] += dot(ds_all[reach, :], jnp.concatenate(q_heads, axis=0), NN)

    @pl.when(step == 0)
    def _():
        dw_out[...] = jnp.zeros_like(dw_out)
        small_out[...] = jnp.zeros_like(small_out)

    for b in range(GROUPS):

        @pl.when(b < blocks)
        def _(b=b):
            start = b * BLOCK
            at = slice(start, start + BLOCK)
            for n, (pad, grad) in enumerate(((pad_q, dq_s), (pad_k, dk_s), (pad_v, dv_s))):
                now = grad[at, :]
                value = taps[3 * n : 3 * n + 1, :] * now
                for m in (1, 2):
                    value += taps[3 * n + m : 3 * n + m + 1, :] * grad[start + m : start + m + BLOCK, :]
                value = value.astype(BF16).astype(F32)
                d_all[b, n * COLS : (n + 1) * COLS, :] = jnp.transpose(value).astype(BF16)
                small_out[9 + n : 10 + n, 0:COLS] += jnp.sum(value, axis=0, keepdims=True)
                for m in range(3):
                    shifted = pad[8 + start - m : 8 + start - m + BLOCK, :]
                    small_out[3 * n + m : 3 * n + m + 1, 0:COLS] += jnp.sum(
                        shifted * now, axis=0, keepdims=True
                    )
            dw_out[...] += dot(d_all[b], normed[0, at, :], NN)

        @pl.when(b >= blocks)
        def _(b=b):
            d_all[b] = jnp.zeros((3 * COLS, BLOCK), BF16)

    far = lax.rem(here + 2, GROUPS)
    d_own[0] = d_all[here]
    d_next[0, 0 : 3 * COLS, :] = d_all[lax.rem(here + 1, GROUPS)]
    d_next[0, 3 * COLS :, :] = d_all[far, 0 : 3 * COLS // 2, :]
    d_prev[0, 0 : 3 * COLS, :] = d_all[lax.rem(here + 3, GROUPS)]
    d_prev[0, 3 * COLS :, :] = d_all[far, 3 * COLS // 2 :, :]

    @pl.when(step == SEQS - 1)
    def _():
        grad_bias = jnp.zeros((1, WIDTH), F32)
        for n in range(3):
            sums = small_out[9 + n : 10 + n, 0:COLS]
            high = sums.astype(BF16)
            rest = (sums - high.astype(F32)).astype(BF16)
            for term in (high, rest):
                wide = jnp.broadcast_to(term.astype(F32), (16, COLS)).astype(BF16)
                grad_bias += dot(wide, w_mine[n * COLS : (n + 1) * COLS, :], NN)[0:1, :]
        grad_normed = jnp.sum(w_mine[...].astype(F32) * dw_out[...], axis=0, keepdims=True)
        grad_gain = (grad_normed - bias[...] * grad_bias) / gain[...]
        pack[0 : 3 * COLS, :] = dw_out[...].astype(BF16)
        tail = jnp.concatenate(
            [
                small_out[0:9, :],
                grad_gain,
                grad_bias,
                ffn_vectors[0:2, :],
                jnp.zeros((3, WIDTH), F32),
            ],
            axis=0,
        )
        pack[3 * COLS : 3 * COLS + 16, :] = tail.astype(BF16)
        pack[3 * COLS + 16 :, :] = jnp.zeros((PACK_ROWS - 3 * COLS - 16, WIDTH), BF16)
        half = WIDTH // 2
        keep[...] = pack[:, pl.ds(pl.multiple_of(core * half, 128), half)]
        send[...] = pack[:, pl.ds(pl.multiple_of((1 - core) * half, 128), half)]


def attend_back(info, grad_mixed, saved, w_mine, taps, gain, bias, ffn_vectors):
    low = lambda *shape: jax.ShapeDtypeStruct(shape, BF16)
    whole = lambda *shape: pl.BlockSpec(shape, lambda i, sc: (0,) * len(shape))
    mine = lambda *shape: pl.BlockSpec((1, *shape), lambda i, sc: (i,) + (0,) * len(shape))
    across = pl.BlockSpec((GROUPS, COLS, BLOCK), lambda i, sc: (0, i, 0))
    long_rows = 3 * COLS * 3 // 2
    return pl.pallas_call(
        attend_back_kernel,
        grid_spec=pltpu.PrefetchScalarGridSpec(
            num_scalar_prefetch=1,
            grid=(SEQS,),
            in_specs=[
                pl.BlockSpec((GROUPS, COLS, BLOCK), lambda i, sc: (0, lax.rem(i + 2, SEQS), 0)),
                mine(FULL, WIDTH),
            ]
            + [mine(FULL, COLS)] * 3
            + [across, mine(8, FULL)]
            + [whole(3 * COLS, WIDTH), whole(9, COLS), whole(1, WIDTH), whole(1, WIDTH), whole(8, WIDTH)],
            out_specs=[mine(3 * COLS, BLOCK), mine(long_rows, BLOCK), mine(long_rows, BLOCK)]
            + [whole(PACK_ROWS, WIDTH // 2)] * 2,
            scratch_shapes=[
                pltpu.VMEM((3 * COLS, WIDTH), F32),
                pltpu.VMEM((16, WIDTH), F32),
                pltpu.VMEM((GROUPS, 3 * COLS, BLOCK), BF16),
                pltpu.VMEM((PACK_ROWS, WIDTH), BF16),
            ]
            + [pltpu.VMEM((FULL + 8, COLS), F32)] * 3
            + [pltpu.VMEM((FULL, COLS), BF16)] * 3
            + [pltpu.VMEM((FULL + 8, COLS), F32)] * 3
            + [pltpu.VMEM((BLOCK, BLOCK), F32)]
            + [pltpu.VMEM((FULL, HEADS_HERE * BLOCK), BF16)] * 2,
        ),
        out_shape=(
            low(SEQS, 3 * COLS, BLOCK), low(SEQS, long_rows, BLOCK), low(SEQS, long_rows, BLOCK),
            low(PACK_ROWS, WIDTH // 2), low(PACK_ROWS, WIDTH // 2),
        ),
        compiler_params=params(60),
        cost_estimate=cost(1e10, 2e7),
        name="attend_back",
    )(info, grad_mixed, *saved, w_mine, taps, gain, bias, ffn_vectors)


def heads_of(source, s):
    return jnp.concatenate([source[k, s * COLS : (s + 1) * COLS, :] for k in range(GROUPS)], axis=0)


def ffn_kernel(first, info, *refs):
    count = 1 if first else SEQS - 1
    base = 0 if first else 1
    x, cotangent, refs = refs[:count], refs[count : 2 * count], refs[2 * count :]
    mixed, w_out, gain, bias, w_up, w_down = refs[:6]
    refs = refs[6:]
    steps = FF // CHUNK
    if first:
        layer_output, grad_middle, grad_mixed, sq_out, gh_out, normed_of, low_of, branch, vectors = refs[:9]
        middle, total_out, total_grad = refs[9:]
        places = [slice(0, BLOCK)]
    else:
        mixed_first, branch_first, vectors_first, sq_first, gh_first, normed_first, low_first = refs[:7]
        layer_output, grad_middle, grad_mixed, grad_up, grad_down, grad_out, vectors = refs[8:15]
        middle, total_out, total_grad, normed_of, low_of, sq_all, gh_all, dw_out = refs[15:]
        places = [slice((s + 1) * BLOCK, (s + 2) * BLOCK) for s in range(count)]
    parts = [slice(s * BLOCK, (s + 1) * BLOCK) for s in range(count)]
    step = pl.program_id(0)
    position = info[0] * BLOCK + lax.broadcasted_iota(jnp.int32, (BLOCK, 1), 0)

    @pl.when(step == 0)
    def _():
        for s, (at, to) in enumerate(zip(parts, places)):
            value = x[s][0].astype(F32) + dot(heads_of(mixed, s), w_out[...], TN)
            middle[at, :] = value
            unit, _ = unit_rows(value)
            normed_of[to, :] = (unit * gain[...] + bias[...]).astype(BF16)
            keep_row = position < info[2 + base + s]
            low_of[to, :] = jnp.where(keep_row, cotangent[s][0].astype(F32), 0.0).astype(BF16)
            total_out[at, :] = jnp.zeros((BLOCK, WIDTH), F32)
            total_grad[at, :] = jnp.zeros((BLOCK, WIDTH), F32)
        if not first:
            normed_of[0:BLOCK, :] = normed_first[...]
            low_of[0:BLOCK, :] = low_first[...]

    def rows_of_chunk(put):
        for at, to in zip(parts, places):
            hidden = jnp.maximum(dot(normed_of[to, :], w_up[...], NN), 0.0)
            squared = (hidden * hidden).astype(BF16)
            back = dot(low_of[to, :], w_down[...], NT)
            grad_hidden = (back * 2.0 * hidden).astype(BF16)
            put(to, squared, grad_hidden)
            total_out[at, :] += dot(squared, w_down[...], NN)
            total_grad[at, :] += dot(grad_hidden, w_up[...], NT)

    def finish(s):
        at, to = parts[s], places[s]
        keep_row = position < info[2 + base + s]
        layer_output[s] = jnp.where(keep_row, middle[at, :] + total_out[at, :], 0.0).astype(BF16)
        unit, inverse = unit_rows(middle[at, :])
        grad_normed = total_grad[at, :]
        scaled = grad_normed * gain[...]
        mean_grad = jnp.mean(scaled, axis=-1, keepdims=True)
        mean_dot = jnp.mean(scaled * unit, axis=-1, keepdims=True)
        value = low_of[to, :].astype(F32) + inverse * (scaled - mean_grad - unit * mean_dot)
        vectors[0:1, :] += jnp.sum(grad_normed * unit, axis=0, keepdims=True)
        vectors[1:2, :] += jnp.sum(grad_normed, axis=0, keepdims=True)
        grad_middle[s] = value
        low = value.astype(BF16)
        heads_grad = dot(w_out[...], low, NT).astype(BF16)
        for k in range(GROUPS):
            grad_mixed[k, s * COLS : (s + 1) * COLS, :] = heads_grad[k * COLS : (k + 1) * COLS]
        return low

    if first:

        def put(to, squared, grad_hidden):
            sq_out[to, :] = squared
            gh_out[to, :] = grad_hidden

        rows_of_chunk(put)

        @pl.when(step == steps - 1)
        def _():
            vectors[...] = jnp.zeros_like(vectors)
            branch[...] = finish(0)

        return

    @pl.when(step < steps)
    def _():
        def put(to, squared, grad_hidden):
            sq_all[step, to, :] = squared
            gh_all[step, to, :] = grad_hidden

        rows_of_chunk(put)
        sq_all[step, 0:BLOCK, :] = sq_first[...]
        gh_all[step, 0:BLOCK, :] = gh_first[...]

    def weights_of_chunk(n):
        grad_up[...] = dot(gh_all[n], normed_of[...], TN).astype(BF16)
        grad_down[...] = dot(sq_all[n], low_of[...], TN).astype(BF16)

    @pl.when(step == steps)
    def _():
        vectors[...] = vectors_first[...]
        weights_of_chunk(0)
        low = finish(0)
        dw_out[...] = dot(heads_of(mixed_first, 0), branch_first[...], NN) + dot(heads_of(mixed, 0), low, NN)

    @pl.when(step == steps + 1)
    def _():
        weights_of_chunk(1)
        low = finish(1)
        dw_out[...] += dot(heads_of(mixed, 1), low, NN)

    @pl.when(step >= steps + 2)
    def _():
        weights_of_chunk(step - steps)
        grad_out[...] = dw_out[...].astype(BF16)


def ffn(first, info, x, cotangent, mixed, w_out, gain, bias, w_up, w_down, earlier=()):
    count = 1 if first else SEQS - 1
    base = 0 if first else 1
    low = lambda *shape: jax.ShapeDtypeStruct(shape, BF16)
    full = lambda *shape: jax.ShapeDtypeStruct(shape, F32)
    rows = count * BLOCK
    all_rows = SEQS * BLOCK
    steps = FF // CHUNK
    whole = lambda *shape: pl.BlockSpec(shape, lambda i, sc: (0,) * len(shape))
    nth = lambda s: pl.BlockSpec((1, BLOCK, WIDTH), lambda i, sc: (sc[5 + base + s], 0, 0))
    early = lambda i: jnp.minimum(i, steps - 1)
    late = lambda i: jnp.maximum(i - steps, 0)
    across = lambda n: pl.BlockSpec((n, CHUNK), lambda i, sc: (0, early(i)))
    grads = pl.BlockSpec((GROUPS, count * COLS, BLOCK), lambda i, sc: (0, SEQS - 1 if first else 0, 0))
    scratch = [pltpu.VMEM((rows, WIDTH), F32)] * 3
    if first:
        extra_specs = []
        out_specs = [across(rows)] * 2 + [whole(rows, WIDTH)] * 3 + [whole(8, WIDTH)]
        out_shape = [low(rows, FF)] * 2 + [low(rows, WIDTH)] * 3 + [full(8, WIDTH)]
        aliases = {}
    else:
        extra_specs = (
            [whole(GROUPS, COLS, BLOCK), whole(BLOCK, WIDTH), whole(8, WIDTH)]
            + [across(BLOCK)] * 2
            + [whole(BLOCK, WIDTH)] * 2
            + [pl.BlockSpec(memory_space=pl.ANY)]
        )
        out_specs = [
            pl.BlockSpec((CHUNK, WIDTH), lambda i, sc: (late(i), 0)),
            pl.BlockSpec((CHUNK, WIDTH), lambda i, sc: (late(i), 0)),
            whole(WIDTH, WIDTH),
            whole(8, WIDTH),
        ]
        out_shape = [low(FF, WIDTH), low(FF, WIDTH), low(WIDTH, WIDTH), full(8, WIDTH)]
        scratch += (
            [pltpu.VMEM((all_rows, WIDTH), BF16)] * 2
            + [pltpu.VMEM((steps, all_rows, CHUNK), BF16)] * 2
            + [pltpu.VMEM((WIDTH, WIDTH), F32)]
        )
        aliases = {1 + 2 * count + 6 + 7: 2}
    return pl.pallas_call(
        functools.partial(ffn_kernel, first),
        grid_spec=pltpu.PrefetchScalarGridSpec(
            num_scalar_prefetch=1,
            grid=(steps if first else 2 * steps,),
            in_specs=[nth(s) for s in range(count)] * 2
            + [
                whole(GROUPS, count * COLS, BLOCK), whole(WIDTH, WIDTH), whole(1, WIDTH), whole(1, WIDTH),
                across(WIDTH),
                pl.BlockSpec((CHUNK, WIDTH), lambda i, sc: (early(i), 0)),
            ]
            + extra_specs,
            out_specs=[whole(count, BLOCK, WIDTH), whole(count, BLOCK, WIDTH), grads] + out_specs,
            scratch_shapes=scratch,
        ),
        out_shape=[low(count, BLOCK, WIDTH), full(count, BLOCK, WIDTH), low(GROUPS, SEQS * COLS, BLOCK)] + out_shape,
        input_output_aliases=aliases,
        compiler_params=params(60),
        cost_estimate=cost(7e9 if first else 2.2e10, 2e7),
        name="ffn",
    )(info, *[x] * count, *[cotangent] * count, mixed, w_out, gain, bias, w_up, w_down, *earlier)


def input_kernel(
    info, x, middle_first, middle_others, output_first, output_others, own, behind, over, ahead, under, w_groups, gain,
    out, layer_output, grad_middle,
):
    @pl.when(pl.program_id(0) == 0)
    def _():
        grad_middle[...] = middle_first[0]
        layer_output[...] = output_first[...]

    @pl.when(pl.program_id(0) > 0)
    def _():
        grad_middle[...] = middle_others[0]
        layer_output[...] = output_others[...]

    here = info[0]
    w_of = lambda k: w_groups[lax.rem(here + k, GROUPS)]
    unit, inverse = unit_rows(x[0].astype(F32))
    grad_normed = dot(own[0], w_of(0), TN)
    grad_normed += dot(ahead[0], w_of(1), TN)
    grad_normed += dot(jnp.concatenate([over[0], under[0]], axis=0), w_of(2), TN)
    grad_normed += dot(behind[0], w_of(3), TN)
    scaled = grad_normed * gain[...]
    mean_grad = jnp.mean(scaled, axis=-1, keepdims=True)
    mean_dot = jnp.mean(scaled * unit, axis=-1, keepdims=True)
    out[0] = grad_middle[...] + inverse * (scaled - mean_grad - unit * mean_dot)


def input_grad_of(info, x, grad_middle, layer_output, pieces, w_groups, gain):
    mine = lambda rows, lanes: pl.BlockSpec((1, rows, lanes), lambda i, sc: (i, 0, 0))
    whole = lambda *shape: pl.BlockSpec(shape, lambda i, sc: (0,) * len(shape))
    placed = pl.BlockSpec((1, BLOCK, WIDTH), lambda i, sc: (sc[5 + i], 0, 0))
    two = [whole(1, BLOCK, WIDTH), pl.BlockSpec((1, BLOCK, WIDTH), lambda i, sc: (jnp.maximum(i - 1, 0), 0, 0))]
    piece = mine(3 * COLS, BLOCK)
    half = mine(3 * COLS // 2, BLOCK)
    return pl.pallas_call(
        input_kernel,
        grid_spec=pltpu.PrefetchScalarGridSpec(
            num_scalar_prefetch=1,
            grid=(SEQS,),
            in_specs=[placed, *two, *two, piece, piece, half, piece, half, whole(*w_groups.shape), whole(1, WIDTH)],
            out_specs=[placed, placed],
            scratch_shapes=[pltpu.VMEM((BLOCK, WIDTH), F32)],
        ),
        out_shape=(
            jax.ShapeDtypeStruct((SEQS, BLOCK, WIDTH), F32),
            jax.ShapeDtypeStruct((SEQS, BLOCK, WIDTH), BF16),
        ),
        compiler_params=params(60),
        cost_estimate=cost(3e9, 1.5e7),
        name="input_grad",
    )(info, x, *grad_middle, *layer_output, *pieces, w_groups, gain)


def place_kernel(up, down, out, grad_up, grad_down, grad_out):
    grad_up[...] = jnp.transpose(up[...].astype(F32))
    grad_down[...] = down[...].astype(F32)
    grad_out[...] = out[...].astype(F32)


def place(up, down, out):
    steps = FF // CHUNK
    rows = lambda n: pl.BlockSpec((n, WIDTH), lambda i: (i, 0))
    specs = [rows(CHUNK), rows(CHUNK), rows(WIDTH // steps)]
    return pl.pallas_call(
        place_kernel,
        grid=(steps,),
        in_specs=specs,
        out_specs=[pl.BlockSpec((WIDTH, CHUNK), lambda i: (0, i))] + specs[1:],
        out_shape=[jax.ShapeDtypeStruct(shape, F32) for shape in ((WIDTH, FF), down.shape, out.shape)],
        compiler_params=params(60),
        cost_estimate=cost(1e6, 3.2e7),
        name="place",
    )(up, down, out)


def unpack_kernel(info, own, other, grad_q, grad_k, grad_v, tails, rows):
    size = PACK_ROWS // 16
    half = WIDTH // 2

    def fill(pieces, base):
        for y in range(GROUPS):
            for n in range(16):
                rows[y, n * size : (n + 1) * size, base : base + half] = pieces[n * GROUPS + y].astype(F32)

    @pl.when(info[0] == 0)
    def _():
        fill(own, 0)
        fill(other, half)

    @pl.when(info[0] != 0)
    def _():
        fill(other, 0)
        fill(own, half)

    for n, grad in enumerate((grad_q, grad_k, grad_v)):
        part = jnp.concatenate([rows[y, n * COLS : (n + 1) * COLS, :] for y in range(GROUPS)], axis=0)
        grad[...] = jnp.transpose(part)
    for y in range(GROUPS):
        tails[y] = rows[y, 3 * COLS : 3 * COLS + 16, :]


def unpack(core, own, other):
    full = lambda *shape: jax.ShapeDtypeStruct(shape, F32)
    return pl.pallas_call(
        unpack_kernel,
        in_specs=[pl.BlockSpec(memory_space=pltpu.SMEM), vmem(), vmem()],
        out_specs=[vmem()] * 4,
        out_shape=(full(WIDTH, WIDTH), full(WIDTH, WIDTH), full(WIDTH, WIDTH), full(GROUPS, 16, WIDTH)),
        scratch_shapes=[pltpu.VMEM((GROUPS, PACK_ROWS, WIDTH), F32)],
        compiler_params=params(60),
        cost_estimate=cost(1e6, 1e5),
        name="unpack",
    )(core.reshape(1), own, other)


def shift(array, axis, by):
    return lax.ppermute(array, axis, [(i, (i + by) % GROUPS) for i in range(GROUPS)])


def gather_rows(rows):
    ahead = shift(rows, "head", -1)
    behind = shift(rows, "head", 1)
    over_lo = shift(ahead[:128], "head", -1)
    over_hi = shift(behind[128:], "head", 1)
    return rows, ahead, over_lo, over_hi, behind


def near_exchange(to_next, to_prev):
    return shift(to_next, "head", 1), shift(to_prev, "head", -1)


def far_exchange(from_prev, from_next, size):
    return shift(from_prev[:, size:], "head", 1), shift(from_next[:, size:], "head", -1)


def trade(array, axes):
    return lax.all_to_all(array, axes, 0, 0, tiled=True)


def swap_cores(array):
    return lax.ppermute(array, "core", [(0, 1), (1, 0)])


def add_low(*terms):
    total = terms[0].astype(F32)
    for term in terms[1:]:
        total = total + term.astype(F32)
    return total.astype(BF16)


def per_device(
    layer_input, lengths, cotangent, w_query, w_key, w_value, conv_query, conv_key, conv_value,
    w_out, w_up, w_down, gain_attn, bias_attn, gain_ffn, bias_ffn,
):
    here = lax.axis_index("head").astype(jnp.int32)
    core = lax.axis_index("core").astype(jnp.int32)
    first_rows, middle_rows, last_rows, info = prepare(lengths, layer_input)
    own, ahead, over_lo, over_hi, behind = gather_rows(first_rows)
    middle_rows = lax.all_gather(middle_rows, "head", axis=0, tiled=True)
    ahead, behind, last_rows = lax.optimization_barrier((ahead, behind, last_rows))
    first_rows = own, ahead, over_lo, over_hi, behind
    last_rows = lax.all_gather(last_rows, "head", axis=0, tiled=True)

    w_groups = jnp.concatenate(
        [w.T.reshape(GROUPS, COLS, WIDTH) for w in (w_query, w_key, w_value)], axis=1
    )
    w_mine = lax.dynamic_index_in_dim(w_groups, here, 0, False)
    taps = lax.dynamic_slice_in_dim(
        jnp.concatenate([conv_query, conv_key, conv_value], axis=0), here * COLS, COLS, 1
    )
    gain_a, bias_a, gain_f, bias_f = (
        v.reshape(1, WIDTH) for v in (gain_attn, bias_attn, gain_ffn, bias_ffn)
    )
    *saved, mixed_first = attend(0, info, first_rows, w_mine, taps, gain_a, bias_a)
    mixed_first = trade(mixed_first, "head")
    *saved, mixed_others = attend(1, info, middle_rows, w_mine, taps, gain_a, bias_a, saved)
    *saved, mixed_others = attend(2, info, last_rows, w_mine, taps, gain_a, bias_a, (*saved, mixed_others))
    mixed_first, mixed_others = lax.optimization_barrier((mixed_first, mixed_others))
    mixed_others = trade(mixed_others, "head")
    weights = (w_out, gain_f, bias_f, w_up, w_down)
    output_a, middle_a, grad_a, *rows_a, branch_a, vectors_a = ffn(
        True, info, layer_input, cotangent, mixed_first, *weights
    )
    output_b, middle_b, grad_mixed, up, down, out, ffn_vectors = ffn(
        False, info, layer_input, cotangent, mixed_others, *weights,
        (mixed_first, branch_a, vectors_a, *rows_a, grad_a),
    )
    weight_sums = lax.psum((up, down, out), ("x", "z", "core", "head"))
    grad_mixed = trade(grad_mixed, "head")

    def attention_grads(grad_mixed, saved, grad_middle, layer_output, ffn_vectors):
        d_own, d_next, d_prev, keep, send = attend_back(
            info, grad_mixed, saved, w_mine, taps, gain_a, bias_a, ffn_vectors
        )
        behind, ahead = near_exchange(d_next, d_prev)

        part = add_low(keep, swap_cores(send)).reshape(16, PACK_ROWS // 16, WIDTH // 2)
        part = add_low(*trade(part, ("x", "z")))
        part, behind, ahead = lax.optimization_barrier((part, behind, ahead))
        over, under = far_exchange(behind, ahead, 3 * COLS)
        for axis in ("head", "z", "x"):
            if axis == "x":
                part, over, under = lax.optimization_barrier((part, over, under))
            part = trade(jnp.broadcast_to(part[None], (GROUPS, *part.shape)), axis)
        part = part.reshape(64, PACK_ROWS // 16, WIDTH // 2)
        input_grad, layer_output = input_grad_of(
            info, layer_input, grad_middle, layer_output, (d_own, behind, over, ahead, under), w_groups, gain_a
        )
        part, input_grad = lax.optimization_barrier((part, input_grad))
        grad_q, grad_k, grad_v, tails = unpack(core, part, swap_cores(part))
        conv = lambda n: jnp.transpose(tails[:, 3 * n : 3 * n + 3, 0:COLS], (1, 0, 2)).reshape(3, WIDTH)
        vector = jnp.sum(tails[:, 9:13, :], axis=0)
        return (
            layer_output, input_grad, grad_q, grad_k, grad_v, conv(0), conv(1), conv(2),
            vector[0], vector[1], vector[2], vector[3],
        )

    operands = (grad_mixed, saved, (middle_a, middle_b), (output_a, output_b), ffn_vectors)
    blank = lambda *args: jax.tree.map(
        lambda a: jnp.zeros(a.shape, a.dtype), jax.eval_shape(attention_grads, *args)
    )
    later = lax.cond(lengths[0] > 0, attention_grads, blank, *operands)
    weight_sums, later = lax.optimization_barrier((weight_sums, later))
    grad_up, grad_down, grad_out = place(*weight_sums)
    return (*later[:8], grad_out, grad_up, grad_down, *later[8:])


def solution(mesh):
    fine = Mesh(mesh.devices.reshape(4, 4, 2, GROUPS), ("x", "z", "core", "head"))
    dp = ("x", "z", "core")
    rows = P(dp, "head", None)
    return jax.shard_map(
        per_device,
        mesh=fine,
        in_specs=(rows, P(dp), rows) + (P(),) * 13,
        out_specs=(rows, rows) + (P(),) * 13,
        check_vma=False,
    )
```

```python
import functools

import jax
import jax.numpy as jnp
from jax import lax
from jax.experimental import pallas as pl
from jax.experimental.pallas import tpu as pltpu
from jax.sharding import Mesh
from jax.sharding import PartitionSpec as P

HDIM = 64
GROUPS = 4
BLOCK = 256
FULL = 1024
WIDTH = 768
COLS = 192
FF = 3072
SEQS = 3
CHUNK = 768
PLACE = 512
HEADS_HERE = 3
PACK_ROWS = 640
F32 = jnp.float32
BF16 = jnp.bfloat16
NN = (((1,), (0,)), ((), ()))
NT = (((1,), (1,)), ((), ()))
TN = (((0,), (0,)), ((), ()))


def dot(left, right, dims):
    return lax.dot_general(left, right, dims, preferred_element_type=F32)


def cost(flops, nbytes, transcendentals=0):
    return pl.CostEstimate(
        flops=int(flops), bytes_accessed=int(nbytes), transcendentals=int(transcendentals)
    )


def vmem():
    return pl.BlockSpec(memory_space=pltpu.VMEM)


def params(mib):
    return pltpu.CompilerParams(vmem_limit_bytes=mib << 20)


def unit_rows(rows):
    average = jnp.mean(rows, axis=-1, keepdims=True)
    centred = rows - average
    variance = jnp.mean(centred * centred, axis=-1, keepdims=True)
    inverse = lax.rsqrt(variance + 1e-05)
    return centred * inverse, inverse


def head_masks():
    lane = lax.broadcasted_iota(jnp.int32, (1, COLS), 1)
    return [
        jnp.where((lane >= h * HDIM) & (lane < (h + 1) * HDIM), 1.0, 0.0).astype(F32)
        for h in range(HEADS_HERE)
    ]


def conv_rows(raw_f, taps, tap_row, start):
    total = taps[tap_row : tap_row + 1, :] * raw_f[8 + start : 8 + start + BLOCK, :]
    for m in (1, 2):
        total += (
            taps[tap_row + m : tap_row + m + 1, :]
            * raw_f[8 + start - m : 8 + start - m + BLOCK, :]
        )
    return total


def order_of(lengths):
    a, b, c = lengths[0], lengths[1], lengths[2]
    first = jnp.where((a >= b) & (a >= c), 0, jnp.where(b >= c, 1, 2)).astype(jnp.int32)
    second = jnp.where(first == 0, 1, 0).astype(jnp.int32)
    third = jnp.where(first == 2, 1, 2).astype(jnp.int32)
    return first, second, third


def prepare_kernel(lengths, row_0, row_1, row_2, first_rows, other_rows, info):
    first_rows[...] = row_0[0]
    other_rows[0] = row_1[0]
    other_rows[1] = row_2[0]
    info[0] = lax.axis_index("head").astype(jnp.int32)
    info[1] = lax.axis_index("core").astype(jnp.int32)
    a, b, c = lengths[0], lengths[1], lengths[2]
    for n, s in enumerate(order_of(lengths)):
        info[2 + n] = jnp.where(s == 0, a, jnp.where(s == 1, b, c))
        info[5 + n] = s


def prepare(lengths, rows):
    nth = lambda n: pl.BlockSpec((1, BLOCK, WIDTH), lambda i, sc: (order_of(sc)[n], 0, 0))
    whole = lambda *shape: pl.BlockSpec(shape, lambda i, sc: (0,) * len(shape))
    return pl.pallas_call(
        prepare_kernel,
        grid_spec=pltpu.PrefetchScalarGridSpec(
            num_scalar_prefetch=1,
            grid=(1,),
            in_specs=[nth(0), nth(1), nth(2)],
            out_specs=[
                whole(BLOCK, WIDTH), whole(SEQS - 1, BLOCK, WIDTH), pl.BlockSpec(memory_space=pltpu.SMEM)
            ],
        ),
        out_shape=(
            jax.ShapeDtypeStruct((BLOCK, WIDTH), BF16),
            jax.ShapeDtypeStruct((SEQS - 1, BLOCK, WIDTH), BF16),
            jax.ShapeDtypeStruct((8,), jnp.int32),
        ),
        compiler_params=params(60),
        cost_estimate=cost(1e3, 2.4e6),
        name="prepare",
    )(lengths, rows, rows, rows)


def attend_kernel(first, info, *refs):
    count = 5 if first else GROUPS
    pieces, refs = refs[:count], refs[count:]
    w_mine, taps, gain, bias = refs[:4]
    refs = refs[4:] if first else refs[10:]
    normed, raw_q, raw_k, raw_v, mixed, lse_t, to_rows = refs[:7]
    pad_q, pad_k, pad_v, q_s, k_s, v_s, below = refs[7:]
    here = info[0]
    length = info[2] if first else info[3 + pl.program_id(0)]
    blocks = (length + BLOCK - 1) // BLOCK
    masks = head_masks()
    if first:
        homes = [(lax.rem(here + ahead, GROUPS), shift) for ahead, shift in ((0, 0), (1, 0), (2, 0), (2, 128), (3, 0))]
    else:
        homes = [(k, 0) for k in range(GROUPS)]

    for piece, (home, shift) in zip(pieces, homes):

        @pl.when(home < blocks)
        def _(piece=piece, home=home, shift=shift):
            rows = piece[...].reshape(piece.shape[-2], WIDTH).astype(F32)
            size = rows.shape[0]
            unit, _ = unit_rows(rows)
            low = (unit * gain[...] + bias[...]).astype(BF16)
            at = home * BLOCK + shift
            at = pl.multiple_of(at, 128) if first else at
            normed[0, pl.ds(at, size), :] = low
            for n, (raw, pad) in enumerate(((raw_q, pad_q), (raw_k, pad_k), (raw_v, pad_v))):
                value = dot(low, w_mine[n * COLS : (n + 1) * COLS, :], NT).astype(BF16)
                raw[0, pl.ds(at, size), :] = value
                pad[pl.ds(at + 8, size), :] = value.astype(F32)

    for pad in (pad_q, pad_k, pad_v):
        pad[0:8, :] = jnp.zeros((8, COLS), F32)
    row = lax.broadcasted_iota(jnp.int32, (BLOCK, BLOCK), 0)
    col = lax.broadcasted_iota(jnp.int32, (BLOCK, BLOCK), 1)
    below[...] = jnp.where(col <= row, 0.0, -1e30).astype(F32)

    for b in range(GROUPS):

        @pl.when(b < blocks)
        def _(b=b):
            at = slice(b * BLOCK, (b + 1) * BLOCK)
            q_s[at, :] = (conv_rows(pad_q, taps, 0, b * BLOCK).astype(BF16).astype(F32) * 0.125).astype(BF16)
            k_s[at, :] = conv_rows(pad_k, taps, 3, b * BLOCK).astype(BF16)
            v_s[at, :] = conv_rows(pad_v, taps, 6, b * BLOCK).astype(BF16)
            lane = lax.broadcasted_iota(jnp.int32, (BLOCK, 128), 1)
            total_out = jnp.zeros((BLOCK, COLS), F32)
            logs = jnp.zeros((BLOCK, 128), F32)
            for h in range(HEADS_HERE):
                q_h = q_s[at, :] * masks[h].astype(BF16)
                diag = dot(q_h, k_s[at, :], NT) + below[...]
                top = jnp.max(diag, axis=-1, keepdims=True)
                if b:
                    left = dot(q_h, k_s[0 : b * BLOCK, :], NT)
                    top = jnp.maximum(top, jnp.max(left, axis=-1, keepdims=True))
                    expo_left = jnp.exp(left - top)
                expo = jnp.exp(diag - top)
                total = jnp.sum(expo, axis=-1, keepdims=True)
                out = dot(expo.astype(BF16), v_s[at, :], NN)
                if b:
                    total += jnp.sum(expo_left, axis=-1, keepdims=True)
                    out += dot(expo_left.astype(BF16), v_s[0 : b * BLOCK, :], NN)
                total_out = total_out + (out * masks[h]) * (1.0 / total)
                logs = jnp.where(lane == h, top + jnp.log(total), logs)
            result = jnp.transpose(total_out).astype(BF16)
            mixed[b] = result
            to_rows[b] = result
            lse_t[0, :, at] = jnp.transpose(logs)[0:8, :]

        @pl.when(b >= blocks)
        def _(b=b):
            mixed[b] = jnp.zeros((COLS, BLOCK), BF16)
            to_rows[b] = jnp.zeros((COLS, BLOCK), BF16)


def attend(first, info, pieces, w_mine, taps, gain, bias, earlier=()):
    base = 0 if first else 1
    whole = lambda *shape: pl.BlockSpec(shape, lambda i, sc: (0,) * len(shape))
    mine = lambda *shape: pl.BlockSpec((1, *shape), lambda i, sc: (base + i,) + (0,) * len(shape))
    if first:
        piece_specs = [whole(*p.shape) for p in pieces]
    else:
        piece_specs = [
            pl.BlockSpec((1, 1, BLOCK, WIDTH), lambda i, sc, k=k: (k, i, 0, 0)) for k in range(GROUPS)
        ]
        pieces = [pieces] * GROUPS
    full = lambda dtype, *shape: jax.ShapeDtypeStruct((SEQS, *shape), dtype)
    return pl.pallas_call(
        functools.partial(attend_kernel, first),
        grid_spec=pltpu.PrefetchScalarGridSpec(
            num_scalar_prefetch=1,
            grid=(1 if first else SEQS - 1,),
            in_specs=piece_specs
            + [whole(3 * COLS, WIDTH), whole(9, COLS), whole(1, WIDTH), whole(1, WIDTH)]
            + [pl.BlockSpec(memory_space=pl.ANY)] * len(earlier),
            out_specs=[mine(FULL, WIDTH)]
            + [mine(FULL, COLS)] * 3
            + [
                pl.BlockSpec((GROUPS, COLS, BLOCK), lambda i, sc: (0, base + i, 0)),
                mine(8, FULL),
                pl.BlockSpec((GROUPS, COLS, BLOCK), lambda i, sc: (0, i, 0)),
            ],
            scratch_shapes=[pltpu.VMEM((FULL + 8, COLS), F32)] * 3
            + [pltpu.VMEM((FULL, COLS), BF16)] * 3
            + [pltpu.VMEM((BLOCK, BLOCK), F32)],
        ),
        out_shape=(
            full(BF16, FULL, WIDTH),
            full(BF16, FULL, COLS), full(BF16, FULL, COLS), full(BF16, FULL, COLS),
            jax.ShapeDtypeStruct((GROUPS, SEQS * COLS, BLOCK), BF16),
            full(F32, 8, FULL),
            jax.ShapeDtypeStruct((GROUPS, (1 if first else SEQS - 1) * COLS, BLOCK), BF16),
        ),
        input_output_aliases={1 + len(pieces) + 4 + n: n for n in range(len(earlier))},
        compiler_params=params(60),
        cost_estimate=cost(3e9, 8e6, 2e6),
        name="attend",
    )(info, *pieces, w_mine, taps, gain, bias, *earlier)


def attend_back_kernel(
    info, g_s, normed, raw_q, raw_k, raw_v, mixed, lse_t,
    w_mine, taps, gain, bias, ffn_vectors,
    d_own, d_next, d_prev, keep, send,
    dw_out, small_out, d_all, pack,
    pad_q, pad_k, pad_v, q_s, k_s, v_s, dq_s, dk_s, dv_s, below, p_all, ds_all,
):
    step = pl.program_id(0)
    here, core, length = info[0], info[1], info[2 + step]

    blocks = (length + BLOCK - 1) // BLOCK
    masks = head_masks()

    row = lax.broadcasted_iota(jnp.int32, (BLOCK, BLOCK), 0)
    col = lax.broadcasted_iota(jnp.int32, (BLOCK, BLOCK), 1)
    below[...] = jnp.where(row <= col, 0.0, -1e30).astype(F32)
    for pad, raw in ((pad_q, raw_q), (pad_k, raw_k), (pad_v, raw_v)):
        pad[0:8, :] = jnp.zeros((8, COLS), F32)
    for total in (dq_s, dk_s, dv_s):
        total[...] = jnp.zeros((FULL + 8, COLS), F32)

    for b in range(GROUPS):

        @pl.when(b < blocks)
        def _(b=b):
            at = slice(b * BLOCK, (b + 1) * BLOCK)
            for pad, raw in ((pad_q, raw_q), (pad_k, raw_k), (pad_v, raw_v)):
                pad[8 + b * BLOCK : 8 + (b + 1) * BLOCK, :] = raw[0, at, :].astype(F32)
            q_s[at, :] = (conv_rows(pad_q, taps, 0, b * BLOCK).astype(BF16).astype(F32) * 0.125).astype(BF16)
            k_s[at, :] = conv_rows(pad_k, taps, 3, b * BLOCK).astype(BF16)
            v_s[at, :] = conv_rows(pad_v, taps, 6, b * BLOCK).astype(BF16)
            both = g_s[b].astype(F32) * mixed[b].astype(F32)
            reach = slice(0, (b + 1) * BLOCK)
            dq_total = jnp.zeros((BLOCK, COLS), F32)
            q_heads, g_heads = [], []
            for h in range(HEADS_HERE):
                lanes = slice(h * BLOCK, (h + 1) * BLOCK)
                q_h = q_s[at, :] * masks[h].astype(BF16)
                own = slice(h * HDIM, (h + 1) * HDIM)
                blank = lambda n: [jnp.zeros((n * HDIM, BLOCK), BF16)] if n else []
                g_h = jnp.concatenate(blank(h) + [g_s[b, own, :]] + blank(HEADS_HERE - 1 - h), axis=0)
                q_heads.append(q_h)
                g_heads.append(g_h)
                row_dot = jnp.sum(both[own, :], axis=0, keepdims=True)
                log_row = lse_t[0, h : h + 1, at]
                for j in range(b + 1):
                    keys = slice(j * BLOCK, (j + 1) * BLOCK)
                    scores = dot(k_s[keys, :], q_h, NT)
                    if j == b:
                        scores = scores + below[...]
                    probs = jnp.exp(scores - log_row)
                    grad_probs = dot(v_s[keys, :], g_h, NN)
                    p_all[keys, lanes] = probs.astype(BF16)
                    ds_all[keys, lanes] = (probs * (grad_probs - row_dot)).astype(BF16)
                dq_total += dot(ds_all[reach, lanes], k_s[reach, :], TN) * masks[h]
            dq_s[at, :] = dq_total * 0.125
            dv_s[reach, :] += dot(p_all[reach, :], jnp.concatenate(g_heads, axis=1), NT)
            dk_s[reach, :] += dot(ds_all[reach, :], jnp.concatenate(q_heads, axis=0), NN)

    @pl.when(step == 0)
    def _():
        dw_out[...] = jnp.zeros_like(dw_out)
        small_out[...] = jnp.zeros_like(small_out)

    for b in range(GROUPS):

        @pl.when(b < blocks)
        def _(b=b):
            start = b * BLOCK
            at = slice(start, start + BLOCK)
            for n, (pad, grad) in enumerate(((pad_q, dq_s), (pad_k, dk_s), (pad_v, dv_s))):
                now = grad[at, :]
                value = taps[3 * n : 3 * n + 1, :] * now
                for m in (1, 2):
                    value += taps[3 * n + m : 3 * n + m + 1, :] * grad[start + m : start + m + BLOCK, :]
                value = value.astype(BF16).astype(F32)
                d_all[b, n * COLS : (n + 1) * COLS, :] = jnp.transpose(value).astype(BF16)
                small_out[9 + n : 10 + n, 0:COLS] += jnp.sum(value, axis=0, keepdims=True)
                for m in range(3):
                    shifted = pad[8 + start - m : 8 + start - m + BLOCK, :]
                    small_out[3 * n + m : 3 * n + m + 1, 0:COLS] += jnp.sum(
                        shifted * now, axis=0, keepdims=True
                    )
            dw_out[...] += dot(d_all[b], normed[0, at, :], NN)

        @pl.when(b >= blocks)
        def _(b=b):
            d_all[b] = jnp.zeros((3 * COLS, BLOCK), BF16)

    far = lax.rem(here + 2, GROUPS)
    d_own[0] = d_all[here]
    d_next[0, 0 : 3 * COLS, :] = d_all[lax.rem(here + 1, GROUPS)]
    d_next[0, 3 * COLS :, :] = d_all[far, 0 : 3 * COLS // 2, :]
    d_prev[0, 0 : 3 * COLS, :] = d_all[lax.rem(here + 3, GROUPS)]
    d_prev[0, 3 * COLS :, :] = d_all[far, 3 * COLS // 2 :, :]

    @pl.when(step == SEQS - 1)
    def _():
        grad_bias = jnp.zeros((1, WIDTH), F32)
        for n in range(3):
            sums = small_out[9 + n : 10 + n, 0:COLS]
            high = sums.astype(BF16)
            rest = (sums - high.astype(F32)).astype(BF16)
            for term in (high, rest):
                wide = jnp.broadcast_to(term.astype(F32), (16, COLS)).astype(BF16)
                grad_bias += dot(wide, w_mine[n * COLS : (n + 1) * COLS, :], NN)[0:1, :]
        grad_normed = jnp.sum(w_mine[...].astype(F32) * dw_out[...], axis=0, keepdims=True)
        grad_gain = (grad_normed - bias[...] * grad_bias) / gain[...]
        pack[0 : 3 * COLS, :] = dw_out[...].astype(BF16)
        tail = jnp.concatenate(
            [
                small_out[0:9, :],
                grad_gain,
                grad_bias,
                ffn_vectors[0:2, :],
                jnp.zeros((3, WIDTH), F32),
            ],
            axis=0,
        )
        pack[3 * COLS : 3 * COLS + 16, :] = tail.astype(BF16)
        pack[3 * COLS + 16 :, :] = jnp.zeros((PACK_ROWS - 3 * COLS - 16, WIDTH), BF16)
        half = WIDTH // 2
        keep[...] = pack[:, pl.ds(pl.multiple_of(core * half, 128), half)]
        send[...] = pack[:, pl.ds(pl.multiple_of((1 - core) * half, 128), half)]


def attend_back(info, grad_mixed, saved, w_mine, taps, gain, bias, ffn_vectors):
    low = lambda *shape: jax.ShapeDtypeStruct(shape, BF16)
    whole = lambda *shape: pl.BlockSpec(shape, lambda i, sc: (0,) * len(shape))
    mine = lambda *shape: pl.BlockSpec((1, *shape), lambda i, sc: (i,) + (0,) * len(shape))
    across = pl.BlockSpec((GROUPS, COLS, BLOCK), lambda i, sc: (0, i, 0))
    long_rows = 3 * COLS * 3 // 2
    return pl.pallas_call(
        attend_back_kernel,
        grid_spec=pltpu.PrefetchScalarGridSpec(
            num_scalar_prefetch=1,
            grid=(SEQS,),
            in_specs=[
                pl.BlockSpec((GROUPS, COLS, BLOCK), lambda i, sc: (0, lax.rem(i + 2, SEQS), 0)),
                mine(FULL, WIDTH),
            ]
            + [mine(FULL, COLS)] * 3
            + [across, mine(8, FULL)]
            + [whole(3 * COLS, WIDTH), whole(9, COLS), whole(1, WIDTH), whole(1, WIDTH), whole(8, WIDTH)],
            out_specs=[mine(3 * COLS, BLOCK), mine(long_rows, BLOCK), mine(long_rows, BLOCK)]
            + [whole(PACK_ROWS, WIDTH // 2)] * 2,
            scratch_shapes=[
                pltpu.VMEM((3 * COLS, WIDTH), F32),
                pltpu.VMEM((16, WIDTH), F32),
                pltpu.VMEM((GROUPS, 3 * COLS, BLOCK), BF16),
                pltpu.VMEM((PACK_ROWS, WIDTH), BF16),
            ]
            + [pltpu.VMEM((FULL + 8, COLS), F32)] * 3
            + [pltpu.VMEM((FULL, COLS), BF16)] * 3
            + [pltpu.VMEM((FULL + 8, COLS), F32)] * 3
            + [pltpu.VMEM((BLOCK, BLOCK), F32)]
            + [pltpu.VMEM((FULL, HEADS_HERE * BLOCK), BF16)] * 2,
        ),
        out_shape=(
            low(SEQS, 3 * COLS, BLOCK), low(SEQS, long_rows, BLOCK), low(SEQS, long_rows, BLOCK),
            low(PACK_ROWS, WIDTH // 2), low(PACK_ROWS, WIDTH // 2),
        ),
        compiler_params=params(60),
        cost_estimate=cost(1e10, 2e7),
        name="attend_back",
    )(info, grad_mixed, *saved, w_mine, taps, gain, bias, ffn_vectors)


def heads_of(source, s):
    return jnp.concatenate([source[k, s * COLS : (s + 1) * COLS, :] for k in range(GROUPS)], axis=0)


def ffn_kernel(first, info, *refs):
    count = 1 if first else SEQS - 1
    base = 0 if first else 1
    x, cotangent, refs = refs[:count], refs[count : 2 * count], refs[2 * count :]
    mixed, w_out, gain, bias, w_up, w_down = refs[:6]
    refs = refs[6:]
    steps = FF // CHUNK
    if first:
        layer_output, grad_middle, grad_mixed, sq_out, gh_out, normed_of, low_of, branch, vectors = refs[:9]
        middle, total_out, total_grad = refs[9:]
        places = [slice(0, BLOCK)]
    else:
        mixed_first, branch_first, vectors_first, sq_first, gh_first, normed_first, low_first = refs[:7]
        layer_output, grad_middle, grad_mixed, grad_up, grad_down, grad_out, vectors = refs[8:15]
        middle, total_out, total_grad, normed_of, normed_t, low_of, sq_all, gh_all, dw_out = refs[15:]
        places = [slice((s + 1) * BLOCK, (s + 2) * BLOCK) for s in range(count)]
    parts = [slice(s * BLOCK, (s + 1) * BLOCK) for s in range(count)]
    step = pl.program_id(0)
    position = info[0] * BLOCK + lax.broadcasted_iota(jnp.int32, (BLOCK, 1), 0)

    @pl.when(step == 0)
    def _():
        for s, (at, to) in enumerate(zip(parts, places)):
            value = x[s][0].astype(F32) + dot(heads_of(mixed, s), w_out[...], TN)
            middle[at, :] = value
            unit, _ = unit_rows(value)
            normed_of[to, :] = (unit * gain[...] + bias[...]).astype(BF16)
            keep_row = position < info[2 + base + s]
            low_of[to, :] = jnp.where(keep_row, cotangent[s][0].astype(F32), 0.0).astype(BF16)
            total_out[at, :] = jnp.zeros((BLOCK, WIDTH), F32)
            total_grad[at, :] = jnp.zeros((BLOCK, WIDTH), F32)
        if not first:
            normed_of[0:BLOCK, :] = normed_first[...]
            low_of[0:BLOCK, :] = low_first[...]
            normed_t[...] = jnp.transpose(normed_of[...])

    def rows_of_chunk(put):
        to = slice(places[0].start, places[-1].stop)
        hidden = jnp.maximum(dot(normed_of[to, :], w_up[...], NN), 0.0)
        squared = (hidden * hidden).astype(BF16)
        back = dot(low_of[to, :], w_down[...], NT)
        grad_hidden = (back * 2.0 * hidden).astype(BF16)
        put(to, squared, grad_hidden)
        total_out[...] += dot(squared, w_down[...], NN)
        total_grad[...] += dot(grad_hidden, w_up[...], NT)

    def finish(s):
        at, to = parts[s], places[s]
        keep_row = position < info[2 + base + s]
        layer_output[s] = jnp.where(keep_row, middle[at, :] + total_out[at, :], 0.0).astype(BF16)
        unit, inverse = unit_rows(middle[at, :])
        grad_normed = total_grad[at, :]
        scaled = grad_normed * gain[...]
        mean_grad = jnp.mean(scaled, axis=-1, keepdims=True)
        mean_dot = jnp.mean(scaled * unit, axis=-1, keepdims=True)
        value = low_of[to, :].astype(F32) + inverse * (scaled - mean_grad - unit * mean_dot)
        vectors[0:1, :] += jnp.sum(grad_normed * unit, axis=0, keepdims=True)
        vectors[1:2, :] += jnp.sum(grad_normed, axis=0, keepdims=True)
        grad_middle[s] = value
        low = value.astype(BF16)
        heads_grad = dot(w_out[...], low, NT).astype(BF16)
        for k in range(GROUPS):
            grad_mixed[k, s * COLS : (s + 1) * COLS, :] = heads_grad[k * COLS : (k + 1) * COLS]
        return low

    if first:

        def put(to, squared, grad_hidden):
            sq_out[to, :] = squared
            gh_out[to, :] = grad_hidden

        rows_of_chunk(put)

        @pl.when(step == steps - 1)
        def _():
            vectors[...] = jnp.zeros_like(vectors)
            branch[...] = finish(0)

        return

    @pl.when(step < steps)
    def _():
        def put(to, squared, grad_hidden):
            sq_all[step, to, :] = squared
            gh_all[step, to, :] = grad_hidden

        rows_of_chunk(put)
        sq_all[step, 0:BLOCK, :] = sq_first[...]
        gh_all[step, 0:BLOCK, :] = gh_first[...]

    def weights_of_chunk(n):
        grad_up[...] = dot(normed_t[...], gh_all[n], NN).astype(BF16)
        grad_down[...] = dot(sq_all[n], low_of[...], TN).astype(BF16)

    @pl.when(step == steps)
    def _():
        vectors[...] = vectors_first[...]
        weights_of_chunk(0)
        low = finish(0)
        dw_out[...] = dot(heads_of(mixed_first, 0), branch_first[...], NN) + dot(heads_of(mixed, 0), low, NN)

    @pl.when(step == steps + 1)
    def _():
        weights_of_chunk(1)
        low = finish(1)
        dw_out[...] += dot(heads_of(mixed, 1), low, NN)

    @pl.when(step >= steps + 2)
    def _():
        weights_of_chunk(step - steps)
        grad_out[...] = dw_out[...].astype(BF16)


def ffn(first, info, x, cotangent, mixed, w_out, gain, bias, w_up, w_down, earlier=()):
    count = 1 if first else SEQS - 1
    base = 0 if first else 1
    low = lambda *shape: jax.ShapeDtypeStruct(shape, BF16)
    full = lambda *shape: jax.ShapeDtypeStruct(shape, F32)
    rows = count * BLOCK
    all_rows = SEQS * BLOCK
    steps = FF // CHUNK
    whole = lambda *shape: pl.BlockSpec(shape, lambda i, sc: (0,) * len(shape))
    nth = lambda s: pl.BlockSpec((1, BLOCK, WIDTH), lambda i, sc: (sc[5 + base + s], 0, 0))
    early = lambda i: jnp.minimum(i, steps - 1)
    late = lambda i: jnp.maximum(i - steps, 0)
    across = lambda n: pl.BlockSpec((n, CHUNK), lambda i, sc: (0, early(i)))
    grads = pl.BlockSpec((GROUPS, count * COLS, BLOCK), lambda i, sc: (0, SEQS - 1 if first else 0, 0))
    scratch = [pltpu.VMEM((rows, WIDTH), F32)] * 3
    if first:
        extra_specs = []
        out_specs = [across(rows)] * 2 + [whole(rows, WIDTH)] * 3 + [whole(8, WIDTH)]
        out_shape = [low(rows, FF)] * 2 + [low(rows, WIDTH)] * 3 + [full(8, WIDTH)]
        aliases = {}
    else:
        extra_specs = (
            [whole(GROUPS, COLS, BLOCK), whole(BLOCK, WIDTH), whole(8, WIDTH)]
            + [across(BLOCK)] * 2
            + [whole(BLOCK, WIDTH)] * 2
            + [pl.BlockSpec(memory_space=pl.ANY)]
        )
        out_specs = [
            pl.BlockSpec((WIDTH, CHUNK), lambda i, sc: (0, late(i))),
            pl.BlockSpec((CHUNK, WIDTH), lambda i, sc: (late(i), 0)),
            whole(WIDTH, WIDTH),
            whole(8, WIDTH),
        ]
        out_shape = [low(WIDTH, FF), low(FF, WIDTH), low(WIDTH, WIDTH), full(8, WIDTH)]
        scratch += (
            [pltpu.VMEM((all_rows, WIDTH), BF16), pltpu.VMEM((WIDTH, all_rows), BF16), pltpu.VMEM((all_rows, WIDTH), BF16)]
            + [pltpu.VMEM((steps, all_rows, CHUNK), BF16)] * 2
            + [pltpu.VMEM((WIDTH, WIDTH), F32)]
        )
        aliases = {1 + 2 * count + 6 + 7: 2}
    return pl.pallas_call(
        functools.partial(ffn_kernel, first),
        grid_spec=pltpu.PrefetchScalarGridSpec(
            num_scalar_prefetch=1,
            grid=(steps if first else 2 * steps,),
            in_specs=[nth(s) for s in range(count)] * 2
            + [
                whole(GROUPS, count * COLS, BLOCK), whole(WIDTH, WIDTH), whole(1, WIDTH), whole(1, WIDTH),
                across(WIDTH),
                pl.BlockSpec((CHUNK, WIDTH), lambda i, sc: (early(i), 0)),
            ]
            + extra_specs,
            out_specs=[whole(count, BLOCK, WIDTH), whole(count, BLOCK, WIDTH), grads] + out_specs,
            scratch_shapes=scratch,
        ),
        out_shape=[low(count, BLOCK, WIDTH), full(count, BLOCK, WIDTH), low(GROUPS, SEQS * COLS, BLOCK)] + out_shape,
        input_output_aliases=aliases,
        compiler_params=params(60),
        cost_estimate=cost(7e9 if first else 2.2e10, 2e7),
        name="ffn",
    )(info, *[x] * count, *[cotangent] * count, mixed, w_out, gain, bias, w_up, w_down, *earlier)


def input_kernel(
    info, x, middle_first, middle_others, output_first, output_others, own, behind, over, ahead, under, w_groups, gain,
    out, layer_output, grad_middle,
):
    @pl.when(pl.program_id(0) == 0)
    def _():
        grad_middle[...] = middle_first[0]
        layer_output[...] = output_first[...]

    @pl.when(pl.program_id(0) > 0)
    def _():
        grad_middle[...] = middle_others[0]
        layer_output[...] = output_others[...]

    here = info[0]
    w_of = lambda k: w_groups[lax.rem(here + k, GROUPS)]
    unit, inverse = unit_rows(x[0].astype(F32))
    grad_normed = dot(own[0], w_of(0), TN)
    grad_normed += dot(ahead[0], w_of(1), TN)
    grad_normed += dot(jnp.concatenate([over[0], under[0]], axis=0), w_of(2), TN)
    grad_normed += dot(behind[0], w_of(3), TN)
    scaled = grad_normed * gain[...]
    mean_grad = jnp.mean(scaled, axis=-1, keepdims=True)
    mean_dot = jnp.mean(scaled * unit, axis=-1, keepdims=True)
    out[0] = grad_middle[...] + inverse * (scaled - mean_grad - unit * mean_dot)


def input_grad_of(info, x, grad_middle, layer_output, pieces, w_groups, gain):
    mine = lambda rows, lanes: pl.BlockSpec((1, rows, lanes), lambda i, sc: (i, 0, 0))
    whole = lambda *shape: pl.BlockSpec(shape, lambda i, sc: (0,) * len(shape))
    placed = pl.BlockSpec((1, BLOCK, WIDTH), lambda i, sc: (sc[5 + i], 0, 0))
    two = [whole(1, BLOCK, WIDTH), pl.BlockSpec((1, BLOCK, WIDTH), lambda i, sc: (jnp.maximum(i - 1, 0), 0, 0))]
    piece = mine(3 * COLS, BLOCK)
    half = mine(3 * COLS // 2, BLOCK)
    return pl.pallas_call(
        input_kernel,
        grid_spec=pltpu.PrefetchScalarGridSpec(
            num_scalar_prefetch=1,
            grid=(SEQS,),
            in_specs=[placed, *two, *two, piece, piece, half, piece, half, whole(*w_groups.shape), whole(1, WIDTH)],
            out_specs=[placed, placed],
            scratch_shapes=[pltpu.VMEM((BLOCK, WIDTH), F32)],
        ),
        out_shape=(
            jax.ShapeDtypeStruct((SEQS, BLOCK, WIDTH), F32),
            jax.ShapeDtypeStruct((SEQS, BLOCK, WIDTH), BF16),
        ),
        compiler_params=params(60),
        cost_estimate=cost(3e9, 1.5e7),
        name="input_grad",
    )(info, x, *grad_middle, *layer_output, *pieces, w_groups, gain)


def place_kernel(up, down, out, grad_up, grad_down, grad_out):
    grad_up[...] = up[...].astype(F32)
    grad_down[...] = down[...].astype(F32)
    grad_out[...] = out[...].astype(F32)


def place(up, down, out):
    steps = FF // PLACE
    rows = lambda n: pl.BlockSpec((n, WIDTH), lambda i: (i, 0))
    specs = [pl.BlockSpec((WIDTH, PLACE), lambda i: (0, i)), rows(PLACE), rows(WIDTH // steps)]
    return pl.pallas_call(
        place_kernel,
        grid=(steps,),
        in_specs=specs,
        out_specs=specs,
        out_shape=[jax.ShapeDtypeStruct(a.shape, F32) for a in (up, down, out)],
        compiler_params=params(60),
        cost_estimate=cost(1e6, 3.2e7),
        name="place",
    )(up, down, out)


def unpack_kernel(info, own, other, grad_q, grad_k, grad_v, tails, rows):
    size = PACK_ROWS // 16
    half = WIDTH // 2

    def fill(pieces, base):
        for y in range(GROUPS):
            for n in range(16):
                rows[y, n * size : (n + 1) * size, base : base + half] = pieces[n * GROUPS + y].astype(F32)

    @pl.when(info[0] == 0)
    def _():
        fill(own, 0)
        fill(other, half)

    @pl.when(info[0] != 0)
    def _():
        fill(other, 0)
        fill(own, half)

    for n, grad in enumerate((grad_q, grad_k, grad_v)):
        part = jnp.concatenate([rows[y, n * COLS : (n + 1) * COLS, :] for y in range(GROUPS)], axis=0)
        grad[...] = jnp.transpose(part)
    for y in range(GROUPS):
        tails[y] = rows[y, 3 * COLS : 3 * COLS + 16, :]


def unpack(core, own, other):
    full = lambda *shape: jax.ShapeDtypeStruct(shape, F32)
    return pl.pallas_call(
        unpack_kernel,
        in_specs=[pl.BlockSpec(memory_space=pltpu.SMEM), vmem(), vmem()],
        out_specs=[vmem()] * 4,
        out_shape=(full(WIDTH, WIDTH), full(WIDTH, WIDTH), full(WIDTH, WIDTH), full(GROUPS, 16, WIDTH)),
        scratch_shapes=[pltpu.VMEM((GROUPS, PACK_ROWS, WIDTH), F32)],
        compiler_params=params(60),
        cost_estimate=cost(1e6, 1e5),
        name="unpack",
    )(core.reshape(1), own, other)


def shift(array, axis, by):
    return lax.ppermute(array, axis, [(i, (i + by) % GROUPS) for i in range(GROUPS)])


def gather_rows(rows):
    ahead = shift(rows, "head", -1)
    behind = shift(rows, "head", 1)
    over_lo = shift(ahead[:128], "head", -1)
    over_hi = shift(behind[128:], "head", 1)
    return rows, ahead, over_lo, over_hi, behind


def near_exchange(to_next, to_prev):
    return shift(to_next, "head", 1), shift(to_prev, "head", -1)


def far_exchange(from_prev, from_next, size):
    return shift(from_prev[:, size:], "head", 1), shift(from_next[:, size:], "head", -1)


def trade(array, axes):
    return lax.all_to_all(array, axes, 0, 0, tiled=True)


def swap_cores(array):
    return lax.ppermute(array, "core", [(0, 1), (1, 0)])


def add_low(*terms):
    total = terms[0].astype(F32)
    for term in terms[1:]:
        total = total + term.astype(F32)
    return total.astype(BF16)


def per_device(
    layer_input, lengths, cotangent, w_query, w_key, w_value, conv_query, conv_key, conv_value,
    w_out, w_up, w_down, gain_attn, bias_attn, gain_ffn, bias_ffn,
):
    here = lax.axis_index("head").astype(jnp.int32)
    core = lax.axis_index("core").astype(jnp.int32)
    first_rows, other_rows, info = prepare(lengths, layer_input)
    first_rows = gather_rows(first_rows)
    other_rows = lax.all_gather(other_rows, "head", axis=0)

    w_groups = jnp.concatenate(
        [w.T.reshape(GROUPS, COLS, WIDTH) for w in (w_query, w_key, w_value)], axis=1
    )
    w_mine = lax.dynamic_index_in_dim(w_groups, here, 0, False)
    taps = lax.dynamic_slice_in_dim(
        jnp.concatenate([conv_query, conv_key, conv_value], axis=0), here * COLS, COLS, 1
    )
    gain_a, bias_a, gain_f, bias_f = (
        v.reshape(1, WIDTH) for v in (gain_attn, bias_attn, gain_ffn, bias_ffn)
    )
    *saved, mixed_first = attend(True, info, first_rows, w_mine, taps, gain_a, bias_a)
    mixed_first = trade(mixed_first, "head")
    *saved, mixed_others = attend(False, info, other_rows, w_mine, taps, gain_a, bias_a, saved)
    mixed_first, mixed_others = lax.optimization_barrier((mixed_first, mixed_others))
    mixed_others = trade(mixed_others, "head")
    weights = (w_out, gain_f, bias_f, w_up, w_down)
    output_a, middle_a, grad_a, *rows_a, branch_a, vectors_a = ffn(
        True, info, layer_input, cotangent, mixed_first, *weights
    )
    output_b, middle_b, grad_mixed, up, down, out, ffn_vectors = ffn(
        False, info, layer_input, cotangent, mixed_others, *weights,
        (mixed_first, branch_a, vectors_a, *rows_a, grad_a),
    )
    weight_sums = lax.psum((up, down, out), ("x", "z", "core", "head"))
    grad_mixed = trade(grad_mixed, "head")

    def attention_grads(grad_mixed, saved, grad_middle, layer_output, ffn_vectors):
        d_own, d_next, d_prev, keep, send = attend_back(
            info, grad_mixed, saved, w_mine, taps, gain_a, bias_a, ffn_vectors
        )
        behind, ahead = near_exchange(d_next, d_prev)

        part = add_low(keep, swap_cores(send)).reshape(16, PACK_ROWS // 16, WIDTH // 2)
        part = add_low(*trade(part, ("x", "z")))
        part, behind, ahead = lax.optimization_barrier((part, behind, ahead))
        over, under = far_exchange(behind, ahead, 3 * COLS)
        for axis in ("head", "z", "x"):
            if axis == "x":
                part, over, under = lax.optimization_barrier((part, over, under))
            part = trade(jnp.broadcast_to(part[None], (GROUPS, *part.shape)), axis)
        part = part.reshape(64, PACK_ROWS // 16, WIDTH // 2)
        input_grad, layer_output = input_grad_of(
            info, layer_input, grad_middle, layer_output, (d_own, behind, over, ahead, under), w_groups, gain_a
        )
        part, input_grad = lax.optimization_barrier((part, input_grad))
        grad_q, grad_k, grad_v, tails = unpack(core, part, swap_cores(part))
        conv = lambda n: jnp.transpose(tails[:, 3 * n : 3 * n + 3, 0:COLS], (1, 0, 2)).reshape(3, WIDTH)
        vector = jnp.sum(tails[:, 9:13, :], axis=0)
        return (
            layer_output, input_grad, grad_q, grad_k, grad_v, conv(0), conv(1), conv(2),
            vector[0], vector[1], vector[2], vector[3],
        )

    operands = (grad_mixed, saved, (middle_a, middle_b), (output_a, output_b), ffn_vectors)
    blank = lambda *args: jax.tree.map(
        lambda a: jnp.zeros(a.shape, a.dtype), jax.eval_shape(attention_grads, *args)
    )
    later = lax.cond(lengths[0] > 0, attention_grads, blank, *operands)
    weight_sums, later = lax.optimization_barrier((weight_sums, later))
    grad_up, grad_down, grad_out = place(*weight_sums)
    return (*later[:8], grad_out, grad_up, grad_down, *later[8:])


def solution(mesh):
    fine = Mesh(mesh.devices.reshape(4, 4, 2, GROUPS), ("x", "z", "core", "head"))
    dp = ("x", "z", "core")
    rows = P(dp, "head", None)
    return jax.shard_map(
        per_device,
        mesh=fine,
        in_specs=(rows, P(dp), rows) + (P(),) * 13,
        out_specs=(rows, rows) + (P(),) * 13,
        check_vma=False,
    )
```

```python
import functools

import jax
import jax.numpy as jnp
from jax import lax
from jax.experimental import pallas as pl
from jax.experimental.pallas import tpu as pltpu
from jax.sharding import Mesh
from jax.sharding import PartitionSpec as P

HDIM = 64
GROUPS = 4
BLOCK = 256
FULL = 1024
WIDTH = 768
COLS = 192
FF = 3072
SEQS = 3
CHUNK = 768
PLACE = 512
HEADS_HERE = 3
PACK_ROWS = 640
F32 = jnp.float32
BF16 = jnp.bfloat16
NN = (((1,), (0,)), ((), ()))
NT = (((1,), (1,)), ((), ()))
TN = (((0,), (0,)), ((), ()))


def dot(left, right, dims):
    return lax.dot_general(left, right, dims, preferred_element_type=F32)


def cost(flops, nbytes, transcendentals=0):
    return pl.CostEstimate(
        flops=int(flops), bytes_accessed=int(nbytes), transcendentals=int(transcendentals)
    )


def vmem():
    return pl.BlockSpec(memory_space=pltpu.VMEM)


def params(mib):
    return pltpu.CompilerParams(vmem_limit_bytes=mib << 20)


def unit_rows(rows):
    average = jnp.mean(rows, axis=-1, keepdims=True)
    centred = rows - average
    variance = jnp.mean(centred * centred, axis=-1, keepdims=True)
    inverse = lax.rsqrt(variance + 1e-05)
    return centred * inverse, inverse


def head_masks():
    lane = lax.broadcasted_iota(jnp.int32, (1, COLS), 1)
    return [
        jnp.where((lane >= h * HDIM) & (lane < (h + 1) * HDIM), 1.0, 0.0).astype(F32)
        for h in range(HEADS_HERE)
    ]


def conv_rows(raw_f, taps, tap_row, start):
    total = taps[tap_row : tap_row + 1, :] * raw_f[8 + start : 8 + start + BLOCK, :]
    for m in (1, 2):
        total += (
            taps[tap_row + m : tap_row + m + 1, :]
            * raw_f[8 + start - m : 8 + start - m + BLOCK, :]
        )
    return total


def order_of(lengths):
    a, b, c = lengths[0], lengths[1], lengths[2]
    first = jnp.where((a >= b) & (a >= c), 0, jnp.where(b >= c, 1, 2)).astype(jnp.int32)
    last = jnp.where((c <= a) & (c <= b), 2, jnp.where(b <= a, 1, 0)).astype(jnp.int32)
    return first, 3 - first - last, last


def prepare_kernel(lengths, row_0, row_1, row_2, out_0, out_1, out_2, info):
    for row, out in ((row_0, out_0), (row_1, out_1), (row_2, out_2)):
        out[...] = row[0]
    info[0] = lax.axis_index("head").astype(jnp.int32)
    info[1] = lax.axis_index("core").astype(jnp.int32)
    a, b, c = lengths[0], lengths[1], lengths[2]
    for n, s in enumerate(order_of(lengths)):
        info[2 + n] = jnp.where(s == 0, a, jnp.where(s == 1, b, c))
        info[5 + n] = s


def prepare(lengths, rows):
    nth = lambda n: pl.BlockSpec((1, BLOCK, WIDTH), lambda i, sc: (order_of(sc)[n], 0, 0))
    whole = lambda *shape: pl.BlockSpec(shape, lambda i, sc: (0,) * len(shape))
    return pl.pallas_call(
        prepare_kernel,
        grid_spec=pltpu.PrefetchScalarGridSpec(
            num_scalar_prefetch=1,
            grid=(1,),
            in_specs=[nth(0), nth(1), nth(2)],
            out_specs=[whole(BLOCK, WIDTH)] * SEQS + [pl.BlockSpec(memory_space=pltpu.SMEM)],
        ),
        out_shape=[jax.ShapeDtypeStruct((BLOCK, WIDTH), BF16)] * SEQS + [jax.ShapeDtypeStruct((8,), jnp.int32)],
        compiler_params=params(60),
        cost_estimate=cost(1e3, 2.4e6),
        name="prepare",
    )(lengths, rows, rows, rows)


def attend_kernel(seq, extra, info, *refs):
    first = seq < SEQS - 1
    count = 5 if first else GROUPS
    pieces, refs = refs[:count], refs[count:]
    w_mine, taps, gain, bias = refs[:4]
    refs = refs[4 + extra :]
    normed, raw_q, raw_k, raw_v, mixed, lse_t, to_rows = refs[:7]
    pad_q, pad_k, pad_v, q_s, k_s, v_s, below = refs[7:]
    here = info[0]
    length = info[2 + seq]
    blocks = (length + BLOCK - 1) // BLOCK
    masks = head_masks()
    if first:
        homes = [(lax.rem(here + ahead, GROUPS), shift) for ahead, shift in ((0, 0), (1, 0), (2, 0), (2, 128), (3, 0))]
    else:
        homes = [(k, 0) for k in range(GROUPS)]

    for piece, (home, shift) in zip(pieces, homes):

        @pl.when(home < blocks)
        def _(piece=piece, home=home, shift=shift):
            rows = piece[...].reshape(piece.shape[-2], WIDTH).astype(F32)
            size = rows.shape[0]
            unit, _ = unit_rows(rows)
            low = (unit * gain[...] + bias[...]).astype(BF16)
            at = home * BLOCK + shift
            at = pl.multiple_of(at, 128) if first else at
            normed[0, pl.ds(at, size), :] = low
            for n, (raw, pad) in enumerate(((raw_q, pad_q), (raw_k, pad_k), (raw_v, pad_v))):
                value = dot(low, w_mine[n * COLS : (n + 1) * COLS, :], NT).astype(BF16)
                raw[0, pl.ds(at, size), :] = value
                pad[pl.ds(at + 8, size), :] = value.astype(F32)

    for pad in (pad_q, pad_k, pad_v):
        pad[0:8, :] = jnp.zeros((8, COLS), F32)
    row = lax.broadcasted_iota(jnp.int32, (BLOCK, BLOCK), 0)
    col = lax.broadcasted_iota(jnp.int32, (BLOCK, BLOCK), 1)
    below[...] = jnp.where(col <= row, 0.0, -1e30).astype(F32)

    for b in range(GROUPS):

        @pl.when(b < blocks)
        def _(b=b):
            at = slice(b * BLOCK, (b + 1) * BLOCK)
            q_s[at, :] = (conv_rows(pad_q, taps, 0, b * BLOCK).astype(BF16).astype(F32) * 0.125).astype(BF16)
            k_s[at, :] = conv_rows(pad_k, taps, 3, b * BLOCK).astype(BF16)
            v_s[at, :] = conv_rows(pad_v, taps, 6, b * BLOCK).astype(BF16)
            lane = lax.broadcasted_iota(jnp.int32, (BLOCK, 128), 1)
            total_out = jnp.zeros((BLOCK, COLS), F32)
            logs = jnp.zeros((BLOCK, 128), F32)
            for h in range(HEADS_HERE):
                q_h = q_s[at, :] * masks[h].astype(BF16)
                diag = dot(q_h, k_s[at, :], NT) + below[...]
                top = jnp.max(diag, axis=-1, keepdims=True)
                if b:
                    left = dot(q_h, k_s[0 : b * BLOCK, :], NT)
                    top = jnp.maximum(top, jnp.max(left, axis=-1, keepdims=True))
                    expo_left = jnp.exp(left - top)
                expo = jnp.exp(diag - top)
                total = jnp.sum(expo, axis=-1, keepdims=True)
                out = dot(expo.astype(BF16), v_s[at, :], NN)
                if b:
                    total += jnp.sum(expo_left, axis=-1, keepdims=True)
                    out += dot(expo_left.astype(BF16), v_s[0 : b * BLOCK, :], NN)
                total_out = total_out + (out * masks[h]) * (1.0 / total)
                logs = jnp.where(lane == h, top + jnp.log(total), logs)
            result = jnp.transpose(total_out).astype(BF16)
            mixed[b] = result
            to_rows[b] = result
            lse_t[0, :, at] = jnp.transpose(logs)[0:8, :]

        @pl.when(b >= blocks)
        def _(b=b):
            mixed[b] = jnp.zeros((COLS, BLOCK), BF16)
            to_rows[b] = jnp.zeros((COLS, BLOCK), BF16)


def attend(seq, info, pieces, w_mine, taps, gain, bias, earlier=()):
    whole = lambda *shape: pl.BlockSpec(shape, lambda i, sc: (0,) * len(shape))
    mine = lambda *shape: pl.BlockSpec((1, *shape), lambda i, sc: (seq,) + (0,) * len(shape))
    heads = lambda n: pl.BlockSpec((GROUPS, COLS, BLOCK), lambda i, sc: (0, n, 0))
    if seq < SEQS - 1:
        piece_specs = [whole(*p.shape) for p in pieces]
    else:
        piece_specs = [pl.BlockSpec((BLOCK, WIDTH), lambda i, sc, k=k: (k, 0)) for k in range(GROUPS)]
        pieces = [pieces] * GROUPS
    full = lambda dtype, *shape: jax.ShapeDtypeStruct((SEQS, *shape), dtype)
    return pl.pallas_call(
        functools.partial(attend_kernel, seq, len(earlier)),
        grid_spec=pltpu.PrefetchScalarGridSpec(
            num_scalar_prefetch=1,
            grid=(1,),
            in_specs=piece_specs
            + [whole(3 * COLS, WIDTH), whole(9, COLS), whole(1, WIDTH), whole(1, WIDTH)]
            + [pl.BlockSpec(memory_space=pl.ANY)] * len(earlier),
            out_specs=[mine(FULL, WIDTH)]
            + [mine(FULL, COLS)] * 3
            + [heads(seq), mine(8, FULL), heads(max(seq - 1, 0))],
            scratch_shapes=[pltpu.VMEM((FULL + 8, COLS), F32)] * 3
            + [pltpu.VMEM((FULL, COLS), BF16)] * 3
            + [pltpu.VMEM((BLOCK, BLOCK), F32)],
        ),
        out_shape=(
            full(BF16, FULL, WIDTH),
            full(BF16, FULL, COLS), full(BF16, FULL, COLS), full(BF16, FULL, COLS),
            jax.ShapeDtypeStruct((GROUPS, SEQS * COLS, BLOCK), BF16),
            full(F32, 8, FULL),
            jax.ShapeDtypeStruct((GROUPS, (SEQS - 1 if seq else 1) * COLS, BLOCK), BF16),
        ),
        input_output_aliases={1 + len(pieces) + 4 + n: n for n in range(len(earlier))},
        compiler_params=params(60),
        cost_estimate=cost(3e9, 8e6, 2e6),
        name="attend",
    )(info, *pieces, w_mine, taps, gain, bias, *earlier)


def attend_back_kernel(
    info, g_s, normed, raw_q, raw_k, raw_v, mixed, lse_t,
    w_mine, taps, gain, bias, ffn_vectors,
    d_own, d_next, d_prev, keep, send,
    dw_out, small_out, d_all, pack,
    pad_q, pad_k, pad_v, q_s, k_s, v_s, dq_s, dk_s, dv_s, below, p_all, ds_all,
):
    step = pl.program_id(0)
    here, core, length = info[0], info[1], info[2 + step]

    blocks = (length + BLOCK - 1) // BLOCK
    masks = head_masks()

    row = lax.broadcasted_iota(jnp.int32, (BLOCK, BLOCK), 0)
    col = lax.broadcasted_iota(jnp.int32, (BLOCK, BLOCK), 1)
    below[...] = jnp.where(row <= col, 0.0, -1e30).astype(F32)
    for pad, raw in ((pad_q, raw_q), (pad_k, raw_k), (pad_v, raw_v)):
        pad[0:8, :] = jnp.zeros((8, COLS), F32)
    for total in (dq_s, dk_s, dv_s):
        total[...] = jnp.zeros((FULL + 8, COLS), F32)

    for b in range(GROUPS):

        @pl.when(b < blocks)
        def _(b=b):
            at = slice(b * BLOCK, (b + 1) * BLOCK)
            for pad, raw in ((pad_q, raw_q), (pad_k, raw_k), (pad_v, raw_v)):
                pad[8 + b * BLOCK : 8 + (b + 1) * BLOCK, :] = raw[0, at, :].astype(F32)
            q_s[at, :] = (conv_rows(pad_q, taps, 0, b * BLOCK).astype(BF16).astype(F32) * 0.125).astype(BF16)
            k_s[at, :] = conv_rows(pad_k, taps, 3, b * BLOCK).astype(BF16)
            v_s[at, :] = conv_rows(pad_v, taps, 6, b * BLOCK).astype(BF16)
            both = g_s[b].astype(F32) * mixed[b].astype(F32)
            reach = slice(0, (b + 1) * BLOCK)
            dq_total = jnp.zeros((BLOCK, COLS), F32)
            q_heads, g_heads = [], []
            for h in range(HEADS_HERE):
                lanes = slice(h * BLOCK, (h + 1) * BLOCK)
                q_h = q_s[at, :] * masks[h].astype(BF16)
                own = slice(h * HDIM, (h + 1) * HDIM)
                blank = lambda n: [jnp.zeros((n * HDIM, BLOCK), BF16)] if n else []
                g_h = jnp.concatenate(blank(h) + [g_s[b, own, :]] + blank(HEADS_HERE - 1 - h), axis=0)
                q_heads.append(q_h)
                g_heads.append(g_h)
                row_dot = jnp.sum(both[own, :], axis=0, keepdims=True)
                log_row = lse_t[0, h : h + 1, at]
                for j in range(b + 1):
                    keys = slice(j * BLOCK, (j + 1) * BLOCK)
                    scores = dot(k_s[keys, :], q_h, NT)
                    if j == b:
                        scores = scores + below[...]
                    probs = jnp.exp(scores - log_row)
                    grad_probs = dot(v_s[keys, :], g_h, NN)
                    p_all[keys, lanes] = probs.astype(BF16)
                    ds_all[keys, lanes] = (probs * (grad_probs - row_dot)).astype(BF16)
                dq_total += dot(ds_all[reach, lanes], k_s[reach, :], TN) * masks[h]
            dq_s[at, :] = dq_total * 0.125
            dv_s[reach, :] += dot(p_all[reach, :], jnp.concatenate(g_heads, axis=1), NT)
            dk_s[reach, :] += dot(ds_all[reach, :], jnp.concatenate(q_heads, axis=0), NN)

    @pl.when(step == 0)
    def _():
        dw_out[...] = jnp.zeros_like(dw_out)
        small_out[...] = jnp.zeros_like(small_out)

    for b in range(GROUPS):

        @pl.when(b < blocks)
        def _(b=b):
            start = b * BLOCK
            at = slice(start, start + BLOCK)
            for n, (pad, grad) in enumerate(((pad_q, dq_s), (pad_k, dk_s), (pad_v, dv_s))):
                now = grad[at, :]
                value = taps[3 * n : 3 * n + 1, :] * now
                for m in (1, 2):
                    value += taps[3 * n + m : 3 * n + m + 1, :] * grad[start + m : start + m + BLOCK, :]
                value = value.astype(BF16).astype(F32)
                d_all[b, n * COLS : (n + 1) * COLS, :] = jnp.transpose(value).astype(BF16)
                small_out[9 + n : 10 + n, 0:COLS] += jnp.sum(value, axis=0, keepdims=True)
                for m in range(3):
                    shifted = pad[8 + start - m : 8 + start - m + BLOCK, :]
                    small_out[3 * n + m : 3 * n + m + 1, 0:COLS] += jnp.sum(
                        shifted * now, axis=0, keepdims=True
                    )
            dw_out[...] += dot(d_all[b], normed[0, at, :], NN)

        @pl.when(b >= blocks)
        def _(b=b):
            d_all[b] = jnp.zeros((3 * COLS, BLOCK), BF16)

    far = lax.rem(here + 2, GROUPS)
    d_own[0] = d_all[here]
    d_next[0, 0 : 3 * COLS, :] = d_all[lax.rem(here + 1, GROUPS)]
    d_next[0, 3 * COLS :, :] = d_all[far, 0 : 3 * COLS // 2, :]
    d_prev[0, 0 : 3 * COLS, :] = d_all[lax.rem(here + 3, GROUPS)]
    d_prev[0, 3 * COLS :, :] = d_all[far, 3 * COLS // 2 :, :]

    @pl.when(step == SEQS - 1)
    def _():
        grad_bias = jnp.zeros((1, WIDTH), F32)
        for n in range(3):
            sums = small_out[9 + n : 10 + n, 0:COLS]
            high = sums.astype(BF16)
            rest = (sums - high.astype(F32)).astype(BF16)
            for term in (high, rest):
                wide = jnp.broadcast_to(term.astype(F32), (16, COLS)).astype(BF16)
                grad_bias += dot(wide, w_mine[n * COLS : (n + 1) * COLS, :], NN)[0:1, :]
        grad_normed = jnp.sum(w_mine[...].astype(F32) * dw_out[...], axis=0, keepdims=True)
        grad_gain = (grad_normed - bias[...] * grad_bias) / gain[...]
        pack[0 : 3 * COLS, :] = dw_out[...].astype(BF16)
        tail = jnp.concatenate(
            [
                small_out[0:9, :],
                grad_gain,
                grad_bias,
                ffn_vectors[0:2, :],
                jnp.zeros((3, WIDTH), F32),
            ],
            axis=0,
        )
        pack[3 * COLS : 3 * COLS + 16, :] = tail.astype(BF16)
        pack[3 * COLS + 16 :, :] = jnp.zeros((PACK_ROWS - 3 * COLS - 16, WIDTH), BF16)
        half = WIDTH // 2
        keep[...] = pack[:, pl.ds(pl.multiple_of(core * half, 128), half)]
        send[...] = pack[:, pl.ds(pl.multiple_of((1 - core) * half, 128), half)]


def attend_back(info, grad_mixed, saved, w_mine, taps, gain, bias, ffn_vectors):
    low = lambda *shape: jax.ShapeDtypeStruct(shape, BF16)
    whole = lambda *shape: pl.BlockSpec(shape, lambda i, sc: (0,) * len(shape))
    mine = lambda *shape: pl.BlockSpec((1, *shape), lambda i, sc: (i,) + (0,) * len(shape))
    across = pl.BlockSpec((GROUPS, COLS, BLOCK), lambda i, sc: (0, i, 0))
    long_rows = 3 * COLS * 3 // 2
    return pl.pallas_call(
        attend_back_kernel,
        grid_spec=pltpu.PrefetchScalarGridSpec(
            num_scalar_prefetch=1,
            grid=(SEQS,),
            in_specs=[
                pl.BlockSpec((GROUPS, COLS, BLOCK), lambda i, sc: (0, lax.rem(i + 2, SEQS), 0)),
                mine(FULL, WIDTH),
            ]
            + [mine(FULL, COLS)] * 3
            + [across, mine(8, FULL)]
            + [whole(3 * COLS, WIDTH), whole(9, COLS), whole(1, WIDTH), whole(1, WIDTH), whole(8, WIDTH)],
            out_specs=[mine(3 * COLS, BLOCK), mine(long_rows, BLOCK), mine(long_rows, BLOCK)]
            + [whole(PACK_ROWS, WIDTH // 2)] * 2,
            scratch_shapes=[
                pltpu.VMEM((3 * COLS, WIDTH), F32),
                pltpu.VMEM((16, WIDTH), F32),
                pltpu.VMEM((GROUPS, 3 * COLS, BLOCK), BF16),
                pltpu.VMEM((PACK_ROWS, WIDTH), BF16),
            ]
            + [pltpu.VMEM((FULL + 8, COLS), F32)] * 3
            + [pltpu.VMEM((FULL, COLS), BF16)] * 3
            + [pltpu.VMEM((FULL + 8, COLS), F32)] * 3
            + [pltpu.VMEM((BLOCK, BLOCK), F32)]
            + [pltpu.VMEM((FULL, HEADS_HERE * BLOCK), BF16)] * 2,
        ),
        out_shape=(
            low(SEQS, 3 * COLS, BLOCK), low(SEQS, long_rows, BLOCK), low(SEQS, long_rows, BLOCK),
            low(PACK_ROWS, WIDTH // 2), low(PACK_ROWS, WIDTH // 2),
        ),
        compiler_params=params(60),
        cost_estimate=cost(1e10, 2e7),
        name="attend_back",
    )(info, grad_mixed, *saved, w_mine, taps, gain, bias, ffn_vectors)


def heads_of(source, s):
    return jnp.concatenate([source[k, s * COLS : (s + 1) * COLS, :] for k in range(GROUPS)], axis=0)


def ffn_kernel(first, info, *refs):
    count = 1 if first else SEQS - 1
    base = 0 if first else 1
    x, cotangent, refs = refs[:count], refs[count : 2 * count], refs[2 * count :]
    mixed, w_out, gain, bias, w_up, w_down = refs[:6]
    refs = refs[6:]
    steps = FF // CHUNK
    if first:
        layer_output, grad_middle, grad_mixed, sq_out, gh_out, normed_of, low_of, branch, vectors = refs[:9]
        middle, total_out, total_grad = refs[9:]
        places = [slice(0, BLOCK)]
    else:
        mixed_first, branch_first, vectors_first, sq_first, gh_first, normed_first, low_first = refs[:7]
        layer_output, grad_middle, grad_mixed, grad_up, grad_down, grad_out, vectors = refs[8:15]
        middle, total_out, total_grad, normed_of, low_of, sq_all, gh_all, dw_out = refs[15:]
        places = [slice((s + 1) * BLOCK, (s + 2) * BLOCK) for s in range(count)]
    parts = [slice(s * BLOCK, (s + 1) * BLOCK) for s in range(count)]
    step = pl.program_id(0)
    position = info[0] * BLOCK + lax.broadcasted_iota(jnp.int32, (BLOCK, 1), 0)

    @pl.when(step == 0)
    def _():
        for s, (at, to) in enumerate(zip(parts, places)):
            value = x[s][0].astype(F32) + dot(heads_of(mixed, s), w_out[...], TN)
            middle[at, :] = value
            unit, _ = unit_rows(value)
            normed_of[to, :] = (unit * gain[...] + bias[...]).astype(BF16)
            keep_row = position < info[2 + base + s]
            low_of[to, :] = jnp.where(keep_row, cotangent[s][0].astype(F32), 0.0).astype(BF16)
            total_out[at, :] = jnp.zeros((BLOCK, WIDTH), F32)
            total_grad[at, :] = jnp.zeros((BLOCK, WIDTH), F32)
        if not first:
            normed_of[0:BLOCK, :] = normed_first[...]
            low_of[0:BLOCK, :] = low_first[...]

    def rows_of_chunk(put):
        to = slice(places[0].start, places[-1].stop)
        hidden = jnp.maximum(dot(normed_of[to, :], w_up[...], NN), 0.0)
        squared = (hidden * hidden).astype(BF16)
        back = dot(low_of[to, :], w_down[...], NT)
        grad_hidden = (back * 2.0 * hidden).astype(BF16)
        put(to, squared, grad_hidden)
        total_out[...] += dot(squared, w_down[...], NN)
        total_grad[...] += dot(grad_hidden, w_up[...], NT)

    def finish(s):
        at, to = parts[s], places[s]
        keep_row = position < info[2 + base + s]
        layer_output[s] = jnp.where(keep_row, middle[at, :] + total_out[at, :], 0.0).astype(BF16)
        unit, inverse = unit_rows(middle[at, :])
        grad_normed = total_grad[at, :]
        scaled = grad_normed * gain[...]
        mean_grad = jnp.mean(scaled, axis=-1, keepdims=True)
        mean_dot = jnp.mean(scaled * unit, axis=-1, keepdims=True)
        value = low_of[to, :].astype(F32) + inverse * (scaled - mean_grad - unit * mean_dot)
        vectors[0:1, :] += jnp.sum(grad_normed * unit, axis=0, keepdims=True)
        vectors[1:2, :] += jnp.sum(grad_normed, axis=0, keepdims=True)
        grad_middle[s] = value
        low = value.astype(BF16)
        heads_grad = dot(w_out[...], low, NT).astype(BF16)
        for k in range(GROUPS):
            grad_mixed[k, s * COLS : (s + 1) * COLS, :] = heads_grad[k * COLS : (k + 1) * COLS]
        return low

    if first:

        def put(to, squared, grad_hidden):
            sq_out[to, :] = squared
            gh_out[to, :] = grad_hidden

        rows_of_chunk(put)

        @pl.when(step == steps - 1)
        def _():
            vectors[...] = jnp.zeros_like(vectors)
            branch[...] = finish(0)

        return

    @pl.when(step < steps)
    def _():
        def put(to, squared, grad_hidden):
            sq_all[step, to, :] = squared
            gh_all[step, to, :] = grad_hidden

        rows_of_chunk(put)
        sq_all[step, 0:BLOCK, :] = sq_first[...]
        gh_all[step, 0:BLOCK, :] = gh_first[...]

    def weights_of_chunk(n):
        grad_up[...] = dot(gh_all[n], normed_of[...], TN).astype(BF16)
        grad_down[...] = dot(sq_all[n], low_of[...], TN).astype(BF16)

    @pl.when(step == steps)
    def _():
        vectors[...] = vectors_first[...]
        weights_of_chunk(0)
        low = finish(0)
        dw_out[...] = dot(heads_of(mixed_first, 0), branch_first[...], NN) + dot(heads_of(mixed, 0), low, NN)

    @pl.when(step == steps + 1)
    def _():
        weights_of_chunk(1)
        low = finish(1)
        dw_out[...] += dot(heads_of(mixed, 1), low, NN)

    @pl.when(step >= steps + 2)
    def _():
        weights_of_chunk(step - steps)
        grad_out[...] = dw_out[...].astype(BF16)


def ffn(first, info, x, cotangent, mixed, w_out, gain, bias, w_up, w_down, earlier=()):
    count = 1 if first else SEQS - 1
    base = 0 if first else 1
    low = lambda *shape: jax.ShapeDtypeStruct(shape, BF16)
    full = lambda *shape: jax.ShapeDtypeStruct(shape, F32)
    rows = count * BLOCK
    all_rows = SEQS * BLOCK
    steps = FF // CHUNK
    whole = lambda *shape: pl.BlockSpec(shape, lambda i, sc: (0,) * len(shape))
    nth = lambda s: pl.BlockSpec((1, BLOCK, WIDTH), lambda i, sc: (sc[5 + base + s], 0, 0))
    early = lambda i: jnp.minimum(i, steps - 1)
    late = lambda i: jnp.maximum(i - steps, 0)
    across = lambda n: pl.BlockSpec((n, CHUNK), lambda i, sc: (0, early(i)))
    grads = pl.BlockSpec((GROUPS, count * COLS, BLOCK), lambda i, sc: (0, SEQS - 1 if first else 0, 0))
    scratch = [pltpu.VMEM((rows, WIDTH), F32)] * 3
    if first:
        extra_specs = []
        out_specs = [across(rows)] * 2 + [whole(rows, WIDTH)] * 3 + [whole(8, WIDTH)]
        out_shape = [low(rows, FF)] * 2 + [low(rows, WIDTH)] * 3 + [full(8, WIDTH)]
        aliases = {}
    else:
        extra_specs = (
            [whole(GROUPS, COLS, BLOCK), whole(BLOCK, WIDTH), whole(8, WIDTH)]
            + [across(BLOCK)] * 2
            + [whole(BLOCK, WIDTH)] * 2
            + [pl.BlockSpec(memory_space=pl.ANY)]
        )
        out_specs = [
            pl.BlockSpec((CHUNK, WIDTH), lambda i, sc: (late(i), 0)),
            pl.BlockSpec((CHUNK, WIDTH), lambda i, sc: (late(i), 0)),
            whole(WIDTH, WIDTH),
            whole(8, WIDTH),
        ]
        out_shape = [low(FF, WIDTH), low(FF, WIDTH), low(WIDTH, WIDTH), full(8, WIDTH)]
        scratch += (
            [pltpu.VMEM((all_rows, WIDTH), BF16)] * 2
            + [pltpu.VMEM((steps, all_rows, CHUNK), BF16)] * 2
            + [pltpu.VMEM((WIDTH, WIDTH), F32)]
        )
        aliases = {1 + 2 * count + 6 + 7: 2}
    return pl.pallas_call(
        functools.partial(ffn_kernel, first),
        grid_spec=pltpu.PrefetchScalarGridSpec(
            num_scalar_prefetch=1,
            grid=(steps if first else 2 * steps,),
            in_specs=[nth(s) for s in range(count)] * 2
            + [
                whole(GROUPS, count * COLS, BLOCK), whole(WIDTH, WIDTH), whole(1, WIDTH), whole(1, WIDTH),
                across(WIDTH),
                pl.BlockSpec((CHUNK, WIDTH), lambda i, sc: (early(i), 0)),
            ]
            + extra_specs,
            out_specs=[whole(count, BLOCK, WIDTH), whole(count, BLOCK, WIDTH), grads] + out_specs,
            scratch_shapes=scratch,
        ),
        out_shape=[low(count, BLOCK, WIDTH), full(count, BLOCK, WIDTH), low(GROUPS, SEQS * COLS, BLOCK)] + out_shape,
        input_output_aliases=aliases,
        compiler_params=params(60),
        cost_estimate=cost(7e9 if first else 2.2e10, 2e7),
        name="ffn",
    )(info, *[x] * count, *[cotangent] * count, mixed, w_out, gain, bias, w_up, w_down, *earlier)


def input_kernel(
    info, x, middle_first, middle_others, output_first, output_others, own, behind, over, ahead, under, w_groups, gain,
    out, layer_output, grad_middle,
):
    @pl.when(pl.program_id(0) == 0)
    def _():
        grad_middle[...] = middle_first[0]
        layer_output[...] = output_first[...]

    @pl.when(pl.program_id(0) > 0)
    def _():
        grad_middle[...] = middle_others[0]
        layer_output[...] = output_others[...]

    here = info[0]
    w_of = lambda k: w_groups[lax.rem(here + k, GROUPS)]
    unit, inverse = unit_rows(x[0].astype(F32))
    grad_normed = dot(own[0], w_of(0), TN)
    grad_normed += dot(ahead[0], w_of(1), TN)
    grad_normed += dot(jnp.concatenate([over[0], under[0]], axis=0), w_of(2), TN)
    grad_normed += dot(behind[0], w_of(3), TN)
    scaled = grad_normed * gain[...]
    mean_grad = jnp.mean(scaled, axis=-1, keepdims=True)
    mean_dot = jnp.mean(scaled * unit, axis=-1, keepdims=True)
    out[0] = grad_middle[...] + inverse * (scaled - mean_grad - unit * mean_dot)


def input_grad_of(info, x, grad_middle, layer_output, pieces, w_groups, gain):
    mine = lambda rows, lanes: pl.BlockSpec((1, rows, lanes), lambda i, sc: (i, 0, 0))
    whole = lambda *shape: pl.BlockSpec(shape, lambda i, sc: (0,) * len(shape))
    placed = pl.BlockSpec((1, BLOCK, WIDTH), lambda i, sc: (sc[5 + i], 0, 0))
    two = [whole(1, BLOCK, WIDTH), pl.BlockSpec((1, BLOCK, WIDTH), lambda i, sc: (jnp.maximum(i - 1, 0), 0, 0))]
    piece = mine(3 * COLS, BLOCK)
    half = mine(3 * COLS // 2, BLOCK)
    return pl.pallas_call(
        input_kernel,
        grid_spec=pltpu.PrefetchScalarGridSpec(
            num_scalar_prefetch=1,
            grid=(SEQS,),
            in_specs=[placed, *two, *two, piece, piece, half, piece, half, whole(*w_groups.shape), whole(1, WIDTH)],
            out_specs=[placed, placed],
            scratch_shapes=[pltpu.VMEM((BLOCK, WIDTH), F32)],
        ),
        out_shape=(
            jax.ShapeDtypeStruct((SEQS, BLOCK, WIDTH), F32),
            jax.ShapeDtypeStruct((SEQS, BLOCK, WIDTH), BF16),
        ),
        compiler_params=params(60),
        cost_estimate=cost(3e9, 1.5e7),
        name="input_grad",
    )(info, x, *grad_middle, *layer_output, *pieces, w_groups, gain)


def place_kernel(up, down, out, grad_up, grad_down, grad_out):
    grad_up[...] = jnp.transpose(up[...].astype(F32))
    grad_down[...] = down[...].astype(F32)
    grad_out[...] = out[...].astype(F32)


def place(up, down, out):
    steps = FF // PLACE
    rows = lambda n: pl.BlockSpec((n, WIDTH), lambda i: (i, 0))
    specs = [rows(PLACE), rows(PLACE), rows(WIDTH // steps)]
    return pl.pallas_call(
        place_kernel,
        grid=(steps,),
        in_specs=specs,
        out_specs=[pl.BlockSpec((WIDTH, PLACE), lambda i: (0, i))] + specs[1:],
        out_shape=[jax.ShapeDtypeStruct(shape, F32) for shape in ((WIDTH, FF), down.shape, out.shape)],
        compiler_params=params(60),
        cost_estimate=cost(1e6, 3.2e7),
        name="place",
    )(up, down, out)


def unpack_kernel(info, own, other, grad_q, grad_k, grad_v, tails, rows):
    size = PACK_ROWS // 16
    half = WIDTH // 2

    def fill(pieces, base):
        for y in range(GROUPS):
            for n in range(16):
                rows[y, n * size : (n + 1) * size, base : base + half] = pieces[n * GROUPS + y].astype(F32)

    @pl.when(info[0] == 0)
    def _():
        fill(own, 0)
        fill(other, half)

    @pl.when(info[0] != 0)
    def _():
        fill(other, 0)
        fill(own, half)

    for n, grad in enumerate((grad_q, grad_k, grad_v)):
        part = jnp.concatenate([rows[y, n * COLS : (n + 1) * COLS, :] for y in range(GROUPS)], axis=0)
        grad[...] = jnp.transpose(part)
    for y in range(GROUPS):
        tails[y] = rows[y, 3 * COLS : 3 * COLS + 16, :]


def unpack(core, own, other):
    full = lambda *shape: jax.ShapeDtypeStruct(shape, F32)
    return pl.pallas_call(
        unpack_kernel,
        in_specs=[pl.BlockSpec(memory_space=pltpu.SMEM), vmem(), vmem()],
        out_specs=[vmem()] * 4,
        out_shape=(full(WIDTH, WIDTH), full(WIDTH, WIDTH), full(WIDTH, WIDTH), full(GROUPS, 16, WIDTH)),
        scratch_shapes=[pltpu.VMEM((GROUPS, PACK_ROWS, WIDTH), F32)],
        compiler_params=params(60),
        cost_estimate=cost(1e6, 1e5),
        name="unpack",
    )(core.reshape(1), own, other)


def shift(array, axis, by):
    return lax.ppermute(array, axis, [(i, (i + by) % GROUPS) for i in range(GROUPS)])


def near_rows(rows):
    return shift(rows, "head", -1), shift(rows, "head", 1)


def far_rows(rows, ahead, behind):
    return rows, ahead, shift(ahead[:128], "head", -1), shift(behind[128:], "head", 1), behind


def near_exchange(to_next, to_prev):
    return shift(to_next, "head", 1), shift(to_prev, "head", -1)


def far_exchange(from_prev, from_next, size):
    return shift(from_prev[:, size:], "head", 1), shift(from_next[:, size:], "head", -1)


def trade(array, axes):
    return lax.all_to_all(array, axes, 0, 0, tiled=True)


def swap_cores(array):
    return lax.ppermute(array, "core", [(0, 1), (1, 0)])


def add_low(*terms):
    total = terms[0].astype(F32)
    for term in terms[1:]:
        total = total + term.astype(F32)
    return total.astype(BF16)


def per_device(
    layer_input, lengths, cotangent, w_query, w_key, w_value, conv_query, conv_key, conv_value,
    w_out, w_up, w_down, gain_attn, bias_attn, gain_ffn, bias_ffn,
):
    here = lax.axis_index("head").astype(jnp.int32)
    core = lax.axis_index("core").astype(jnp.int32)
    first_rows, middle_rows, last_rows, info = prepare(lengths, layer_input)
    last_rows = lax.all_gather(last_rows, "head", axis=0, tiled=True)
    ahead, behind = near_rows(first_rows)
    ahead, behind, middle_rows = lax.optimization_barrier((ahead, behind, middle_rows))
    first_rows = far_rows(first_rows, ahead, behind)
    ahead, behind = near_rows(middle_rows)
    first_rows, ahead, behind = lax.optimization_barrier((first_rows, ahead, behind))
    middle_rows = far_rows(middle_rows, ahead, behind)

    w_groups = jnp.concatenate(
        [w.T.reshape(GROUPS, COLS, WIDTH) for w in (w_query, w_key, w_value)], axis=1
    )
    w_mine = lax.dynamic_index_in_dim(w_groups, here, 0, False)
    taps = lax.dynamic_slice_in_dim(
        jnp.concatenate([conv_query, conv_key, conv_value], axis=0), here * COLS, COLS, 1
    )
    gain_a, bias_a, gain_f, bias_f = (
        v.reshape(1, WIDTH) for v in (gain_attn, bias_attn, gain_ffn, bias_ffn)
    )
    *saved, mixed_first = attend(0, info, first_rows, w_mine, taps, gain_a, bias_a)
    mixed_first = trade(mixed_first, "head")
    *saved, mixed_others = attend(2, info, last_rows, w_mine, taps, gain_a, bias_a, saved)
    *saved, mixed_others = attend(1, info, middle_rows, w_mine, taps, gain_a, bias_a, (*saved, mixed_others))
    mixed_first, mixed_others = lax.optimization_barrier((mixed_first, mixed_others))
    mixed_others = trade(mixed_others, "head")
    weights = (w_out, gain_f, bias_f, w_up, w_down)
    output_a, middle_a, grad_a, *rows_a, branch_a, vectors_a = ffn(
        True, info, layer_input, cotangent, mixed_first, *weights
    )
    output_b, middle_b, grad_mixed, up, down, out, ffn_vectors = ffn(
        False, info, layer_input, cotangent, mixed_others, *weights,
        (mixed_first, branch_a, vectors_a, *rows_a, grad_a),
    )
    weight_sums = lax.psum((up, down, out), ("x", "z", "core", "head"))
    grad_mixed = trade(grad_mixed, "head")

    def attention_grads(grad_mixed, saved, grad_middle, layer_output, ffn_vectors):
        d_own, d_next, d_prev, keep, send = attend_back(
            info, grad_mixed, saved, w_mine, taps, gain_a, bias_a, ffn_vectors
        )
        behind, ahead = near_exchange(d_next, d_prev)

        part = add_low(keep, swap_cores(send)).reshape(16, PACK_ROWS // 16, WIDTH // 2)
        part = add_low(*trade(part, ("x", "z")))
        part, behind, ahead = lax.optimization_barrier((part, behind, ahead))
        over, under = far_exchange(behind, ahead, 3 * COLS)
        for axis in ("head", "z", "x"):
            if axis == "x":
                part, over, under = lax.optimization_barrier((part, over, under))
            part = trade(jnp.broadcast_to(part[None], (GROUPS, *part.shape)), axis)
        part = part.reshape(64, PACK_ROWS // 16, WIDTH // 2)
        input_grad, layer_output = input_grad_of(
            info, layer_input, grad_middle, layer_output, (d_own, behind, over, ahead, under), w_groups, gain_a
        )
        part, input_grad = lax.optimization_barrier((part, input_grad))
        grad_q, grad_k, grad_v, tails = unpack(core, part, swap_cores(part))
        conv = lambda n: jnp.transpose(tails[:, 3 * n : 3 * n + 3, 0:COLS], (1, 0, 2)).reshape(3, WIDTH)
        vector = jnp.sum(tails[:, 9:13, :], axis=0)
        return (
            layer_output, input_grad, grad_q, grad_k, grad_v, conv(0), conv(1), conv(2),
            vector[0], vector[1], vector[2], vector[3],
        )

    operands = (grad_mixed, saved, (middle_a, middle_b), (output_a, output_b), ffn_vectors)
    blank = lambda *args: jax.tree.map(
        lambda a: jnp.zeros(a.shape, a.dtype), jax.eval_shape(attention_grads, *args)
    )
    later = lax.cond(lengths[0] > 0, attention_grads, blank, *operands)
    weight_sums, later = lax.optimization_barrier((weight_sums, later))
    grad_up, grad_down, grad_out = place(*weight_sums)
    return (*later[:8], grad_out, grad_up, grad_down, *later[8:])


def solution(mesh):
    fine = Mesh(mesh.devices.reshape(4, 4, 2, GROUPS), ("x", "z", "core", "head"))
    dp = ("x", "z", "core")
    rows = P(dp, "head", None)
    return jax.shard_map(
        per_device,
        mesh=fine,
        in_specs=(rows, P(dp), rows) + (P(),) * 13,
        out_specs=(rows, rows) + (P(),) * 13,
        check_vma=False,
    )
```

```python
import functools

import jax
import jax.numpy as jnp
from jax import lax
from jax.experimental import pallas as pl
from jax.experimental.pallas import tpu as pltpu
from jax.sharding import Mesh
from jax.sharding import PartitionSpec as P

HDIM = 64
GROUPS = 4
BLOCK = 256
FULL = 1024
WIDTH = 768
COLS = 192
FF = 3072
SEQS = 3
CHUNK = 768
PLACE = 1024
HEADS_HERE = 3
PACK_ROWS = 640
F32 = jnp.float32
BF16 = jnp.bfloat16
NN = (((1,), (0,)), ((), ()))
NT = (((1,), (1,)), ((), ()))
TN = (((0,), (0,)), ((), ()))


def dot(left, right, dims):
    return lax.dot_general(left, right, dims, preferred_element_type=F32)


def cost(flops, nbytes, transcendentals=0):
    return pl.CostEstimate(
        flops=int(flops), bytes_accessed=int(nbytes), transcendentals=int(transcendentals)
    )


def vmem():
    return pl.BlockSpec(memory_space=pltpu.VMEM)


def params(mib):
    return pltpu.CompilerParams(vmem_limit_bytes=mib << 20)


def unit_rows(rows):
    average = jnp.mean(rows, axis=-1, keepdims=True)
    centred = rows - average
    variance = jnp.mean(centred * centred, axis=-1, keepdims=True)
    inverse = lax.rsqrt(variance + 1e-05)
    return centred * inverse, inverse


def head_masks():
    lane = lax.broadcasted_iota(jnp.int32, (1, COLS), 1)
    return [
        jnp.where((lane >= h * HDIM) & (lane < (h + 1) * HDIM), 1.0, 0.0).astype(F32)
        for h in range(HEADS_HERE)
    ]


def conv_rows(raw_f, taps, tap_row, start):
    total = taps[tap_row : tap_row + 1, :] * raw_f[8 + start : 8 + start + BLOCK, :]
    for m in (1, 2):
        total += (
            taps[tap_row + m : tap_row + m + 1, :]
            * raw_f[8 + start - m : 8 + start - m + BLOCK, :]
        )
    return total


def order_of(lengths):
    a, b, c = lengths[0], lengths[1], lengths[2]
    first = jnp.where((a >= b) & (a >= c), 0, jnp.where(b >= c, 1, 2)).astype(jnp.int32)
    second = jnp.where(first == 0, 1, 0).astype(jnp.int32)
    third = jnp.where(first == 2, 1, 2).astype(jnp.int32)
    return first, second, third


def prepare_kernel(lengths, row_0, row_1, row_2, first_rows, other_rows, info):
    first_rows[...] = row_0[0]
    other_rows[0] = row_1[0]
    other_rows[1] = row_2[0]
    info[0] = lax.axis_index("head").astype(jnp.int32)
    info[1] = lax.axis_index("core").astype(jnp.int32)
    a, b, c = lengths[0], lengths[1], lengths[2]
    for n, s in enumerate(order_of(lengths)):
        info[2 + n] = jnp.where(s == 0, a, jnp.where(s == 1, b, c))
        info[5 + n] = s


def prepare(lengths, rows):
    nth = lambda n: pl.BlockSpec((1, BLOCK, WIDTH), lambda i, sc: (order_of(sc)[n], 0, 0))
    whole = lambda *shape: pl.BlockSpec(shape, lambda i, sc: (0,) * len(shape))
    return pl.pallas_call(
        prepare_kernel,
        grid_spec=pltpu.PrefetchScalarGridSpec(
            num_scalar_prefetch=1,
            grid=(1,),
            in_specs=[nth(0), nth(1), nth(2)],
            out_specs=[
                whole(BLOCK, WIDTH), whole(SEQS - 1, BLOCK, WIDTH), pl.BlockSpec(memory_space=pltpu.SMEM)
            ],
        ),
        out_shape=(
            jax.ShapeDtypeStruct((BLOCK, WIDTH), BF16),
            jax.ShapeDtypeStruct((SEQS - 1, BLOCK, WIDTH), BF16),
            jax.ShapeDtypeStruct((8,), jnp.int32),
        ),
        compiler_params=params(60),
        cost_estimate=cost(1e3, 2.4e6),
        name="prepare",
    )(lengths, rows, rows, rows)


def attend_kernel(first, info, *refs):
    count = 5 if first else GROUPS
    pieces, refs = refs[:count], refs[count:]
    w_mine, taps, gain, bias = refs[:4]
    refs = refs[4:] if first else refs[10:]
    normed, raw_q, raw_k, raw_v, mixed, lse_t, to_rows = refs[:7]
    pad_q, pad_k, pad_v, q_s, k_s, v_s, below = refs[7:]
    here = info[0]
    length = info[2] if first else info[3 + pl.program_id(0)]
    blocks = (length + BLOCK - 1) // BLOCK
    masks = head_masks()
    if first:
        homes = [(lax.rem(here + ahead, GROUPS), shift) for ahead, shift in ((0, 0), (1, 0), (2, 0), (2, 128), (3, 0))]
    else:
        homes = [(k, 0) for k in range(GROUPS)]

    for piece, (home, shift) in zip(pieces, homes):

        @pl.when(home < blocks)
        def _(piece=piece, home=home, shift=shift):
            rows = piece[...].reshape(piece.shape[-2], WIDTH).astype(F32)
            size = rows.shape[0]
            unit, _ = unit_rows(rows)
            low = (unit * gain[...] + bias[...]).astype(BF16)
            at = home * BLOCK + shift
            at = pl.multiple_of(at, 128) if first else at
            normed[0, pl.ds(at, size), :] = low
            for n, (raw, pad) in enumerate(((raw_q, pad_q), (raw_k, pad_k), (raw_v, pad_v))):
                value = dot(low, w_mine[n * COLS : (n + 1) * COLS, :], NT).astype(BF16)
                raw[0, pl.ds(at, size), :] = value
                pad[pl.ds(at + 8, size), :] = value.astype(F32)

    for pad in (pad_q, pad_k, pad_v):
        pad[0:8, :] = jnp.zeros((8, COLS), F32)
    row = lax.broadcasted_iota(jnp.int32, (BLOCK, BLOCK), 0)
    col = lax.broadcasted_iota(jnp.int32, (BLOCK, BLOCK), 1)
    below[...] = jnp.where(col <= row, 0.0, -1e30).astype(F32)

    for b in range(GROUPS):

        @pl.when(b < blocks)
        def _(b=b):
            at = slice(b * BLOCK, (b + 1) * BLOCK)
            q_s[at, :] = (conv_rows(pad_q, taps, 0, b * BLOCK).astype(BF16).astype(F32) * 0.125).astype(BF16)
            k_s[at, :] = conv_rows(pad_k, taps, 3, b * BLOCK).astype(BF16)
            v_s[at, :] = conv_rows(pad_v, taps, 6, b * BLOCK).astype(BF16)
            lane = lax.broadcasted_iota(jnp.int32, (BLOCK, 128), 1)
            total_out = jnp.zeros((BLOCK, COLS), F32)
            logs = jnp.zeros((BLOCK, 128), F32)
            for h in range(HEADS_HERE):
                q_h = q_s[at, :] * masks[h].astype(BF16)
                diag = dot(q_h, k_s[at, :], NT) + below[...]
                top = jnp.max(diag, axis=-1, keepdims=True)
                if b:
                    left = dot(q_h, k_s[0 : b * BLOCK, :], NT)
                    top = jnp.maximum(top, jnp.max(left, axis=-1, keepdims=True))
                    expo_left = jnp.exp(left - top)
                expo = jnp.exp(diag - top)
                total = jnp.sum(expo, axis=-1, keepdims=True)
                out = dot(expo.astype(BF16), v_s[at, :], NN)
                if b:
                    total += jnp.sum(expo_left, axis=-1, keepdims=True)
                    out += dot(expo_left.astype(BF16), v_s[0 : b * BLOCK, :], NN)
                total_out = total_out + (out * masks[h]) * (1.0 / total)
                logs = jnp.where(lane == h, top + jnp.log(total), logs)
            result = jnp.transpose(total_out).astype(BF16)
            mixed[b] = result
            to_rows[b] = result
            lse_t[0, :, at] = jnp.transpose(logs)[0:8, :]

        @pl.when(b >= blocks)
        def _(b=b):
            mixed[b] = jnp.zeros((COLS, BLOCK), BF16)
            to_rows[b] = jnp.zeros((COLS, BLOCK), BF16)


def attend(first, info, pieces, w_mine, taps, gain, bias, earlier=()):
    base = 0 if first else 1
    whole = lambda *shape: pl.BlockSpec(shape, lambda i, sc: (0,) * len(shape))
    mine = lambda *shape: pl.BlockSpec((1, *shape), lambda i, sc: (base + i,) + (0,) * len(shape))
    if first:
        piece_specs = [whole(*p.shape) for p in pieces]
    else:
        piece_specs = [
            pl.BlockSpec((1, 1, BLOCK, WIDTH), lambda i, sc, k=k: (k, i, 0, 0)) for k in range(GROUPS)
        ]
        pieces = [pieces] * GROUPS
    full = lambda dtype, *shape: jax.ShapeDtypeStruct((SEQS, *shape), dtype)
    return pl.pallas_call(
        functools.partial(attend_kernel, first),
        grid_spec=pltpu.PrefetchScalarGridSpec(
            num_scalar_prefetch=1,
            grid=(1 if first else SEQS - 1,),
            in_specs=piece_specs
            + [whole(3 * COLS, WIDTH), whole(9, COLS), whole(1, WIDTH), whole(1, WIDTH)]
            + [pl.BlockSpec(memory_space=pl.ANY)] * len(earlier),
            out_specs=[mine(FULL, WIDTH)]
            + [mine(FULL, COLS)] * 3
            + [
                pl.BlockSpec((GROUPS, COLS, BLOCK), lambda i, sc: (0, base + i, 0)),
                mine(8, FULL),
                pl.BlockSpec((GROUPS, COLS, BLOCK), lambda i, sc: (0, i, 0)),
            ],
            scratch_shapes=[pltpu.VMEM((FULL + 8, COLS), F32)] * 3
            + [pltpu.VMEM((FULL, COLS), BF16)] * 3
            + [pltpu.VMEM((BLOCK, BLOCK), F32)],
        ),
        out_shape=(
            full(BF16, FULL, WIDTH),
            full(BF16, FULL, COLS), full(BF16, FULL, COLS), full(BF16, FULL, COLS),
            jax.ShapeDtypeStruct((GROUPS, SEQS * COLS, BLOCK), BF16),
            full(F32, 8, FULL),
            jax.ShapeDtypeStruct((GROUPS, (1 if first else SEQS - 1) * COLS, BLOCK), BF16),
        ),
        input_output_aliases={1 + len(pieces) + 4 + n: n for n in range(len(earlier))},
        compiler_params=params(60),
        cost_estimate=cost(3e9, 8e6, 2e6),
        name="attend",
    )(info, *pieces, w_mine, taps, gain, bias, *earlier)


def attend_back_kernel(
    info, g_s, normed, raw_q, raw_k, raw_v, mixed, lse_t,
    w_mine, taps, gain, bias, ffn_vectors,
    d_own, d_next, d_prev, keep, send,
    dw_out, small_out, d_all, pack,
    pad_q, pad_k, pad_v, q_s, k_s, v_s, dq_s, dk_s, dv_s, below, p_all, ds_all,
):
    step = pl.program_id(0)
    here, core, length = info[0], info[1], info[2 + step]

    blocks = (length + BLOCK - 1) // BLOCK
    masks = head_masks()

    row = lax.broadcasted_iota(jnp.int32, (BLOCK, BLOCK), 0)
    col = lax.broadcasted_iota(jnp.int32, (BLOCK, BLOCK), 1)
    below[...] = jnp.where(row <= col, 0.0, -1e30).astype(F32)
    for pad, raw in ((pad_q, raw_q), (pad_k, raw_k), (pad_v, raw_v)):
        pad[0:8, :] = jnp.zeros((8, COLS), F32)
    for total in (dq_s, dk_s, dv_s):
        total[...] = jnp.zeros((FULL + 8, COLS), F32)

    for b in range(GROUPS):

        @pl.when(b < blocks)
        def _(b=b):
            at = slice(b * BLOCK, (b + 1) * BLOCK)
            for pad, raw in ((pad_q, raw_q), (pad_k, raw_k), (pad_v, raw_v)):
                pad[8 + b * BLOCK : 8 + (b + 1) * BLOCK, :] = raw[0, at, :].astype(F32)
            q_s[at, :] = (conv_rows(pad_q, taps, 0, b * BLOCK).astype(BF16).astype(F32) * 0.125).astype(BF16)
            k_s[at, :] = conv_rows(pad_k, taps, 3, b * BLOCK).astype(BF16)
            v_s[at, :] = conv_rows(pad_v, taps, 6, b * BLOCK).astype(BF16)
            both = g_s[b].astype(F32) * mixed[b].astype(F32)
            reach = slice(0, (b + 1) * BLOCK)
            dq_total = jnp.zeros((BLOCK, COLS), F32)
            q_heads, g_heads = [], []
            for h in range(HEADS_HERE):
                lanes = slice(h * BLOCK, (h + 1) * BLOCK)
                q_h = q_s[at, :] * masks[h].astype(BF16)
                own = slice(h * HDIM, (h + 1) * HDIM)
                blank = lambda n: [jnp.zeros((n * HDIM, BLOCK), BF16)] if n else []
                g_h = jnp.concatenate(blank(h) + [g_s[b, own, :]] + blank(HEADS_HERE - 1 - h), axis=0)
                q_heads.append(q_h)
                g_heads.append(g_h)
                row_dot = jnp.sum(both[own, :], axis=0, keepdims=True)
                log_row = lse_t[0, h : h + 1, at]
                for j in range(b + 1):
                    keys = slice(j * BLOCK, (j + 1) * BLOCK)
                    scores = dot(k_s[keys, :], q_h, NT)
                    if j == b:
                        scores = scores + below[...]
                    probs = jnp.exp(scores - log_row)
                    grad_probs = dot(v_s[keys, :], g_h, NN)
                    p_all[keys, lanes] = probs.astype(BF16)
                    ds_all[keys, lanes] = (probs * (grad_probs - row_dot)).astype(BF16)
                dq_total += dot(ds_all[reach, lanes], k_s[reach, :], TN) * masks[h]
            dq_s[at, :] = dq_total * 0.125
            dv_s[reach, :] += dot(p_all[reach, :], jnp.concatenate(g_heads, axis=1), NT)
            dk_s[reach, :] += dot(ds_all[reach, :], jnp.concatenate(q_heads, axis=0), NN)

    @pl.when(step == 0)
    def _():
        dw_out[...] = jnp.zeros_like(dw_out)
        small_out[...] = jnp.zeros_like(small_out)

    for b in range(GROUPS):

        @pl.when(b < blocks)
        def _(b=b):
            start = b * BLOCK
            at = slice(start, start + BLOCK)
            for n, (pad, grad) in enumerate(((pad_q, dq_s), (pad_k, dk_s), (pad_v, dv_s))):
                now = grad[at, :]
                value = taps[3 * n : 3 * n + 1, :] * now
                for m in (1, 2):
                    value += taps[3 * n + m : 3 * n + m + 1, :] * grad[start + m : start + m + BLOCK, :]
                value = value.astype(BF16).astype(F32)
                d_all[b, n * COLS : (n + 1) * COLS, :] = jnp.transpose(value).astype(BF16)
                small_out[9 + n : 10 + n, 0:COLS] += jnp.sum(value, axis=0, keepdims=True)
                for m in range(3):
                    shifted = pad[8 + start - m : 8 + start - m + BLOCK, :]
                    small_out[3 * n + m : 3 * n + m + 1, 0:COLS] += jnp.sum(
                        shifted * now, axis=0, keepdims=True
                    )
            dw_out[...] += dot(d_all[b], normed[0, at, :], NN)

        @pl.when(b >= blocks)
        def _(b=b):
            d_all[b] = jnp.zeros((3 * COLS, BLOCK), BF16)

    far = lax.rem(here + 2, GROUPS)
    d_own[0] = d_all[here]
    d_next[0, 0 : 3 * COLS, :] = d_all[lax.rem(here + 1, GROUPS)]
    d_next[0, 3 * COLS :, :] = d_all[far, 0 : 3 * COLS // 2, :]
    d_prev[0, 0 : 3 * COLS, :] = d_all[lax.rem(here + 3, GROUPS)]
    d_prev[0, 3 * COLS :, :] = d_all[far, 3 * COLS // 2 :, :]

    @pl.when(step == SEQS - 1)
    def _():
        grad_bias = jnp.zeros((1, WIDTH), F32)
        for n in range(3):
            sums = small_out[9 + n : 10 + n, 0:COLS]
            high = sums.astype(BF16)
            rest = (sums - high.astype(F32)).astype(BF16)
            for term in (high, rest):
                wide = jnp.broadcast_to(term.astype(F32), (16, COLS)).astype(BF16)
                grad_bias += dot(wide, w_mine[n * COLS : (n + 1) * COLS, :], NN)[0:1, :]
        grad_normed = jnp.sum(w_mine[...].astype(F32) * dw_out[...], axis=0, keepdims=True)
        grad_gain = (grad_normed - bias[...] * grad_bias) / gain[...]
        pack[0 : 3 * COLS, :] = dw_out[...].astype(BF16)
        tail = jnp.concatenate(
            [
                small_out[0:9, :],
                grad_gain,
                grad_bias,
                ffn_vectors[0:2, :],
                jnp.zeros((3, WIDTH), F32),
            ],
            axis=0,
        )
        pack[3 * COLS : 3 * COLS + 16, :] = tail.astype(BF16)
        pack[3 * COLS + 16 :, :] = jnp.zeros((PACK_ROWS - 3 * COLS - 16, WIDTH), BF16)
        half = WIDTH // 2
        keep[...] = pack[:, pl.ds(pl.multiple_of(core * half, 128), half)]
        send[...] = pack[:, pl.ds(pl.multiple_of((1 - core) * half, 128), half)]


def attend_back(info, grad_mixed, saved, w_mine, taps, gain, bias, ffn_vectors):
    low = lambda *shape: jax.ShapeDtypeStruct(shape, BF16)
    whole = lambda *shape: pl.BlockSpec(shape, lambda i, sc: (0,) * len(shape))
    mine = lambda *shape: pl.BlockSpec((1, *shape), lambda i, sc: (i,) + (0,) * len(shape))
    across = pl.BlockSpec((GROUPS, COLS, BLOCK), lambda i, sc: (0, i, 0))
    long_rows = 3 * COLS * 3 // 2
    return pl.pallas_call(
        attend_back_kernel,
        grid_spec=pltpu.PrefetchScalarGridSpec(
            num_scalar_prefetch=1,
            grid=(SEQS,),
            in_specs=[
                pl.BlockSpec((GROUPS, COLS, BLOCK), lambda i, sc: (0, lax.rem(i + 2, SEQS), 0)),
                mine(FULL, WIDTH),
            ]
            + [mine(FULL, COLS)] * 3
            + [across, mine(8, FULL)]
            + [whole(3 * COLS, WIDTH), whole(9, COLS), whole(1, WIDTH), whole(1, WIDTH), whole(8, WIDTH)],
            out_specs=[mine(3 * COLS, BLOCK), mine(long_rows, BLOCK), mine(long_rows, BLOCK)]
            + [whole(PACK_ROWS, WIDTH // 2)] * 2,
            scratch_shapes=[
                pltpu.VMEM((3 * COLS, WIDTH), F32),
                pltpu.VMEM((16, WIDTH), F32),
                pltpu.VMEM((GROUPS, 3 * COLS, BLOCK), BF16),
                pltpu.VMEM((PACK_ROWS, WIDTH), BF16),
            ]
            + [pltpu.VMEM((FULL + 8, COLS), F32)] * 3
            + [pltpu.VMEM((FULL, COLS), BF16)] * 3
            + [pltpu.VMEM((FULL + 8, COLS), F32)] * 3
            + [pltpu.VMEM((BLOCK, BLOCK), F32)]
            + [pltpu.VMEM((FULL, HEADS_HERE * BLOCK), BF16)] * 2,
        ),
        out_shape=(
            low(SEQS, 3 * COLS, BLOCK), low(SEQS, long_rows, BLOCK), low(SEQS, long_rows, BLOCK),
            low(PACK_ROWS, WIDTH // 2), low(PACK_ROWS, WIDTH // 2),
        ),
        compiler_params=params(60),
        cost_estimate=cost(1e10, 2e7),
        name="attend_back",
    )(info, grad_mixed, *saved, w_mine, taps, gain, bias, ffn_vectors)


def heads_of(source, s):
    return jnp.concatenate([source[k, s * COLS : (s + 1) * COLS, :] for k in range(GROUPS)], axis=0)


def ffn_kernel(first, info, *refs):
    count = 1 if first else SEQS - 1
    base = 0 if first else 1
    x, cotangent, refs = refs[:count], refs[count : 2 * count], refs[2 * count :]
    mixed, w_out, gain, bias, w_up, w_down = refs[:6]
    refs = refs[6:]
    steps = FF // CHUNK
    if first:
        layer_output, grad_middle, grad_mixed, sq_out, gh_out, normed_of, low_of, branch, vectors = refs[:9]
        middle, total_out, total_grad = refs[9:]
        places = [slice(0, BLOCK)]
    else:
        mixed_first, branch_first, vectors_first, sq_first, gh_first, normed_first, low_first = refs[:7]
        layer_output, grad_middle, grad_mixed, grad_up, grad_down, grad_out, vectors = refs[8:15]
        middle, total_out, total_grad, normed_of, normed_t, low_of, sq_all, gh_all, dw_out = refs[15:]
        places = [slice((s + 1) * BLOCK, (s + 2) * BLOCK) for s in range(count)]
    parts = [slice(s * BLOCK, (s + 1) * BLOCK) for s in range(count)]
    step = pl.program_id(0)
    position = info[0] * BLOCK + lax.broadcasted_iota(jnp.int32, (BLOCK, 1), 0)

    @pl.when(step == 0)
    def _():
        for s, (at, to) in enumerate(zip(parts, places)):
            value = x[s][0].astype(F32) + dot(heads_of(mixed, s), w_out[...], TN)
            middle[at, :] = value
            unit, _ = unit_rows(value)
            normed_of[to, :] = (unit * gain[...] + bias[...]).astype(BF16)
            keep_row = position < info[2 + base + s]
            low_of[to, :] = jnp.where(keep_row, cotangent[s][0].astype(F32), 0.0).astype(BF16)
            total_out[at, :] = jnp.zeros((BLOCK, WIDTH), F32)
            total_grad[at, :] = jnp.zeros((BLOCK, WIDTH), F32)
        if not first:
            normed_of[0:BLOCK, :] = normed_first[...]
            low_of[0:BLOCK, :] = low_first[...]
            normed_t[...] = jnp.transpose(normed_of[...])

    def rows_of_chunk(put):
        to = slice(places[0].start, places[-1].stop)
        hidden = jnp.maximum(dot(normed_of[to, :], w_up[...], NN), 0.0)
        squared = (hidden * hidden).astype(BF16)
        back = dot(low_of[to, :], w_down[...], NT)
        grad_hidden = (back * 2.0 * hidden).astype(BF16)
        put(to, squared, grad_hidden)
        total_out[...] += dot(squared, w_down[...], NN)
        total_grad[...] += dot(grad_hidden, w_up[...], NT)

    def finish(s):
        at, to = parts[s], places[s]
        keep_row = position < info[2 + base + s]
        layer_output[s] = jnp.where(keep_row, middle[at, :] + total_out[at, :], 0.0).astype(BF16)
        unit, inverse = unit_rows(middle[at, :])
        grad_normed = total_grad[at, :]
        scaled = grad_normed * gain[...]
        mean_grad = jnp.mean(scaled, axis=-1, keepdims=True)
        mean_dot = jnp.mean(scaled * unit, axis=-1, keepdims=True)
        value = low_of[to, :].astype(F32) + inverse * (scaled - mean_grad - unit * mean_dot)
        vectors[0:1, :] += jnp.sum(grad_normed * unit, axis=0, keepdims=True)
        vectors[1:2, :] += jnp.sum(grad_normed, axis=0, keepdims=True)
        grad_middle[s] = value
        low = value.astype(BF16)
        heads_grad = dot(w_out[...], low, NT).astype(BF16)
        for k in range(GROUPS):
            grad_mixed[k, s * COLS : (s + 1) * COLS, :] = heads_grad[k * COLS : (k + 1) * COLS]
        return low

    if first:

        def put(to, squared, grad_hidden):
            sq_out[to, :] = squared
            gh_out[to, :] = grad_hidden

        rows_of_chunk(put)

        @pl.when(step == steps - 1)
        def _():
            vectors[...] = jnp.zeros_like(vectors)
            branch[...] = finish(0)

        return

    @pl.when(step < steps)
    def _():
        def put(to, squared, grad_hidden):
            sq_all[step, to, :] = squared
            gh_all[step, to, :] = grad_hidden

        rows_of_chunk(put)
        sq_all[step, 0:BLOCK, :] = sq_first[...]
        gh_all[step, 0:BLOCK, :] = gh_first[...]

    def weights_of_chunk(n):
        grad_up[...] = dot(normed_t[...], gh_all[n], NN).astype(BF16)
        grad_down[...] = dot(sq_all[n], low_of[...], TN).astype(BF16)

    @pl.when(step == steps)
    def _():
        vectors[...] = vectors_first[...]
        weights_of_chunk(0)
        low = finish(0)
        dw_out[...] = dot(heads_of(mixed_first, 0), branch_first[...], NN) + dot(heads_of(mixed, 0), low, NN)

    @pl.when(step == steps + 1)
    def _():
        weights_of_chunk(1)
        low = finish(1)
        dw_out[...] += dot(heads_of(mixed, 1), low, NN)

    @pl.when(step >= steps + 2)
    def _():
        weights_of_chunk(step - steps)
        grad_out[...] = dw_out[...].astype(BF16)


def ffn(first, info, x, cotangent, mixed, w_out, gain, bias, w_up, w_down, earlier=()):
    count = 1 if first else SEQS - 1
    base = 0 if first else 1
    low = lambda *shape: jax.ShapeDtypeStruct(shape, BF16)
    full = lambda *shape: jax.ShapeDtypeStruct(shape, F32)
    rows = count * BLOCK
    all_rows = SEQS * BLOCK
    steps = FF // CHUNK
    whole = lambda *shape: pl.BlockSpec(shape, lambda i, sc: (0,) * len(shape))
    nth = lambda s: pl.BlockSpec((1, BLOCK, WIDTH), lambda i, sc: (sc[5 + base + s], 0, 0))
    early = lambda i: jnp.minimum(i, steps - 1)
    late = lambda i: jnp.maximum(i - steps, 0)
    across = lambda n: pl.BlockSpec((n, CHUNK), lambda i, sc: (0, early(i)))
    grads = pl.BlockSpec((GROUPS, count * COLS, BLOCK), lambda i, sc: (0, SEQS - 1 if first else 0, 0))
    scratch = [pltpu.VMEM((rows, WIDTH), F32)] * 3
    if first:
        extra_specs = []
        out_specs = [across(rows)] * 2 + [whole(rows, WIDTH)] * 3 + [whole(8, WIDTH)]
        out_shape = [low(rows, FF)] * 2 + [low(rows, WIDTH)] * 3 + [full(8, WIDTH)]
        aliases = {}
    else:
        extra_specs = (
            [whole(GROUPS, COLS, BLOCK), whole(BLOCK, WIDTH), whole(8, WIDTH)]
            + [across(BLOCK)] * 2
            + [whole(BLOCK, WIDTH)] * 2
            + [pl.BlockSpec(memory_space=pl.ANY)]
        )
        out_specs = [
            pl.BlockSpec((WIDTH, CHUNK), lambda i, sc: (0, late(i))),
            pl.BlockSpec((CHUNK, WIDTH), lambda i, sc: (late(i), 0)),
            whole(WIDTH, WIDTH),
            whole(8, WIDTH),
        ]
        out_shape = [low(WIDTH, FF), low(FF, WIDTH), low(WIDTH, WIDTH), full(8, WIDTH)]
        scratch += (
            [pltpu.VMEM((all_rows, WIDTH), BF16), pltpu.VMEM((WIDTH, all_rows), BF16), pltpu.VMEM((all_rows, WIDTH), BF16)]
            + [pltpu.VMEM((steps, all_rows, CHUNK), BF16)] * 2
            + [pltpu.VMEM((WIDTH, WIDTH), F32)]
        )
        aliases = {1 + 2 * count + 6 + 7: 2}
    return pl.pallas_call(
        functools.partial(ffn_kernel, first),
        grid_spec=pltpu.PrefetchScalarGridSpec(
            num_scalar_prefetch=1,
            grid=(steps if first else 2 * steps,),
            in_specs=[nth(s) for s in range(count)] * 2
            + [
                whole(GROUPS, count * COLS, BLOCK), whole(WIDTH, WIDTH), whole(1, WIDTH), whole(1, WIDTH),
                across(WIDTH),
                pl.BlockSpec((CHUNK, WIDTH), lambda i, sc: (early(i), 0)),
            ]
            + extra_specs,
            out_specs=[whole(count, BLOCK, WIDTH), whole(count, BLOCK, WIDTH), grads] + out_specs,
            scratch_shapes=scratch,
        ),
        out_shape=[low(count, BLOCK, WIDTH), full(count, BLOCK, WIDTH), low(GROUPS, SEQS * COLS, BLOCK)] + out_shape,
        input_output_aliases=aliases,
        compiler_params=params(60),
        cost_estimate=cost(7e9 if first else 2.2e10, 2e7),
        name="ffn",
    )(info, *[x] * count, *[cotangent] * count, mixed, w_out, gain, bias, w_up, w_down, *earlier)


def input_kernel(
    info, x, middle_first, middle_others, output_first, output_others, own, behind, over, ahead, under, w_groups, gain,
    out, layer_output, grad_middle,
):
    @pl.when(pl.program_id(0) == 0)
    def _():
        grad_middle[...] = middle_first[0]
        layer_output[...] = output_first[...]

    @pl.when(pl.program_id(0) > 0)
    def _():
        grad_middle[...] = middle_others[0]
        layer_output[...] = output_others[...]

    here = info[0]
    w_of = lambda k: w_groups[lax.rem(here + k, GROUPS)]
    unit, inverse = unit_rows(x[0].astype(F32))
    grad_normed = dot(own[0], w_of(0), TN)
    grad_normed += dot(ahead[0], w_of(1), TN)
    grad_normed += dot(jnp.concatenate([over[0], under[0]], axis=0), w_of(2), TN)
    grad_normed += dot(behind[0], w_of(3), TN)
    scaled = grad_normed * gain[...]
    mean_grad = jnp.mean(scaled, axis=-1, keepdims=True)
    mean_dot = jnp.mean(scaled * unit, axis=-1, keepdims=True)
    out[0] = grad_middle[...] + inverse * (scaled - mean_grad - unit * mean_dot)


def input_grad_of(info, x, grad_middle, layer_output, pieces, w_groups, gain):
    mine = lambda rows, lanes: pl.BlockSpec((1, rows, lanes), lambda i, sc: (i, 0, 0))
    whole = lambda *shape: pl.BlockSpec(shape, lambda i, sc: (0,) * len(shape))
    placed = pl.BlockSpec((1, BLOCK, WIDTH), lambda i, sc: (sc[5 + i], 0, 0))
    two = [whole(1, BLOCK, WIDTH), pl.BlockSpec((1, BLOCK, WIDTH), lambda i, sc: (jnp.maximum(i - 1, 0), 0, 0))]
    piece = mine(3 * COLS, BLOCK)
    half = mine(3 * COLS // 2, BLOCK)
    return pl.pallas_call(
        input_kernel,
        grid_spec=pltpu.PrefetchScalarGridSpec(
            num_scalar_prefetch=1,
            grid=(SEQS,),
            in_specs=[placed, *two, *two, piece, piece, half, piece, half, whole(*w_groups.shape), whole(1, WIDTH)],
            out_specs=[placed, placed],
            scratch_shapes=[pltpu.VMEM((BLOCK, WIDTH), F32)],
        ),
        out_shape=(
            jax.ShapeDtypeStruct((SEQS, BLOCK, WIDTH), F32),
            jax.ShapeDtypeStruct((SEQS, BLOCK, WIDTH), BF16),
        ),
        compiler_params=params(60),
        cost_estimate=cost(3e9, 1.5e7),
        name="input_grad",
    )(info, x, *grad_middle, *layer_output, *pieces, w_groups, gain)


def place_kernel(up, down, out, grad_up, grad_down, grad_out):
    grad_up[...] = up[...].astype(F32)
    grad_down[...] = down[...].astype(F32)
    grad_out[...] = out[...].astype(F32)


def place(up, down, out):
    steps = FF // PLACE
    rows = lambda n: pl.BlockSpec((n, WIDTH), lambda i: (i, 0))
    specs = [pl.BlockSpec((WIDTH, PLACE), lambda i: (0, i)), rows(PLACE), rows(WIDTH // steps)]
    return pl.pallas_call(
        place_kernel,
        grid=(steps,),
        in_specs=specs,
        out_specs=specs,
        out_shape=[jax.ShapeDtypeStruct(a.shape, F32) for a in (up, down, out)],
        compiler_params=params(60),
        cost_estimate=cost(1e6, 3.2e7),
        name="place",
    )(up, down, out)


def unpack_kernel(info, own, other, grad_q, grad_k, grad_v, tails, rows):
    size = PACK_ROWS // 16
    half = WIDTH // 2

    def fill(pieces, base):
        for y in range(GROUPS):
            for n in range(16):
                rows[y, n * size : (n + 1) * size, base : base + half] = pieces[n * GROUPS + y].astype(F32)

    @pl.when(info[0] == 0)
    def _():
        fill(own, 0)
        fill(other, half)

    @pl.when(info[0] != 0)
    def _():
        fill(other, 0)
        fill(own, half)

    for n, grad in enumerate((grad_q, grad_k, grad_v)):
        part = jnp.concatenate([rows[y, n * COLS : (n + 1) * COLS, :] for y in range(GROUPS)], axis=0)
        grad[...] = jnp.transpose(part)
    for y in range(GROUPS):
        tails[y] = rows[y, 3 * COLS : 3 * COLS + 16, :]


def unpack(core, own, other):
    full = lambda *shape: jax.ShapeDtypeStruct(shape, F32)
    return pl.pallas_call(
        unpack_kernel,
        in_specs=[pl.BlockSpec(memory_space=pltpu.SMEM), vmem(), vmem()],
        out_specs=[vmem()] * 4,
        out_shape=(full(WIDTH, WIDTH), full(WIDTH, WIDTH), full(WIDTH, WIDTH), full(GROUPS, 16, WIDTH)),
        scratch_shapes=[pltpu.VMEM((GROUPS, PACK_ROWS, WIDTH), F32)],
        compiler_params=params(60),
        cost_estimate=cost(1e6, 1e5),
        name="unpack",
    )(core.reshape(1), own, other)


def shift(array, axis, by):
    return lax.ppermute(array, axis, [(i, (i + by) % GROUPS) for i in range(GROUPS)])


def gather_rows(rows):
    ahead = shift(rows, "head", -1)
    behind = shift(rows, "head", 1)
    over_lo = shift(ahead[:128], "head", -1)
    over_hi = shift(behind[128:], "head", 1)
    return rows, ahead, over_lo, over_hi, behind


def near_exchange(to_next, to_prev):
    return shift(to_next, "head", 1), shift(to_prev, "head", -1)


def far_exchange(from_prev, from_next, size):
    return shift(from_prev[:, size:], "head", 1), shift(from_next[:, size:], "head", -1)


def trade(array, axes):
    return lax.all_to_all(array, axes, 0, 0, tiled=True)


def swap_cores(array):
    return lax.ppermute(array, "core", [(0, 1), (1, 0)])


def add_low(*terms):
    total = terms[0].astype(F32)
    for term in terms[1:]:
        total = total + term.astype(F32)
    return total.astype(BF16)


def per_device(
    layer_input, lengths, cotangent, w_query, w_key, w_value, conv_query, conv_key, conv_value,
    w_out, w_up, w_down, gain_attn, bias_attn, gain_ffn, bias_ffn,
):
    here = lax.axis_index("head").astype(jnp.int32)
    core = lax.axis_index("core").astype(jnp.int32)
    first_rows, other_rows, info = prepare(lengths, layer_input)
    first_rows = gather_rows(first_rows)
    other_rows = lax.all_gather(other_rows, "head", axis=0)

    w_groups = jnp.concatenate(
        [w.T.reshape(GROUPS, COLS, WIDTH) for w in (w_query, w_key, w_value)], axis=1
    )
    w_mine = lax.dynamic_index_in_dim(w_groups, here, 0, False)
    taps = lax.dynamic_slice_in_dim(
        jnp.concatenate([conv_query, conv_key, conv_value], axis=0), here * COLS, COLS, 1
    )
    gain_a, bias_a, gain_f, bias_f = (
        v.reshape(1, WIDTH) for v in (gain_attn, bias_attn, gain_ffn, bias_ffn)
    )
    *saved, mixed_first = attend(True, info, first_rows, w_mine, taps, gain_a, bias_a)
    mixed_first = trade(mixed_first, "head")
    *saved, mixed_others = attend(False, info, other_rows, w_mine, taps, gain_a, bias_a, saved)
    mixed_first, mixed_others = lax.optimization_barrier((mixed_first, mixed_others))
    mixed_others = trade(mixed_others, "head")
    weights = (w_out, gain_f, bias_f, w_up, w_down)
    output_a, middle_a, grad_a, *rows_a, branch_a, vectors_a = ffn(
        True, info, layer_input, cotangent, mixed_first, *weights
    )
    output_b, middle_b, grad_mixed, up, down, out, ffn_vectors = ffn(
        False, info, layer_input, cotangent, mixed_others, *weights,
        (mixed_first, branch_a, vectors_a, *rows_a, grad_a),
    )
    weight_sums = lax.psum((up, down, out), ("x", "z", "core", "head"))
    grad_mixed = trade(grad_mixed, "head")

    def attention_grads(grad_mixed, saved, grad_middle, layer_output, ffn_vectors):
        d_own, d_next, d_prev, keep, send = attend_back(
            info, grad_mixed, saved, w_mine, taps, gain_a, bias_a, ffn_vectors
        )
        behind, ahead = near_exchange(d_next, d_prev)

        part = add_low(keep, swap_cores(send)).reshape(16, PACK_ROWS // 16, WIDTH // 2)
        part = add_low(*trade(part, ("x", "z")))
        part, behind, ahead = lax.optimization_barrier((part, behind, ahead))
        over, under = far_exchange(behind, ahead, 3 * COLS)
        for axis in ("head", "z", "x"):
            if axis == "x":
                part, over, under = lax.optimization_barrier((part, over, under))
            part = trade(jnp.broadcast_to(part[None], (GROUPS, *part.shape)), axis)
        part = part.reshape(64, PACK_ROWS // 16, WIDTH // 2)
        input_grad, layer_output = input_grad_of(
            info, layer_input, grad_middle, layer_output, (d_own, behind, over, ahead, under), w_groups, gain_a
        )
        part, input_grad = lax.optimization_barrier((part, input_grad))
        grad_q, grad_k, grad_v, tails = unpack(core, part, swap_cores(part))
        conv = lambda n: jnp.transpose(tails[:, 3 * n : 3 * n + 3, 0:COLS], (1, 0, 2)).reshape(3, WIDTH)
        vector = jnp.sum(tails[:, 9:13, :], axis=0)
        return (
            layer_output, input_grad, grad_q, grad_k, grad_v, conv(0), conv(1), conv(2),
            vector[0], vector[1], vector[2], vector[3],
        )

    operands = (grad_mixed, saved, (middle_a, middle_b), (output_a, output_b), ffn_vectors)
    blank = lambda *args: jax.tree.map(
        lambda a: jnp.zeros(a.shape, a.dtype), jax.eval_shape(attention_grads, *args)
    )
    later = lax.cond(lengths[0] > 0, attention_grads, blank, *operands)
    weight_sums, later = lax.optimization_barrier((weight_sums, later))
    grad_up, grad_down, grad_out = place(*weight_sums)
    return (*later[:8], grad_out, grad_up, grad_down, *later[8:])


def solution(mesh):
    fine = Mesh(mesh.devices.reshape(4, 4, 2, GROUPS), ("x", "z", "core", "head"))
    dp = ("x", "z", "core")
    rows = P(dp, "head", None)
    return jax.shard_map(
        per_device,
        mesh=fine,
        in_specs=(rows, P(dp), rows) + (P(),) * 13,
        out_specs=(rows, rows) + (P(),) * 13,
        check_vma=False,
    )
```
